128 devices in a mesh: dp: 16 (over y_lo, x, core), tensor: 8 (over y_hi, z).
Axes of the slice: x: 4, y: 4 (y_hi: 2, y_lo: 2; y = y_hi * 2 + y_lo), z: 4, core: 2. Of those that a mesh axis runs over, the one named last changes fastest.
Arguments:
- tokens: bfloat16 [32768, 1536], P(('dp', 'tensor')), may hold values from -6 to 6
- norm_gain: float32 [1536], replicated, may hold values from 0.5 to 1.5
- w_gate: bfloat16 [1536, 3072], P('dp', 'tensor'), may hold values from -0.15625 to 0.15625
- w_inner: bfloat16 [1536, 3072], P('dp', 'tensor'), may hold values from -0.15625 to 0.15625
- w_bc: bfloat16 [1536, 256], P('dp'), may hold values from -0.15625 to 0.15625
- w_step: bfloat16 [1536, 48], P('dp', 'tensor'), may hold values from -0.15625 to 0.15625
- conv_inner: float32 [4, 3072], P(None, 'tensor'), may hold values from -3 to 3
- bias_inner: float32 [3072], P('tensor'), may hold values from -3 to 3
- conv_bc: float32 [4, 256], replicated, may hold values from -3 to 3
- bias_bc: float32 [256], replicated, may hold values from -3 to 3
- step_bias: float32 [48], P('tensor'), may hold values from -5 to -1
- decay_log: float32 [48], P('tensor'), may hold values from -2 to 2.5
- skip_gain: float32 [48], P('tensor'), may hold values from 0.5 to 1.5
- gate_gain: float32 [3072], P('tensor'), may hold values from 0.5 to 1.5
- w_out: bfloat16 [1536, 3072], P('dp', 'tensor'), may hold values from -0.109375 to 0.109375
- cotangent: bfloat16 [32768, 1536], P(('dp', 'tensor')), may hold values from -6 to 6
Outputs:
- output: bfloat16 [32768, 1536], P(('dp', 'tensor'))
- tokens_grad: float32 [32768, 1536], P(('dp', 'tensor'))
- norm_gain_grad: float32 [1536], replicated
- w_gate_grad: float32 [1536, 3072], P('dp', 'tensor')
- w_inner_grad: float32 [1536, 3072], P('dp', 'tensor')
- w_bc_grad: float32 [1536, 256], P('dp')
- w_step_grad: float32 [1536, 48], P('dp', 'tensor')
- conv_inner_grad: float32 [4, 3072], P(None, 'tensor')
- bias_inner_grad: float32 [3072], P('tensor')
- conv_bc_grad: float32 [4, 256], replicated
- bias_bc_grad: float32 [256], replicated
- step_bias_grad: float32 [48], P('tensor')
- decay_log_grad: float32 [48], P('tensor')
- skip_gain_grad: float32 [48], P('tensor')
- gate_gain_grad: float32 [3072], P('tensor')
- w_out_grad: float32 [1536, 3072], P('dp', 'tensor')
The draws below stay inside these ranges and needn't reach their ends.
All inputs are finite; a program needn't handle non-finite values.
Results may differ from the reference program's by a relative error of at most 0.012.
Values may be sent and summed in bfloat16 or wider, within the bound.
A program may use at most 192 MiB of HBM per device.

```python
import jax
import jax.numpy as jnp
from jax import lax

D = 1536
HEADS = 48
HEAD_DIM = 64
STATE = 128
CONV = 4
BLOCK = 256
LEN = 1024
SEQ = 2
INNER = 3072
TOKENS = 32768
N_DP = 16


def block_scale(stream_key, shape, cuts, least, largest):
    level = 1.0
    for axis_at, parts in cuts:
        draws = jax.random.uniform(jax.random.fold_in(jax.random.fold_in(stream_key, 6), axis_at), (parts,), jnp.float32, least / len(cuts), largest / len(cuts))
        level = level * jnp.repeat(jnp.exp(draws), shape[axis_at] // parts).reshape((-1,) + (1,) * (len(shape) - 1 - axis_at))
    return level


def scatter_about(own_key, extent, deviation, reach, shards=(), held_as=jnp.bfloat16):
    drawn = deviation * jax.random.normal(own_key, extent, jnp.float32)
    if shards:
        drawn = drawn * block_scale(own_key, extent, shards, -0.22, 0.18)
    return jnp.clip(drawn, -reach, reach).astype(held_as)


def setup_inputs(seed: int = 0) -> dict:
    splits = jax.random.split(jax.random.key(seed), 17)
    return {
        "tokens": scatter_about(splits[0], (TOKENS, D), 1.0, 6.0, ((0, 128),)),
        "norm_gain": jnp.clip(1.0 + 0.1 * jax.random.normal(splits[1], (D,), jnp.float32), 0.5, 1.5),
        "w_gate": scatter_about(splits[2], (D, INNER), D ** -0.5, 0.15625, ((0, 16), (1, 8))),
        "w_inner": scatter_about(splits[3], (D, INNER), D ** -0.5, 0.15625, ((0, 16), (1, 8))),
        "w_bc": scatter_about(splits[4], (D, 2 * STATE), D ** -0.5, 0.15625, ((0, 16),)),
        "w_step": scatter_about(splits[5], (D, HEADS), D ** -0.5, 0.15625, ((0, 16), (1, 8))),
        "conv_inner": scatter_about(splits[6], (CONV, INNER), CONV ** -0.5, 3.0, ((1, 8),), jnp.float32),
        "bias_inner": scatter_about(splits[7], (INNER,), 0.5, 3.0, ((0, 8),), jnp.float32),
        "conv_bc": scatter_about(splits[8], (CONV, 2 * STATE), CONV ** -0.5, 3.0, (), jnp.float32),
        "bias_bc": scatter_about(splits[9], (2 * STATE,), 0.5, 3.0, (), jnp.float32),
        "step_bias": jnp.clip(-5.0 + 4.0 * jax.random.uniform(splits[10], (HEADS,), jnp.float32) ** block_scale(splits[10], (HEADS,), ((0, 8),), -0.2, 0.2), -5.0, -1.0),
        "decay_log": jnp.clip(-2.0 + 4.5 * jax.random.uniform(splits[11], (HEADS,), jnp.float32) ** block_scale(splits[11], (HEADS,), ((0, 8),), -0.2, 0.2), -2.0, 2.5),
        "skip_gain": jnp.clip(0.5 + 1.0 * jax.random.uniform(splits[12], (HEADS,), jnp.float32) ** block_scale(splits[12], (HEADS,), ((0, 8),), -0.2, 0.2), 0.5, 1.5),
        "gate_gain": jnp.clip(1.0 + 0.1 * jax.random.normal(splits[13], (INNER,), jnp.float32), 0.5, 1.5),
        "w_out": scatter_about(splits[14], (D, INNER), INNER ** -0.5, 0.109375, ((0, 16), (1, 8))),
        "cotangent": scatter_about(splits[15], (TOKENS, D), 1.0, 6.0, ((0, 128),)),
    }


@jax.custom_vjp
def low(v):
    return lax.optimization_barrier(v.astype(jnp.bfloat16)).astype(jnp.float32)

@jax.custom_vjp
def low_back(v):
    return v

def low_keep(v):
    return (low(v), None)

def low_pass(kept, grad):
    return (grad,)

def back_keep(v):
    return (v, None)

def back_low(kept, grad):
    return (low(grad),)
low.defvjp(low_keep, low_pass)
low_back.defvjp(back_keep, back_low)
epsilon = 1e-05
highest = lax.Precision.HIGHEST

def causal_conv(values, weight, shift_bias):
    kernel_taps = weight.shape[0]
    padded = jnp.pad(values, ((0, 0), (kernel_taps - 1, 0), (0, 0)))
    summed = jnp.zeros_like(values) + shift_bias
    for offset in range(kernel_taps):
        summed = summed + weight[offset] * padded[:, offset:offset + values.shape[1], :]
    return jax.nn.silu(summed)

def block_scan(inputs, b_proj, c_proj, step_sizes, decay_rate, skip_gain):
    length, head_count, head_width = inputs.shape
    blocks = length // BLOCK
    step_logs = (step_sizes * decay_rate).reshape(blocks, BLOCK, head_count).transpose(0, 2, 1)
    running = jnp.cumsum(step_logs, axis=2)
    weighted = (inputs * step_sizes[:, :, None]).reshape(blocks, BLOCK, head_count, head_width)
    b_block = b_proj.reshape(blocks, BLOCK, -1)
    c_block = c_proj.reshape(blocks, BLOCK, -1)
    scores = jnp.einsum('ktn,ksn->kts', c_block, b_block, precision=highest)
    causal = jnp.arange(BLOCK)[:, None] >= jnp.arange(BLOCK)[None, :]
    log_gaps = running[:, :, :, None] - running[:, :, None, :]
    decays = jnp.where(causal, jnp.exp(jnp.where(causal, log_gaps, 0.0)), 0.0)
    mixing = decays * scores[:, None, :, :]
    within = jnp.einsum('khts,kshp->kthp', mixing, weighted, precision=highest)
    to_end = jnp.exp(running[:, :, -1:] - running)
    states = jnp.einsum('khs,kshp,ksn->khpn', to_end, weighted, b_block, precision=highest)
    factors = jnp.exp(running[:, :, -1])

    def carry_step(carried, block_in):
        block_state, factor = block_in
        return (carried * factor[:, None, None] + block_state, carried)
    start_state = jnp.zeros((head_count, head_width, b_proj.shape[1]), jnp.float32)
    _, entering = lax.scan(carry_step, start_state, (states, factors))
    across = jnp.einsum('ktn,khpn,kht->kthp', c_block, entering, jnp.exp(running), precision=highest)
    result = within + across + skip_gain[None, None, :, None] * inputs.reshape(blocks, BLOCK, head_count, head_width)
    return result.reshape(length, head_count, head_width)

def local_mixer(inner_in, step_in, conv_inner, bias_inner, step_bias, decay_log, skip_gain, b_proj, c_proj):
    sequences = inner_in.shape[0] // LEN
    head_count = step_in.shape[1]
    inner_conv = causal_conv(inner_in.reshape(sequences, LEN, -1), conv_inner, bias_inner)
    step_sizes = jax.nn.softplus(step_in.reshape(sequences, LEN, head_count) + step_bias)
    decay_rate = -jnp.exp(decay_log)
    scanned = jax.vmap(block_scan, in_axes=(0, 0, 0, 0, None, None))(inner_conv.reshape(sequences, LEN, head_count, HEAD_DIM), b_proj, c_proj, step_sizes, decay_rate, skip_gain)
    return scanned.reshape(inner_in.shape[0], -1)

def bc_branch(bc_in, conv_bc, bias_bc):
    sequences = bc_in.shape[0] // LEN
    bc_conv = causal_conv(bc_in.reshape(sequences, LEN, -1), conv_bc, bias_bc)
    return (bc_conv[:, :, :STATE], bc_conv[:, :, STATE:])

def layer_forward(residual, norm_gain, w_gate, w_inner, w_bc, w_step, conv_inner, bias_inner, conv_bc, bias_bc, step_bias, decay_log, skip_gain, gate_gain, w_out):
    inv_root = lax.rsqrt(lax.optimization_barrier(jnp.mean(residual * residual, axis=1, keepdims=True)) + epsilon)
    normed = low(residual * inv_root * norm_gain)
    gate_in = low_back(jnp.dot(normed, w_gate, precision=highest))
    inner_in = low_back(jnp.dot(normed, w_inner, precision=highest))
    bc_in = low_back(jnp.dot(normed, w_bc, precision=highest))
    step_in = low_back(jnp.dot(normed, w_step, precision=highest))
    b_proj, c_proj = bc_branch(bc_in, conv_bc, bias_bc)
    scanned = local_mixer(inner_in, step_in, conv_inner, bias_inner, step_bias, decay_log, skip_gain, b_proj, c_proj)
    gate_prod = scanned * jax.nn.silu(gate_in)
    inner_root = lax.rsqrt(lax.optimization_barrier(jnp.mean(gate_prod * gate_prod, axis=1, keepdims=True)) + epsilon)
    mixed_out = low(gate_prod * inner_root * gate_gain)
    return residual + jnp.dot(mixed_out, w_out.T, precision=highest)

def reference(tokens, norm_gain, w_gate, w_inner, w_bc, w_step, conv_inner, bias_inner, conv_bc, bias_bc, step_bias, decay_log, skip_gain, gate_gain, w_out, cotangent):
    weights = tuple((weight_arg.astype(jnp.float32) for weight_arg in (norm_gain, w_gate, w_inner, w_bc, w_step, conv_inner, bias_inner, conv_bc, bias_bc, step_bias, decay_log, skip_gain, gate_gain, w_out)))
    groups = tokens.astype(jnp.float32).reshape(N_DP, SEQ * LEN, D)
    cot_groups = cotangent.astype(jnp.float32).reshape(N_DP, SEQ * LEN, D)

    def one_group(totals, paired):
        rows_in, cot_in = paired
        result, pullback = jax.vjp(layer_forward, rows_in, *weights)
        all_grads = pullback(cot_in)
        updated = tuple((running + update for running, update in zip(totals, all_grads[1:])))
        return (updated, (result.astype(jnp.bfloat16), all_grads[0]))
    start_totals = tuple((jnp.zeros_like(weight_arg) for weight_arg in weights))
    totals, (outputs, input_grads) = lax.scan(one_group, start_totals, (groups, cot_groups))
    grad_norm, grad_gate, grad_inner, grad_bc, grad_step, grad_conv_inner, grad_bias_inner, grad_conv_bc, grad_bias_bc, grad_step_bias, grad_decay, grad_skip, grad_gate_gain, grad_out = totals
    return (outputs.reshape(TOKENS, D), input_grads.reshape(TOKENS, D), grad_norm, grad_gate, grad_inner, grad_bc, grad_step, grad_conv_inner, grad_bias_inner, grad_conv_bc, grad_bias_bc, grad_step_bias, grad_decay, grad_skip, grad_gate_gain, grad_out)
```

```python
import functools

import jax
import jax.numpy as jnp
from jax import lax
from jax.experimental import pallas as pl
from jax.experimental.pallas import tpu as pltpu
from jax.sharding import Mesh
from jax.sharding import PartitionSpec as P

D = 1536
LEN = 1024
INNER = 3072
STATE = 128
BLOCK = 256
BLOCKS = LEN // BLOCK
GROUPS = 2
HEADS = 6
COLS = HEADS * 64
LOG2E = 1.4426950408889634
EPS = 1e-05
F32 = jnp.float32
BF16 = jnp.bfloat16
MESH = pl.DeviceIdType.MESH
AXES = ("yl", "x", "c", "yh", "z")
ANY = pl.BlockSpec(memory_space=pl.ANY)


def dot(a, b):
    return jnp.dot(a, b, preferred_element_type=F32)


def dot_nt(a, b):
    return lax.dot_general(a, b, (((1,), (1,)), ((), ())), preferred_element_type=F32)


def dot_tn(a, b):
    return lax.dot_general(a, b, (((0,), (0,)), ((), ())), preferred_element_type=F32)


def pieces(v, n):
    out = []
    for _ in range(n):
        hi = v.astype(BF16)
        out.append(hi)
        v = v - hi.astype(F32)
    return out


def dot_left(v, ones, n):
    return sum(dot(p, ones) for p in pieces(v, n))


def dot_right(ones, v, n):
    return sum(dot(ones, p) for p in pieces(v, n))


def iota(shape, axis):
    return lax.broadcasted_iota(jnp.int32, shape, axis)


def expander():
    row, col = iota((128, COLS), 0), iota((128, COLS), 1)
    return (row == lax.shift_right_logical(col, 6)).astype(BF16)


def reducer():
    row, col = iota((COLS, 128), 0), iota((COLS, 128), 1)
    return (col == lax.shift_right_logical(row, 6)).astype(BF16)


def sigmoid(v):
    return 1.0 / (1.0 + jnp.exp(-v))


def causal(shape=(BLOCK, BLOCK)):
    return iota(shape, 0) >= iota(shape, 1)


def lower(strict=False):
    row, col = iota((BLOCK, BLOCK), 0), iota((BLOCK, BLOCK), 1)
    return ((row > col) if strict else (row >= col)).astype(BF16)


def upper():
    return (iota((BLOCK, BLOCK), 0) <= iota((BLOCK, BLOCK), 1)).astype(BF16)


def maps_kernel(normed, wsm, prm, conv_bc, bias_bc, bc_in_out, z_out, bc_out, s_out, st_out, dt_out, r_out, rt_out, u_out, ext):
    k = pl.program_id(0)
    x = normed[...]
    proj = dot(x, wsm[...])
    bc_in = jnp.concatenate([proj[:, 0:128], proj[:, 256:384]], axis=1)
    bc_in_out[...] = bc_in

    @pl.when(k == 0)
    def _():
        ext[0:8, :] = jnp.zeros((8, 256), F32)

    @pl.when(k > 0)
    def _():
        ext[0:8, :] = ext[BLOCK : BLOCK + 8, :]

    ext[8 : BLOCK + 8, :] = bc_in
    z = bias_bc[...] + sum(conv_bc[j : j + 1, :] * ext[5 + j : 5 + j + BLOCK, :] for j in range(4))
    z_out[...] = z
    bc = (z * sigmoid(z)).astype(BF16)
    bc_out[...] = bc
    b, c = bc[:, :STATE], bc[:, STATE:]
    s_out[0] = jnp.where(causal(), dot_nt(c, b), 0.0)
    st_out[0] = jnp.where(iota((BLOCK, BLOCK), 1) >= iota((BLOCK, BLOCK), 0), dot_nt(b, c), 0.0)
    tri = lower()
    for g in range(GROUPS):
        u = proj[:, 128 + 256 * g : 256 + 256 * g] + prm[g, 6:7, 0:128]
        dt = jnp.maximum(u, 0.0) + jnp.log(1.0 + jnp.exp(-jnp.abs(u)))
        rate = -jnp.exp(prm[g, 7:8, 0:128]) * LOG2E
        r = dot_right(tri, dt * rate, 3)
        u_out[g] = u
        dt_out[g] = dt
        r_out[g] = r
        rt_out[g] = jnp.transpose(r)[0:8, :]


def run_maps(normed_all, wsm, prm, conv_bc, bias_bc):
    full = lambda *s: pl.BlockSpec(s, lambda k: (0,) * len(s))
    small = lambda: pl.BlockSpec((GROUPS, BLOCK, 128), lambda k: (0, k, 0))
    rows = lambda n: pl.BlockSpec((BLOCK, n), lambda k: (k, 0))
    sq = lambda: pl.BlockSpec((1, BLOCK, BLOCK), lambda k: (k, 0, 0))
    shape = jax.ShapeDtypeStruct
    return pl.pallas_call(
        maps_kernel,
        grid=(BLOCKS,),
        out_shape=[
            shape((LEN, 256), F32),
            shape((LEN, 256), F32),
            shape((LEN, 256), BF16),
            shape((BLOCKS, BLOCK, BLOCK), F32),
            shape((BLOCKS, BLOCK, BLOCK), F32),
            shape((GROUPS, LEN, 128), F32),
            shape((GROUPS, LEN, 128), F32),
            shape((GROUPS, 8, LEN), F32),
            shape((GROUPS, LEN, 128), F32),
        ],
        in_specs=[rows(D), full(D, 512), full(GROUPS, 16, COLS), full(4, 256), full(1, 256)],
        out_specs=[rows(256), rows(256), rows(256), sq(), sq(), small(), small(), pl.BlockSpec((GROUPS, 8, BLOCK), lambda k: (0, 0, k)), small()],
        scratch_shapes=[pltpu.VMEM((BLOCK + 8, 256), F32)],
        compiler_params=pltpu.CompilerParams(vmem_limit_bytes=40 * 2**20),
        name="state_maps",
    )(normed_all, wsm, prm, conv_bc, bias_bc)


def fwd_kernel(normed, wcat, prm, bc, s, dt, r, rt, gate_out, inner_out, z_out, y_out, gp_out, h_out, ss_out, ext, state):
    k, g = pl.program_id(0), pl.program_id(1)
    proj = dot(normed[...], wcat[...])
    gate = proj[:, :COLS]
    inner = proj[:, COLS:]
    gate_out[...] = gate
    inner_out[...] = inner

    @pl.when(k == 0)
    def _():
        ext[g, 0:8, :] = jnp.zeros((8, COLS), F32)
        state[g] = jnp.zeros((STATE, COLS), F32)

    @pl.when(k > 0)
    def _():
        ext[g, 0:8, :] = ext[g, BLOCK : BLOCK + 8, :]

    ext[g, 8 : BLOCK + 8, :] = inner
    z = prm[0, 4:5, :] + sum(prm[0, j : j + 1, :] * ext[g, 5 + j : 5 + j + BLOCK, :] for j in range(4))
    z_out[...] = z
    x = z * sigmoid(z)
    spread = expander()
    rv = r[0]
    last = rv[BLOCK - 1 : BLOCK, :]
    w = x * dot_left(dt[0], spread, 2)
    grow = dot_left(jnp.exp2(rv), spread, 2)
    tail = dot_left(jnp.exp2(last - rv), spread, 2)
    wl = w.astype(BF16)
    b, c = bc[:, :STATE], bc[:, STATE:]
    h = state[g]
    h_out[0, 0] = h
    scores = s[0]
    left = iota((BLOCK, 128), 1) < 64
    parts = []
    for p in range(HEADS // 2):
        halves = []
        for q in (2 * p, 2 * p + 1):
            gap = jnp.minimum(rv[:, q : q + 1] - rt[0, q : q + 1, :], 0.0)
            halves.append(dot((scores * jnp.exp2(gap)).astype(BF16), wl[:, 128 * p : 128 * (p + 1)]))
        parts.append(jnp.where(left, halves[0], halves[1]))
    y = jnp.concatenate(parts, axis=1) + grow * dot(c, h.astype(BF16)) + prm[0, 9:10, :] * x
    y_out[...] = y
    state[g] = grow[BLOCK - 1 : BLOCK, :] * h + dot_tn(b, (tail * w).astype(BF16))
    gp = y * (gate * sigmoid(gate))
    gp_out[...] = gp
    sq = gp * gp
    ss = sq[:, 0:128] + sq[:, 128:256] + sq[:, 256:384]

    @pl.when(g == 0)
    def _():
        ss_out[...] = ss

    @pl.when(g > 0)
    def _():
        ss_out[...] += ss


def run_fwd(normed_all, wcat, prm, bc, s, dt, r, rt):
    shape = jax.ShapeDtypeStruct
    cols = lambda: pl.BlockSpec((BLOCK, COLS), lambda k, g: (k, g))
    small = lambda: pl.BlockSpec((1, BLOCK, 128), lambda k, g: (g, k, 0))
    wide = shape((LEN, GROUPS * COLS), F32)
    return pl.pallas_call(
        fwd_kernel,
        grid=(BLOCKS, GROUPS),
        out_shape=[wide, wide, wide, wide, wide, shape((BLOCKS, GROUPS, STATE, COLS), F32), shape((LEN, 128), F32)],
        in_specs=[
            pl.BlockSpec((BLOCK, D), lambda k, g: (k, 0)),
            pl.BlockSpec((D, 2 * COLS), lambda k, g: (0, g)),
            pl.BlockSpec((1, 16, COLS), lambda k, g: (g, 0, 0)),
            pl.BlockSpec((BLOCK, 256), lambda k, g: (k, 0)),
            pl.BlockSpec((1, BLOCK, BLOCK), lambda k, g: (k, 0, 0)),
            small(),
            small(),
            pl.BlockSpec((1, 8, BLOCK), lambda k, g: (g, 0, k)),
        ],
        out_specs=[
            cols(),
            cols(),
            cols(),
            cols(),
            cols(),
            pl.BlockSpec((1, 1, STATE, COLS), lambda k, g: (k, g, 0, 0)),
            pl.BlockSpec((BLOCK, 128), lambda k, g: (k, 0)),
        ],
        scratch_shapes=[pltpu.VMEM((GROUPS, BLOCK + 8, COLS), F32), pltpu.VMEM((GROUPS, STATE, COLS), F32)],
        compiler_params=pltpu.CompilerParams(vmem_limit_bytes=48 * 2**20),
        cost_estimate=pl.CostEstimate(flops=16 * 2**30, bytes_accessed=40 * 2**20, transcendentals=2**23),
        name="scan_forward",
    )(normed_all, wcat, prm, bc, s, dt, r, rt)


def bwd_kernel(gm, gate, inner, zin, yin, hin, prm, bc, st, dt, r, rt, u, root, cross, cat_out, gstep_out, dbc_out, acc, ext, dstate, dst, dbc):
    k, g = pl.program_id(0), pl.program_id(1)

    @pl.when((k == 0) & (g == 0))
    def _():
        acc[...] = jnp.zeros_like(acc)

    @pl.when(k == 0)
    def _():
        ext[g, BLOCK : BLOCK + 8, :] = jnp.zeros((8, COLS), F32)
        dstate[g] = jnp.zeros((STATE, COLS), F32)

    @pl.when(k > 0)
    def _():
        ext[g, BLOCK : BLOCK + 8, :] = ext[g, 0:8, :]

    @pl.when(g == 0)
    def _():
        dst[...] = jnp.zeros_like(dst)
        dbc[...] = jnp.zeros_like(dbc)

    y = yin[...]
    gv = gate[...]
    sig = sigmoid(gv)
    act = gv * sig
    ir = root[...]
    gain = prm[0, 5:6, :]
    gp = y * act
    gmix = gm[...]
    gain_grad = gmix * gp * ir
    gated = ir * (gmix * gain) - gp * cross[...]
    gs = gated * act
    cat_out[:, :COLS] = (gated * y * sig * (1.0 + gv * (1.0 - sig))).astype(BF16)
    z = zin[...]
    zs = sigmoid(z)
    x = z * zs
    spread, fold = expander(), reducer()
    rv = r[0]
    last = rv[BLOCK - 1 : BLOCK, :]
    dte = dot_left(dt[0], spread, 2)
    grow = dot_left(jnp.exp2(rv), spread, 2)
    tail = dot_left(jnp.exp2(last - rv), spread, 2)
    w = x * dte
    wl = w.astype(BF16)
    gl = gs.astype(BF16)
    b, c = bc[:, :STATE], bc[:, STATE:]
    h = hin[0, 0]
    dh = dstate[g]
    dhl = dh.astype(BF16)
    scores = st[0]
    left = iota((BLOCK, 128), 1) < 64
    parts = []
    for p in range(HEADS // 2):
        halves = []
        cut = slice(128 * p, 128 * (p + 1))
        wp, gpair = wl[:, cut], gl[:, cut]
        zero = jnp.zeros_like(wp)
        for q in (2 * p, 2 * p + 1):
            decay = jnp.exp2(jnp.minimum(rt[0, q : q + 1, :] - rv[:, q : q + 1], 0.0))
            halves.append(dot((scores * decay).astype(BF16), gpair))
            mine = jnp.where(left, wp, zero) if q % 2 == 0 else jnp.where(left, zero, wp)
            dst[...] += dot_nt(mine, gpair) * decay
        parts.append(jnp.where(left, halves[0], halves[1]))
    dwi = jnp.concatenate(parts, axis=1)
    dws = tail * dot(b, dhl)
    dw = dwi + dws
    skip = prm[0, 9:10, :]
    skipgrad = gs * x
    glf = gl.astype(F32)
    diff = dot_left(glf * (y - skip * x) - wl.astype(F32) * dwi, fold, 3)
    zsum = dot_left(w * dws, fold, 3)
    const = dot_left(jnp.sum(h * dh, axis=0, keepdims=True) * grow[BLOCK - 1 : BLOCK, :] + jnp.zeros((8, COLS), F32), fold, 3)
    da = dot_right(upper(), diff, 3) + dot_right(lower(strict=True), zsum, 3) + const[0:1, :]
    rate = -jnp.exp(prm[0, 7:8, 0:128])
    ddt = dot_left(x * dw, fold, 3) + rate * da
    uu = u[0]
    dstep = ddt * sigmoid(uu)
    gstep_out[0] = dstep.astype(BF16)
    gx = grow * gs
    gxl = gx.astype(BF16)
    dbc[:, STATE:] += dot_nt(gxl, h.astype(BF16))
    dbc[:, :STATE] += dot_nt((tail * w).astype(BF16), dhl)
    dstate[g] = grow[BLOCK - 1 : BLOCK, :] * dh + dot_tn(c, gxl)
    dx = dte * dw + skip * gs
    dz = dx * (zs * (1.0 + z * (1.0 - zs)))
    ext[g, 0:BLOCK, :] = dz
    xi = inner[...]
    gi = jnp.zeros((BLOCK, COLS), F32)
    for j in range(4):
        moved = ext[g, 3 - j : 3 - j + BLOCK, :]
        gi = gi + prm[0, j : j + 1, :] * moved
        acc[g, j : j + 1, :] += jnp.sum(xi * moved, axis=0, keepdims=True)
    cat_out[:, COLS:] = gi.astype(BF16)
    acc[g, 4:5, :] += jnp.sum(dz, axis=0, keepdims=True)
    acc[g, 5:6, :] += jnp.sum(gain_grad, axis=0, keepdims=True)
    acc[g, 6:7, 0:128] += jnp.sum(dstep, axis=0, keepdims=True)
    acc[g, 7:8, 0:128] += jnp.sum(da * dt[0], axis=0, keepdims=True) * rate
    acc[g, 9:10, :] += jnp.sum(skipgrad, axis=0, keepdims=True)

    @pl.when(g == GROUPS - 1)
    def _():
        ds = jnp.where(iota((BLOCK, BLOCK), 1) >= iota((BLOCK, BLOCK), 0), dst[...], 0.0).astype(BF16)
        dbc_out[:, STATE:] = (dbc[:, STATE:] + dot_tn(ds, b)).astype(BF16)
        dbc_out[:, :STATE] = (dbc[:, :STATE] + dot(ds, c)).astype(BF16)


def run_bwd(gm, gate, inner, z, y, hin, prm, bc, st, dt, r, rt, u, root, cross):
    shape = jax.ShapeDtypeStruct
    rev = lambda k: BLOCKS - 1 - k
    cols = lambda: pl.BlockSpec((BLOCK, COLS), lambda k, g: (rev(k), g))
    small = lambda: pl.BlockSpec((1, BLOCK, 128), lambda k, g: (g, rev(k), 0))
    column = lambda: pl.BlockSpec((BLOCK, 1), lambda k, g: (rev(k), 0))
    return pl.pallas_call(
        bwd_kernel,
        grid=(BLOCKS, GROUPS),
        out_shape=[
            shape((LEN, GROUPS * 2 * COLS), BF16),
            shape((GROUPS, LEN, 128), BF16),
            shape((LEN, 256), BF16),
            shape((GROUPS, 16, COLS), F32),
        ],
        in_specs=[
            cols(),
            cols(),
            cols(),
            cols(),
            cols(),
            pl.BlockSpec((1, 1, STATE, COLS), lambda k, g: (rev(k), g, 0, 0)),
            pl.BlockSpec((1, 16, COLS), lambda k, g: (g, 0, 0)),
            pl.BlockSpec((BLOCK, 256), lambda k, g: (rev(k), 0)),
            pl.BlockSpec((1, BLOCK, BLOCK), lambda k, g: (rev(k), 0, 0)),
            small(),
            small(),
            pl.BlockSpec((1, 8, BLOCK), lambda k, g: (g, 0, rev(k))),
            small(),
            column(),
            column(),
        ],
        out_specs=[
            pl.BlockSpec((BLOCK, 2 * COLS), lambda k, g: (rev(k), g)),
            small(),
            pl.BlockSpec((BLOCK, 256), lambda k, g: (rev(k), 0)),
            pl.BlockSpec((GROUPS, 16, COLS), lambda k, g: (0, 0, 0)),
        ],
        scratch_shapes=[
            pltpu.VMEM((GROUPS, BLOCK + 8, COLS), F32),
            pltpu.VMEM((GROUPS, STATE, COLS), F32),
            pltpu.VMEM((BLOCK, BLOCK), F32),
            pltpu.VMEM((BLOCK, 256), F32),
        ],
        compiler_params=pltpu.CompilerParams(vmem_limit_bytes=48 * 2**20),
        cost_estimate=pl.CostEstimate(flops=16 * 2**30, bytes_accessed=40 * 2**20, transcendentals=2**23),
        name="scan_backward",
    )(gm, gate, inner, z, y, hin, prm, bc, st, dt, r, rt, u, root, cross)


class Net:
    def __init__(self, send, recv):
        self.send, self.recv, self.copies = send, recv, []
        self.at = {name: lax.axis_index(name) for name in AXES}
        self.at["y"] = self.at["yh"] * 2 + self.at["yl"]

    def near(self, axis, step):
        return lax.rem(self.at[axis] + step + 4, 4)

    def device(self, axis, step):
        if axis == "c":
            return {"c": 1 - self.at["c"]}
        if axis == "yh":
            return {"yh": 1 - self.at["yh"]}
        place = self.near(axis, step)
        if axis == "y":
            return {"yh": place // 2, "yl": lax.rem(place, 2)}
        return {axis: place}

    def start(self, src, dst, axis, step=1):
        copy = Copy(
            pltpu.make_async_remote_copy(
                src_ref=src,
                dst_ref=dst,
                send_sem=self.send.at[len(self.copies)],
                recv_sem=self.recv.at[len(self.copies)],
                device_id=self.device(axis, step),
                device_id_type=MESH,
            )
        )
        self.copies.append(copy)
        return copy

    def barrier(self, peers):
        here = pltpu.get_barrier_semaphore()
        for axis, step in peers:
            pl.semaphore_signal(here, inc=1, device_id=self.device(axis, step), device_id_type=MESH)
        pl.semaphore_wait(here, len(peers))

    def finish(self):
        for copy in self.copies:
            copy.arrived()
        for copy in self.copies:
            copy.left()


class Copy:
    def __init__(self, copy):
        self.copy, self.here, self.gone = copy, False, False
        copy.start()

    def arrived(self):
        if not self.here:
            self.here = True
            self.copy.wait_recv()

    def left(self):
        if not self.gone:
            self.gone = True
            self.copy.wait_send()


def sems(n):
    return [pltpu.SemaphoreType.DMA((n,)), pltpu.SemaphoreType.DMA((n,))]


def rows(ref, first, count):
    return ref.at[pl.ds(pl.multiple_of(first, 16), count)]


def gather_kernel(x, cot, gain, wa, wo, ws, pk, normed_all, cot_all, wcat, wout, wsm, prm, low, send, recv, local):
    net = Net(send, recv)
    at = net.at
    yh, yl, cx, cc, z = at["yh"], at["yl"], at["x"], at["c"], at["z"]
    net.barrier([("z", 1), ("z", -1), ("x", 1), ("x", -1), ("y", 1), ("y", -1), ("c", 1), ("yh", 1)])
    wide = ((wcat, wa, 768),)
    thin = ((wout, wo, 384), (wsm, ws, 256))

    def spot(ref, n, y, xx, part=None):
        cut = pl.ds(0, 96) if part is None else pl.ds(48 * part, 48)
        return ref.at[lax.rem(y, 2), xx, cc, cut, pl.ds(pl.multiple_of((y // 2) * n, 128), n)]

    def line(ref, n, y, part=None):
        cut = pl.ds(0, 96) if part is None else pl.ds(48 * part, 48)
        return ref.at[lax.rem(y, 2), :, cc, cut, pl.ds(pl.multiple_of((y // 2) * n, 128), n)]

    def column(ref, xx, part=None):
        cut = pl.ds(0, 96) if part is None else pl.ds(48 * part, 48)
        return ref.at[:, xx, cc, cut, :]

    own = []
    for i, (ref, src, n) in enumerate(wide + thin):
        own.append(pltpu.make_async_copy(src, spot(ref, n, at["y"], cx), local.at[i]))
    own.append(pltpu.make_async_copy(pk, prm.at[yh], local.at[3]))
    own.append(pltpu.make_async_copy(cot, rows(cot_all, z * 256, 256), local.at[4]))
    for copy in own:
        copy.start()
    a1, b1 = [], []
    for ref, src, n in wide:
        for step in (1, -1):
            a1.append(net.start(src, spot(ref, n, at["y"], cx), "x", step))
    for ref, src, n in thin:
        for step in (1, -1):
            b1.append(net.start(src, spot(ref, n, at["y"], cx), "y", step))
    for ref, src, n in wide + thin:
        net.start(src, spot(ref, n, at["y"], cx), "c")
    net.start(pk, prm.at[yh], "yh")
    v = x[...].astype(F32)
    root = lax.rsqrt(jnp.mean(v * v, axis=1, keepdims=True) + EPS)
    low[...] = (v * root * gain[...]).astype(BF16)
    own_normed = pltpu.make_async_copy(low, rows(normed_all, z * 256, 256), local.at[5])
    own_normed.start()
    zs = [net.start(low, rows(normed_all, z * 256, 256), "z", step) for step in (1, -1)]
    a2, b2 = [], []
    for (part, step), copy in zip(((0, 1), (1, -1)), a1):
        copy.arrived()
        here = spot(wcat, 768, at["y"], net.near("x", -step), part)
        a2.append(net.start(here, here, "x", step))
    for i, (ref, src, n) in enumerate(thin):
        for (part, step), copy in zip(((0, 1), (1, -1)), b1[2 * i : 2 * i + 2]):
            copy.arrived()
            here = spot(ref, n, net.near("y", -step), cx, part)
            b2.append(net.start(here, here, "y", step))
    for i in (0, 1, 2):
        own[i].wait()
    for copy in a2:
        copy.arrived()
    here = line(wcat, 768, at["y"])
    a3 = [net.start(here, here, "y", step) for step in (1, -1)]
    for copy in b2:
        copy.arrived()
    b3 = []
    for ref, src, n in thin:
        here = column(ref, cx)
        b3 += [net.start(here, here, "x", step) for step in (1, -1)]
    for step in (1, 2, 3):
        here = spot(wcat, 768, at["y"], net.near("x", step))
        net.start(here, here, "c")
        for ref, src, n in thin:
            here = spot(ref, n, net.near("y", step), cx)
            net.start(here, here, "c")
    def hop(ref, first):
        out = []
        for (part, step), copy in zip(((0, 1), (1, -1)), first):
            copy.arrived()
            here = rows(ref, net.near("z", -step) * 256 + 128 * part, 128)
            out.append(net.start(here, here, "z", step))
        return out

    zs2 = hop(normed_all, zs)
    cs = [net.start(cot, rows(cot_all, z * 256, 256), "z", step) for step in (1, -1)]
    a4, b4 = [], []
    for (part, step), copy in zip(((0, 1), (1, -1)), a3):
        copy.arrived()
        here = line(wcat, 768, net.near("y", -step), part)
        a4.append(net.start(here, here, "y", step))
        here = line(wcat, 768, net.near("y", -step))
        net.start(here, here, "c")
    for i, (ref, src, n) in enumerate(thin):
        for (part, step), copy in zip(((0, 1), (1, -1)), b3[2 * i : 2 * i + 2]):
            copy.arrived()
            here = column(ref, net.near("x", -step), part)
            b4.append(net.start(here, here, "x", step))
            here = column(ref, net.near("x", -step))
            net.start(here, here, "c")
    for copy in a4:
        copy.arrived()
    here = line(wcat, 768, net.near("y", 2))
    net.start(here, here, "c")
    for copy in b4:
        copy.arrived()
    for ref, src, n in thin:
        here = column(ref, net.near("x", 2))
        net.start(here, here, "c")
    hop(cot_all, cs)
    net.finish()
    for i in (3, 4):
        own[i].wait()
    own_normed.wait()


def run_gather(x, cot, gain, wa, wo, ws, pk):
    shape = jax.ShapeDtypeStruct
    vmem = pl.BlockSpec(memory_space=pltpu.VMEM)
    return pl.pallas_call(
        gather_kernel,
        out_shape=[
            shape((LEN, D), BF16),
            shape((LEN, D), BF16),
            shape((2, 4, 2, 96, 1536), BF16),
            shape((2, 4, 2, 96, 768), BF16),
            shape((2, 4, 2, 96, 512), BF16),
            shape((2, 16, COLS), F32),
        ],
        in_specs=[vmem, ANY, vmem, ANY, ANY, ANY, ANY],
        out_specs=[ANY] * 6,
        scratch_shapes=[pltpu.VMEM((256, D), BF16)] + sems(64) + [pltpu.SemaphoreType.DMA((6,))],
        compiler_params=pltpu.CompilerParams(collective_id=0, has_side_effects=True, vmem_limit_bytes=24 * 2**20),
        name="gather_all",
    )(x, cot, gain, wa, wo, ws, pk)


def stats_kernel(part, out, slots, send, recv):
    net = Net(send, recv)
    peers = [("z", 1), ("z", -1), ("z", 2)]
    net.barrier(peers)
    z = net.at["z"]
    for axis, step in peers:
        net.start(part, slots.at[z], axis, step)
    slots[z] = part[...]
    net.finish()
    out[...] = (slots[0] + slots[1]) + (slots[2] + slots[3])


def run_stats(part):
    return pl.pallas_call(
        stats_kernel,
        out_shape=jax.ShapeDtypeStruct((16, 128), F32),
        in_specs=[pl.BlockSpec(memory_space=pltpu.VMEM)],
        out_specs=pl.BlockSpec(memory_space=pltpu.VMEM),
        scratch_shapes=[pltpu.VMEM((4, 16, 128), F32)] + sems(3),
        compiler_params=pltpu.CompilerParams(collective_id=1, has_side_effects=True),
        name="token_stats",
    )(part)


def maps_back_kernel(dbc, zin, bc_in, conv, gbc, acc, mine, slots, ext, send, recv):
    net = Net(send, recv)
    peers = [("z", 1), ("z", -1), ("z", 2)]
    net.barrier(peers)
    z = net.at["z"]
    mine[0:LEN, :] = dbc[...]
    mine[LEN : LEN + 16, :] = jnp.zeros((16, 256), BF16)
    for axis, step in peers:
        net.start(rows(mine, net.near("z", step) * 256, 272), slots.at[z], axis, step)
    slots[z] = mine[pl.ds(pl.multiple_of(z * 256, 16), 272), :]
    net.finish()
    total = (slots[0].astype(F32) + slots[1].astype(F32)) + (slots[2].astype(F32) + slots[3].astype(F32))
    zv = zin[...]
    sig = sigmoid(zv)
    dz = total * (sig * (1.0 + zv * (1.0 - sig)))
    live = iota((272, 256), 0) + z * 256 < LEN
    ext[...] = jnp.where(live, dz, 0.0)
    xi = bc_in[...]
    out = jnp.zeros((256, 256), F32)
    acc[...] = jnp.zeros_like(acc)
    for j in range(4):
        moved = ext[3 - j : 3 - j + 256, :]
        out = out + conv[j : j + 1, :] * moved
        acc[j : j + 1, :] = jnp.sum(xi * moved, axis=0, keepdims=True)
    acc[4:5, :] = jnp.sum(ext[0:256, :], axis=0, keepdims=True)
    gbc[...] = out.astype(BF16)


def run_maps_back(dbc, zin, bc_in, conv):
    vmem = pl.BlockSpec(memory_space=pltpu.VMEM)
    return pl.pallas_call(
        maps_back_kernel,
        out_shape=[jax.ShapeDtypeStruct((256, 256), BF16), jax.ShapeDtypeStruct((8, 256), F32)],
        in_specs=[vmem] * 4,
        out_specs=[vmem] * 2,
        scratch_shapes=[pltpu.VMEM((LEN + 16, 256), BF16), pltpu.VMEM((4, 272, 256), BF16), pltpu.VMEM((272, 256), F32)] + sems(3),
        compiler_params=pltpu.CompilerParams(collective_id=2, has_side_effects=True, vmem_limit_bytes=16 * 2**20),
        name="state_maps_back",
    )(dbc, zin, bc_in, conv)


def scatter_kernel(gn, dcat, dout, dsm, small, gn_out, cat_out, out_out, bc_out, step_out, small_out, ra, rb, rc, hcat, hout, hsm, gz, fa, fb, fc, s1a, s1b, s1c, s2a, s2b, s2c, e1a, e1b, e1c, e2a, e2b, e2c, gh, ge, sp0, sp1, sp2, sp3, bz, by, send, recv):
    net = Net(send, recv)
    at = net.at
    yh, yl, cx, cc, z, y = at["yh"], at["yl"], at["x"], at["c"], at["z"], at["y"]
    near = net.near
    net.barrier([("z", 1), ("z", -1), ("z", 2), ("x", 1), ("x", -1), ("x", 2), ("y", 1), ("y", -1), ("y", 2), ("c", 1)])
    cross = []
    for src, dst in ((dcat, ra), (dout, rb), (dsm, rc)):
        cross.append(net.start(src.at[:, :, 1 - cc], dst, "c"))
    far = near("z", 2) * 256
    g1 = [net.start(rows(gn, far + 128 * part, 128), gh.at[part], "z", step) for part, step in ((0, 1), (1, -1))]
    sp0[z] = small[32:48, :]
    q = [net.start(small.at[pl.ds(32, 16)], sp0.at[z], "z", step) for step in (1, -1, 2)]
    cross[0].arrived()
    hcat[...] = dcat[:, :, cc] + ra[...]
    fary = near("y", 2)

    def ycut(ref, owner, n, part=None):
        cut = pl.ds(0, 96) if part is None else pl.ds(48 * part, 48)
        return ref.at[lax.rem(owner, 2), :, cut, pl.ds(pl.multiple_of((owner // 2) * n, 128), n)]

    def xcut(ref, owner, part=None):
        cut = pl.ds(0, 96) if part is None else pl.ds(48 * part, 48)
        return ref.at[:, owner, cut, :]

    a1 = [net.start(ycut(hcat, fary, 768, part), s1a.at[part], "y", step) for part, step in ((0, 1), (1, -1))]
    cross[1].arrived()
    hout[...] = dout[:, :, cc] + rb[...]
    farx = near("x", 2)
    b1 = [net.start(xcut(hout, farx, part), s1b.at[part], "x", step) for part, step in ((0, 1), (1, -1))]
    cross[2].arrived()
    hsm[...] = dsm[:, :, cc] + rc[...]
    c1 = [net.start(xcut(hsm, farx, part), s1c.at[part], "x", step) for part, step in ((0, 1), (1, -1))]
    for copy in q:
        copy.arrived()
    sp1[cx, 0:32, :] = small[0:32, :]
    sp1[cx, 32:48, :] = (sp0[0] + sp0[1]) + (sp0[2] + sp0[3])
    q = [net.start(sp1.at[cx], sp1.at[cx], "x", step) for step in (1, -1, 2)]
    a2, b2, c2, g2 = [], [], [], []
    for (part, step), copy in zip(((0, 1), (1, -1)), g1):
        copy.arrived()
        block = near("z", step) * 256
        gz[part] = gn[pl.ds(pl.multiple_of(block, 16), 256), :]
        gz[part, 128 * part : 128 * part + 128, :] += gh[part]
        g2.append(net.start(gz.at[part], ge.at[part], "z", step))
    for (part, step), copy in zip(((0, 1), (1, -1)), a1):
        copy.arrived()
        owner = near("y", step)
        fa[part] = hcat[lax.rem(owner, 2), :, :, pl.ds(pl.multiple_of((owner // 2) * 768, 128), 768)]
        fa[part, :, 48 * part : 48 * part + 48, :] += s1a[part]
        a2.append(net.start(fa.at[part], s2a.at[part], "y", step))
    for first, held, fold, got, nxt, out in ((b1, hout, fb, s1b, s2b, b2), (c1, hsm, fc, s1c, s2c, c2)):
        for (part, step), copy in zip(((0, 1), (1, -1)), first):
            copy.arrived()
            fold[part] = held[:, near("x", step)]
            fold[part, :, 48 * part : 48 * part + 48, :] += got[part]
            out.append(net.start(fold.at[part], nxt.at[part], "x", step))
    for copy in q:
        copy.arrived()
    sp2[y] = (sp1[0] + sp1[1]) + (sp1[2] + sp1[3])
    q = [net.start(sp2.at[y], sp2.at[y], "y", step) for step in (1, -1, 2)]
    for copy in a2 + b2 + c2:
        copy.arrived()
    own = hcat[yl, :, :, pl.ds(pl.multiple_of(yh * 768, 128), 768)]
    e1a[...] = (own.astype(F32) + s2a[0].astype(F32) + s2a[1].astype(F32)).astype(BF16)
    e1b[...] = (hout[:, cx].astype(F32) + s2b[0].astype(F32) + s2b[1].astype(F32)).astype(BF16)
    e1c[...] = (hsm[:, cx].astype(F32) + s2c[0].astype(F32) + s2c[1].astype(F32)).astype(BF16)

    def ypart(ref, owner, n, part=None):
        cut = pl.ds(0, 96) if part is None else pl.ds(48 * part, 48)
        return ref.at[lax.rem(owner, 2), cut, pl.ds(pl.multiple_of((owner // 2) * n, 128), n)]

    def xpart(ref, owner, part):
        return ref.at[owner, pl.ds(48 * part, 48)]

    pa = [net.start(xpart(e1a, farx, part), e2a.at[2 + part, pl.ds(0, 48)], "x", step) for part, step in ((0, 1), (1, -1))]
    pb = [net.start(ypart(e1b, fary, 384, part), e2b.at[2 + part, pl.ds(0, 48)], "y", step) for part, step in ((0, 1), (1, -1))]
    pc = [net.start(ypart(e1c, fary, 256, part), e2c.at[2 + part, pl.ds(0, 48)], "y", step) for part, step in ((0, 1), (1, -1))]
    for copy in q:
        copy.arrived()
    sp3[cc] = (sp2[0] + sp2[1]) + (sp2[2] + sp2[3])
    q = [net.start(sp3.at[cc], sp3.at[cc], "c")]
    la, lb, lc = [], [], []
    for (part, step), copy in zip(((0, 1), (1, -1)), pa):
        copy.arrived()
        a2[part].left()
        fa[part, 0] = e1a[near("x", step)]
        fa[part, 0, 48 * part : 48 * part + 48, :] += e2a[2 + part, 0:48, :]
        la.append(net.start(fa.at[part, 0], e2a.at[part], "x", step))
    for first, held, fold, n, land, prev, out in ((pb, e1b, fb, 384, e2b, b2, lb), (pc, e1c, fc, 256, e2c, c2, lc)):
        for (part, step), copy in zip(((0, 1), (1, -1)), first):
            copy.arrived()
            owner = near("y", step)
            prev[part].left()
            fold[part, 0, :, 0:n] = held[lax.rem(owner, 2), :, pl.ds(pl.multiple_of((owner // 2) * n, 128), n)]
            fold[part, 0, 48 * part : 48 * part + 48, 0:n] += land[2 + part, 0:48, :]
            out.append(net.start(fold.at[part, 0, :, pl.ds(0, n)], land.at[part], "y", step))
    for copy in g2:
        copy.arrived()
    gn_out[...] = gn[pl.ds(pl.multiple_of(z * 256, 16), 256), :].astype(F32) + ge[0].astype(F32) + ge[1].astype(F32)
    for copy in q:
        copy.arrived()
    small_out[...] = sp3[0] + sp3[1]
    for copy in lc:
        copy.arrived()
    mine = e1c[yl, :, pl.ds(pl.multiple_of(yh * 256, 128), 256)]
    sm = mine.astype(F32) + e2c[0].astype(F32) + e2c[1].astype(F32)
    step_out[...] = sm[:, 128:]
    bz[z] = sm[:, :128]
    q = [net.start(bz.at[z], bz.at[z], "z", step) for step in (1, -1, 2)]
    for copy in lb:
        copy.arrived()
    mine = e1b[yl, :, pl.ds(pl.multiple_of(yh * 384, 128), 384)]
    out_out[...] = mine.astype(F32) + e2b[0].astype(F32) + e2b[1].astype(F32)
    for copy in la:
        copy.arrived()
    cat_out[...] = e1a[cx].astype(F32) + e2a[0].astype(F32) + e2a[1].astype(F32)
    for copy in q:
        copy.arrived()
    by[yh] = (bz[0] + bz[1]) + (bz[2] + bz[3])
    net.start(by.at[yh], by.at[yh], "y", 2).arrived()
    bc_out[:, :128] = by[0]
    bc_out[:, 128:] = by[1]
    net.finish()


def run_scatter(gn, dcat, dout, dsm, small):
    shape = jax.ShapeDtypeStruct
    vmem = pl.BlockSpec(memory_space=pltpu.VMEM)
    bf = lambda *s: pltpu.VMEM(s, BF16)
    f32 = lambda *s: pltpu.VMEM(s, F32)
    widths = (1536, 768, 512)
    scratch = [bf(2, 4, 96, n) for n in widths]
    scratch += [bf(2, 4, 96, n) for n in widths]
    scratch += [bf(2, 256, D)]
    scratch += [bf(2, 4, 96, 768), bf(2, 2, 96, 768), bf(2, 2, 96, 512)]
    scratch += [bf(2, 4, 48, 768), bf(2, 2, 48, 768), bf(2, 2, 48, 512)]
    scratch += [bf(2, 4, 96, 768), bf(2, 2, 96, 768), bf(2, 2, 96, 512)]
    scratch += [bf(4, 96, 768), bf(2, 96, 768), bf(2, 96, 512)]
    scratch += [bf(4, 96, 768), bf(4, 96, 384), bf(4, 96, 256)]
    scratch += [bf(2, 128, D), bf(2, 256, D)]
    scratch += [f32(4, 16, COLS), f32(4, 48, COLS), f32(4, 48, COLS), f32(2, 48, COLS)]
    scratch += [f32(4, 96, 128), f32(2, 96, 128)]
    return pl.pallas_call(
        scatter_kernel,
        out_shape=[
            shape((256, D), F32),
            shape((96, 768), F32),
            shape((96, 384), F32),
            shape((96, 256), F32),
            shape((96, 128), F32),
            shape((48, COLS), F32),
        ],
        in_specs=[vmem] * 5,
        out_specs=[vmem] * 6,
        scratch_shapes=scratch + sems(48),
        compiler_params=pltpu.CompilerParams(collective_id=3, has_side_effects=True, vmem_limit_bytes=56 * 2**20),
        name="scatter_all",
    )(gn, dcat, dout, dsm, small)


def ring_scatter(blocks, z):
    ahead = [(i, (i + 1) % 4) for i in range(4)]
    back = [(i, (i + 3) % 4) for i in range(4)]
    pick = lambda step: lax.dynamic_index_in_dim(blocks, lax.rem(z + step, 4), 0, keepdims=False)
    far = pick(2)
    first = lax.ppermute(far[:128], "z", ahead)
    second = lax.ppermute(far[128:], "z", back)
    right, left = pick(1), pick(3)
    right = jnp.concatenate([right[:128] + first, right[128:]], axis=0)
    left = jnp.concatenate([left[:128], left[128:] + second], axis=0)
    from_left = lax.ppermute(right, "z", ahead)
    from_right = lax.ppermute(left, "z", back)
    return pick(0).astype(F32) + from_left.astype(F32) + from_right.astype(F32)


def shards(tokens, norm_gain, w_gate, w_inner, w_bc, w_step, conv_inner, bias_inner, conv_bc, bias_bc, step_bias, decay_log, skip_gain, gate_gain, w_out, cotangent):
    z, yh = lax.axis_index("z"), lax.axis_index("yh")
    pad = lambda v, n: jnp.pad(v, ((0, 0), (0, n - v.shape[1])))
    head_row = lambda v: pad(v[None], COLS)
    pk = jnp.concatenate(
        [
            conv_inner,
            bias_inner[None],
            gate_gain[None],
            head_row(step_bias),
            head_row(decay_log),
            head_row(skip_gain),
            jnp.repeat(skip_gain, 64)[None],
            jnp.zeros((6, COLS), F32),
        ],
        axis=0,
    )
    wa = jnp.concatenate([w_gate, w_inner], axis=1)
    ws = jnp.concatenate([lax.dynamic_slice_in_dim(w_bc, yh * 128, 128, 1), pad(w_step, 128)], axis=1)
    normed_all, cot_all, wcat, wout, wsm, prm = run_gather(tokens, cotangent, norm_gain[None], wa, w_out, ws, pk)
    wcat, wout, wsm = wcat.reshape(D, 1536), wout.reshape(D, 768), wsm.reshape(D, 512)
    bc_in, z_bc, bc, s, st, dt, r, rt, u = run_maps(normed_all, wsm, prm, conv_bc, bias_bc[None])
    gate, inner, zs, y, gp, h, ss = run_fwd(normed_all, wcat, prm, bc, s, dt, r, rt)
    gain = prm[:, 5].reshape(-1)
    gm = dot(cot_all, wout)
    part = jnp.concatenate([jnp.sum(ss, axis=1).reshape(8, 128), jnp.sum(gm * gain * gp, axis=1).reshape(8, 128)], axis=0)
    stats = run_stats(part)
    root = lax.rsqrt(stats[:8].reshape(LEN, 1) / INNER + EPS)
    cross = root * root * root * (stats[8:].reshape(LEN, 1) / INNER)
    mixed = (gp * root * gain).astype(BF16)
    branch = ring_scatter(dot_nt(mixed, wout).astype(BF16).reshape(4, 256, D), z)
    residual = tokens.astype(F32)
    output = (residual + branch).astype(BF16)
    dout = dot_tn(cot_all, mixed).astype(BF16)
    cat, gstep, dbc, acc = run_bwd(gm, gate, inner, zs, y, h, prm, bc, st, dt, r, rt, u, root, cross)
    own = lambda v, n: lax.dynamic_slice_in_dim(v, z * 256, n, 0)
    z_own = lax.dynamic_slice_in_dim(jnp.pad(z_bc, ((0, 16), (0, 0))), z * 256, 272, 0)
    gbc, bc_acc = run_maps_back(dbc, z_own, own(bc_in, 256), conv_bc)
    dcat = dot_tn(normed_all, cat).astype(BF16)
    gsteps = jnp.concatenate([gstep[0], gstep[1]], axis=1)
    wsteps = jnp.concatenate([wsm[:, 128:256], wsm[:, 384:]], axis=1)
    gn32 = dot_nt(cat, wcat) + dot_nt(gsteps, wsteps)
    dstep = dot_tn(normed_all, gsteps)
    dbcw = dot_tn(own(normed_all, 256), gbc)
    dsm = jnp.concatenate([dbcw[:, :128], dstep[:, :128], dbcw[:, 128:], dstep[:, 128:]], axis=1).astype(BF16)
    wbc = jnp.concatenate([wsm[:, :128], wsm[:, 256:384]], axis=1)
    gn_bc = dot_nt(gbc, wbc)
    norm_part = (
        jnp.sum(gn32 * normed_all.astype(F32), axis=0) + jnp.sum(gn_bc * own(normed_all, 256).astype(F32), axis=0)
    ) / norm_gain
    small = jnp.concatenate(
        [acc.reshape(32, COLS), norm_part.reshape(4, COLS), pad(bc_acc, COLS), jnp.zeros((4, COLS), F32)], axis=0
    )
    gn_own, cat_g, out_g, bc_g, step_g, sums = run_scatter(
        gn32.astype(BF16), dcat.reshape(2, 4, 2, 96, 1536), dout.reshape(2, 4, 2, 96, 768), dsm.reshape(2, 4, 2, 96, 512), small
    )
    grad_normed = gn_own + gn_bc
    inv_root = lax.rsqrt(jnp.mean(residual * residual, axis=1, keepdims=True) + EPS)
    scaled = grad_normed * norm_gain
    tokens_grad = (
        cotangent.astype(F32)
        + inv_root * scaled
        - residual * (inv_root * inv_root * inv_root) * jnp.mean(scaled * residual, axis=1, keepdims=True)
    )
    mine = lax.dynamic_slice_in_dim(sums, yh * 16, 16, 0)
    return (
        output,
        tokens_grad,
        sums[32:36].reshape(-1),
        cat_g[:, :COLS],
        cat_g[:, COLS:],
        bc_g,
        step_g[:, :HEADS],
        mine[0:4],
        mine[4],
        sums[36:40, :256],
        sums[40, :256],
        mine[6, :HEADS],
        mine[7, :HEADS],
        jnp.sum(mine[9].reshape(HEADS, 64), axis=1),
        mine[5],
        out_g,
    )


def solution(mesh):
    fine = Mesh(mesh.devices.reshape(2, 4, 2, 2, 4), AXES)
    dp, tensor = ("yl", "x", "c"), ("yh", "z")
    tokens, weight = P(dp + tensor, None), P(dp, tensor)
    return jax.shard_map(
        shards,
        mesh=fine,
        in_specs=(
            tokens,
            P(),
            weight,
            weight,
            P(dp, None),
            weight,
            P(None, tensor),
            P(tensor),
            P(),
            P(),
            P(tensor),
            P(tensor),
            P(tensor),
            P(tensor),
            weight,
            tokens,
        ),
        out_specs=(
            tokens,
            tokens,
            P(),
            weight,
            weight,
            P(dp, None),
            weight,
            P(None, tensor),
            P(tensor),
            P(),
            P(),
            P(tensor),
            P(tensor),
            P(tensor),
            P(tensor),
            weight,
        ),
        check_vma=False,
    )
```

```python
import jax
import jax.numpy as jnp
from jax import lax
from jax.experimental import pallas as pl
from jax.experimental.pallas import tpu as pltpu
from jax.sharding import Mesh
from jax.sharding import PartitionSpec as P

D = 1536
LEN = 1024
INNER = 3072
STATE = 128
BLOCK = 256
BLOCKS = LEN // BLOCK
GROUPS = 2
HEADS = 6
COLS = HEADS * 64
WIDE = GROUPS * COLS
STEPS = 2 * WIDE
PROJ = STEPS + GROUPS * 128
LOG2E = 1.4426950408889634
EPS = 1e-05
F32 = jnp.float32
BF16 = jnp.bfloat16
MESH = pl.DeviceIdType.MESH
AXES = ("yl", "x", "c", "yh", "z")
ANY = pl.BlockSpec(memory_space=pl.ANY)
VMEM = pl.BlockSpec(memory_space=pltpu.VMEM)
SHAPE = jax.ShapeDtypeStruct
ROOM = 60 * 2**20


def dot(a, b):
    return jnp.dot(a, b, preferred_element_type=F32)


def dot_nt(a, b):
    return lax.dot_general(a, b, (((1,), (1,)), ((), ())), preferred_element_type=F32)


def dot_tn(a, b):
    return lax.dot_general(a, b, (((0,), (0,)), ((), ())), preferred_element_type=F32)


def pieces(v, n):
    out = []
    for _ in range(n):
        hi = v.astype(BF16)
        out.append(hi)
        v = v - hi.astype(F32)
    return out


def dot_left(v, ones, n):
    return sum(dot(p, ones) for p in pieces(v, n))


def dot_right(ones, v, n):
    return sum(dot(ones, p) for p in pieces(v, n))


def iota(shape, axis):
    return lax.broadcasted_iota(jnp.int32, shape, axis)


def expander():
    row, col = iota((128, COLS), 0), iota((128, COLS), 1)
    return (row == lax.shift_right_logical(col, 6)).astype(BF16)


def reducer():
    row, col = iota((COLS, 128), 0), iota((COLS, 128), 1)
    return (col == lax.shift_right_logical(row, 6)).astype(BF16)


def sigmoid(v):
    return 1.0 / (1.0 + jnp.exp(-v))


def lower(strict=False):
    row, col = iota((BLOCK, BLOCK), 0), iota((BLOCK, BLOCK), 1)
    return ((row > col) if strict else (row >= col)).astype(BF16)


def upper():
    return (iota((BLOCK, BLOCK), 0) <= iota((BLOCK, BLOCK), 1)).astype(BF16)


def token_row(v):
    v = sum(v[:, 128 * i : 128 * (i + 1)] for i in range(v.shape[1] // 128))
    ones = jnp.ones((8, 128), BF16)
    return sum(dot_nt(ones, p) for p in pieces(v, 3))[0:1, :]


class Net:
    def __init__(self, send, recv):
        self.send, self.recv, self.copies = send, recv, []
        self.at = {name: lax.axis_index(name) for name in AXES}
        self.at["y"] = self.at["yh"] * 2 + self.at["yl"]
        self.places = {(a, s): lax.rem(self.at[a] + s + 4, 4) for a in ("x", "y", "z") for s in (1, -1, 2)}
        self.other = 1 - self.at["c"]
        self.targets = {("c", 1): {"c": self.other}}
        for (a, s), place in self.places.items():
            self.targets[a, s] = {"yh": place // 2, "yl": lax.rem(place, 2)} if a == "y" else {a: place}

    def near(self, axis, step):
        return self.places[axis, step]

    def plan(self, src, dst, axis, step=1):
        copy = Copy(self, len(self.copies), src, dst, self.targets[axis, step])
        self.copies.append(copy)
        return copy

    def start(self, src, dst, axis, step=1):
        return self.plan(lambda: src, lambda: dst, axis, step).start()

    def around(self, src, dst, axis):
        return [self.start(src, dst, axis, step) for step in (1, -1, 2)]

    def barrier(self, peers):
        here = pltpu.get_barrier_semaphore()
        for peer in peers:
            pl.semaphore_signal(here, inc=1, device_id=self.targets[peer], device_id_type=MESH)
        pl.semaphore_wait(here, len(peers))

    def finish(self):
        for copy in self.copies:
            copy.arrived()
        for copy in self.copies:
            copy.left()


class Copy:
    def __init__(self, net, index, src, dst, target):
        self.net, self.index, self.src, self.dst, self.target = net, index, src, dst, target
        self.here, self.gone = False, False

    def made(self):
        return pltpu.make_async_remote_copy(
            src_ref=self.src(),
            dst_ref=self.dst(),
            send_sem=self.net.send.at[self.index],
            recv_sem=self.net.recv.at[self.index],
            device_id=self.target,
            device_id_type=MESH,
        )

    def start(self):
        self.made().start()
        return self

    def arrived(self):
        if not self.here:
            self.here = True
            self.made().wait_recv()

    def left(self):
        if not self.gone:
            self.gone = True
            self.made().wait_send()


def sems(n):
    return [pltpu.SemaphoreType.DMA((n,)), pltpu.SemaphoreType.DMA((n,))]


def rows(ref, first, count):
    return ref.at[pl.ds(pl.multiple_of(first, 16), count)]


def lanes(first, count):
    return pl.ds(pl.multiple_of(first, 128), count)


def arrive(copies):
    for copy in copies:
        copy.arrived()


HALVES = ((0, 1), (1, -1))


class RingSum:
    def __init__(self, net, first, held, spans, scratch):
        self.net, self.first, self.second, self.held, self.spans = net, first, "y" if first == "x" else "x", held, spans
        self.half, self.fold, self.whole, self.mid, self.half2, self.fold2, self.whole2 = scratch
        self.width = sum(n for _, n in spans)
        self.one, self.two, self.three, self.four = [], [], [], []
        for part, step in HALVES:
            cut = pl.ds(48 * part, 48)
            if first == "x":
                self.plan(self.one, lambda cut=cut: held.at[:, net.near("x", 2), cut, lanes(spans[0][0], 2 * self.width)], lambda part=part: self.half.at[part], "x", step)
            else:
                lane = 0
                for base, n in spans:
                    self.plan(
                        self.one,
                        lambda cut=cut, base=base, n=n: self.ycut(held, net.near("y", 2), base, n, cut),
                        lambda part=part, lane=lane, n=n: self.half.at[part, :, :, lanes(lane, n)],
                        "y",
                        step,
                    )
                    lane += n
            self.plan(self.two, lambda part=part: self.fold.at[part], lambda part=part: self.whole.at[part], first, step)
            if first == "x":
                self.plan(self.three, lambda cut=cut: self.mid.at[lax.rem(net.near("y", 2), 2), cut, self.ylanes(net.near("y", 2))], lambda part=part: self.half2.at[part], "y", step)
            else:
                self.plan(self.three, lambda cut=cut: self.mid.at[net.near("x", 2), cut], lambda part=part: self.half2.at[part], "x", step)
            self.plan(self.four, lambda part=part: self.fold2.at[part], lambda part=part: self.whole2.at[part], self.second, step)

    def plan(self, to, src, dst, axis, step):
        to.append(self.net.plan(src, dst, axis, step))

    def ycut(self, ref, owner, base, n, cut):
        return ref.at[lax.rem(owner, 2), :, cut, lanes(base + (owner // 2) * n, n)]

    def ylanes(self, owner):
        return lanes((owner // 2) * self.width, self.width)

    def block(self, owner):
        if self.first == "x":
            return self.held[:, owner, :, lanes(self.spans[0][0], 2 * self.width)]
        got = [self.held[lax.rem(owner, 2), :, :, lanes(base + (owner // 2) * n, n)] for base, n in self.spans]
        return got[0] if len(got) == 1 else jnp.concatenate(got, axis=-1)

    def mid_block(self, owner):
        if self.first == "x":
            return self.mid[lax.rem(owner, 2), :, self.ylanes(owner)]
        return self.mid[owner]

    def step1(self):
        for copy in self.one:
            copy.start()

    def step2(self):
        arrive(self.one)
        for part, step in HALVES:
            self.fold[part] = self.block(self.net.near(self.first, step))
            self.fold[part, :, 48 * part : 48 * part + 48, :] += self.half[part]
            self.two[part].start()

    def step3(self):
        arrive(self.two)
        own = self.block(self.net.at[self.first]).astype(F32)
        self.mid[...] = (own + self.whole[0].astype(F32) + self.whole[1].astype(F32)).astype(BF16)
        for copy in self.three:
            copy.start()

    def step4(self):
        arrive(self.three)
        for part, step in HALVES:
            self.fold2[part] = self.mid_block(self.net.near(self.second, step))
            self.fold2[part, 48 * part : 48 * part + 48, :] += self.half2[part]
            self.four[part].start()

    def step5(self):
        arrive(self.four)
        own = self.mid_block(self.net.at[self.second]).astype(F32)
        return own + self.whole2[0].astype(F32) + self.whole2[1].astype(F32)


def ring_scratch(first, width):
    blocks, wide = (2, 2 * width) if first == "x" else (4, width)
    shapes = [(2, blocks, 48, wide), (2, blocks, 96, wide), (2, blocks, 96, wide), (blocks, 96, wide), (2, 48, width), (2, 96, width), (2, 96, width)]
    return [pltpu.VMEM(s, BF16) for s in shapes]


class TokenSum:
    def __init__(self, net, part, scratch):
        self.net, self.half, self.fold, self.whole = net, *scratch
        self.one = [
            net.plan(lambda p=p: rows(part, net.near("z", 2) * 256 + 128 * p, 128), lambda p=p: self.half.at[p], "z", step)
            for p, step in HALVES
        ]
        self.two = [net.plan(lambda p=p: self.fold.at[p], lambda p=p: self.whole.at[p], "z", step) for p, step in HALVES]

    def step1(self):
        for copy in self.one:
            copy.start()

    def step2(self):
        arrive(self.one)
        for p, _ in HALVES:
            self.fold[p, 128 * p : 128 * p + 128, :] += self.half[p]
            self.two[p].start()

    def step3(self):
        arrive(self.two)
        return self.whole[0].astype(F32) + self.whole[1].astype(F32)


def token_scratch():
    return [pltpu.VMEM((2, 128, D), BF16), pltpu.VMEM((2, 256, D), BF16), pltpu.VMEM((2, 256, D), BF16)]


def gather_kernel(x, gain, w_gate, w_inner, w_out, w_bc, w_step, conv, bias, gate_gain, step_bias, decay_log, skip, normed_all, wx, wout, wbc, prm, xv, low, stepv, pk, send, recv, local):
    net = Net(send, recv)
    at = net.at
    yh, cx, cc, z, y = at["yh"], at["x"], at["c"], at["z"], at["y"]
    load = pltpu.make_async_copy(x, xv, local.at[0])
    load.start()
    stepv[...] = jnp.zeros_like(stepv)
    stepv[:, 0:HEADS] = w_step[...]
    pk[...] = jnp.zeros_like(pk)
    pk[0:4, :] = conv[...]
    pk[4:5, :] = bias[...]
    pk[5:6, :] = gate_gain[...]
    pk[6:7, 0:HEADS] = step_bias[...]
    pk[7:8, 0:HEADS] = decay_log[...]
    pk[8:9, 0:HEADS] = skip[...]
    net.barrier([("z", 1), ("z", -1), ("x", 1), ("x", -1), ("y", 1), ("y", -1), ("y", 2), ("c", 1)])
    first = {
        "x": ((w_gate, wx, 0, COLS), (w_out, wout, 0, COLS)),
        "y": ((w_inner, wx, WIDE, COLS), (stepv, wx, STEPS, 128), (w_bc.at[:, lanes(yh * 128, 128)], wbc, 0, 128)),
    }

    def spot(ref, base, n, yy, xx, cut=slice(None)):
        cut = pl.ds(0, 96) if cut == slice(None) else cut
        return ref.at[lax.rem(yy, 2), xx, cc, cut, lanes(base + (yy // 2) * n, n)]

    own = [pltpu.make_async_copy(src, spot(ref, base, n, y, cx), local.at[1 + i]) for i, (src, ref, base, n) in enumerate(first["x"] + first["y"])]
    own.append(pltpu.make_async_copy(pk, prm.at[yh], local.at[6]))
    sent = {"x": [], "y": []}
    for axis in ("x", "y"):
        for src, ref, base, n in first[axis]:
            sent[axis].append([net.start(src, spot(ref, base, n, y, cx), axis, step) for _, step in HALVES])
    load.wait()
    v = xv[...].astype(F32)
    root = lax.rsqrt(jnp.mean(v * v, axis=1, keepdims=True) + EPS)
    low[...] = (v * root * gain[...]).astype(BF16)
    zs = [net.start(low, rows(normed_all, z * 256, 256), "z", step) for _, step in HALVES]
    own.append(pltpu.make_async_copy(low, rows(normed_all, z * 256, 256), local.at[7]))
    for copy in own:
        copy.start()
    for axis in ("x", "y"):
        for src, ref, base, n in first[axis]:
            net.start(src, spot(ref, base, n, y, cx), "c")
    net.start(pk, prm.at[yh], "y", 2)
    second = {"x": [], "y": []}
    for axis in ("x", "y"):
        for (src, ref, base, n), copies in zip(first[axis], sent[axis]):
            for (part, step), copy in zip(HALVES, copies):
                copy.arrived()
                cut = pl.ds(48 * part, 48)
                here = spot(ref, base, n, y, net.near("x", -step), cut) if axis == "x" else spot(ref, base, n, net.near("y", -step), cx, cut)
                second[axis].append(net.start(here, here, axis, step))
    for copy in own[:5]:
        copy.wait()
    third = {"x": [], "y": []}

    def line(axis, ref, base, n, place, cut=None):
        cut = pl.ds(0, 96) if cut is None else cut
        if axis == "x":
            return ref.at[lax.rem(place, 2), :, cc, cut, lanes(base + (place // 2) * n, n)]
        return ref.at[:, place, cc, cut, lanes(base, 2 * n)]

    then = {"x": "y", "y": "x"}
    for axis in ("x", "y"):
        arrive(second[axis])
        for src, ref, base, n in first[axis]:
            here = line(axis, ref, base, n, at[then[axis]])
            third[axis].append([net.start(here, here, then[axis], step) for _, step in HALVES])
    for axis in ("x", "y"):
        for src, ref, base, n in first[axis]:
            for step in (1, -1, 2):
                here = spot(ref, base, n, y, net.near("x", step)) if axis == "x" else spot(ref, base, n, net.near("y", step), cx)
                net.start(here, here, "c")
    fourth = {"x": [], "y": []}

    def pass_on(axis):
        for (src, ref, base, n), copies in zip(first[axis], third[axis]):
            for (part, step), copy in zip(HALVES, copies):
                copy.arrived()
                place = net.near(then[axis], -step)
                here = line(axis, ref, base, n, place, pl.ds(48 * part, 48))
                fourth[axis].append(net.start(here, here, then[axis], step))
                here = line(axis, ref, base, n, place)
                net.start(here, here, "c")

    pass_on("y")
    pass_on("x")
    for (part, step), copy in zip(HALVES, zs):
        copy.arrived()
        here = rows(normed_all, net.near("z", -step) * 256 + 128 * part, 128)
        net.start(here, here, "z", step)
    for axis in ("y", "x"):
        arrive(fourth[axis])
        for src, ref, base, n in first[axis]:
            here = line(axis, ref, base, n, net.near(then[axis], 2))
            net.start(here, here, "c")
    net.finish()
    for copy in own[5:]:
        copy.wait()


def run_gather(*args):
    return pl.pallas_call(
        gather_kernel,
        out_shape=[
            SHAPE((LEN, D), BF16),
            SHAPE((2, 4, 2, 96, PROJ), BF16),
            SHAPE((2, 4, 2, 96, WIDE), BF16),
            SHAPE((2, 4, 2, 96, 256), BF16),
            SHAPE((GROUPS, 16, COLS), F32),
        ],
        in_specs=[ANY, VMEM, ANY, ANY, ANY, ANY] + [VMEM] * 7,
        out_specs=[ANY] * 5,
        scratch_shapes=[
            pltpu.VMEM((256, D), BF16),
            pltpu.VMEM((256, D), BF16),
            pltpu.VMEM((96, 128), BF16),
            pltpu.VMEM((16, COLS), F32),
        ]
        + sems(96)
        + [pltpu.SemaphoreType.DMA((8,))],
        compiler_params=pltpu.CompilerParams(collective_id=0, has_side_effects=True, vmem_limit_bytes=ROOM),
        name="gather_all",
    )(*args)


def forward_kernel(
    x, wx, wout, wbc, prm, conv_bc, bias_bc, cot,
    gate_out, inner_out, z_out, y_out, gm_out, mixed_out, h_out, dt_out, r_out, u_out, bc_out, bcin_out, zbc_out, stats_out, cot_all,
    cots, gps, ext, extbc, state, stat, slots, send, recv, local,
):
    i = pl.program_id(0)
    net = Net(send, recv)
    z = net.at["z"]
    here = lambda step=0: rows(cots, (net.near("z", step) if step else z) * 256, 256)
    part = lambda p, step: rows(cots, net.near("z", -step) * 256 + 128 * p, 128)
    c1 = [net.plan(lambda: cot, lambda: here(), "z", step) for _, step in HALVES]
    c2 = [net.plan(lambda p=p, s=s: part(p, s), lambda p=p, s=s: part(p, s), "z", s) for p, s in HALVES]
    q = [net.plan(lambda: stat, lambda: slots.at[z], "z", step) for step in (1, -1, 2)]
    own = lambda: pltpu.make_async_copy(cot, here(), local.at[0])
    out = lambda: pltpu.make_async_copy(cots, cot_all, local.at[1])

    @pl.when(i == 0)
    def _():
        net.barrier([("z", 1), ("z", -1), ("z", 2)])
        own().start()
        for copy in c1:
            copy.start()
        ext[0:8, :] = jnp.zeros((8, WIDE), F32)
        extbc[0:8, :] = jnp.zeros((8, 256), F32)
        state[...] = jnp.zeros_like(state)

    @pl.when((i > 0) & (i < BLOCKS))
    def _():
        ext[0:8, :] = ext[BLOCK : BLOCK + 8, :]
        extbc[0:8, :] = extbc[BLOCK : BLOCK + 8, :]

    @pl.when(i == BLOCKS - 1)
    def _():
        for copy in c1:
            copy.arrived()
        for copy in c2:
            copy.start()

    @pl.when(i < BLOCKS)
    def _():
        xb = x[...]
        bc_in = dot(xb, wbc[...])
        bcin_out[...] = bc_in
        extbc[8 : BLOCK + 8, :] = bc_in
        zb = bias_bc[...] + sum(conv_bc[j : j + 1, :] * extbc[5 + j : 5 + j + BLOCK, :] for j in range(4))
        zbc_out[...] = zb
        bc = (zb * sigmoid(zb)).astype(BF16)
        bc_out[...] = bc
        b, c = bc[:, :STATE], bc[:, STATE:]
        scores = jnp.where(iota((BLOCK, BLOCK), 0) >= iota((BLOCK, BLOCK), 1), dot_nt(c, b), 0.0)
        tri, spread = lower(), expander()
        left = iota((BLOCK, 128), 1) < 64
        steps = dot(xb, wx[:, STEPS:])
        total = jnp.zeros((BLOCK, 128), F32)
        for g in range(GROUPS):
            cut = slice(g * COLS, (g + 1) * COLS)
            u = steps[:, 128 * g : 128 * (g + 1)] + prm[g, 6:7, 0:128]
            dt = jnp.maximum(u, 0.0) + jnp.log(1.0 + jnp.exp(-jnp.abs(u)))
            rate = -jnp.exp(prm[g, 7:8, 0:128]) * LOG2E
            r = dot_right(tri, dt * rate, 3)
            u_out[g] = u
            dt_out[g] = dt
            r_out[g] = r
            rt = jnp.transpose(r)
            gate = dot(xb, wx[:, cut])
            inner = dot(xb, wx[:, WIDE + g * COLS : WIDE + (g + 1) * COLS])
            gate_out[:, cut] = gate
            inner_out[:, cut] = inner
            ext[8 : BLOCK + 8, cut] = inner
            zv = prm[g, 4:5, :] + sum(prm[g, j : j + 1, :] * ext[5 + j : 5 + j + BLOCK, cut] for j in range(4))
            z_out[:, cut] = zv
            xv = zv * sigmoid(zv)
            last = r[BLOCK - 1 : BLOCK, :]
            w = xv * dot_left(dt, spread, 2)
            grow = dot_left(jnp.exp2(r), spread, 2)
            tail = dot_left(jnp.exp2(last - r), spread, 2)
            skip = dot_left(prm[g, 8:16, 0:128], spread, 3)[0:1, :]
            wl = w.astype(BF16)
            h = state[:, cut]
            h_out[0, g] = h
            parts = []
            for p in range(HEADS // 2):
                halves = []
                for n in (2 * p, 2 * p + 1):
                    gap = jnp.minimum(r[:, n : n + 1] - rt[n : n + 1, :], 0.0)
                    halves.append(dot((scores * jnp.exp2(gap)).astype(BF16), wl[:, 128 * p : 128 * (p + 1)]))
                parts.append(jnp.where(left, halves[0], halves[1]))
            yv = jnp.concatenate(parts, axis=1) + grow * dot(c, h.astype(BF16)) + skip * xv
            y_out[:, cut] = yv
            state[:, cut] = grow[BLOCK - 1 : BLOCK, :] * h + dot_tn(b, (tail * w).astype(BF16))
            gp = yv * (gate * sigmoid(gate))
            gps[pl.ds(pl.multiple_of(i * BLOCK, BLOCK), BLOCK), cut] = gp
            sq = gp * gp
            total = total + (sq[:, 0:128] + sq[:, 128:256] + sq[:, 256:384])
        stat[pl.ds(i, 1), :] = token_row(total)

    @pl.when(i == BLOCKS)
    def _():
        own().wait()

    @pl.when(i == 2 * BLOCKS - 1)
    def _():
        for copy in c2:
            copy.arrived()
        out().start()

    @pl.when(i >= BLOCKS)
    def _():
        t = i - BLOCKS
        block = lax.rem(z + t + lax.div(t, 2) - 2 * lax.div(t, 3), 4)
        at = pl.ds(pl.multiple_of(block * BLOCK, BLOCK), BLOCK)
        gm = dot(cots[at, :], wout[...])
        gm_out[at, :] = gm
        gain = jnp.concatenate([prm[0, 5:6, :], prm[1, 5:6, :]], axis=1)
        stat[pl.ds(BLOCKS + block, 1), :] = token_row(gm * gain * gps[at, :])

    @pl.when(i == 2 * BLOCKS - 1)
    def _():
        for copy in q:
            copy.start()
        slots[z] = stat[...]
        for copy in q:
            copy.arrived()
        sums = (slots[0] + slots[1]) + (slots[2] + slots[3])
        root = lax.rsqrt(sums[0:4, :] * (1.0 / INNER) + EPS)
        stats_out[0:4, :] = root
        stats_out[4:8, :] = root * root * root * (sums[4:8, :] * (1.0 / INNER))
        columns = jnp.transpose(stats_out[...])
        gain = jnp.concatenate([prm[0, 5:6, :], prm[1, 5:6, :]], axis=1)
        for k in range(BLOCKS):
            at = slice(k * BLOCK, (k + 1) * BLOCK)
            mixed_out[at, :] = (gps[at, :] * columns[:, k : k + 1] * gain).astype(BF16)
        for copy in c1 + c2 + q:
            copy.left()
        out().wait()


def run_forward(x, wx, wout, wbc, prm, conv_bc, bias_bc, cot):
    first = lambda k: jnp.minimum(k, BLOCKS - 1)
    const = lambda *s: pl.BlockSpec(s, lambda k: (0,) * len(s), pipeline_mode=pl.Buffered(1))
    keep = lambda *s: pl.BlockSpec(s, lambda k: (0,) * len(s))
    block = lambda n: pl.BlockSpec((BLOCK, n), lambda k: (first(k), 0))
    small = lambda: pl.BlockSpec((GROUPS, BLOCK, 128), lambda k: (0, first(k), 0))
    wide = SHAPE((LEN, WIDE), F32)
    narrow = SHAPE((GROUPS, LEN, 128), F32)
    return pl.pallas_call(
        forward_kernel,
        grid=(2 * BLOCKS,),
        out_shape=[
            wide,
            wide,
            wide,
            wide,
            wide,
            SHAPE((LEN, WIDE), BF16),
            SHAPE((BLOCKS, GROUPS, STATE, COLS), F32),
            narrow,
            narrow,
            narrow,
            SHAPE((LEN, 256), BF16),
            SHAPE((LEN, 256), F32),
            SHAPE((LEN, 256), F32),
            SHAPE((8, 256), F32),
            SHAPE((LEN, D), BF16),
        ],
        in_specs=[
            block(D),
            const(D, PROJ),
            const(D, WIDE),
            const(D, 256),
            const(GROUPS, 16, COLS),
            const(4, 256),
            const(1, 256),
            ANY,
        ],
        out_specs=[
            block(WIDE),
            block(WIDE),
            block(WIDE),
            block(WIDE),
            keep(LEN, WIDE),
            keep(LEN, WIDE),
            pl.BlockSpec((1, GROUPS, STATE, COLS), lambda k: (first(k), 0, 0, 0)),
            small(),
            small(),
            small(),
            block(256),
            block(256),
            block(256),
            keep(8, 256),
            ANY,
        ],
        scratch_shapes=[
            pltpu.VMEM((LEN, D), BF16),
            pltpu.VMEM((LEN, WIDE), F32),
            pltpu.VMEM((BLOCK + 8, WIDE), F32),
            pltpu.VMEM((BLOCK + 8, 256), F32),
            pltpu.VMEM((STATE, WIDE), F32),
            pltpu.VMEM((8, BLOCK), F32),
            pltpu.VMEM((4, 8, BLOCK), F32),
        ]
        + sems(7)
        + [pltpu.SemaphoreType.DMA((2,))],
        compiler_params=pltpu.CompilerParams(collective_id=1, has_side_effects=True, vmem_limit_bytes=ROOM),
        name="forward",
    )(x, wx, wout, wbc, prm, conv_bc, bias_bc, cot)


def backward_kernel(
    gm, gate, inner, zin, y, hin, prm, bc, dt, r, u, stats, part, dout, tokens,
    cat_out, dbc_out, acc, branch_out, wout_out,
    ext, dstate, dst, dbc, held, got, g1, g2, g3, s1, s2, s3, s4, s5, s6, s7, send, recv, local,
):
    k = pl.program_id(0)
    net = Net(send, recv)
    cc, z = net.at["c"], net.at["z"]
    cross = net.plan(lambda: dout.at[:, :, net.other], lambda: got, "c")
    token = TokenSum(net, part, (g1, g2, g3))
    ring = RingSum(net, "y", held, ((0, COLS),), (s1, s2, s3, s4, s5, s6, s7))
    loads = lambda: [
        pltpu.make_async_copy(dout.at[:, :, cc], held, local.at[0]),
        pltpu.make_async_copy(rows(part, net.near("z", 1) * 256, 256), g2.at[0], local.at[1]),
        pltpu.make_async_copy(rows(part, net.near("z", -1) * 256, 256), g2.at[1], local.at[2]),
        pltpu.make_async_copy(rows(part, z * 256, 256), branch_out, local.at[3]),
    ]

    @pl.when(k == 0)
    def _():
        net.barrier([("z", 1), ("z", -1), ("x", 1), ("x", -1), ("y", 1), ("y", -1), ("c", 1)])
        cross.start()
        token.step1()
        for copy in loads():
            copy.start()
        acc[...] = jnp.zeros_like(acc)
        ext[BLOCK : BLOCK + 8, :] = jnp.zeros((8, WIDE), F32)
        dstate[...] = jnp.zeros_like(dstate)

    @pl.when(k > 0)
    def _():
        ext[BLOCK : BLOCK + 8, :] = ext[0:8, :]

    b, c = bc[:, :STATE], bc[:, STATE:]
    valid = iota((BLOCK, BLOCK), 1) >= iota((BLOCK, BLOCK), 0)
    scores = jnp.where(valid, dot_nt(b, c), 0.0)
    both = jnp.concatenate([stats[pl.ds(BLOCKS - 1 - k, 1), :], stats[pl.ds(2 * BLOCKS - 1 - k, 1), :], jnp.zeros((6, BLOCK), F32)], axis=0)
    column = jnp.transpose(both)
    ir, cr = column[:, 0:1], column[:, 1:2]
    spread, fold = expander(), reducer()
    left = iota((BLOCK, 128), 1) < 64
    suffix, prefix = upper(), lower(strict=True)
    dst[...] = jnp.zeros_like(dst)
    dbc[...] = jnp.zeros_like(dbc)
    for g in range(GROUPS):
        if g == 0:

            @pl.when(k == 1)
            def _():
                ring.step2()

            @pl.when(k == 2)
            def _():
                ring.step3()

        else:

            @pl.when(k == 0)
            def _():
                for copy in loads():
                    copy.wait()
                cross.arrived()
                held[...] += got[...]
                ring.step1()

            @pl.when(k == 1)
            def _():
                token.step2()

            @pl.when(k == 2)
            def _():
                ring.step4()

        cut = slice(g * COLS, (g + 1) * COLS)
        yv = y[:, cut]
        gv = gate[:, cut]
        sig = sigmoid(gv)
        act = gv * sig
        gain = prm[g, 5:6, :]
        gp = yv * act
        gmix = gm[:, cut]
        gain_grad = gmix * gp * ir
        gated = ir * (gmix * gain) - gp * cr
        gs = gated * act
        cat_out[:, cut] = (gated * yv * sig * (1.0 + gv * (1.0 - sig))).astype(BF16)
        xi = inner[:, cut]
        zv = zin[:, cut]
        zs = sigmoid(zv)
        xv = zv * zs
        rv = r[g]
        rt = jnp.transpose(rv)
        last = rv[BLOCK - 1 : BLOCK, :]
        dte = dot_left(dt[g], spread, 2)
        grow = dot_left(jnp.exp2(rv), spread, 2)
        tail = dot_left(jnp.exp2(last - rv), spread, 2)
        skip = dot_left(prm[g, 8:16, 0:128], spread, 3)[0:1, :]
        w = xv * dte
        wl = w.astype(BF16)
        gl = gs.astype(BF16)
        h = hin[0, g]
        dh = dstate[:, cut]
        dhl = dh.astype(BF16)
        parts = []
        for p in range(HEADS // 2):
            halves = []
            pair = slice(128 * p, 128 * (p + 1))
            wp, gpair = wl[:, pair], gl[:, pair]
            zero = jnp.zeros_like(wp)
            for n in (2 * p, 2 * p + 1):
                decay = jnp.exp2(jnp.minimum(rt[n : n + 1, :] - rv[:, n : n + 1], 0.0))
                halves.append(dot((scores * decay).astype(BF16), gpair))
                mine = jnp.where(left, wp, zero) if n % 2 == 0 else jnp.where(left, zero, wp)
                dst[...] += dot_nt(mine, gpair) * decay
            parts.append(jnp.where(left, halves[0], halves[1]))
        dwi = jnp.concatenate(parts, axis=1)
        dws = tail * dot(b, dhl)
        dw = dwi + dws
        skipgrad = gs * xv
        diff = dot_left(gl.astype(F32) * (yv - skip * xv) - wl.astype(F32) * dwi, fold, 3)
        zsum = dot_left(w * dws, fold, 3)
        const = dot_left(jnp.sum(h * dh, axis=0, keepdims=True) * grow[BLOCK - 1 : BLOCK, :] + jnp.zeros((8, COLS), F32), fold, 3)
        da = dot_right(suffix, diff, 3) + dot_right(prefix, zsum, 3) + const[0:1, :]
        rate = -jnp.exp(prm[g, 7:8, 0:128])
        dstep = (dot_left(xv * dw, fold, 3) + rate * da) * sigmoid(u[g])
        cat_out[:, STEPS + 128 * g : STEPS + 128 * (g + 1)] = dstep.astype(BF16)
        gx = (grow * gs).astype(BF16)
        dbc[:, STATE:] += dot_nt(gx, h.astype(BF16))
        dbc[:, :STATE] += dot_nt((tail * w).astype(BF16), dhl)
        dstate[:, cut] = grow[BLOCK - 1 : BLOCK, :] * dh + dot_tn(c, gx)
        dx = dte * dw + skip * gs
        dz = dx * (zs * (1.0 + zv * (1.0 - zs)))
        ext[0:BLOCK, cut] = dz
        gi = jnp.zeros((BLOCK, COLS), F32)
        for j in range(4):
            moved = ext[3 - j : 3 - j + BLOCK, cut]
            gi = gi + prm[g, j : j + 1, :] * moved
            acc[g, j : j + 1, :] += jnp.sum(xi * moved, axis=0, keepdims=True)
        cat_out[:, WIDE + g * COLS : WIDE + (g + 1) * COLS] = gi.astype(BF16)
        acc[g, 4:5, :] += jnp.sum(dz, axis=0, keepdims=True)
        acc[g, 5:6, :] += jnp.sum(gain_grad, axis=0, keepdims=True)
        acc[g, 6:7, 0:128] += jnp.sum(dstep, axis=0, keepdims=True)
        acc[g, 7:8, 0:128] += jnp.sum(da * dt[g], axis=0, keepdims=True) * rate
        acc[g, 8:9, 0:128] += dot_left(jnp.sum(skipgrad, axis=0, keepdims=True) + jnp.zeros((8, COLS), F32), fold, 3)[0:1, :]
    ds = jnp.where(valid, dst[...], 0.0).astype(BF16)
    dbc_out[:, STATE:] = (dbc[:, STATE:] + dot_tn(ds, b)).astype(BF16)
    dbc_out[:, :STATE] = (dbc[:, :STATE] + dot(ds, c)).astype(BF16)

    @pl.when(k == BLOCKS - 1)
    def _():
        wout_out[...] = ring.step5()
        branch = branch_out[...].astype(F32) + token.step3()
        branch_out[...] = (tokens[...].astype(F32) + branch).astype(BF16)
        for copy in net.copies:
            copy.left()


def run_backward(gm, gate, inner, zin, y, hin, prm, bc, dt, r, u, stats, part, dout, tokens):
    rev = lambda k: BLOCKS - 1 - k
    cols = lambda n: pl.BlockSpec((BLOCK, n), lambda k: (rev(k), 0))
    small = lambda: pl.BlockSpec((GROUPS, BLOCK, 128), lambda k: (0, rev(k), 0))
    keep = lambda *s: pl.BlockSpec(s, lambda k: (0,) * len(s))
    return pl.pallas_call(
        backward_kernel,
        grid=(BLOCKS,),
        out_shape=[
            SHAPE((LEN, PROJ), BF16),
            SHAPE((LEN, 256), BF16),
            SHAPE((GROUPS, 16, COLS), F32),
            SHAPE((256, D), BF16),
            SHAPE((96, COLS), F32),
        ],
        in_specs=[cols(WIDE)] * 5
        + [
            pl.BlockSpec((1, GROUPS, STATE, COLS), lambda k: (rev(k), 0, 0, 0)),
            keep(GROUPS, 16, COLS),
            cols(256),
            small(),
            small(),
            small(),
            keep(8, 256),
            ANY,
            ANY,
            keep(256, D),
        ],
        out_specs=[cols(PROJ), cols(256), keep(GROUPS, 16, COLS), keep(256, D), keep(96, COLS)],
        scratch_shapes=[
            pltpu.VMEM((BLOCK + 8, WIDE), F32),
            pltpu.VMEM((STATE, WIDE), F32),
            pltpu.VMEM((BLOCK, BLOCK), F32),
            pltpu.VMEM((BLOCK, 256), F32),
            pltpu.VMEM((2, 4, 96, WIDE), BF16),
            pltpu.VMEM((2, 4, 96, WIDE), BF16),
        ]
        + token_scratch()
        + ring_scratch("y", COLS)
        + sems(13)
        + [pltpu.SemaphoreType.DMA((4,))],
        compiler_params=pltpu.CompilerParams(collective_id=2, has_side_effects=True, vmem_limit_bytes=ROOM),
        name="backward",
    )(gm, gate, inner, zin, y, hin, prm, bc, dt, r, u, stats, part, dout, tokens)


def tail_kernel(
    gn, dcat, dbc, zbc, bc_in, normed, acc, wbc, tokens, cot, gain, conv,
    tokens_out, gate_out, inner_out, bc_out, small_out,
    gnv, nv, mine, slots, zv, xi, wv, xv, ov, ext, gnbc, held, got, dbw, heldb, gotb, small, sp0, sp1, sp2, sp3, bz, by,
    g1, g2, g3, a1, a2, a3, a4, a5, a6, a7, b1, b2, b3, b4, b5, b6, b7, c1, c2, c3, c4, c5, c6, c7, send, recv, local,
):
    net = Net(send, recv)
    at = net.at
    yh, cx, cc, z, y = at["yh"], at["x"], at["c"], at["z"], at["y"]
    loads = [
        pltpu.make_async_copy(src, dst, local.at[i])
        for i, (src, dst) in enumerate(
            (
                (dcat.at[:, :, cc], held),
                (rows(gn, net.near("z", 1) * 256, 256), g2.at[0]),
                (rows(gn, net.near("z", -1) * 256, 256), g2.at[1]),
                (gn, gnv),
                (normed, nv),
                (rows(zbc, z * 256, 256), zv.at[pl.ds(0, 256)]),
                (rows(zbc, lax.rem(z * 256 + 256, LEN), 16), zv.at[pl.ds(256, 16)]),
                (rows(bc_in, z * 256, 256), xi),
                (wbc, wv),
                (tokens, xv),
                (cot, ov),
            )
        )
    ]
    token = TokenSum(net, gn, (g1, g2, g3))
    ring_gate = RingSum(net, "x", held, ((0, COLS),), (a1, a2, a3, a4, a5, a6, a7))
    ring_inner = RingSum(net, "y", held, ((WIDE, COLS), (STEPS, 128)), (b1, b2, b3, b4, b5, b6, b7))
    ring_bc = RingSum(net, "x", heldb, ((0, 128),), (c1, c2, c3, c4, c5, c6, c7))
    net.barrier([(a, s) for a in ("z", "x", "y") for s in (1, -1, 2)] + [("c", 1)])
    cross = net.start(dcat.at[:, :, net.other], got, "c")
    mine[0:LEN, :] = dbc[...]
    mine[LEN : LEN + 16, :] = jnp.zeros((16, 256), BF16)
    swap = [net.start(rows(mine, net.near("z", s) * 256, 272), slots.at[z], "z", s) for s in (1, -1, 2)]
    token.step1()
    for copy in loads:
        copy.start()
    slots[z] = mine[pl.ds(pl.multiple_of(z * 256, 16), 272), :]
    arrive(swap)
    for copy in loads:
        copy.wait()
    total = (slots[0].astype(F32) + slots[1].astype(F32)) + (slots[2].astype(F32) + slots[3].astype(F32))
    sig = sigmoid(zv[...])
    dz = total * (sig * (1.0 + zv[...] * (1.0 - sig)))
    ext[...] = jnp.where(iota((272, 256), 0) + z * 256 < LEN, dz, 0.0)
    gbc = jnp.zeros((256, 256), F32)
    small[0:16, :] = acc[0]
    small[16:32, :] = acc[1]
    small[32:48, :] = jnp.zeros((16, COLS), F32)
    for j in range(4):
        moved = ext[3 - j : 3 - j + 256, :]
        gbc = gbc + conv[j : j + 1, :] * moved
        small[36 + j : 37 + j, 0:256] = jnp.sum(xi[...] * moved, axis=0, keepdims=True)
    small[40:41, 0:256] = jnp.sum(ext[0:256, :], axis=0, keepdims=True)
    gbc = gbc.astype(BF16)
    own = pl.ds(pl.multiple_of(z * 256, 16), 256)
    dbw[...] = dot_tn(nv[own, :], gbc).astype(BF16).reshape(2, 4, 2, 96, 256)
    crossb = net.start(dbw.at[:, :, net.other], gotb, "c")
    gnbc[...] = dot_nt(gbc, wv[...])
    gain_row = gain[...]
    part = jnp.sum(gnbc[...] * nv[own, :].astype(F32), axis=0, keepdims=True)
    for k in range(BLOCKS):
        cut = slice(k * 256, (k + 1) * 256)
        part = part + jnp.sum(gnv[cut, :].astype(F32) * nv[cut, :].astype(F32), axis=0, keepdims=True)
    part = part / gain_row
    for k in range(4):
        small[32 + k : 33 + k, :] = part[:, k * COLS : (k + 1) * COLS]
    sp0[z] = small[32:48, :]
    q = net.around(sp0.at[z], sp0.at[z], "z")
    cross.arrived()
    held[...] += got[...]
    ring_inner.step1()
    ring_gate.step1()
    token.step2()
    crossb.arrived()
    heldb[...] = dbw[:, :, cc] + gotb[...]
    ring_bc.step1()
    arrive(q)
    sp1[cx, 0:32, :] = small[0:32, :]
    sp1[cx, 32:48, :] = (sp0[0] + sp0[1]) + (sp0[2] + sp0[3])
    q = net.around(sp1.at[cx], sp1.at[cx], "x")
    ring_gate.step2()
    ring_inner.step2()
    ring_bc.step2()
    arrive(q)
    sp2[y] = (sp1[0] + sp1[1]) + (sp1[2] + sp1[3])
    q = net.around(sp2.at[y], sp2.at[y], "y")
    ring_bc.step3()
    ring_gate.step3()
    ring_inner.step3()
    arrive(q)
    sp3[cc] = (sp2[0] + sp2[1]) + (sp2[2] + sp2[3])
    q = [net.start(sp3.at[cc], sp3.at[cc], "c")]
    ring_bc.step4()
    ring_gate.step4()
    ring_inner.step4()
    arrive(q)
    small_out[...] = sp3[0] + sp3[1]
    bz[z] = ring_bc.step5()
    q = net.around(bz.at[z], bz.at[z], "z")
    gate_out[...] = ring_gate.step5()
    inner_out[...] = ring_inner.step5()
    arrive(q)
    by[yh] = (bz[0] + bz[1]) + (bz[2] + bz[3])
    q = [net.start(by.at[yh], by.at[yh], "y", 2)]
    v = xv[...].astype(F32)
    root = lax.rsqrt(jnp.mean(v * v, axis=1, keepdims=True) + EPS)
    g = token.step3() + gnv[own, :].astype(F32) + gnbc[...]
    scaled = g * gain_row
    tokens_out[...] = ov[...].astype(F32) + root * scaled - v * (root * root * root) * jnp.mean(scaled * v, axis=1, keepdims=True)
    arrive(q)
    bc_out[:, :128] = by[0]
    bc_out[:, 128:] = by[1]
    net.finish()


def run_tail(gn, dcat, dbc, zbc, bc_in, normed, acc, wbc, tokens, cot, gain, conv):
    bf = lambda *s: pltpu.VMEM(s, BF16)
    f32 = lambda *s: pltpu.VMEM(s, F32)
    return pl.pallas_call(
        tail_kernel,
        out_shape=[
            SHAPE((256, D), F32),
            SHAPE((96, COLS), F32),
            SHAPE((96, COLS + 128), F32),
            SHAPE((96, 256), F32),
            SHAPE((48, COLS), F32),
        ],
        in_specs=[ANY, ANY, VMEM, ANY, ANY, ANY, VMEM, ANY, ANY, ANY, VMEM, VMEM],
        out_specs=[VMEM] * 5,
        scratch_shapes=[
            bf(LEN, D),
            bf(LEN, D),
            bf(LEN + 16, 256),
            bf(4, 272, 256),
            f32(272, 256),
            f32(256, 256),
            bf(D, 256),
            bf(256, D),
            bf(256, D),
            f32(272, 256),
            f32(256, D),
            bf(2, 4, 96, PROJ),
            bf(2, 4, 96, PROJ),
            bf(2, 4, 2, 96, 256),
            bf(2, 4, 96, 256),
            bf(2, 4, 96, 256),
            f32(48, COLS),
            f32(4, 16, COLS),
            f32(4, 48, COLS),
            f32(4, 48, COLS),
            f32(2, 48, COLS),
            f32(4, 96, 128),
            f32(2, 96, 128),
        ]
        + token_scratch()
        + ring_scratch("x", COLS)
        + ring_scratch("y", COLS + 128)
        + ring_scratch("x", 128)
        + sems(64)
        + [pltpu.SemaphoreType.DMA((11,))],
        compiler_params=pltpu.CompilerParams(collective_id=3, has_side_effects=True, vmem_limit_bytes=ROOM),
        name="tail",
    )(gn, dcat, dbc, zbc, bc_in, normed, acc, wbc, tokens, cot, gain, conv)


def finish_kernel(tokens, branch, inner, bc, small, gate, wout, tokens_out, branch_out, step_out, inner_out, bc_out, gate_out, wout_out, norm, conv, bias, conv_bc, bias_bc, step_bias, decay, skip, gain, sem):
    big = [
        pltpu.make_async_copy(src, dst, sem.at[i])
        for i, (src, dst) in enumerate(
            ((tokens, tokens_out), (branch, branch_out), (inner.at[:, pl.ds(0, COLS)], inner_out), (bc, bc_out), (gate, gate_out), (wout, wout_out))
        )
    ]
    for copy in big:
        copy.start()
    step_out[...] = inner[:, COLS : COLS + HEADS]
    for k in range(4):
        norm[:, k * COLS : (k + 1) * COLS] = small[32 + k : 33 + k, :]
    conv_bc[...] = small[36:40, 0:256]
    bias_bc[...] = small[40:41, 0:256]
    mine = small[pl.ds(pl.multiple_of(lax.axis_index("yh") * 16, 8), 16), :]
    conv[...] = mine[0:4, :]
    bias[...] = mine[4:5, :]
    gain[...] = mine[5:6, :]
    step_bias[...] = mine[6:7, 0:HEADS]
    decay[...] = mine[7:8, 0:HEADS]
    skip[...] = mine[8:9, 0:HEADS]
    for copy in big:
        copy.wait()


def run_finish(tokens, branch, inner, bc, small, gate, wout):
    f32 = lambda *s: SHAPE(s, F32)
    return pl.pallas_call(
        finish_kernel,
        out_shape=[
            f32(256, D),
            SHAPE((256, D), BF16),
            f32(96, HEADS),
            f32(96, COLS),
            f32(96, 256),
            f32(96, COLS),
            f32(96, COLS),
            f32(1, D),
            f32(4, COLS),
            f32(1, COLS),
            f32(4, 256),
            f32(1, 256),
            f32(1, HEADS),
            f32(1, HEADS),
            f32(1, HEADS),
            f32(1, COLS),
        ],
        in_specs=[ANY, ANY, VMEM, ANY, VMEM, ANY, ANY],
        out_specs=[ANY, ANY, VMEM] + [ANY] * 4 + [VMEM] * 9,
        scratch_shapes=[pltpu.SemaphoreType.DMA((6,))],
        compiler_params=pltpu.CompilerParams(vmem_limit_bytes=16 * 2**20),
        name="finish",
    )(tokens, branch, inner, bc, small, gate, wout)


def shards(tokens, norm_gain, w_gate, w_inner, w_bc, w_step, conv_inner, bias_inner, conv_bc, bias_bc, step_bias, decay_log, skip_gain, gate_gain, w_out, cotangent):
    row = lambda v: v.reshape(1, -1)
    gain = row(norm_gain)
    normed, wx, wout, wbc, prm = run_gather(
        tokens, gain, w_gate, w_inner, w_out, w_bc, w_step, conv_inner, row(bias_inner), row(gate_gain), row(step_bias), row(decay_log), row(skip_gain)
    )
    wx, wout, wbc = wx.reshape(D, PROJ), wout.reshape(D, WIDE), wbc.reshape(D, 256)
    gate, inner, zin, y, gm, mixed, hin, dt, r, u, bc, bc_in, zbc, stats, cot_all = run_forward(
        normed, wx, wout, wbc, prm, conv_bc, row(bias_bc), cotangent
    )
    part = dot_nt(mixed, wout).astype(BF16)
    dout = dot_tn(cot_all, mixed).astype(BF16).reshape(2, 4, 2, 96, WIDE)
    cat, dbc, acc, output, wout_grad = run_backward(gm, gate, inner, zin, y, hin, prm, bc, dt, r, u, stats, part, dout, tokens)
    gn = dot_nt(cat, wx).astype(BF16)
    dcat = dot_tn(normed, cat).astype(BF16).reshape(2, 4, 2, 96, PROJ)
    tokens_grad, gate_grad, inner_grad, bc_grad, small = run_tail(gn, dcat, dbc, zbc, bc_in, normed, acc, wbc, tokens, cotangent, gain, conv_bc)
    (
        tokens_grad, output, step_grad, inner_grad, bc_grad, gate_grad, wout_grad,
        norm, conv, bias, conv_bc_grad, bias_bc_grad, step_bias_grad, decay, skip, gate_gain_grad,
    ) = run_finish(tokens_grad, output, inner_grad, bc_grad, small, gate_grad, wout_grad)
    flat = lambda v: v.reshape(-1)
    return (
        output, tokens_grad, flat(norm), gate_grad, inner_grad, bc_grad, step_grad, conv, flat(bias), conv_bc_grad,
        flat(bias_bc_grad), flat(step_bias_grad), flat(decay), flat(skip), flat(gate_gain_grad), wout_grad,
    )


def solution(mesh):
    fine = Mesh(mesh.devices.reshape(2, 4, 2, 2, 4), AXES)
    dp, tensor = ("yl", "x", "c"), ("yh", "z")
    tokens, weight = P(dp + tensor, None), P(dp, tensor)
    heads, shared = P(tensor), P()
    return jax.shard_map(
        shards,
        mesh=fine,
        in_specs=(
            tokens, shared, weight, weight, P(dp, None), weight, P(None, tensor), heads,
            shared, shared, heads, heads, heads, heads, weight, tokens,
        ),
        out_specs=(
            tokens, tokens, shared, weight, weight, P(dp, None), weight, P(None, tensor), heads,
            shared, shared, heads, heads, heads, heads, weight,
        ),
        check_vma=False,
    )
```

```python
import jax
import jax.numpy as jnp
from jax import lax
from jax.experimental import pallas as pl
from jax.experimental.pallas import tpu as pltpu
from jax.sharding import Mesh
from jax.sharding import PartitionSpec as P

D = 1536
LEN = 1024
INNER = 3072
STATE = 128
BLOCK = 256
BLOCKS = LEN // BLOCK
GROUPS = 2
HEADS = 6
COLS = HEADS * 64
WIDE = GROUPS * COLS
STEPS = 2 * WIDE
PROJ = STEPS + GROUPS * 128
LOG2E = 1.4426950408889634
EPS = 1e-05
F32 = jnp.float32
BF16 = jnp.bfloat16
MESH = pl.DeviceIdType.MESH
AXES = ("yl", "x", "c", "yh", "z")
ANY = pl.BlockSpec(memory_space=pl.ANY)
VMEM = pl.BlockSpec(memory_space=pltpu.VMEM)
SHAPE = jax.ShapeDtypeStruct
ROOM = 60 * 2**20


def dot(a, b):
    return jnp.dot(a, b, preferred_element_type=F32)


def dot_nt(a, b):
    return lax.dot_general(a, b, (((1,), (1,)), ((), ())), preferred_element_type=F32)


def dot_tn(a, b):
    return lax.dot_general(a, b, (((0,), (0,)), ((), ())), preferred_element_type=F32)


def pieces(v, n):
    out = []
    for _ in range(n):
        hi = v.astype(BF16)
        out.append(hi)
        v = v - hi.astype(F32)
    return out


def dot_left(v, ones, n):
    return sum(dot(p, ones) for p in pieces(v, n))


def dot_right(ones, v, n):
    return sum(dot(ones, p) for p in pieces(v, n))


def iota(shape, axis):
    return lax.broadcasted_iota(jnp.int32, shape, axis)


def expander():
    row, col = iota((128, COLS), 0), iota((128, COLS), 1)
    return (row == lax.shift_right_logical(col, 6)).astype(BF16)


def reducer():
    row, col = iota((COLS, 128), 0), iota((COLS, 128), 1)
    return (col == lax.shift_right_logical(row, 6)).astype(BF16)


def sigmoid(v):
    return 1.0 / (1.0 + jnp.exp(-v))


def lower(strict=False):
    row, col = iota((BLOCK, BLOCK), 0), iota((BLOCK, BLOCK), 1)
    return ((row > col) if strict else (row >= col)).astype(BF16)


def upper():
    return (iota((BLOCK, BLOCK), 0) <= iota((BLOCK, BLOCK), 1)).astype(BF16)


def token_row(v):
    v = sum(v[:, 128 * i : 128 * (i + 1)] for i in range(v.shape[1] // 128))
    ones = jnp.ones((8, 128), BF16)
    return sum(dot_nt(ones, p) for p in pieces(v, 3))[0:1, :]


class Net:
    def __init__(self, send, recv):
        self.send, self.recv, self.copies = send, recv, []
        self.at = {name: lax.axis_index(name) for name in AXES}
        self.at["y"] = self.at["yh"] * 2 + self.at["yl"]
        self.places = {(a, s): lax.rem(self.at[a] + s + 4, 4) for a in ("x", "y", "z") for s in (1, -1, 2)}
        self.other = 1 - self.at["c"]
        self.targets = {("c", 1): {"c": self.other}}
        for (a, s), place in self.places.items():
            self.targets[a, s] = {"yh": place // 2, "yl": lax.rem(place, 2)} if a == "y" else {a: place}

    def near(self, axis, step):
        return self.places[axis, step]

    def plan(self, src, dst, axis, step=1):
        copy = Copy(self, len(self.copies), src, dst, self.targets[axis, step])
        self.copies.append(copy)
        return copy

    def start(self, src, dst, axis, step=1):
        return self.plan(lambda: src, lambda: dst, axis, step).start()

    def around(self, src, dst, axis):
        return [self.start(src, dst, axis, step) for step in (1, -1, 2)]

    def barrier(self, peers):
        here = pltpu.get_barrier_semaphore()
        for peer in peers:
            pl.semaphore_signal(here, inc=1, device_id=self.targets[peer], device_id_type=MESH)
        pl.semaphore_wait(here, len(peers))

    def finish(self):
        for copy in self.copies:
            copy.arrived()
        for copy in self.copies:
            copy.left()


class Copy:
    def __init__(self, net, index, src, dst, target):
        self.net, self.index, self.src, self.dst, self.target = net, index, src, dst, target
        self.here, self.gone = False, False

    def made(self):
        return pltpu.make_async_remote_copy(
            src_ref=self.src(),
            dst_ref=self.dst(),
            send_sem=self.net.send.at[self.index],
            recv_sem=self.net.recv.at[self.index],
            device_id=self.target,
            device_id_type=MESH,
        )

    def start(self):
        self.made().start()
        return self

    def arrived(self):
        if not self.here:
            self.here = True
            self.made().wait_recv()

    def left(self):
        if not self.gone:
            self.gone = True
            self.made().wait_send()


def sems(n):
    return [pltpu.SemaphoreType.DMA((n,)), pltpu.SemaphoreType.DMA((n,))]


def rows(ref, first, count):
    return ref.at[pl.ds(pl.multiple_of(first, 16), count)]


def lanes(first, count):
    return pl.ds(pl.multiple_of(first, 128), count)


def arrive(copies):
    for copy in copies:
        copy.arrived()


HALVES = ((0, 1), (1, -1))


class RingSum:
    def __init__(self, net, first, held, spans, scratch):
        self.net, self.first, self.second, self.held, self.spans = net, first, "y" if first == "x" else "x", held, spans
        self.half, self.fold, self.whole, self.mid, self.half2, self.fold2, self.whole2 = scratch
        self.width = sum(n for _, n in spans)
        self.one, self.two, self.three, self.four = [], [], [], []
        for part, step in HALVES:
            cut = pl.ds(48 * part, 48)
            if first == "x":
                self.plan(self.one, lambda cut=cut: held.at[:, net.near("x", 2), cut, lanes(spans[0][0], 2 * self.width)], lambda part=part: self.half.at[part], "x", step)
            else:
                lane = 0
                for base, n in spans:
                    self.plan(
                        self.one,
                        lambda cut=cut, base=base, n=n: self.ycut(held, net.near("y", 2), base, n, cut),
                        lambda part=part, lane=lane, n=n: self.half.at[part, :, :, lanes(lane, n)],
                        "y",
                        step,
                    )
                    lane += n
            self.plan(self.two, lambda part=part: self.fold.at[part], lambda part=part: self.whole.at[part], first, step)
            if first == "x":
                self.plan(self.three, lambda cut=cut: self.mid.at[lax.rem(net.near("y", 2), 2), cut, self.ylanes(net.near("y", 2))], lambda part=part: self.half2.at[part], "y", step)
            else:
                self.plan(self.three, lambda cut=cut: self.mid.at[net.near("x", 2), cut], lambda part=part: self.half2.at[part], "x", step)
            self.plan(self.four, lambda part=part: self.fold2.at[part], lambda part=part: self.whole2.at[part], self.second, step)

    def plan(self, to, src, dst, axis, step):
        to.append(self.net.plan(src, dst, axis, step))

    def ycut(self, ref, owner, base, n, cut):
        return ref.at[lax.rem(owner, 2), :, cut, lanes(base + (owner // 2) * n, n)]

    def ylanes(self, owner):
        return lanes((owner // 2) * self.width, self.width)

    def block(self, owner):
        if self.first == "x":
            return self.held[:, owner, :, lanes(self.spans[0][0], 2 * self.width)]
        got = [self.held[lax.rem(owner, 2), :, :, lanes(base + (owner // 2) * n, n)] for base, n in self.spans]
        return got[0] if len(got) == 1 else jnp.concatenate(got, axis=-1)

    def mid_block(self, owner):
        if self.first == "x":
            return self.mid[lax.rem(owner, 2), :, self.ylanes(owner)]
        return self.mid[owner]

    def step1(self):
        for copy in self.one:
            copy.start()

    def step2(self):
        arrive(self.one)
        for part, step in HALVES:
            self.fold[part] = self.block(self.net.near(self.first, step))
            self.fold[part, :, 48 * part : 48 * part + 48, :] += self.half[part]
            self.two[part].start()

    def step3(self):
        arrive(self.two)
        own = self.block(self.net.at[self.first]).astype(F32)
        self.mid[...] = (own + self.whole[0].astype(F32) + self.whole[1].astype(F32)).astype(BF16)
        for copy in self.three:
            copy.start()

    def step4(self):
        arrive(self.three)
        for part, step in HALVES:
            self.fold2[part] = self.mid_block(self.net.near(self.second, step))
            self.fold2[part, 48 * part : 48 * part + 48, :] += self.half2[part]
            self.four[part].start()

    def step5(self):
        arrive(self.four)
        own = self.mid_block(self.net.at[self.second]).astype(F32)
        return own + self.whole2[0].astype(F32) + self.whole2[1].astype(F32)


def ring_scratch(first, width):
    blocks, wide = (2, 2 * width) if first == "x" else (4, width)
    shapes = [(2, blocks, 48, wide), (2, blocks, 96, wide), (2, blocks, 96, wide), (blocks, 96, wide), (2, 48, width), (2, 96, width), (2, 96, width)]
    return [pltpu.VMEM(s, BF16) for s in shapes]


class TokenSum:
    def __init__(self, net, scratch):
        self.net, self.far, self.half, self.fold, self.whole = net, *scratch
        self.one = [
            net.plan(lambda p=p: self.far.at[pl.ds(128 * p, 128)], lambda p=p: self.half.at[p], "z", step) for p, step in HALVES
        ]
        self.two = [net.plan(lambda p=p: self.fold.at[p], lambda p=p: self.whole.at[p], "z", step) for p, step in HALVES]

    def step1(self):
        for copy in self.one:
            copy.start()

    def step2(self):
        arrive(self.one)
        for p, _ in HALVES:
            self.fold[p, 128 * p : 128 * p + 128, :] += self.half[p]
            self.two[p].start()

    def step3(self):
        arrive(self.two)
        return self.whole[0].astype(F32) + self.whole[1].astype(F32)


def token_scratch():
    return [pltpu.VMEM((256, D), BF16), pltpu.VMEM((2, 128, D), BF16), pltpu.VMEM((2, 256, D), BF16), pltpu.VMEM((2, 256, D), BF16)]


def gather_kernel(x, gain, w_gate, w_inner, w_out, w_bc, w_step, conv, bias, gate_gain, step_bias, decay_log, skip, normed_all, wx, wout, wbc, prm, xv, low, stepv, stept, pk, send, recv, local):
    net = Net(send, recv)
    at = net.at
    yh, cx, cc, z, y = at["yh"], at["x"], at["c"], at["z"], at["y"]
    load = pltpu.make_async_copy(x, xv, local.at[0])
    load.start()
    stept[...] = jnp.zeros_like(stept)
    stept[0:HEADS, 0:96] = w_step[...].astype(F32)
    stepv[...] = jnp.transpose(stept[...])[0:96, :].astype(BF16)
    pk[...] = jnp.zeros_like(pk)
    pk[0:4, :] = conv[...]
    pk[4:5, :] = bias[...].reshape(1, COLS)
    pk[5:6, :] = gate_gain[...].reshape(1, COLS)
    pk[6:7, 0:HEADS] = step_bias[...].reshape(1, HEADS)
    pk[7:8, 0:HEADS] = decay_log[...].reshape(1, HEADS)
    pk[8:9, 0:HEADS] = skip[...].reshape(1, HEADS)
    net.barrier([("z", 1), ("z", -1), ("x", 1), ("x", -1), ("y", 1), ("y", -1), ("y", 2), ("c", 1)])
    first = {
        "x": ((w_gate, wx, 0, COLS), (w_out, wout, 0, COLS)),
        "y": ((w_inner, wx, WIDE, COLS), (stepv, wx, STEPS, 128), (w_bc.at[:, lanes(yh * 128, 128)], wbc, 0, 128)),
    }

    def spot(ref, base, n, yy, xx, cut=slice(None)):
        cut = pl.ds(0, 96) if cut == slice(None) else cut
        return ref.at[lax.rem(yy, 2), xx, cc, cut, lanes(base + (yy // 2) * n, n)]

    own = [pltpu.make_async_copy(src, spot(ref, base, n, y, cx), local.at[1 + i]) for i, (src, ref, base, n) in enumerate(first["x"] + first["y"])]
    own.append(pltpu.make_async_copy(pk, prm.at[yh], local.at[6]))
    sent = {"x": [], "y": []}
    for axis in ("x", "y"):
        for src, ref, base, n in first[axis]:
            sent[axis].append([net.start(src, spot(ref, base, n, y, cx), axis, step) for _, step in HALVES])
    load.wait()
    v = xv[...].astype(F32)
    root = lax.rsqrt(jnp.mean(v * v, axis=1, keepdims=True) + EPS)
    low[...] = (v * root * gain[...].reshape(1, D)).astype(BF16)
    zs = [net.start(low, rows(normed_all, z * 256, 256), "z", step) for _, step in HALVES]
    own.append(pltpu.make_async_copy(low, rows(normed_all, z * 256, 256), local.at[7]))
    for copy in own:
        copy.start()
    for axis in ("x", "y"):
        for src, ref, base, n in first[axis]:
            net.start(src, spot(ref, base, n, y, cx), "c")
    net.start(pk, prm.at[yh], "y", 2)
    second = {"x": [], "y": []}
    for axis in ("x", "y"):
        for (src, ref, base, n), copies in zip(first[axis], sent[axis]):
            for (part, step), copy in zip(HALVES, copies):
                copy.arrived()
                cut = pl.ds(48 * part, 48)
                here = spot(ref, base, n, y, net.near("x", -step), cut) if axis == "x" else spot(ref, base, n, net.near("y", -step), cx, cut)
                second[axis].append(net.start(here, here, axis, step))
    for copy in own[:5]:
        copy.wait()
    third = {"x": [], "y": []}

    def line(axis, ref, base, n, place, cut=None):
        cut = pl.ds(0, 96) if cut is None else cut
        if axis == "x":
            return ref.at[lax.rem(place, 2), :, cc, cut, lanes(base + (place // 2) * n, n)]
        return ref.at[:, place, cc, cut, lanes(base, 2 * n)]

    then = {"x": "y", "y": "x"}
    for axis in ("x", "y"):
        arrive(second[axis])
        for src, ref, base, n in first[axis]:
            here = line(axis, ref, base, n, at[then[axis]])
            third[axis].append([net.start(here, here, then[axis], step) for _, step in HALVES])
    for axis in ("x", "y"):
        for src, ref, base, n in first[axis]:
            for step in (1, -1, 2):
                here = spot(ref, base, n, y, net.near("x", step)) if axis == "x" else spot(ref, base, n, net.near("y", step), cx)
                net.start(here, here, "c")
    fourth = {"x": [], "y": []}

    def pass_on(axis):
        for (src, ref, base, n), copies in zip(first[axis], third[axis]):
            for (part, step), copy in zip(HALVES, copies):
                copy.arrived()
                place = net.near(then[axis], -step)
                here = line(axis, ref, base, n, place, pl.ds(48 * part, 48))
                fourth[axis].append(net.start(here, here, then[axis], step))
                here = line(axis, ref, base, n, place)
                net.start(here, here, "c")

    pass_on("y")
    pass_on("x")
    for (part, step), copy in zip(HALVES, zs):
        copy.arrived()
        here = rows(normed_all, net.near("z", -step) * 256 + 128 * part, 128)
        net.start(here, here, "z", step)
    for axis in ("y", "x"):
        arrive(fourth[axis])
        for src, ref, base, n in first[axis]:
            here = line(axis, ref, base, n, net.near(then[axis], 2))
            net.start(here, here, "c")
    net.finish()
    for copy in own[5:]:
        copy.wait()


def run_gather(*args):
    return pl.pallas_call(
        gather_kernel,
        out_shape=[
            SHAPE((LEN, D), BF16),
            SHAPE((2, 4, 2, 96, PROJ), BF16),
            SHAPE((2, 4, 2, 96, WIDE), BF16),
            SHAPE((2, 4, 2, 96, 256), BF16),
            SHAPE((GROUPS, 16, COLS), F32),
        ],
        in_specs=[ANY, VMEM, ANY, ANY, ANY, ANY] + [VMEM] * 7,
        out_specs=[ANY] * 5,
        scratch_shapes=[
            pltpu.VMEM((256, D), BF16),
            pltpu.VMEM((256, D), BF16),
            pltpu.VMEM((96, 128), BF16),
            pltpu.VMEM((128, 128), F32),
            pltpu.VMEM((16, COLS), F32),
        ]
        + sems(96)
        + [pltpu.SemaphoreType.DMA((8,))],
        compiler_params=pltpu.CompilerParams(collective_id=0, has_side_effects=True, vmem_limit_bytes=ROOM),
        name="gather_all",
    )(*args)


def forward_kernel(
    x, wx, wout, wbc, prm, conv_bc, bias_bc, cot,
    gate_out, inner_out, z_out, y_out, gm_out, mixed_out, h_out, dt_out, r_out, u_out, bc_out, bcin_out, zbc_out, stats_out, normed_t, cot_t,
    cots, gps, ext, extbc, state, stat, slots, send, recv, local,
):
    i = pl.program_id(0)
    net = Net(send, recv)
    z = net.at["z"]
    here = lambda step=0: rows(cots, (net.near("z", step) if step else z) * 256, 256)
    part = lambda p, step: rows(cots, net.near("z", -step) * 256 + 128 * p, 128)
    c1 = [net.plan(lambda: cot, lambda: here(), "z", step) for _, step in HALVES]
    c2 = [net.plan(lambda p=p, s=s: part(p, s), lambda p=p, s=s: part(p, s), "z", s) for p, s in HALVES]
    q = [net.plan(lambda: stat, lambda: slots.at[z], "z", step) for step in (1, -1, 2)]
    own = lambda: pltpu.make_async_copy(cot, here(), local.at[0])

    @pl.when(i == 0)
    def _():
        net.barrier([("z", 1), ("z", -1), ("z", 2)])
        own().start()
        for copy in c1:
            copy.start()
        ext[0:8, :] = jnp.zeros((8, WIDE), F32)
        extbc[0:8, :] = jnp.zeros((8, 256), F32)
        state[...] = jnp.zeros_like(state)

    @pl.when((i > 0) & (i < BLOCKS))
    def _():
        ext[0:8, :] = ext[BLOCK : BLOCK + 8, :]
        extbc[0:8, :] = extbc[BLOCK : BLOCK + 8, :]

    @pl.when(i == BLOCKS - 1)
    def _():
        for copy in c1:
            copy.arrived()
        for copy in c2:
            copy.start()

    @pl.when(i < BLOCKS)
    def _():
        xb = x[...]
        turned = jnp.transpose(xb).reshape(2, 4, 2, 96, BLOCK)
        for core in range(2):
            normed_t[core] = turned[:, :, core]
        bc_in = dot(xb, wbc[...])
        bcin_out[...] = bc_in
        extbc[8 : BLOCK + 8, :] = bc_in
        zb = bias_bc[...] + sum(conv_bc[j : j + 1, :] * extbc[5 + j : 5 + j + BLOCK, :] for j in range(4))
        zbc_out[...] = zb
        bc = (zb * sigmoid(zb)).astype(BF16)
        bc_out[...] = bc
        b, c = bc[:, :STATE], bc[:, STATE:]
        scores = jnp.where(iota((BLOCK, BLOCK), 0) >= iota((BLOCK, BLOCK), 1), dot_nt(c, b), 0.0)
        tri, spread = lower(), expander()
        left = iota((BLOCK, 128), 1) < 64
        steps = dot(xb, wx[:, STEPS:])
        total = jnp.zeros((BLOCK, 128), F32)
        for g in range(GROUPS):
            cut = slice(g * COLS, (g + 1) * COLS)
            u = steps[:, 128 * g : 128 * (g + 1)] + prm[g, 6:7, 0:128]
            dt = jnp.maximum(u, 0.0) + jnp.log(1.0 + jnp.exp(-jnp.abs(u)))
            rate = -jnp.exp(prm[g, 7:8, 0:128]) * LOG2E
            r = dot_right(tri, dt * rate, 3)
            u_out[g] = u
            dt_out[g] = dt
            r_out[g] = r
            rt = jnp.transpose(r)
            gate = dot(xb, wx[:, cut])
            inner = dot(xb, wx[:, WIDE + g * COLS : WIDE + (g + 1) * COLS])
            gate_out[:, cut] = gate
            inner_out[:, cut] = inner
            ext[8 : BLOCK + 8, cut] = inner
            zv = prm[g, 4:5, :] + sum(prm[g, j : j + 1, :] * ext[5 + j : 5 + j + BLOCK, cut] for j in range(4))
            z_out[:, cut] = zv
            xv = zv * sigmoid(zv)
            last = r[BLOCK - 1 : BLOCK, :]
            w = xv * dot_left(dt, spread, 2)
            grow = dot_left(jnp.exp2(r), spread, 2)
            tail = dot_left(jnp.exp2(last - r), spread, 2)
            skip = dot_left(prm[g, 8:16, 0:128], spread, 3)[0:1, :]
            wl = w.astype(BF16)
            h = state[:, cut]
            h_out[0, g] = h
            parts = []
            for p in range(HEADS // 2):
                halves = []
                for n in (2 * p, 2 * p + 1):
                    gap = jnp.minimum(r[:, n : n + 1] - rt[n : n + 1, :], 0.0)
                    halves.append(dot((scores * jnp.exp2(gap)).astype(BF16), wl[:, 128 * p : 128 * (p + 1)]))
                parts.append(jnp.where(left, halves[0], halves[1]))
            yv = jnp.concatenate(parts, axis=1) + grow * dot(c, h.astype(BF16)) + skip * xv
            y_out[:, cut] = yv
            state[:, cut] = grow[BLOCK - 1 : BLOCK, :] * h + dot_tn(b, (tail * w).astype(BF16))
            gp = yv * (gate * sigmoid(gate))
            gps[pl.ds(pl.multiple_of(i * BLOCK, BLOCK), BLOCK), cut] = gp
            sq = gp * gp
            total = total + (sq[:, 0:128] + sq[:, 128:256] + sq[:, 256:384])
        stat[pl.ds(i, 1), :] = token_row(total)

    @pl.when(i == BLOCKS)
    def _():
        own().wait()

    @pl.when(i == 2 * BLOCKS - 1)
    def _():
        for copy in c2:
            copy.arrived()

    @pl.when(i >= BLOCKS)
    def _():
        t = i - BLOCKS
        block = lax.rem(z + t + lax.div(t, 2) - 2 * lax.div(t, 3), 4)
        at = pl.ds(pl.multiple_of(block * BLOCK, BLOCK), BLOCK)
        cb = cots[at, :]
        turned = jnp.transpose(cb).reshape(2, 4, 2, 96, BLOCK)
        for core in range(2):
            cot_t[core, :, :, :, at] = turned[:, :, core]
        gm = dot(cb, wout[...])
        gm_out[at, :] = gm
        gain = jnp.concatenate([prm[0, 5:6, :], prm[1, 5:6, :]], axis=1)
        stat[pl.ds(BLOCKS + block, 1), :] = token_row(gm * gain * gps[at, :])

    @pl.when(i == 2 * BLOCKS - 1)
    def _():
        for copy in q:
            copy.start()
        slots[z] = stat[...]
        for copy in q:
            copy.arrived()
        sums = (slots[0] + slots[1]) + (slots[2] + slots[3])
        root = lax.rsqrt(sums[0:4, :] * (1.0 / INNER) + EPS)
        stats_out[0:4, :] = root
        stats_out[4:8, :] = root * root * root * (sums[4:8, :] * (1.0 / INNER))
        columns = jnp.transpose(stats_out[...])
        gain = jnp.concatenate([prm[0, 5:6, :], prm[1, 5:6, :]], axis=1)
        for k in range(BLOCKS):
            at = slice(k * BLOCK, (k + 1) * BLOCK)
            mixed_out[at, :] = (gps[at, :] * columns[:, k : k + 1] * gain).astype(BF16)
        for copy in c1 + c2 + q:
            copy.left()


def run_forward(x, wx, wout, wbc, prm, conv_bc, bias_bc, cot):
    first = lambda k: jnp.minimum(k, BLOCKS - 1)
    const = lambda *s: pl.BlockSpec(s, lambda k: (0,) * len(s), pipeline_mode=pl.Buffered(1))
    keep = lambda *s: pl.BlockSpec(s, lambda k: (0,) * len(s))
    block = lambda n: pl.BlockSpec((BLOCK, n), lambda k: (first(k), 0))
    small = lambda: pl.BlockSpec((GROUPS, BLOCK, 128), lambda k: (0, first(k), 0))
    wide = SHAPE((LEN, WIDE), F32)
    narrow = SHAPE((GROUPS, LEN, 128), F32)
    return pl.pallas_call(
        forward_kernel,
        grid=(2 * BLOCKS,),
        out_shape=[
            wide,
            wide,
            wide,
            wide,
            wide,
            SHAPE((LEN, WIDE), BF16),
            SHAPE((BLOCKS, GROUPS, STATE, COLS), F32),
            narrow,
            narrow,
            narrow,
            SHAPE((LEN, 256), BF16),
            SHAPE((LEN, 256), F32),
            SHAPE((LEN, 256), F32),
            SHAPE((8, 256), F32),
            SHAPE((2, 2, 4, 96, LEN), BF16),
            SHAPE((2, 2, 4, 96, LEN), BF16),
        ],
        in_specs=[
            block(D),
            const(D, PROJ),
            const(D, WIDE),
            const(D, 256),
            const(GROUPS, 16, COLS),
            const(4, 256),
            const(1, 256),
            ANY,
        ],
        out_specs=[
            block(WIDE),
            block(WIDE),
            block(WIDE),
            block(WIDE),
            keep(LEN, WIDE),
            keep(LEN, WIDE),
            pl.BlockSpec((1, GROUPS, STATE, COLS), lambda k: (first(k), 0, 0, 0)),
            small(),
            small(),
            small(),
            block(256),
            block(256),
            block(256),
            keep(8, 256),
            pl.BlockSpec((2, 2, 4, 96, BLOCK), lambda k: (0, 0, 0, 0, first(k))),
            keep(2, 2, 4, 96, LEN),
        ],
        scratch_shapes=[
            pltpu.VMEM((LEN, D), BF16),
            pltpu.VMEM((LEN, WIDE), F32),
            pltpu.VMEM((BLOCK + 8, WIDE), F32),
            pltpu.VMEM((BLOCK + 8, 256), F32),
            pltpu.VMEM((STATE, WIDE), F32),
            pltpu.VMEM((8, BLOCK), F32),
            pltpu.VMEM((4, 8, BLOCK), F32),
        ]
        + sems(7)
        + [pltpu.SemaphoreType.DMA((1,))],
        compiler_params=pltpu.CompilerParams(collective_id=1, has_side_effects=True, vmem_limit_bytes=ROOM),
        name="forward",
    )(x, wx, wout, wbc, prm, conv_bc, bias_bc, cot)


def backward_kernel(
    gm, gate, inner, zin, y, hin, prm, bc, dt, r, u, stats, mixed, wout, cot_t, tokens,
    cat_out, dbc_out, acc, branch_out, wout_out,
    ext, dstate, dst, dbc, held, got, away, mv, wv, cv, ownb, g0, g1, g2, g3, s1, s2, s3, s4, s5, s6, s7, send, recv, local,
):
    k = pl.program_id(0)
    net = Net(send, recv)
    cc, z = net.at["c"], net.at["z"]
    cross = net.plan(lambda: away, lambda: got, "c")
    token = TokenSum(net, (g0, g1, g2, g3))
    ring = RingSum(net, "y", held, ((0, COLS),), (s1, s2, s3, s4, s5, s6, s7))

    @pl.when(k == 0)
    def _():
        net.barrier([("z", 1), ("z", -1), ("x", 1), ("x", -1), ("y", 1), ("y", -1), ("c", 1)])
        loads = [pltpu.make_async_copy(src, dst, local.at[n]) for n, (src, dst) in enumerate(((mixed, mv), (wout, wv), (cot_t, cv)))]
        for copy in loads:
            copy.start()
        loads[0].wait()
        loads[1].wait()
        branch = lambda place: dot_nt(mv[pl.ds(pl.multiple_of(place * 256, 256), 256), :], wv[...])
        grads = lambda core: dot(cv[core].reshape(8 * 96, LEN), mv[...]).astype(BF16).reshape(2, 4, 96, WIDE)
        g0[...] = branch(net.near("z", 2)).astype(BF16)
        token.step1()
        loads[2].wait()
        away[...] = grads(net.other)
        cross.start()
        g2[0] = branch(net.near("z", 1)).astype(BF16)
        g2[1] = branch(net.near("z", -1)).astype(BF16)
        ownb[...] = branch(z)
        held[...] = grads(cc)
        acc[...] = jnp.zeros_like(acc)
        ext[BLOCK : BLOCK + 8, :] = jnp.zeros((8, WIDE), F32)
        dstate[...] = jnp.zeros_like(dstate)

    @pl.when(k > 0)
    def _():
        ext[BLOCK : BLOCK + 8, :] = ext[0:8, :]

    b, c = bc[:, :STATE], bc[:, STATE:]
    valid = iota((BLOCK, BLOCK), 1) >= iota((BLOCK, BLOCK), 0)
    scores = jnp.where(valid, dot_nt(b, c), 0.0)
    both = jnp.concatenate([stats[pl.ds(BLOCKS - 1 - k, 1), :], stats[pl.ds(2 * BLOCKS - 1 - k, 1), :], jnp.zeros((6, BLOCK), F32)], axis=0)
    column = jnp.transpose(both)
    ir, cr = column[:, 0:1], column[:, 1:2]
    spread, fold = expander(), reducer()
    left = iota((BLOCK, 128), 1) < 64
    suffix, prefix = upper(), lower(strict=True)
    dst[...] = jnp.zeros_like(dst)
    dbc[...] = jnp.zeros_like(dbc)
    for g in range(GROUPS):
        if g == 0:

            @pl.when(k == 1)
            def _():
                cross.arrived()
                held[...] += got[...]
                ring.step1()

            @pl.when(k == 3)
            def _():
                ring.step4()

        else:

            @pl.when(k == 0)
            def _():
                token.step2()

            @pl.when(k == 1)
            def _():
                ring.step2()

            @pl.when(k == 2)
            def _():
                ring.step3()

        cut = slice(g * COLS, (g + 1) * COLS)
        yv = y[:, cut]
        gv = gate[:, cut]
        sig = sigmoid(gv)
        act = gv * sig
        gain = prm[g, 5:6, :]
        gp = yv * act
        gmix = gm[:, cut]
        gain_grad = gmix * gp * ir
        gated = ir * (gmix * gain) - gp * cr
        gs = gated * act
        cat_out[:, cut] = (gated * yv * sig * (1.0 + gv * (1.0 - sig))).astype(BF16)
        xi = inner[:, cut]
        zv = zin[:, cut]
        zs = sigmoid(zv)
        xv = zv * zs
        rv = r[g]
        rt = jnp.transpose(rv)
        last = rv[BLOCK - 1 : BLOCK, :]
        dte = dot_left(dt[g], spread, 2)
        grow = dot_left(jnp.exp2(rv), spread, 2)
        tail = dot_left(jnp.exp2(last - rv), spread, 2)
        skip = dot_left(prm[g, 8:16, 0:128], spread, 3)[0:1, :]
        w = xv * dte
        wl = w.astype(BF16)
        gl = gs.astype(BF16)
        h = hin[0, g]
        dh = dstate[:, cut]
        dhl = dh.astype(BF16)
        parts = []
        for p in range(HEADS // 2):
            halves = []
            pair = slice(128 * p, 128 * (p + 1))
            wp, gpair = wl[:, pair], gl[:, pair]
            zero = jnp.zeros_like(wp)
            for n in (2 * p, 2 * p + 1):
                decay = jnp.exp2(jnp.minimum(rt[n : n + 1, :] - rv[:, n : n + 1], 0.0))
                halves.append(dot((scores * decay).astype(BF16), gpair))
                mine = jnp.where(left, wp, zero) if n % 2 == 0 else jnp.where(left, zero, wp)
                dst[...] += dot_nt(mine, gpair) * decay
            parts.append(jnp.where(left, halves[0], halves[1]))
        dwi = jnp.concatenate(parts, axis=1)
        dws = tail * dot(b, dhl)
        dw = dwi + dws
        skipgrad = gs * xv
        diff = dot_left(gl.astype(F32) * (yv - skip * xv) - wl.astype(F32) * dwi, fold, 3)
        zsum = dot_left(w * dws, fold, 3)
        const = dot_left(jnp.sum(h * dh, axis=0, keepdims=True) * grow[BLOCK - 1 : BLOCK, :] + jnp.zeros((8, COLS), F32), fold, 3)
        da = dot_right(suffix, diff, 3) + dot_right(prefix, zsum, 3) + const[0:1, :]
        rate = -jnp.exp(prm[g, 7:8, 0:128])
        dstep = (dot_left(xv * dw, fold, 3) + rate * da) * sigmoid(u[g])
        cat_out[:, STEPS + 128 * g : STEPS + 128 * (g + 1)] = dstep.astype(BF16)
        gx = (grow * gs).astype(BF16)
        dbc[:, STATE:] += dot_nt(gx, h.astype(BF16))
        dbc[:, :STATE] += dot_nt((tail * w).astype(BF16), dhl)
        dstate[:, cut] = grow[BLOCK - 1 : BLOCK, :] * dh + dot_tn(c, gx)
        dx = dte * dw + skip * gs
        dz = dx * (zs * (1.0 + zv * (1.0 - zs)))
        ext[0:BLOCK, cut] = dz
        gi = jnp.zeros((BLOCK, COLS), F32)
        for j in range(4):
            moved = ext[3 - j : 3 - j + BLOCK, cut]
            gi = gi + prm[g, j : j + 1, :] * moved
            acc[g, j : j + 1, :] += jnp.sum(xi * moved, axis=0, keepdims=True)
        cat_out[:, WIDE + g * COLS : WIDE + (g + 1) * COLS] = gi.astype(BF16)
        acc[g, 4:5, :] += jnp.sum(dz, axis=0, keepdims=True)
        acc[g, 5:6, :] += jnp.sum(gain_grad, axis=0, keepdims=True)
        acc[g, 6:7, 0:128] += jnp.sum(dstep, axis=0, keepdims=True)
        acc[g, 7:8, 0:128] += jnp.sum(da * dt[g], axis=0, keepdims=True) * rate
        acc[g, 8:9, 0:128] += dot_left(jnp.sum(skipgrad, axis=0, keepdims=True) + jnp.zeros((8, COLS), F32), fold, 3)[0:1, :]
    ds = jnp.where(valid, dst[...], 0.0).astype(BF16)
    dbc_out[:, STATE:] = (dbc[:, STATE:] + dot_tn(ds, b)).astype(BF16)
    dbc_out[:, :STATE] = (dbc[:, :STATE] + dot(ds, c)).astype(BF16)

    @pl.when(k == BLOCKS - 1)
    def _():
        wout_out[...] = ring.step5()
        branch_out[...] = (tokens[...].astype(F32) + (ownb[...] + token.step3())).astype(BF16)
        for copy in net.copies:
            copy.left()


def run_backward(gm, gate, inner, zin, y, hin, prm, bc, dt, r, u, stats, mixed, wout, cot_t, tokens):
    rev = lambda k: BLOCKS - 1 - k
    cols = lambda n: pl.BlockSpec((BLOCK, n), lambda k: (rev(k), 0))
    small = lambda: pl.BlockSpec((GROUPS, BLOCK, 128), lambda k: (0, rev(k), 0))
    keep = lambda *s: pl.BlockSpec(s, lambda k: (0,) * len(s))
    return pl.pallas_call(
        backward_kernel,
        grid=(BLOCKS,),
        out_shape=[
            SHAPE((LEN, PROJ), BF16),
            SHAPE((LEN, 256), BF16),
            SHAPE((GROUPS, 16, COLS), F32),
            SHAPE((256, D), BF16),
            SHAPE((96, COLS), F32),
        ],
        in_specs=[cols(WIDE)] * 5
        + [
            pl.BlockSpec((1, GROUPS, STATE, COLS), lambda k: (rev(k), 0, 0, 0)),
            keep(GROUPS, 16, COLS),
            cols(256),
            small(),
            small(),
            small(),
            keep(8, 256),
            ANY,
            ANY,
            ANY,
            keep(256, D),
        ],
        out_specs=[cols(PROJ), cols(256), keep(GROUPS, 16, COLS), keep(256, D), keep(96, COLS)],
        scratch_shapes=[
            pltpu.VMEM((BLOCK + 8, WIDE), F32),
            pltpu.VMEM((STATE, WIDE), F32),
            pltpu.VMEM((BLOCK, BLOCK), F32),
            pltpu.VMEM((BLOCK, 256), F32),
            pltpu.VMEM((2, 4, 96, WIDE), BF16),
            pltpu.VMEM((2, 4, 96, WIDE), BF16),
            pltpu.VMEM((2, 4, 96, WIDE), BF16),
            pltpu.VMEM((LEN, WIDE), BF16),
            pltpu.VMEM((D, WIDE), BF16),
            pltpu.VMEM((2, 2, 4, 96, LEN), BF16),
            pltpu.VMEM((256, D), F32),
        ]
        + token_scratch()
        + ring_scratch("y", COLS)
        + sems(13)
        + [pltpu.SemaphoreType.DMA((3,))],
        compiler_params=pltpu.CompilerParams(collective_id=2, has_side_effects=True, vmem_limit_bytes=ROOM),
        name="backward",
    )(gm, gate, inner, zin, y, hin, prm, bc, dt, r, u, stats, mixed, wout, cot_t, tokens)


def tail_kernel(
    cat, wx, normed_t, normed, dbc, zbc, bc_in, acc, wbc, tokens, cot, gain, conv,
    tokens_out, gate_out, inner_out, bc_out, small_out,
    catv, wxv, ntv, nv, mine, slots, zv, xi, wv, xv, ov, ext, gnbc, ownb, held, got, away, dbw, heldb, gotb, small, sp0, sp1, sp2, sp3, bz, by,
    g0, g1, g2, g3, a1, a2, a3, a4, a5, a6, a7, b1, b2, b3, b4, b5, b6, b7, c1, c2, c3, c4, c5, c6, c7, send, recv, local,
):
    net = Net(send, recv)
    at = net.at
    yh, cx, cc, z, y = at["yh"], at["x"], at["c"], at["z"], at["y"]
    pairs = (
        (cat, catv),
        (wx, wxv),
        (normed, nv),
        (normed_t, ntv),
        (rows(zbc, z * 256, 256), zv.at[pl.ds(0, 256)]),
        (rows(zbc, lax.rem(z * 256 + 256, LEN), 16), zv.at[pl.ds(256, 16)]),
        (rows(bc_in, z * 256, 256), xi),
        (wbc, wv),
        (tokens, xv),
        (cot, ov),
    )
    loads = [pltpu.make_async_copy(src, dst, local.at[i]) for i, (src, dst) in enumerate(pairs)]
    for copy in loads:
        copy.start()
    token = TokenSum(net, (g0, g1, g2, g3))
    ring_gate = RingSum(net, "x", held, ((0, COLS),), (a1, a2, a3, a4, a5, a6, a7))
    ring_inner = RingSum(net, "y", held, ((WIDE, COLS), (STEPS, 128)), (b1, b2, b3, b4, b5, b6, b7))
    ring_bc = RingSum(net, "x", heldb, ((0, 128),), (c1, c2, c3, c4, c5, c6, c7))
    mine[0:LEN, :] = dbc[...]
    mine[LEN : LEN + 16, :] = jnp.zeros((16, 256), BF16)
    slots[z] = mine[pl.ds(pl.multiple_of(z * 256, 16), 272), :]
    net.barrier([(a, s) for a in ("z", "x", "y") for s in (1, -1, 2)] + [("c", 1)])
    swap = [net.start(rows(mine, net.near("z", s) * 256, 272), slots.at[z], "z", s) for s in (1, -1, 2)]
    gain_row = gain[...].reshape(1, D)
    norm_part = jnp.zeros((1, D), F32)

    def block(place):
        cut = pl.ds(pl.multiple_of(place * 256, 256), 256)
        got = dot_nt(catv[cut, :], wxv[...])
        return got, jnp.sum(got * nv[cut, :].astype(F32), axis=0, keepdims=True)

    for copy in loads[:3]:
        copy.wait()
    out, part = block(net.near("z", 2))
    norm_part = norm_part + part
    g0[...] = out.astype(BF16)
    token.step1()
    grads = lambda core: dot(ntv[core].reshape(8 * 96, LEN), catv[...]).astype(BF16).reshape(2, 4, 96, PROJ)
    loads[3].wait()
    away[...] = grads(net.other)
    cross = net.start(away, got, "c")
    for copy in loads[4:]:
        copy.wait()
    arrive(swap)
    total = (slots[0].astype(F32) + slots[1].astype(F32)) + (slots[2].astype(F32) + slots[3].astype(F32))
    sig = sigmoid(zv[...])
    dz = total * (sig * (1.0 + zv[...] * (1.0 - sig)))
    ext[...] = jnp.where(iota((272, 256), 0) + z * 256 < LEN, dz, 0.0)
    gbc = jnp.zeros((256, 256), F32)
    small[0:16, :] = acc[0]
    small[16:32, :] = acc[1]
    small[32:48, :] = jnp.zeros((16, COLS), F32)
    for j in range(4):
        moved = ext[3 - j : 3 - j + 256, :]
        gbc = gbc + conv[j : j + 1, :] * moved
        small[36 + j : 37 + j, 0:256] = jnp.sum(xi[...] * moved, axis=0, keepdims=True)
    small[40:41, 0:256] = jnp.sum(ext[0:256, :], axis=0, keepdims=True)
    gbc = gbc.astype(BF16)
    own = pl.ds(pl.multiple_of(z * 256, 256), 256)
    for core in range(2):
        dbw[core] = dot(ntv[core, :, :, :, own].reshape(8 * 96, 256), gbc).astype(BF16).reshape(2, 4, 96, 256)
    crossb = net.start(dbw.at[net.other], gotb, "c")
    gnbc[...] = dot_nt(gbc, wv[...])
    norm_part = norm_part + jnp.sum(gnbc[...] * nv[own, :].astype(F32), axis=0, keepdims=True)
    for p, step in HALVES:
        out, part = block(net.near("z", step))
        norm_part = norm_part + part
        g2[p] = out.astype(BF16)
    token.step2()
    held[...] = grads(cc)
    cross.arrived()
    held[...] += got[...]
    ring_inner.step1()
    ring_gate.step1()
    crossb.arrived()
    heldb[...] = dbw[cc] + gotb[...]
    ring_bc.step1()
    out, part = block(z)
    norm_part = (norm_part + part) / gain_row
    ownb[...] = out + gnbc[...]
    for k in range(4):
        small[32 + k : 33 + k, :] = norm_part[:, k * COLS : (k + 1) * COLS]
    sp0[z] = small[32:48, :]
    q = net.around(sp0.at[z], sp0.at[z], "z")
    ring_gate.step2()
    ring_inner.step2()
    ring_bc.step2()
    arrive(q)
    sp1[cx, 0:32, :] = small[0:32, :]
    sp1[cx, 32:48, :] = (sp0[0] + sp0[1]) + (sp0[2] + sp0[3])
    q = net.around(sp1.at[cx], sp1.at[cx], "x")
    ring_bc.step3()
    arrive(q)
    sp2[y] = (sp1[0] + sp1[1]) + (sp1[2] + sp1[3])
    q = net.around(sp2.at[y], sp2.at[y], "y")
    ring_bc.step4()
    arrive(q)
    sp3[cc] = (sp2[0] + sp2[1]) + (sp2[2] + sp2[3])
    q = [net.start(sp3.at[cc], sp3.at[cc], "c")]
    bz[z] = ring_bc.step5()
    q += net.around(bz.at[z], bz.at[z], "z")
    ring_gate.step3()
    ring_inner.step3()
    arrive(q)
    small_out[...] = sp3[0] + sp3[1]
    by[yh] = (bz[0] + bz[1]) + (bz[2] + bz[3])
    q = [net.start(by.at[yh], by.at[yh], "y", 2)]
    ring_gate.step4()
    ring_inner.step4()
    arrive(q)
    bc_out[:, :128] = by[0]
    bc_out[:, 128:] = by[1]
    gate_out[...] = ring_gate.step5()
    inner_out[...] = ring_inner.step5()
    v = xv[...].astype(F32)
    root = lax.rsqrt(jnp.mean(v * v, axis=1, keepdims=True) + EPS)
    g = token.step3() + ownb[...]
    scaled = g * gain_row
    tokens_out[...] = ov[...].astype(F32) + root * scaled - v * (root * root * root) * jnp.mean(scaled * v, axis=1, keepdims=True)
    net.finish()


def run_tail(*args):
    bf = lambda *s: pltpu.VMEM(s, BF16)
    f32 = lambda *s: pltpu.VMEM(s, F32)
    return pl.pallas_call(
        tail_kernel,
        out_shape=[
            SHAPE((256, D), F32),
            SHAPE((96, COLS), F32),
            SHAPE((96, COLS + 128), F32),
            SHAPE((96, 256), F32),
            SHAPE((48, COLS), F32),
        ],
        in_specs=[ANY] * 4 + [VMEM, ANY, ANY, VMEM, ANY, ANY, ANY, VMEM, VMEM],
        out_specs=[VMEM] * 5,
        scratch_shapes=[
            bf(LEN, PROJ),
            bf(D, PROJ),
            bf(2, 2, 4, 96, LEN),
            bf(LEN, D),
            bf(LEN + 16, 256),
            bf(4, 272, 256),
            f32(272, 256),
            f32(256, 256),
            bf(D, 256),
            bf(256, D),
            bf(256, D),
            f32(272, 256),
            f32(256, D),
            f32(256, D),
            bf(2, 4, 96, PROJ),
            bf(2, 4, 96, PROJ),
            bf(2, 4, 96, PROJ),
            bf(2, 2, 4, 96, 256),
            bf(2, 4, 96, 256),
            bf(2, 4, 96, 256),
            f32(48, COLS),
            f32(4, 16, COLS),
            f32(4, 48, COLS),
            f32(4, 48, COLS),
            f32(2, 48, COLS),
            f32(4, 96, 128),
            f32(2, 96, 128),
        ]
        + token_scratch()
        + ring_scratch("x", COLS)
        + ring_scratch("y", COLS + 128)
        + ring_scratch("x", 128)
        + sems(64)
        + [pltpu.SemaphoreType.DMA((10,))],
        compiler_params=pltpu.CompilerParams(collective_id=3, has_side_effects=True, vmem_limit_bytes=ROOM),
        name="tail",
    )(*args)


def finish_kernel(tokens, branch, inner, bc, small, gate, wout, tokens_out, branch_out, step_out, inner_out, bc_out, gate_out, wout_out, norm, conv, bias, conv_bc, bias_bc, step_bias, decay, skip, gain, sem):
    big = [
        pltpu.make_async_copy(src, dst, sem.at[i])
        for i, (src, dst) in enumerate(
            ((tokens, tokens_out), (branch, branch_out), (inner.at[:, pl.ds(0, COLS)], inner_out), (bc, bc_out), (gate, gate_out), (wout, wout_out))
        )
    ]
    for copy in big:
        copy.start()
    step_out[...] = jnp.transpose(jnp.concatenate([inner[:, COLS:], jnp.zeros((32, 128), F32)], axis=0))[0:HEADS, 0:96]
    norm[...] = jnp.concatenate([small[32 + k : 33 + k, :] for k in range(4)], axis=1).reshape(D)
    conv_bc[...] = small[36:40, 0:256]
    bias_bc[...] = small[40:41, 0:256].reshape(256)
    mine = small[pl.ds(pl.multiple_of(lax.axis_index("yh") * 16, 8), 16), :]
    conv[...] = mine[0:4, :]
    bias[...] = mine[4:5, :].reshape(COLS)
    gain[...] = mine[5:6, :].reshape(COLS)
    step_bias[...] = mine[6:7, 0:HEADS].reshape(HEADS)
    decay[...] = mine[7:8, 0:HEADS].reshape(HEADS)
    skip[...] = mine[8:9, 0:HEADS].reshape(HEADS)
    for copy in big:
        copy.wait()


def run_finish(tokens, branch, inner, bc, small, gate, wout):
    f32 = lambda *s: SHAPE(s, F32)
    return pl.pallas_call(
        finish_kernel,
        out_shape=[
            f32(256, D),
            SHAPE((256, D), BF16),
            f32(HEADS, 96),
            f32(96, COLS),
            f32(96, 256),
            f32(96, COLS),
            f32(96, COLS),
            f32(D),
            f32(4, COLS),
            f32(COLS),
            f32(4, 256),
            f32(256),
            f32(HEADS),
            f32(HEADS),
            f32(HEADS),
            f32(COLS),
        ],
        in_specs=[ANY, ANY, VMEM, ANY, VMEM, ANY, ANY],
        out_specs=[ANY, ANY, VMEM] + [ANY] * 4 + [VMEM] * 9,
        scratch_shapes=[pltpu.SemaphoreType.DMA((6,))],
        compiler_params=pltpu.CompilerParams(vmem_limit_bytes=ROOM),
        name="finish",
    )(tokens, branch, inner, bc, small, gate, wout)


def shards(tokens, norm_gain, w_gate, w_inner, w_bc, w_step, conv_inner, bias_inner, conv_bc, bias_bc, step_bias, decay_log, skip_gain, gate_gain, w_out, cotangent):
    normed, wx, wout, wbc, prm = run_gather(
        tokens, norm_gain, w_gate, w_inner, w_out, w_bc, w_step.T, conv_inner, bias_inner, gate_gain, step_bias, decay_log, skip_gain
    )
    wx, wout, wbc = wx.reshape(D, PROJ), wout.reshape(D, WIDE), wbc.reshape(D, 256)
    gate, inner, zin, y, gm, mixed, hin, dt, r, u, bc, bc_in, zbc, stats, normed_t, cot_t = run_forward(
        normed, wx, wout, wbc, prm, conv_bc, bias_bc.reshape(1, 256), cotangent
    )
    cat, dbc, acc, output, wout_grad = run_backward(gm, gate, inner, zin, y, hin, prm, bc, dt, r, u, stats, mixed, wout, cot_t, tokens)
    tokens_grad, gate_grad, inner_grad, bc_grad, small = run_tail(
        cat, wx, normed_t, normed, dbc, zbc, bc_in, acc, wbc, tokens, cotangent, norm_gain, conv_bc
    )
    (
        tokens_grad, output, step_grad, inner_grad, bc_grad, gate_grad, wout_grad,
        norm, conv, bias, conv_bc_grad, bias_bc_grad, step_bias_grad, decay, skip, gate_gain_grad,
    ) = run_finish(tokens_grad, output, inner_grad, bc_grad, small, gate_grad, wout_grad)
    return (
        output, tokens_grad, norm, gate_grad, inner_grad, bc_grad, step_grad.T, conv, bias, conv_bc_grad,
        bias_bc_grad, step_bias_grad, decay, skip, gate_gain_grad, wout_grad,
    )


def solution(mesh):
    fine = Mesh(mesh.devices.reshape(2, 4, 2, 2, 4), AXES)
    dp, tensor = ("yl", "x", "c"), ("yh", "z")
    tokens, weight = P(dp + tensor, None), P(dp, tensor)
    heads, shared = P(tensor), P()
    return jax.shard_map(
        shards,
        mesh=fine,
        in_specs=(
            tokens, shared, weight, weight, P(dp, None), weight, P(None, tensor), heads,
            shared, shared, heads, heads, heads, heads, weight, tokens,
        ),
        out_specs=(
            tokens, tokens, shared, weight, weight, P(dp, None), weight, P(None, tensor), heads,
            shared, shared, heads, heads, heads, heads, weight,
        ),
        check_vma=False,
    )
```

```python
import jax
import jax.numpy as jnp
from jax import lax
from jax.experimental import pallas as pl
from jax.experimental.pallas import tpu as pltpu
from jax.sharding import Mesh
from jax.sharding import PartitionSpec as P

D = 1536
LEN = 1024
INNER = 3072
STATE = 128
BLOCK = 256
BLOCKS = LEN // BLOCK
GROUPS = 2
HEADS = 6
COLS = HEADS * 64
WIDE = GROUPS * COLS
STEPS = 2 * WIDE
PROJ = STEPS + GROUPS * 128
MORE = PROJ - WIDE
LOG2E = 1.4426950408889634
EPS = 1e-05
F32 = jnp.float32
BF16 = jnp.bfloat16
MESH = pl.DeviceIdType.MESH
AXES = ("yl", "x", "c", "yh", "z")
ANY = pl.BlockSpec(memory_space=pl.ANY)
VMEM = pl.BlockSpec(memory_space=pltpu.VMEM)
SHAPE = jax.ShapeDtypeStruct
ROOM = 60 * 2**20


def dot(a, b):
    return jnp.dot(a, b, preferred_element_type=F32)


def dot_nt(a, b):
    return lax.dot_general(a, b, (((1,), (1,)), ((), ())), preferred_element_type=F32)


def dot_tn(a, b):
    return lax.dot_general(a, b, (((0,), (0,)), ((), ())), preferred_element_type=F32)


def pieces(v, n):
    out = []
    for _ in range(n):
        hi = v.astype(BF16)
        out.append(hi)
        v = v - hi.astype(F32)
    return out


def dot_left(v, ones, n):
    return sum(dot(p, ones) for p in pieces(v, n))


def spread(v, ones):
    hi = v.astype(BF16).astype(F32)
    low = pltpu.roll(v - hi, 64, 1)
    return dot(jnp.where(iota(v.shape, 1) < 64, hi, low).astype(BF16), ones)


def folded(v, ones):
    hi = v.astype(BF16)
    low = (v - hi.astype(F32)).astype(BF16)
    return dot(hi, ones) + dot(low, ones)


def dot_right(ones, v, n):
    return sum(dot(ones, p) for p in pieces(v, n))


def iota(shape, axis):
    return lax.broadcasted_iota(jnp.int32, shape, axis)


def expander():
    row, col = iota((128, COLS), 0), iota((128, COLS), 1)
    return ((row & 63) == lax.shift_right_logical(col, 6)).astype(BF16)


def reducer():
    row, col = iota((COLS, 128), 0), iota((COLS, 128), 1)
    return (col == lax.shift_right_logical(row, 6)).astype(BF16)


def sigmoid(v):
    return 0.5 * jnp.tanh(0.5 * v) + 0.5


def lower(strict=False):
    row, col = iota((BLOCK, BLOCK), 0), iota((BLOCK, BLOCK), 1)
    return ((row > col) if strict else (row >= col)).astype(BF16)


def upper():
    return (iota((BLOCK, BLOCK), 0) <= iota((BLOCK, BLOCK), 1)).astype(BF16)


def token_row(v):
    v = sum(v[:, 128 * i : 128 * (i + 1)] for i in range(v.shape[1] // 128))
    ones = jnp.ones((8, 128), BF16)
    return sum(dot_nt(ones, p) for p in pieces(v, 3))[0:1, :]


class Net:
    def __init__(self, send, recv):
        self.send, self.recv, self.copies = send, recv, []
        self.at = {name: lax.axis_index(name) for name in AXES}
        self.at["y"] = self.at["yh"] * 2 + self.at["yl"]
        self.places = {(a, s): lax.rem(self.at[a] + s + 4, 4) for a in ("x", "y", "z") for s in (1, -1, 2)}
        self.other = 1 - self.at["c"]
        self.targets = {("c", 1): {"c": self.other}}
        for (a, s), place in self.places.items():
            self.targets[a, s] = {"yh": place // 2, "yl": lax.rem(place, 2)} if a == "y" else {a: place}

    def near(self, axis, step):
        return self.places[axis, step]

    def plan(self, src, dst, axis, step=1):
        copy = Copy(self, len(self.copies), src, dst, self.targets[axis, step])
        self.copies.append(copy)
        return copy

    def start(self, src, dst, axis, step=1):
        return self.plan(lambda: src, lambda: dst, axis, step).start()

    def around(self, src, dst, axis):
        return [self.start(src, dst, axis, step) for step in (1, -1, 2)]

    def barrier(self, peers):
        here = pltpu.get_barrier_semaphore()
        for peer in peers:
            pl.semaphore_signal(here, inc=1, device_id=self.targets[peer], device_id_type=MESH)
        pl.semaphore_wait(here, len(peers))

    def finish(self):
        for copy in self.copies:
            copy.arrived()
        for copy in self.copies:
            copy.left()


class Copy:
    def __init__(self, net, index, src, dst, target):
        self.net, self.index, self.src, self.dst, self.target = net, index, src, dst, target
        self.here, self.gone = False, False

    def made(self):
        return pltpu.make_async_remote_copy(
            src_ref=self.src(),
            dst_ref=self.dst(),
            send_sem=self.net.send.at[self.index],
            recv_sem=self.net.recv.at[self.index],
            device_id=self.target,
            device_id_type=MESH,
        )

    def start(self):
        self.made().start()
        return self

    def arrived(self):
        if not self.here:
            self.here = True
            self.made().wait_recv()

    def left(self):
        if not self.gone:
            self.gone = True
            self.made().wait_send()


def sems(n):
    return [pltpu.SemaphoreType.DMA((n,)), pltpu.SemaphoreType.DMA((n,))]


def rows(ref, first, count):
    return ref.at[pl.ds(pl.multiple_of(first, 16), count)]


def lanes(first, count):
    return pl.ds(pl.multiple_of(first, 128), count)


def arrive(copies):
    for copy in copies:
        copy.arrived()


HALVES = ((0, 1), (1, -1))


class GridSum:
    def __init__(self, net, first, held, spans, scratch, cut=(0, 96)):
        self.net, self.first, self.held, self.spans = net, first, held, spans
        self.land, self.mid, self.last = scratch
        self.rows = pl.ds(*cut)
        self.one, self.two = [], []
        for slot, step in enumerate((2, 1, -1)):
            if first == "x":
                self.plan(self.one, lambda step=step: held.at[:, net.near("x", step), self.rows], lambda slot=slot: self.land.at[slot], "x", step)
            else:
                self.plan(self.two, lambda step=step: self.mid.at[net.near("x", step)], lambda slot=slot: self.last.at[slot], "x", step)
            lane = 0
            for base, n in spans:
                there = lambda step=step, base=base, n=n: lanes(base + (net.near("y", step) // 2) * n, n)
                if first == "x":
                    src = lambda step=step, there=there: self.mid.at[lax.rem(net.near("y", step), 2), :, there()]
                    self.plan(self.two, src, lambda slot=slot, lane=lane, n=n: self.last.at[slot, :, pl.ds(lane, n)], "y", step)
                else:
                    src = lambda step=step, there=there: held.at[lax.rem(net.near("y", step), 2), :, self.rows, there()]
                    self.plan(self.one, src, lambda slot=slot, lane=lane, n=n: self.land.at[slot, :, :, pl.ds(lane, n)], "y", step)
                lane += n

    def plan(self, to, src, dst, axis, step):
        to.append(self.net.plan(src, dst, axis, step))

    def step1(self):
        for copy in self.one:
            copy.start()

    def step2(self):
        arrive(self.one)
        at = self.net.at
        if self.first == "x":
            self.mid[...] = self.total(self.held[:, at["x"], self.rows], self.land, slice(None)).astype(BF16)
        else:
            lane = 0
            for base, n in self.spans:
                cut = slice(lane, lane + n)
                own = self.held[at["yl"], :, self.rows, lanes(base + at["yh"] * n, n)]
                self.mid[:, :, cut] = self.total(own, self.land, cut).astype(BF16)
                lane += n
        for copy in self.two:
            copy.start()

    def total(self, own, others, cut):
        return (own.astype(F32) + others[0, ..., cut].astype(F32)) + (others[1, ..., cut].astype(F32) + others[2, ..., cut].astype(F32))

    def step3(self, out):
        arrive(self.two)
        at = self.net.at
        if self.first == "y":
            out[self.rows, :] = self.total(self.mid[at["x"]], self.last, slice(None))
            return
        lane = 0
        for base, n in self.spans:
            cut = slice(lane, lane + n)
            out[self.rows, cut] = self.total(self.mid[at["yl"], :, lanes(base + at["yh"] * n, n)], self.last, cut)
            lane += n


def grid_scratch(first, width, count=96):
    blocks, wide = (2, 2 * width) if first == "x" else (4, width)
    return [pltpu.VMEM(s, BF16) for s in ((3, blocks, count, wide), (blocks, count, wide), (3, count, width))]


class TokenSum:
    def __init__(self, net, scratch):
        self.net, self.far, self.half, self.fold, self.whole = net, *scratch
        self.one = [
            net.plan(lambda p=p: self.far.at[pl.ds(128 * p, 128)], lambda p=p: self.half.at[p], "z", step) for p, step in HALVES
        ]
        self.two = [net.plan(lambda p=p: self.fold.at[p], lambda p=p: self.whole.at[p], "z", step) for p, step in HALVES]

    def step1(self):
        for copy in self.one:
            copy.start()

    def step2(self):
        arrive(self.one)
        for p, _ in HALVES:
            self.fold[p, 128 * p : 128 * p + 128, :] += self.half[p]
            self.two[p].start()

    def step3(self):
        arrive(self.two)
        return self.whole[0].astype(F32) + self.whole[1].astype(F32)


def token_scratch():
    return [pltpu.VMEM((256, D), BF16), pltpu.VMEM((2, 128, D), BF16), pltpu.VMEM((2, 256, D), BF16), pltpu.VMEM((2, 256, D), BF16)]


def gather_kernel(x, gain, w_gate, w_inner, w_out, w_bc, w_step, conv, bias, gate_gain, step_bias, decay_log, skip, normed_all, wx, wout, wbc, prm, xv, low, stepv, stept, pk, send, recv, local):
    net = Net(send, recv)
    at = net.at
    yh, cx, cc, z, y = at["yh"], at["x"], at["c"], at["z"], at["y"]
    load = pltpu.make_async_copy(x, xv, local.at[0])
    load.start()
    stept[...] = jnp.zeros_like(stept)
    stept[0:HEADS, 0:96] = w_step[...].astype(F32)
    stepv[...] = jnp.transpose(stept[...])[0:96, :].astype(BF16)
    pk[...] = jnp.zeros_like(pk)
    pk[0:4, :] = conv[...]
    pk[4:5, :] = bias[...].reshape(1, COLS)
    pk[5:6, :] = gate_gain[...].reshape(1, COLS)
    pk[6:7, 0:HEADS] = step_bias[...].reshape(1, HEADS)
    pk[7:8, 0:HEADS] = decay_log[...].reshape(1, HEADS)
    pk[8:9, 0:HEADS] = skip[...].reshape(1, HEADS)
    net.barrier([("z", 1), ("z", -1), ("x", 1), ("x", -1), ("y", 1), ("y", -1), ("y", 2), ("c", 1)])
    first = {
        "x": ((w_gate, wx, 0, COLS), (w_out, wout, 0, COLS)),
        "y": ((w_inner, wx, WIDE, COLS), (stepv, wx, STEPS, 128), (w_bc.at[:, lanes(yh * 128, 128)], wbc, 0, 128)),
    }

    def spot(ref, base, n, yy, xx, cut=slice(None)):
        cut = pl.ds(0, 96) if cut == slice(None) else cut
        return ref.at[lax.rem(yy, 2), xx, cc, cut, lanes(base + (yy // 2) * n, n)]

    own = [pltpu.make_async_copy(src, spot(ref, base, n, y, cx), local.at[1 + i]) for i, (src, ref, base, n) in enumerate(first["x"] + first["y"])]
    own.append(pltpu.make_async_copy(pk, prm.at[yh], local.at[6]))
    sent = {"x": [], "y": []}
    for axis in ("x", "y"):
        for src, ref, base, n in first[axis]:
            sent[axis].append([net.start(src, spot(ref, base, n, y, cx), axis, step) for _, step in HALVES])
    load.wait()
    v = xv[...].astype(F32)
    root = lax.rsqrt(jnp.mean(v * v, axis=1, keepdims=True) + EPS)
    low[...] = (v * root * gain[...].reshape(1, D)).astype(BF16)
    zs = [net.start(low, rows(normed_all, z * 256, 256), "z", step) for _, step in HALVES]
    own.append(pltpu.make_async_copy(low, rows(normed_all, z * 256, 256), local.at[7]))
    for copy in own:
        copy.start()
    for axis in ("x", "y"):
        for src, ref, base, n in first[axis]:
            net.start(src, spot(ref, base, n, y, cx), "c")
    net.start(pk, prm.at[yh], "y", 2)
    second = {"x": [], "y": []}
    for axis in ("x", "y"):
        for (src, ref, base, n), copies in zip(first[axis], sent[axis]):
            for (part, step), copy in zip(HALVES, copies):
                copy.arrived()
                cut = pl.ds(48 * part, 48)
                here = spot(ref, base, n, y, net.near("x", -step), cut) if axis == "x" else spot(ref, base, n, net.near("y", -step), cx, cut)
                second[axis].append(net.start(here, here, axis, step))
    for copy in own[:5]:
        copy.wait()
    third = {"x": [], "y": []}

    def line(axis, ref, base, n, place, cut=None):
        cut = pl.ds(0, 96) if cut is None else cut
        if axis == "x":
            return ref.at[lax.rem(place, 2), :, cc, cut, lanes(base + (place // 2) * n, n)]
        return ref.at[:, place, cc, cut, lanes(base, 2 * n)]

    then = {"x": "y", "y": "x"}
    for axis in ("x", "y"):
        arrive(second[axis])
        for src, ref, base, n in first[axis]:
            here = line(axis, ref, base, n, at[then[axis]])
            third[axis].append([net.start(here, here, then[axis], step) for _, step in HALVES])
    for axis in ("x", "y"):
        for src, ref, base, n in first[axis]:
            for step in (1, -1, 2):
                here = spot(ref, base, n, y, net.near("x", step)) if axis == "x" else spot(ref, base, n, net.near("y", step), cx)
                net.start(here, here, "c")
    fourth = {"x": [], "y": []}

    def pass_on(axis):
        for (src, ref, base, n), copies in zip(first[axis], third[axis]):
            for (part, step), copy in zip(HALVES, copies):
                copy.arrived()
                place = net.near(then[axis], -step)
                here = line(axis, ref, base, n, place, pl.ds(48 * part, 48))
                fourth[axis].append(net.start(here, here, then[axis], step))
                here = line(axis, ref, base, n, place)
                net.start(here, here, "c")

    pass_on("y")
    pass_on("x")
    for (part, step), copy in zip(HALVES, zs):
        copy.arrived()
        here = rows(normed_all, net.near("z", -step) * 256 + 128 * part, 128)
        net.start(here, here, "z", step)
    for axis in ("y", "x"):
        arrive(fourth[axis])
        for src, ref, base, n in first[axis]:
            here = line(axis, ref, base, n, net.near(then[axis], 2))
            net.start(here, here, "c")
    net.finish()
    for copy in own[5:]:
        copy.wait()


def run_gather(*args):
    return pl.pallas_call(
        gather_kernel,
        out_shape=[
            SHAPE((LEN, D), BF16),
            SHAPE((2, 4, 2, 96, PROJ), BF16),
            SHAPE((2, 4, 2, 96, WIDE), BF16),
            SHAPE((2, 4, 2, 96, 256), BF16),
            SHAPE((GROUPS, 16, COLS), F32),
        ],
        in_specs=[ANY, VMEM, ANY, ANY, ANY, ANY] + [VMEM] * 7,
        out_specs=[ANY] * 5,
        scratch_shapes=[
            pltpu.VMEM((256, D), BF16),
            pltpu.VMEM((256, D), BF16),
            pltpu.VMEM((96, 128), BF16),
            pltpu.VMEM((128, 128), F32),
            pltpu.VMEM((16, COLS), F32),
        ]
        + sems(96)
        + [pltpu.SemaphoreType.DMA((8,))],
        compiler_params=pltpu.CompilerParams(collective_id=0, has_side_effects=True, vmem_limit_bytes=ROOM),
        name="gather_all",
    )(*args)


def forward_kernel(
    x, wx, wout, wbc, prm, conv_bc, bias_bc, cot,
    inner_out, z_out, y_out, h_out, dt_out, r_out, u_out, bc_out, bcin_out, zbc_out, normed_t, gains_out, mixed_out, gs_out, gg_out, cot_t,
    cots, gps, acts, slopes, gms, mixed, gg, turned_c, ext, extbc, state, stat, slots, send, recv, local,
):
    i = pl.program_id(0)
    net = Net(send, recv)
    z = net.at["z"]
    here = lambda step=0: rows(cots, (net.near("z", step) if step else z) * 256, 256)
    part = lambda p, step: rows(cots, net.near("z", -step) * 256 + 128 * p, 128)
    c1 = [net.plan(lambda: cot, lambda: here(), "z", step) for _, step in HALVES]
    c2 = [net.plan(lambda p=p, s=s: part(p, s), lambda p=p, s=s: part(p, s), "z", s) for p, s in HALVES]
    q = [net.plan(lambda: stat, lambda: slots.at[z], "z", step) for step in (1, -1, 2)]
    own = lambda: pltpu.make_async_copy(cot, here(), local.at[0])
    turn_out = lambda: pltpu.make_async_copy(turned_c, cot_t, local.at[1])

    @pl.when(i == 0)
    def _():
        net.barrier([("z", 1), ("z", -1), ("z", 2)])
        own().start()
        for copy in c1:
            copy.start()
        ext[0:8, :] = jnp.zeros((8, WIDE), F32)
        extbc[0:8, :] = jnp.zeros((8, 256), F32)
        state[...] = jnp.zeros_like(state)

    @pl.when((i > 0) & (i < BLOCKS))
    def _():
        ext[0:8, :] = ext[BLOCK : BLOCK + 8, :]
        extbc[0:8, :] = extbc[BLOCK : BLOCK + 8, :]

    @pl.when(i == BLOCKS - 1)
    def _():
        for copy in c1:
            copy.arrived()
        for copy in c2:
            copy.start()

    @pl.when(i < BLOCKS)
    def _():
        xb = x[...]
        turned = jnp.transpose(xb).reshape(2, 4, 2, 96, BLOCK)
        for core in range(2):
            normed_t[core] = turned[:, :, core]
        bc_in = dot(xb, wbc[...])
        bcin_out[...] = bc_in
        extbc[8 : BLOCK + 8, :] = bc_in
        zb = bias_bc[...] + sum(conv_bc[j : j + 1, :] * extbc[5 + j : 5 + j + BLOCK, :] for j in range(4))
        zbc_out[...] = zb
        bc = (zb * sigmoid(zb)).astype(BF16)
        bc_out[...] = bc
        b, c = bc[:, :STATE], bc[:, STATE:]
        scores = jnp.where(iota((BLOCK, BLOCK), 0) >= iota((BLOCK, BLOCK), 1), dot_nt(c, b), 0.0)
        tri, ones = lower(), expander()
        left = iota((BLOCK, 128), 1) < 64
        steps = dot(xb, wx[:, STEPS:])
        total = jnp.zeros((BLOCK, 128), F32)
        for g in range(GROUPS):
            cut = slice(g * COLS, (g + 1) * COLS)
            u = steps[:, 128 * g : 128 * (g + 1)] + prm[g, 6:7, 0:128]
            dt = jnp.maximum(u, 0.0) + jnp.log(1.0 + jnp.exp(-jnp.abs(u)))
            rate = -jnp.exp(prm[g, 7:8, 0:128]) * LOG2E
            r = dot_right(tri, dt * rate, 3)
            u_out[g] = u
            dt_out[g] = dt
            r_out[g] = r
            rt = jnp.transpose(r)
            gate = dot(xb, wx[:, cut])
            inner = dot(xb, wx[:, WIDE + g * COLS : WIDE + (g + 1) * COLS])
            inner_out[:, cut] = inner
            ext[8 : BLOCK + 8, cut] = inner
            zv = prm[g, 4:5, :] + sum(prm[g, j : j + 1, :] * ext[5 + j : 5 + j + BLOCK, cut] for j in range(4))
            z_out[:, cut] = zv
            xv = zv * sigmoid(zv)
            last = r[BLOCK - 1 : BLOCK, :]
            w = xv * spread(dt, ones)
            grow = spread(jnp.exp2(r), ones)
            tail = spread(jnp.exp2(last - r), ones)
            skip = spread(prm[g, 8:16, 0:128], ones)[0:1, :]
            wl = w.astype(BF16)
            h = state[:, cut]
            h_out[0, g] = h
            parts = []
            for p in range(HEADS // 2):
                halves = []
                for n in (2 * p, 2 * p + 1):
                    gap = jnp.minimum(r[:, n : n + 1] - rt[n : n + 1, :], 0.0)
                    halves.append(dot((scores * jnp.exp2(gap)).astype(BF16), wl[:, 128 * p : 128 * (p + 1)]))
                parts.append(jnp.where(left, halves[0], halves[1]))
            yv = jnp.concatenate(parts, axis=1) + grow * dot(c, h.astype(BF16)) + skip * xv
            y_out[:, cut] = yv
            state[:, cut] = grow[BLOCK - 1 : BLOCK, :] * h + dot_tn(b, (tail * w).astype(BF16))
            sig = sigmoid(gate)
            act = gate * sig
            gp = yv * act
            here_now = pl.ds(pl.multiple_of(i * BLOCK, BLOCK), BLOCK)
            gps[here_now, cut] = gp
            acts[here_now, cut] = act
            slopes[here_now, cut] = yv * (sig + act * (1.0 - sig))
            sq = gp * gp
            total = total + (sq[:, 0:128] + sq[:, 128:256] + sq[:, 256:384])
        stat[pl.ds(i, 1), :] = token_row(total)

    @pl.when(i == BLOCKS)
    def _():
        own().wait()

    @pl.when(i == 2 * BLOCKS - 1)
    def _():
        for copy in c2:
            copy.arrived()

    @pl.when(i >= BLOCKS)
    def _():
        t = i - BLOCKS
        block = lax.rem(z + t + lax.div(t, 2) - 2 * lax.div(t, 3), 4)
        at = pl.ds(pl.multiple_of(block * BLOCK, BLOCK), BLOCK)
        cb = cots[at, :]
        turned = jnp.transpose(cb).reshape(2, 4, 2, 96, BLOCK)
        for core in range(2):
            turned_c[core, :, :, :, at] = turned[:, :, core]
        gm = dot(cb, wout[...])
        gms[at, :] = gm
        gain = jnp.concatenate([prm[0, 5:6, :], prm[1, 5:6, :]], axis=1)
        stat[pl.ds(BLOCKS + block, 1), :] = token_row(gm * gain * gps[at, :])

    @pl.when(i == 2 * BLOCKS - 1)
    def _():
        for copy in q:
            copy.start()
        slots[z] = stat[...]
        for copy in q:
            copy.arrived()
            copy.left()
        sums = (slots[0] + slots[1]) + (slots[2] + slots[3])
        root = lax.rsqrt(sums[0:4, :] * (1.0 / INNER) + EPS)
        stat[0:4, :] = root
        stat[4:8, :] = root * root * root * (sums[4:8, :] * (1.0 / INNER))
        columns = jnp.transpose(stat[...])
        gain = jnp.concatenate([prm[0, 5:6, :], prm[1, 5:6, :]], axis=1)
        turn_out().start()
        gain_grad = jnp.zeros((1, WIDE), F32)
        outs = []
        for k in range(BLOCKS):
            at = slice(k * BLOCK, (k + 1) * BLOCK)
            gp, gm = gps[at, :], gms[at, :]
            normal = gp * columns[:, k : k + 1]
            gain_grad = gain_grad + jnp.sum(gm * normal, axis=0, keepdims=True)
            mixed[at, :] = (normal * gain).astype(BF16)
            gated = (gm * gain) * columns[:, k : k + 1] - gp * columns[:, BLOCKS + k : BLOCKS + k + 1]
            gms[at, :] = gated * acts[at, :]
            gg[at, :] = (gated * slopes[at, :]).astype(BF16)
            block = pl.ds(k * BLOCK, BLOCK)
            for src, dst in ((mixed, mixed_out), (gms, gs_out), (gg, gg_out)):
                outs.append(pltpu.make_async_copy(src.at[block], dst.at[block], local.at[2 + len(outs)]))
                outs[-1].start()
        gains_out[...] = jnp.concatenate([gain_grad, jnp.zeros((7, WIDE), F32)], axis=0)
        for copy in c1 + c2 + q:
            copy.left()
        for copy in outs:
            copy.wait()
        turn_out().wait()


def run_forward(x, wx, wout, wbc, prm, conv_bc, bias_bc, cot):
    first = lambda k: jnp.minimum(k, BLOCKS - 1)
    const = lambda *s: pl.BlockSpec(s, lambda k: (0,) * len(s), pipeline_mode=pl.Buffered(1))
    keep = lambda *s: pl.BlockSpec(s, lambda k: (0,) * len(s))
    block = lambda n: pl.BlockSpec((BLOCK, n), lambda k: (first(k), 0))
    small = lambda: pl.BlockSpec((GROUPS, BLOCK, 128), lambda k: (0, first(k), 0))
    wide = SHAPE((LEN, WIDE), F32)
    narrow = SHAPE((GROUPS, LEN, 128), F32)
    return pl.pallas_call(
        forward_kernel,
        grid=(2 * BLOCKS,),
        out_shape=[
            wide,
            wide,
            wide,
            SHAPE((BLOCKS, GROUPS, STATE, COLS), F32),
            narrow,
            narrow,
            narrow,
            SHAPE((LEN, 256), BF16),
            SHAPE((LEN, 256), F32),
            SHAPE((LEN, 256), F32),
            SHAPE((2, 2, 4, 96, LEN), BF16),
            SHAPE((8, WIDE), F32),
            SHAPE((LEN, WIDE), BF16),
            wide,
            SHAPE((LEN, WIDE), BF16),
            SHAPE((2, 2, 4, 96, LEN), BF16),
        ],
        in_specs=[
            block(D),
            const(D, PROJ),
            const(D, WIDE),
            const(D, 256),
            const(GROUPS, 16, COLS),
            const(4, 256),
            const(1, 256),
            ANY,
        ],
        out_specs=[
            block(WIDE),
            block(WIDE),
            block(WIDE),
            pl.BlockSpec((1, GROUPS, STATE, COLS), lambda k: (first(k), 0, 0, 0)),
            small(),
            small(),
            small(),
            block(256),
            block(256),
            block(256),
            pl.BlockSpec((2, 2, 4, 96, BLOCK), lambda k: (0, 0, 0, 0, first(k))),
            keep(8, WIDE),
        ]
        + [ANY] * 4,
        scratch_shapes=[
            pltpu.VMEM((LEN, D), BF16),
            pltpu.VMEM((LEN, WIDE), F32),
            pltpu.VMEM((LEN, WIDE), F32),
            pltpu.VMEM((LEN, WIDE), F32),
            pltpu.VMEM((LEN, WIDE), F32),
            pltpu.VMEM((LEN, WIDE), BF16),
            pltpu.VMEM((LEN, WIDE), BF16),
            pltpu.VMEM((2, 2, 4, 96, LEN), BF16),
            pltpu.VMEM((BLOCK + 8, WIDE), F32),
            pltpu.VMEM((BLOCK + 8, 256), F32),
            pltpu.VMEM((STATE, WIDE), F32),
            pltpu.VMEM((8, BLOCK), F32),
            pltpu.VMEM((4, 8, BLOCK), F32),
        ]
        + sems(7)
        + [pltpu.SemaphoreType.DMA((14,))],
        compiler_params=pltpu.CompilerParams(collective_id=1, has_side_effects=True, vmem_limit_bytes=ROOM),
        name="forward",
    )(x, wx, wout, wbc, prm, conv_bc, bias_bc, cot)


def backward_kernel(
    gs_in, inner, zin, y, hin, prm, bc, dt, r, u, gains, mixed, wout, cot_t, gg, normed_t, tokens,
    cat_out, dbc_out, acc, branch_out, wout_out, wgate_out,
    ext, dstate, dst, dbc, held, got, away, mv, wv, cv, gv, nv, ownb, g0, g1, g2, g3, s1, s2, s3, t1, t2, t3, send, recv, local,
):
    k = pl.program_id(0)
    net = Net(send, recv)
    cc, z = net.at["c"], net.at["z"]
    cross = [net.plan(lambda n=n: away.at[n], lambda n=n: got.at[n], "c") for n in range(2)]
    token = TokenSum(net, (g0, g1, g2, g3))
    rings = (GridSum(net, "y", held.at[0], ((0, COLS),), (s1, s2, s3)), GridSum(net, "x", held.at[1], ((0, COLS),), (t1, t2, t3)))

    @pl.when(k == 0)
    def _():
        loads = [pltpu.make_async_copy(src, dst, local.at[n]) for n, (src, dst) in enumerate(((mixed, mv), (wout, wv), (cot_t, cv), (gg, gv), (normed_t, nv)))]
        for copy in loads:
            copy.start()
        net.barrier([("z", 1), ("z", -1)] + [(a, s) for a in ("x", "y") for s in (1, -1, 2)] + [("c", 1)])
        loads[0].wait()
        loads[1].wait()
        branch = lambda place: dot_nt(mv[pl.ds(pl.multiple_of(place * 256, 256), 256), :], wv[...])
        grads = lambda left, right, core: dot(left[core].reshape(8 * 96, LEN), right[...]).astype(BF16).reshape(2, 4, 96, WIDE)
        g0[...] = branch(net.near("z", 2)).astype(BF16)
        token.step1()
        loads[2].wait()
        away[0] = grads(cv, mv, net.other)
        cross[0].start()
        loads[3].wait()
        loads[4].wait()
        away[1] = grads(nv, gv, net.other)
        cross[1].start()
        g2[0] = branch(net.near("z", 1)).astype(BF16)
        g2[1] = branch(net.near("z", -1)).astype(BF16)
        ownb[...] = branch(z)
        held[0] = grads(cv, mv, cc)
        held[1] = grads(nv, gv, cc)
        acc[...] = jnp.zeros_like(acc)
        for g in range(GROUPS):
            acc[g, 5:6, :] = gains[0:1, g * COLS : (g + 1) * COLS]
        ext[BLOCK : BLOCK + 8, :] = jnp.zeros((8, WIDE), F32)
        dstate[...] = jnp.zeros_like(dstate)

    @pl.when(k > 0)
    def _():
        ext[BLOCK : BLOCK + 8, :] = ext[0:8, :]

    b, c = bc[:, :STATE], bc[:, STATE:]
    valid = iota((BLOCK, BLOCK), 1) >= iota((BLOCK, BLOCK), 0)
    scores = jnp.where(valid, dot_nt(b, c), 0.0)
    ones, fold = expander(), reducer()
    left = iota((BLOCK, 128), 1) < 64
    suffix, prefix = upper(), lower(strict=True)
    dst[...] = jnp.zeros_like(dst)
    dbc[...] = jnp.zeros_like(dbc)
    for g in range(GROUPS):
        if g == 0:

            @pl.when(k == 1)
            def _():
                token.step2()

            @pl.when(k == 3)
            def _():
                for ring in rings:
                    ring.step2()

        else:

            @pl.when(k == 0)
            def _():
                for n in range(2):
                    cross[n].arrived()
                    held[n] += got[n]
                    rings[n].step1()

        cut = slice(g * COLS, (g + 1) * COLS)
        yv = y[:, cut]
        gs = gs_in[:, cut]
        xi = inner[:, cut]
        zv = zin[:, cut]
        zs = sigmoid(zv)
        xv = zv * zs
        rv = r[g]
        rt = jnp.transpose(rv)
        last = rv[BLOCK - 1 : BLOCK, :]
        dte = spread(dt[g], ones)
        grow = spread(jnp.exp2(rv), ones)
        tail = spread(jnp.exp2(last - rv), ones)
        skip = spread(prm[g, 8:16, 0:128], ones)[0:1, :]
        w = xv * dte
        wl = w.astype(BF16)
        gl = gs.astype(BF16)
        h = hin[0, g]
        dh = dstate[:, cut]
        dhl = dh.astype(BF16)
        parts = []
        for p in range(HEADS // 2):
            halves = []
            pair = slice(128 * p, 128 * (p + 1))
            wp, gpair = wl[:, pair], gl[:, pair]
            zero = jnp.zeros_like(wp)
            w_low = pltpu.roll(w[:, pair] - wp.astype(F32), 64, 1).astype(BF16)
            g_low = (gs[:, pair] - gpair.astype(F32)).astype(BF16)
            g_turn = pltpu.roll(gpair.astype(F32), 64, 1).astype(BF16)
            for n in (2 * p, 2 * p + 1):
                decay = jnp.exp2(jnp.minimum(rt[n : n + 1, :] - rv[:, n : n + 1], 0.0))
                halves.append(dot((scores * decay).astype(BF16), gpair))
                pick = (lambda a, b: jnp.where(left, a, b)) if n % 2 == 0 else (lambda a, b: jnp.where(left, b, a))
                one = jnp.concatenate([pick(wp, w_low), pick(wp, zero)], axis=1)
                two = jnp.concatenate([pick(gpair, g_turn), g_low], axis=1)
                dst[...] += dot_nt(one, two) * decay
            parts.append(jnp.where(left, halves[0], halves[1]))
        dwi = jnp.concatenate(parts, axis=1)
        dws = tail * dot(b, dhl)
        dw = dwi + dws
        skipgrad = gs * xv
        diff = folded(gl.astype(F32) * (yv - skip * xv) - wl.astype(F32) * dwi, fold)
        zsum = folded(w * dws, fold)
        const = folded(jnp.sum(h * dh, axis=0, keepdims=True) * grow[BLOCK - 1 : BLOCK, :] + jnp.zeros((8, COLS), F32), fold)
        da = dot_right(suffix, diff, 3) + dot_right(prefix, zsum, 3) + const[0:1, :]
        rate = -jnp.exp(prm[g, 7:8, 0:128])
        dstep = (folded(xv * dw, fold) + rate * da) * sigmoid(u[g])
        cat_out[:, WIDE + 128 * g : WIDE + 128 * (g + 1)] = dstep.astype(BF16)
        gx = (grow * gs).astype(BF16)
        dbc[:, STATE:] += dot_nt(gx, h.astype(BF16))
        dbc[:, :STATE] += dot_nt((tail * w).astype(BF16), dhl)
        dstate[:, cut] = grow[BLOCK - 1 : BLOCK, :] * dh + dot_tn(c, gx)
        dx = dte * dw + skip * gs
        dz = dx * (zs * (1.0 + zv * (1.0 - zs)))
        ext[0:BLOCK, cut] = dz
        gi = jnp.zeros((BLOCK, COLS), F32)
        for j in range(4):
            moved = ext[3 - j : 3 - j + BLOCK, cut]
            gi = gi + prm[g, j : j + 1, :] * moved
            acc[g, j : j + 1, :] += jnp.sum(xi * moved, axis=0, keepdims=True)
        cat_out[:, cut] = gi.astype(BF16)
        acc[g, 4:5, :] += jnp.sum(dz, axis=0, keepdims=True)
        acc[g, 6:7, 0:128] += jnp.sum(dstep, axis=0, keepdims=True)
        acc[g, 7:8, 0:128] += jnp.sum(da * dt[g], axis=0, keepdims=True) * rate
        acc[g, 8:9, 0:128] += folded(jnp.sum(skipgrad, axis=0, keepdims=True) + jnp.zeros((8, COLS), F32), fold)[0:1, :]
    ds = jnp.where(valid, dst[...], 0.0).astype(BF16)
    dbc_out[:, STATE:] = (dbc[:, STATE:] + dot_tn(ds, b)).astype(BF16)
    dbc_out[:, :STATE] = (dbc[:, :STATE] + dot(ds, c)).astype(BF16)

    @pl.when(k == BLOCKS - 1)
    def _():
        rings[0].step3(wout_out)
        rings[1].step3(wgate_out)
        branch_out[...] = (tokens[...].astype(F32) + (ownb[...] + token.step3())).astype(BF16)
        for copy in net.copies:
            copy.left()


def run_backward(*args):
    rev = lambda k: BLOCKS - 1 - k
    cols = lambda n: pl.BlockSpec((BLOCK, n), lambda k: (rev(k), 0))
    small = lambda: pl.BlockSpec((GROUPS, BLOCK, 128), lambda k: (0, rev(k), 0))
    keep = lambda *s: pl.BlockSpec(s, lambda k: (0,) * len(s))
    bf = lambda *s: pltpu.VMEM(s, BF16)
    f32 = lambda *s: pltpu.VMEM(s, F32)
    return pl.pallas_call(
        backward_kernel,
        grid=(BLOCKS,),
        out_shape=[
            SHAPE((LEN, MORE), BF16),
            SHAPE((LEN, 256), BF16),
            SHAPE((GROUPS, 16, COLS), F32),
            SHAPE((256, D), BF16),
            SHAPE((96, COLS), F32),
            SHAPE((96, COLS), F32),
        ],
        in_specs=[cols(WIDE)] * 4
        + [
            pl.BlockSpec((1, GROUPS, STATE, COLS), lambda k: (rev(k), 0, 0, 0)),
            keep(GROUPS, 16, COLS),
            cols(256),
            small(),
            small(),
            small(),
            keep(8, WIDE),
        ]
        + [ANY] * 5
        + [keep(256, D)],
        out_specs=[cols(MORE), cols(256), keep(GROUPS, 16, COLS), keep(256, D), keep(96, COLS), keep(96, COLS)],
        scratch_shapes=[
            f32(BLOCK + 8, WIDE),
            f32(STATE, WIDE),
            f32(BLOCK, BLOCK),
            f32(BLOCK, 256),
            bf(2, 2, 4, 96, WIDE),
            bf(2, 2, 4, 96, WIDE),
            bf(2, 2, 4, 96, WIDE),
            bf(LEN, WIDE),
            bf(D, WIDE),
            bf(2, 2, 4, 96, LEN),
            bf(LEN, WIDE),
            bf(2, 2, 4, 96, LEN),
            f32(256, D),
        ]
        + token_scratch()
        + grid_scratch("y", COLS)
        + grid_scratch("x", COLS)
        + sems(24)
        + [pltpu.SemaphoreType.DMA((5,))],
        compiler_params=pltpu.CompilerParams(collective_id=2, has_side_effects=True, vmem_limit_bytes=ROOM),
        name="backward",
    )(*args)


def tail_kernel(
    gg, cat, wx, normed_t, normed, dbc, zbc, bc_in, acc, wbc, tokens, cot, gain, conv,
    tokens_out, inner_out, bc_out, small_out,
    ggv, catv, wxv, ntv, nv, mine, slots, zv, xi, wv, xv, ov, ext, gnbc, ownb, held, got, away, dbw, heldb, gotb, small, sp0, sp1, sp2, sp3, bz, by,
    g0, g1, g2, g3, a1, a2, a3, b1, b2, b3, c1, c2, c3, send, recv, local,
):
    net = Net(send, recv)
    at = net.at
    yh, cx, cc, z, y = at["yh"], at["x"], at["c"], at["z"], at["y"]
    pairs = (
        (gg, ggv),
        (cat, catv),
        (wx, wxv),
        (normed, nv),
        (normed_t, ntv),
        (rows(zbc, z * 256, 256), zv.at[pl.ds(0, 256)]),
        (rows(zbc, lax.rem(z * 256 + 256, LEN), 16), zv.at[pl.ds(256, 16)]),
        (rows(bc_in, z * 256, 256), xi),
        (wbc, wv),
        (tokens, xv),
        (cot, ov),
    )
    loads = [pltpu.make_async_copy(src, dst, local.at[i]) for i, (src, dst) in enumerate(pairs)]
    for copy in loads:
        copy.start()
    token = TokenSum(net, (g0, g1, g2, g3))
    spans = ((0, COLS), (WIDE, 128))
    rings = (GridSum(net, "x", held, spans, (a1, a2, a3), (0, 48)), GridSum(net, "y", held, spans, (b1, b2, b3), (48, 48)))
    ring_bc = GridSum(net, "x", heldb, ((0, 128),), (c1, c2, c3))
    mine[0:LEN, :] = dbc[...]
    mine[LEN : LEN + 16, :] = jnp.zeros((16, 256), BF16)
    slots[z] = mine[pl.ds(pl.multiple_of(z * 256, 16), 272), :]
    net.barrier([(a, s) for a in ("z", "x", "y") for s in (1, -1, 2)] + [("c", 1)])
    swap = [net.start(rows(mine, net.near("z", s) * 256, 272), slots.at[z], "z", s) for s in (1, -1, 2)]
    gain_row = gain[...].reshape(1, D)
    norm_part = jnp.zeros((1, D), F32)

    def block(place):
        cut = pl.ds(pl.multiple_of(place * 256, 256), 256)
        got = dot_nt(ggv[cut, :], wxv[:, 0:WIDE]) + dot_nt(catv[cut, :], wxv[:, WIDE:])
        return got, jnp.sum(got * nv[cut, :].astype(F32), axis=0, keepdims=True)

    for copy in loads[:4]:
        copy.wait()
    out, part = block(net.near("z", 2))
    norm_part = norm_part + part
    g0[...] = out.astype(BF16)
    token.step1()
    grads = lambda core: dot(ntv[core].reshape(8 * 96, LEN), catv[...]).astype(BF16).reshape(2, 4, 96, MORE)
    loads[4].wait()
    away[...] = grads(net.other)
    cross = net.start(away, got, "c")
    for copy in loads[5:]:
        copy.wait()
    arrive(swap)
    total = (slots[0].astype(F32) + slots[1].astype(F32)) + (slots[2].astype(F32) + slots[3].astype(F32))
    sig = sigmoid(zv[...])
    dz = total * (sig * (1.0 + zv[...] * (1.0 - sig)))
    ext[...] = jnp.where(iota((272, 256), 0) + z * 256 < LEN, dz, 0.0)
    gbc = jnp.zeros((256, 256), F32)
    small[0:16, :] = acc[0]
    small[16:32, :] = acc[1]
    small[32:48, :] = jnp.zeros((16, COLS), F32)
    for j in range(4):
        moved = ext[3 - j : 3 - j + 256, :]
        gbc = gbc + conv[j : j + 1, :] * moved
        small[36 + j : 37 + j, 0:256] = jnp.sum(xi[...] * moved, axis=0, keepdims=True)
    small[40:41, 0:256] = jnp.sum(ext[0:256, :], axis=0, keepdims=True)
    gbc = gbc.astype(BF16)
    own = pl.ds(pl.multiple_of(z * 256, 256), 256)
    for core in range(2):
        dbw[core] = dot(ntv[core, :, :, :, own].reshape(8 * 96, 256), gbc).astype(BF16).reshape(2, 4, 96, 256)
    crossb = net.start(dbw.at[net.other], gotb, "c")
    gnbc[...] = dot_nt(gbc, wv[...])
    norm_part = norm_part + jnp.sum(gnbc[...] * nv[own, :].astype(F32), axis=0, keepdims=True)
    held[...] = grads(cc)
    cross.arrived()
    held[...] += got[...]
    for ring in rings:
        ring.step1()
    crossb.arrived()
    heldb[...] = dbw[cc] + gotb[...]
    ring_bc.step1()
    for p, step in HALVES:
        out, part = block(net.near("z", step))
        norm_part = norm_part + part
        g2[p] = out.astype(BF16)
    token.step2()
    out, part = block(z)
    norm_part = (norm_part + part) / gain_row
    ownb[...] = out + gnbc[...]
    for k in range(4):
        small[32 + k : 33 + k, :] = norm_part[:, k * COLS : (k + 1) * COLS]
    sp1[cx] = small[...]
    q = net.around(sp1.at[cx], sp1.at[cx], "x")
    ring_bc.step2()
    v = xv[...].astype(F32)
    root = lax.rsqrt(jnp.mean(v * v, axis=1, keepdims=True) + EPS)
    arrive(q)
    sp2[y] = (sp1[0] + sp1[1]) + (sp1[2] + sp1[3])
    q = net.around(sp2.at[y], sp2.at[y], "y")
    ring_bc.step3(by.at[yh])
    qb = [net.start(by.at[yh], by.at[yh], "y", 2)]
    for ring in rings:
        ring.step2()
    arrive(q)
    sp3[cc] = (sp2[0] + sp2[1]) + (sp2[2] + sp2[3])
    q = [net.start(sp3.at[cc], sp3.at[cc], "c")]
    arrive(qb)
    bz[z, :, 0:128] = by[0]
    bz[z, :, 128:256] = by[1]
    qb = net.around(bz.at[z], bz.at[z], "z")
    arrive(q)
    small[...] = sp3[0] + sp3[1]
    sp0[z] = small[32:48, :]
    q = net.around(sp0.at[z], sp0.at[z], "z")
    small_out[0:32, :] = small[0:32, :]
    for ring in rings:
        ring.step3(inner_out)
    g = token.step3() + ownb[...]
    scaled = g * gain_row
    tokens_out[...] = ov[...].astype(F32) + root * scaled - v * (root * root * root) * jnp.mean(scaled * v, axis=1, keepdims=True)
    arrive(qb)
    bc_out[...] = (bz[0] + bz[1]) + (bz[2] + bz[3])
    arrive(q)
    small_out[32:48, :] = (sp0[0] + sp0[1]) + (sp0[2] + sp0[3])
    net.finish()


def run_tail(*args):
    bf = lambda *s: pltpu.VMEM(s, BF16)
    f32 = lambda *s: pltpu.VMEM(s, F32)
    return pl.pallas_call(
        tail_kernel,
        out_shape=[
            SHAPE((256, D), F32),
            SHAPE((96, COLS + 128), F32),
            SHAPE((96, 256), F32),
            SHAPE((48, COLS), F32),
        ],
        in_specs=[ANY] * 5 + [VMEM, ANY, ANY, VMEM, ANY, ANY, ANY, VMEM, VMEM],
        out_specs=[VMEM] * 4,
        scratch_shapes=[
            bf(LEN, WIDE),
            bf(LEN, MORE),
            bf(D, PROJ),
            bf(2, 2, 4, 96, LEN),
            bf(LEN, D),
            bf(LEN + 16, 256),
            bf(4, 272, 256),
            f32(272, 256),
            f32(256, 256),
            bf(D, 256),
            bf(256, D),
            bf(256, D),
            f32(272, 256),
            f32(256, D),
            f32(256, D),
            bf(2, 4, 96, MORE),
            bf(2, 4, 96, MORE),
            bf(2, 4, 96, MORE),
            bf(2, 2, 4, 96, 256),
            bf(2, 4, 96, 256),
            bf(2, 4, 96, 256),
            f32(48, COLS),
            f32(4, 16, COLS),
            f32(4, 48, COLS),
            f32(4, 48, COLS),
            f32(2, 48, COLS),
            f32(4, 96, 256),
            f32(2, 96, 128),
        ]
        + token_scratch()
        + grid_scratch("x", COLS + 128, 48)
        + grid_scratch("y", COLS + 128, 48)
        + grid_scratch("x", 128)
        + sems(64)
        + [pltpu.SemaphoreType.DMA((11,))],
        compiler_params=pltpu.CompilerParams(collective_id=3, has_side_effects=True, vmem_limit_bytes=ROOM),
        name="tail",
    )(*args)


def finish_kernel(tokens, branch, inner, bc, small, gate, wout, tokens_out, branch_out, inner_out, bc_out, gate_out, wout_out, step_out, norm, conv, bias, conv_bc, bias_bc, step_bias, decay, skip, gain, tv, rv, iv, cv, gv, wv, sem):
    trips = (
        (tokens, tv, tokens_out),
        (branch, rv, branch_out),
        (inner.at[:, pl.ds(0, COLS)], iv, inner_out),
        (bc, cv, bc_out),
        (gate, gv, gate_out),
        (wout, wv, wout_out),
    )
    reads = [pltpu.make_async_copy(src, via, sem.at[i]) for i, (src, via, dst) in enumerate(trips)]
    copies = [pltpu.make_async_copy(via, dst, sem.at[len(trips) + i]) for i, (src, via, dst) in enumerate(trips)]
    for copy in reads:
        copy.start()
    for read, copy in zip(reads, copies):
        read.wait()
        copy.start()
    step_out[...] = jnp.transpose(jnp.concatenate([inner[:, COLS:], jnp.zeros((32, 128), F32)], axis=0))[0:HEADS, 0:96]
    for k in range(4):
        norm[:, k * COLS : (k + 1) * COLS] = small[32 + k : 33 + k, :]
    conv_bc[...] = small[36:40, 0:256]
    bias_bc[...] = small[40:41, 0:256]
    mine = small[pl.ds(pl.multiple_of(lax.axis_index("yh") * 16, 8), 16), :]
    conv[...] = mine[0:4, :]
    bias[...] = mine[4:5, :]
    gain[...] = mine[5:6, :]
    step_bias[...] = mine[6:7, 0:HEADS]
    decay[...] = mine[7:8, 0:HEADS]
    skip[...] = mine[8:9, 0:HEADS]
    for copy in copies:
        copy.wait()


def run_finish(*args):
    f32 = lambda *s: SHAPE(s, F32)
    return pl.pallas_call(
        finish_kernel,
        out_shape=[
            f32(256, D),
            SHAPE((256, D), BF16),
            f32(96, COLS),
            f32(96, 256),
            f32(96, COLS),
            f32(96, COLS),
            f32(HEADS, 96),
            f32(1, D),
            f32(4, COLS),
            f32(1, COLS),
            f32(4, 256),
            f32(1, 256),
            f32(1, HEADS),
            f32(1, HEADS),
            f32(1, HEADS),
            f32(1, COLS),
        ],
        in_specs=[ANY, ANY, VMEM, ANY, VMEM, ANY, ANY],
        out_specs=[ANY] * 6 + [VMEM] * 10,
        scratch_shapes=[
            pltpu.VMEM((256, D), F32),
            pltpu.VMEM((256, D), BF16),
            pltpu.VMEM((96, COLS), F32),
            pltpu.VMEM((96, 256), F32),
            pltpu.VMEM((96, COLS), F32),
            pltpu.VMEM((96, COLS), F32),
            pltpu.SemaphoreType.DMA((12,)),
        ],
        compiler_params=pltpu.CompilerParams(vmem_limit_bytes=ROOM),
        name="finish",
    )(*args)


def shards(tokens, norm_gain, w_gate, w_inner, w_bc, w_step, conv_inner, bias_inner, conv_bc, bias_bc, step_bias, decay_log, skip_gain, gate_gain, w_out, cotangent):
    normed, wx, wout, wbc, prm = run_gather(
        tokens, norm_gain, w_gate, w_inner, w_out, w_bc, w_step.T, conv_inner, bias_inner, gate_gain, step_bias, decay_log, skip_gain
    )
    wx, wout, wbc = wx.reshape(D, PROJ), wout.reshape(D, WIDE), wbc.reshape(D, 256)
    inner, zin, y, hin, dt, r, u, bc, bc_in, zbc, normed_t, gains, mixed, gs, gg, cot_t = run_forward(
        normed, wx, wout, wbc, prm, conv_bc, bias_bc.reshape(1, 256), cotangent
    )
    cat, dbc, acc, output, wout_grad, gate_grad = run_backward(
        gs, inner, zin, y, hin, prm, bc, dt, r, u, gains, mixed, wout, cot_t, gg, normed_t, tokens
    )
    tokens_grad, inner_grad, bc_grad, small = run_tail(
        gg, cat, wx, normed_t, normed, dbc, zbc, bc_in, acc, wbc, tokens, cotangent, norm_gain, conv_bc
    )
    (
        tokens_grad, output, inner_grad, bc_grad, gate_grad, wout_grad, step_grad,
        norm, conv, bias, conv_bc_grad, bias_bc_grad, step_bias_grad, decay, skip, gate_gain_grad,
    ) = run_finish(tokens_grad, output, inner_grad, bc_grad, small, gate_grad, wout_grad)
    flat = lambda v: v.reshape(-1)
    return (
        output, tokens_grad, flat(norm), gate_grad, inner_grad, bc_grad, step_grad.T, conv, flat(bias), conv_bc_grad,
        flat(bias_bc_grad), flat(step_bias_grad), flat(decay), flat(skip), flat(gate_gain_grad), wout_grad,
    )


def solution(mesh):
    fine = Mesh(mesh.devices.reshape(2, 4, 2, 2, 4), AXES)
    dp, tensor = ("yl", "x", "c"), ("yh", "z")
    tokens, weight = P(dp + tensor, None), P(dp, tensor)
    heads, shared = P(tensor), P()
    return jax.shard_map(
        shards,
        mesh=fine,
        in_specs=(
            tokens, shared, weight, weight, P(dp, None), weight, P(None, tensor), heads,
            shared, shared, heads, heads, heads, heads, weight, tokens,
        ),
        out_specs=(
            tokens, tokens, shared, weight, weight, P(dp, None), weight, P(None, tensor), heads,
            shared, shared, heads, heads, heads, heads, weight,
        ),
        check_vma=False,
    )
```

```python
import jax
import jax.numpy as jnp
from jax import lax
from jax.experimental import pallas as pl
from jax.experimental.pallas import tpu as pltpu
from jax.sharding import Mesh
from jax.sharding import PartitionSpec as P

D = 1536
LEN = 1024
INNER = 3072
STATE = 128
BLOCK = 256
BLOCKS = LEN // BLOCK
GROUPS = 2
HEADS = 6
COLS = HEADS * 64
WIDE = GROUPS * COLS
STEPS = 2 * WIDE
PROJ = STEPS + GROUPS * 128
MORE = PROJ - WIDE
LOG2E = 1.4426950408889634
EPS = 1e-05
F32 = jnp.float32
BF16 = jnp.bfloat16
MESH = pl.DeviceIdType.MESH
AXES = ("yl", "x", "c", "yh", "z")
ANY = pl.BlockSpec(memory_space=pl.ANY)
VMEM = pl.BlockSpec(memory_space=pltpu.VMEM)
SHAPE = jax.ShapeDtypeStruct
ROOM = 60 * 2**20


def dot(a, b):
    return jnp.dot(a, b, preferred_element_type=F32)


def dot_nt(a, b):
    return lax.dot_general(a, b, (((1,), (1,)), ((), ())), preferred_element_type=F32)


def dot_tn(a, b):
    return lax.dot_general(a, b, (((0,), (0,)), ((), ())), preferred_element_type=F32)


def pieces(v, n):
    out = []
    for _ in range(n):
        hi = v.astype(BF16)
        out.append(hi)
        v = v - hi.astype(F32)
    return out


def dot_left(v, ones, n):
    return sum(dot(p, ones) for p in pieces(v, n))


def spread(v, ones):
    hi = v.astype(BF16).astype(F32)
    low = pltpu.roll(v - hi, 64, 1)
    return dot(jnp.where(iota(v.shape, 1) < 64, hi, low).astype(BF16), ones)


def folded(v, ones):
    hi = v.astype(BF16)
    low = (v - hi.astype(F32)).astype(BF16)
    return dot(hi, ones) + dot(low, ones)


def dot_right(ones, v, n):
    return sum(dot(ones, p) for p in pieces(v, n))


def iota(shape, axis):
    return lax.broadcasted_iota(jnp.int32, shape, axis)


def expander():
    row, col = iota((128, COLS), 0), iota((128, COLS), 1)
    return ((row & 63) == lax.shift_right_logical(col, 6)).astype(BF16)


def reducer():
    row, col = iota((COLS, 128), 0), iota((COLS, 128), 1)
    return (col == lax.shift_right_logical(row, 6)).astype(BF16)


def sigmoid(v):
    return 0.5 * jnp.tanh(0.5 * v) + 0.5


def lower(strict=False):
    row, col = iota((BLOCK, BLOCK), 0), iota((BLOCK, BLOCK), 1)
    return ((row > col) if strict else (row >= col)).astype(BF16)


def upper():
    return (iota((BLOCK, BLOCK), 0) <= iota((BLOCK, BLOCK), 1)).astype(BF16)


def token_row(v):
    v = sum(v[:, 128 * i : 128 * (i + 1)] for i in range(v.shape[1] // 128))
    ones = jnp.ones((8, 128), BF16)
    return sum(dot_nt(ones, p) for p in pieces(v, 3))[0:1, :]


class Net:
    def __init__(self, send, recv):
        self.send, self.recv, self.copies = send, recv, []
        self.at = {name: lax.axis_index(name) for name in AXES}
        self.at["y"] = self.at["yh"] * 2 + self.at["yl"]
        self.places = {(a, s): lax.rem(self.at[a] + s + 4, 4) for a in ("x", "y", "z") for s in (1, -1, 2)}
        self.other = 1 - self.at["c"]
        self.targets = {("c", 1): {"c": self.other}}
        for (a, s), place in self.places.items():
            self.targets[a, s] = {"yh": place // 2, "yl": lax.rem(place, 2)} if a == "y" else {a: place}

    def near(self, axis, step):
        return self.places[axis, step]

    def plan(self, src, dst, axis, step=1):
        copy = Copy(self, len(self.copies), src, dst, self.targets[axis, step])
        self.copies.append(copy)
        return copy

    def start(self, src, dst, axis, step=1):
        return self.plan(lambda: src, lambda: dst, axis, step).start()

    def around(self, src, dst, axis):
        return [self.start(src, dst, axis, step) for step in (1, -1, 2)]

    def barrier(self, peers):
        here = pltpu.get_barrier_semaphore()
        for peer in peers:
            pl.semaphore_signal(here, inc=1, device_id=self.targets[peer], device_id_type=MESH)
        pl.semaphore_wait(here, len(peers))

    def finish(self):
        for copy in self.copies:
            copy.arrived()
        for copy in self.copies:
            copy.left()


class Copy:
    def __init__(self, net, index, src, dst, target):
        self.net, self.index, self.src, self.dst, self.target = net, index, src, dst, target
        self.here, self.gone = False, False

    def made(self):
        return pltpu.make_async_remote_copy(
            src_ref=self.src(),
            dst_ref=self.dst(),
            send_sem=self.net.send.at[self.index],
            recv_sem=self.net.recv.at[self.index],
            device_id=self.target,
            device_id_type=MESH,
        )

    def start(self):
        self.made().start()
        return self

    def arrived(self):
        if not self.here:
            self.here = True
            self.made().wait_recv()

    def left(self):
        if not self.gone:
            self.gone = True
            self.made().wait_send()


def sems(n):
    return [pltpu.SemaphoreType.DMA((n,)), pltpu.SemaphoreType.DMA((n,))]


def rows(ref, first, count):
    return ref.at[pl.ds(pl.multiple_of(first, 16), count)]


def lanes(first, count):
    return pl.ds(pl.multiple_of(first, 128), count)


def arrive(copies):
    for copy in copies:
        copy.arrived()


HALVES = ((0, 1), (1, -1))


class GridSum:
    def __init__(self, net, first, held, spans, scratch, cut=(0, 96)):
        self.net, self.first, self.held, self.spans = net, first, held, spans
        self.land, self.mid, self.last = scratch
        self.rows = pl.ds(*cut)
        self.one, self.two = [], []
        for slot, step in enumerate((2, 1, -1)):
            if first == "x":
                self.plan(self.one, lambda step=step: held.at[:, net.near("x", step), self.rows], lambda slot=slot: self.land.at[slot], "x", step)
            else:
                self.plan(self.two, lambda step=step: self.mid.at[net.near("x", step)], lambda slot=slot: self.last.at[slot], "x", step)
            lane = 0
            for base, n in spans:
                there = lambda step=step, base=base, n=n: lanes(base + (net.near("y", step) // 2) * n, n)
                if first == "x":
                    src = lambda step=step, there=there: self.mid.at[lax.rem(net.near("y", step), 2), :, there()]
                    self.plan(self.two, src, lambda slot=slot, lane=lane, n=n: self.last.at[slot, :, pl.ds(lane, n)], "y", step)
                else:
                    src = lambda step=step, there=there: held.at[lax.rem(net.near("y", step), 2), :, self.rows, there()]
                    self.plan(self.one, src, lambda slot=slot, lane=lane, n=n: self.land.at[slot, :, :, pl.ds(lane, n)], "y", step)
                lane += n

    def plan(self, to, src, dst, axis, step):
        to.append(self.net.plan(src, dst, axis, step))

    def step1(self):
        for copy in self.one:
            copy.start()

    def step2(self):
        arrive(self.one)
        at = self.net.at
        if self.first == "x":
            self.mid[...] = self.total(self.held[:, at["x"], self.rows], self.land, slice(None)).astype(BF16)
        else:
            lane = 0
            for base, n in self.spans:
                cut = slice(lane, lane + n)
                own = self.held[at["yl"], :, self.rows, lanes(base + at["yh"] * n, n)]
                self.mid[:, :, cut] = self.total(own, self.land, cut).astype(BF16)
                lane += n
        for copy in self.two:
            copy.start()

    def total(self, own, others, cut):
        return (own.astype(F32) + others[0, ..., cut].astype(F32)) + (others[1, ..., cut].astype(F32) + others[2, ..., cut].astype(F32))

    def step3(self, out):
        arrive(self.two)
        at = self.net.at
        if self.first == "y":
            out[self.rows, :] = self.total(self.mid[at["x"]], self.last, slice(None))
            return
        lane = 0
        for base, n in self.spans:
            cut = slice(lane, lane + n)
            out[self.rows, cut] = self.total(self.mid[at["yl"], :, lanes(base + at["yh"] * n, n)], self.last, cut)
            lane += n


def grid_scratch(first, width, count=96):
    blocks, wide = (2, 2 * width) if first == "x" else (4, width)
    return [pltpu.VMEM(s, BF16) for s in ((3, blocks, count, wide), (blocks, count, wide), (3, count, width))]


class TokenSum:
    def __init__(self, net, scratch):
        self.net, self.far, self.half, self.fold, self.whole = net, *scratch
        self.one = [
            net.plan(lambda p=p: self.far.at[pl.ds(128 * p, 128)], lambda p=p: self.half.at[p], "z", step) for p, step in HALVES
        ]
        self.two = [net.plan(lambda p=p: self.fold.at[p], lambda p=p: self.whole.at[p], "z", step) for p, step in HALVES]

    def step1(self):
        for copy in self.one:
            copy.start()

    def step2(self):
        arrive(self.one)
        for p, _ in HALVES:
            self.fold[p, 128 * p : 128 * p + 128, :] += self.half[p]
            self.two[p].start()

    def step3(self):
        arrive(self.two)
        return self.whole[0].astype(F32) + self.whole[1].astype(F32)


def token_scratch():
    return [pltpu.VMEM((256, D), BF16), pltpu.VMEM((2, 128, D), BF16), pltpu.VMEM((2, 256, D), BF16), pltpu.VMEM((2, 256, D), BF16)]


def front_kernel(
    x, gain, w_gate, w_inner, w_out, w_bc, w_step, conv, bias, gate_gain, step_bias, decay_log, skip_gain, conv_bc, bias_bc, cot,
    inner_out, z_out, y_out, h_out, dt_out, r_out, u_out, bc_out, bcin_out, zbc_out, normed_t, gains_out,
    mixed_out, gs_out, gg_out, cot_t, normed_out, wx_out, wout_out, wbc_out, prm_out,
    normed, wx, wout, wbc, prm, xv, stepv, stept, pk,
    cots, gps, acts, slopes, gms, mixed, gg, turned_c, ext, extbc, state, stat, slots, send, recv, local,
):
    i = pl.program_id(0)
    net = Net(send, recv)
    at = net.at
    yh, cx, cc, z, y = at["yh"], at["x"], at["c"], at["z"], at["y"]
    own_rows = lambda ref: rows(ref, z * 256, 256)
    order = ((0, 1), (1, -1), (1, 1), (0, -1))
    part = lambda ref, p, s: rows(ref, net.near("z", -s) * 256 + 128 * p, 128)
    c1 = [
        net.plan(lambda p=p: cot.at[pl.ds(128 * p, 128)], lambda p=p: rows(cots, z * 256 + 128 * p, 128), "z", s) for p, s in order
    ]
    c2 = [net.plan(lambda p=p, s=s: part(cots, p, s), lambda p=p, s=s: part(cots, p, s), "z", s) for p, s in HALVES]
    q = [net.plan(lambda: stat, lambda: slots.at[z], "z", step) for step in (1, -1, 2)]
    spot_o = lambda xx, cut=pl.ds(0, 96): wout.at[at["yl"], xx, cc, cut, lanes(yh * COLS, COLS)]
    line_o = lambda yy, cut=pl.ds(0, 96): wout.at[lax.rem(yy, 2), :, cc, cut, lanes((yy // 2) * COLS, COLS)]
    same = lambda ref, axis, step=1: net.plan(ref, ref, axis, step)
    o1 = [net.plan(lambda: w_out, lambda: spot_o(cx), "x", step) for _, step in HALVES]
    o2 = [same(lambda p=p, s=s: spot_o(net.near("x", -s), pl.ds(48 * p, 48)), "x", s) for p, s in HALVES]
    o3 = [same(lambda: line_o(y), "y", step) for _, step in HALVES]
    o4 = [same(lambda p=p, s=s: line_o(net.near("y", -s), pl.ds(48 * p, 48)), "y", s) for p, s in HALVES]
    oc = [same(lambda: line_o(y), "c")] + [same(lambda s=s: line_o(net.near("y", s)), "c") for s in (1, -1, 2)]
    own = lambda: pltpu.make_async_copy(cot, own_rows(cots), local.at[0])
    pairs = ((normed, normed_out), (wx, wx_out), (wbc, wbc_out), (prm, prm_out), (wout, wout_out), (turned_c, cot_t))
    leave = lambda n: pltpu.make_async_copy(*pairs[n], local.at[1 + n])

    @pl.when(i == 0)
    def _():
        load = pltpu.make_async_copy(x, xv, local.at[7])
        load.start()
        own().start()
        stept[...] = jnp.zeros_like(stept)
        stept[0:HEADS, 0:96] = w_step[...].astype(F32)
        stepv[...] = jnp.transpose(stept[...])[0:96, :].astype(BF16)
        pk[...] = jnp.zeros_like(pk)
        pk[0:4, :] = conv[...]
        pk[4:5, :] = bias[...].reshape(1, COLS)
        pk[5:6, :] = gate_gain[...].reshape(1, COLS)
        pk[6:7, 0:HEADS] = step_bias[...].reshape(1, HEADS)
        pk[7:8, 0:HEADS] = decay_log[...].reshape(1, HEADS)
        pk[8:9, 0:HEADS] = skip_gain[...].reshape(1, HEADS)
        net.barrier([("z", 1), ("z", -1), ("z", 2), ("x", 1), ("x", -1), ("y", 1), ("y", -1), ("y", 2), ("c", 1)])
        first = {
            "x": ((w_gate, wx, 0, COLS), (w_bc.at[:, lanes(yh * 128, 128)], wbc, 0, 128)),
            "y": ((w_inner, wx, WIDE, COLS), (stepv, wx, STEPS, 128)),
        }
        then = {"x": "y", "y": "x"}
        done = []

        def go(src, dst, axis, step=1):
            done.append(net.start(src, dst, axis, step))
            return done[-1]

        def spot(ref, base, n, yy, xx, cut=pl.ds(0, 96)):
            return ref.at[lax.rem(yy, 2), xx, cc, cut, lanes(base + (yy // 2) * n, n)]

        def line(axis, ref, base, n, place, cut=pl.ds(0, 96)):
            if axis == "x":
                return ref.at[lax.rem(place, 2), :, cc, cut, lanes(base + (place // 2) * n, n)]
            return ref.at[:, place, cc, cut, lanes(base, 2 * n)]

        sent = {"x": [], "y": []}
        for axis in ("x", "y"):
            for src, ref, base, n in first[axis]:
                sent[axis].append([go(src, spot(ref, base, n, y, cx), axis, step) for _, step in HALVES])
        load.wait()
        v = xv[...].astype(F32)
        root = lax.rsqrt(jnp.mean(v * v, axis=1, keepdims=True) + EPS)
        normed[pl.ds(pl.multiple_of(z * 256, 256), 256), :] = (v * root * gain[...].reshape(1, D)).astype(BF16)
        zs = {}
        for p, s in order:
            here = rows(normed, z * 256 + 128 * p, 128)
            zs[p, s] = go(here, here, "z", s)
        mine = [
            pltpu.make_async_copy(src, spot(ref, base, n, y, cx), local.at[8 + k])
            for k, (src, ref, base, n) in enumerate(first["x"] + first["y"])
        ]
        mine.append(pltpu.make_async_copy(pk, prm.at[yh], local.at[12]))
        mine.append(pltpu.make_async_copy(w_out, spot_o(cx), local.at[13]))
        for copy in mine:
            copy.start()
        for copy in o1:
            copy.start()
        for axis in ("x", "y"):
            for src, ref, base, n in first[axis]:
                go(src, spot(ref, base, n, y, cx), "c")
        go(pk, prm.at[yh], "y", 2)
        second = {"x": [], "y": []}
        for axis in ("x", "y"):
            for (src, ref, base, n), copies in zip(first[axis], sent[axis]):
                for (p, s), copy in zip(HALVES, copies):
                    copy.arrived()
                    cut = pl.ds(48 * p, 48)
                    here = spot(ref, base, n, y, net.near("x", -s), cut) if axis == "x" else spot(ref, base, n, net.near("y", -s), cx, cut)
                    second[axis].append(go(here, here, axis, s))
        for copy in mine:
            copy.wait()
        third = {"x": [], "y": []}
        for axis in ("x", "y"):
            arrive(second[axis])
            for src, ref, base, n in first[axis]:
                here = line(axis, ref, base, n, at[then[axis]])
                third[axis].append([go(here, here, then[axis], s) for _, s in HALVES])
        for copy, start in zip(o1, o2):
            copy.arrived()
            start.start()
        for axis in ("x", "y"):
            for src, ref, base, n in first[axis]:
                for s in (1, -1, 2):
                    here = spot(ref, base, n, y, net.near("x", s)) if axis == "x" else spot(ref, base, n, net.near("y", s), cx)
                    go(here, here, "c")
        for p, s in HALVES:
            zs[p, s].arrived()
            here = part(normed, p, s)
            go(here, here, "z", s)
        for copy in c1:
            copy.start()
        fourth = {"x": [], "y": []}
        for axis in ("x", "y"):
            for (src, ref, base, n), copies in zip(first[axis], third[axis]):
                for (p, s), copy in zip(HALVES, copies):
                    copy.arrived()
                    place = net.near(then[axis], -s)
                    here = line(axis, ref, base, n, place, pl.ds(48 * p, 48))
                    fourth[axis].append(go(here, here, then[axis], s))
                    here = line(axis, ref, base, n, place)
                    go(here, here, "c")
        arrive(o2)
        for copy in o3:
            copy.start()
        for axis in ("x", "y"):
            arrive(fourth[axis])
            for src, ref, base, n in first[axis]:
                here = line(axis, ref, base, n, net.near(then[axis], 2))
                go(here, here, "c")
        for copy in done:
            copy.arrived()
        for copy in done:
            copy.left()
        for n in range(4):
            leave(n).start()
        ext[0:8, :] = jnp.zeros((8, WIDE), F32)
        extbc[0:8, :] = jnp.zeros((8, 256), F32)
        state[...] = jnp.zeros_like(state)

    @pl.when((i > 0) & (i < BLOCKS))
    def _():
        ext[0:8, :] = ext[BLOCK : BLOCK + 8, :]
        extbc[0:8, :] = extbc[BLOCK : BLOCK + 8, :]

    @pl.when(i == 2)
    def _():
        for copy, start in zip(c1[:2], c2):
            copy.arrived()
            start.start()
        for copy, start in zip(o3, o4):
            copy.arrived()
            start.start()
        for copy in oc[:3]:
            copy.start()

    @pl.when(i < BLOCKS)
    def _():
        xb = normed[pl.ds(pl.multiple_of(i * BLOCK, BLOCK), BLOCK), :]
        turned = jnp.transpose(xb).reshape(2, 4, 2, 96, BLOCK)
        for core in range(2):
            normed_t[core] = turned[:, :, core]
        bc_in = dot(xb, wbc[...].reshape(D, 256))
        bcin_out[...] = bc_in
        extbc[8 : BLOCK + 8, :] = bc_in
        zb = bias_bc[...].reshape(1, 256) + sum(conv_bc[j : j + 1, :] * extbc[5 + j : 5 + j + BLOCK, :] for j in range(4))
        zbc_out[...] = zb
        bc = (zb * sigmoid(zb)).astype(BF16)
        bc_out[...] = bc
        b, c = bc[:, :STATE], bc[:, STATE:]
        scores = jnp.where(iota((BLOCK, BLOCK), 0) >= iota((BLOCK, BLOCK), 1), dot_nt(c, b), 0.0)
        tri, ones = lower(), expander()
        left = iota((BLOCK, 128), 1) < 64
        weight = lambda first, n: wx[:, :, :, :, first : first + n].reshape(D, n)
        steps = dot(xb, weight(STEPS, 256))
        total = jnp.zeros((BLOCK, 128), F32)
        for g in range(GROUPS):
            if g == 1:

                @pl.when(i == BLOCKS - 1)
                def _():
                    arrive(o4)
                    oc[3].start()

            cut = slice(g * COLS, (g + 1) * COLS)
            u = steps[:, 128 * g : 128 * (g + 1)] + prm[g, 6:7, 0:128]
            dt = jnp.maximum(u, 0.0) + jnp.log(1.0 + jnp.exp(-jnp.abs(u)))
            rate = -jnp.exp(prm[g, 7:8, 0:128]) * LOG2E
            r = dot_right(tri, dt * rate, 3)
            u_out[g] = u
            dt_out[g] = dt
            r_out[g] = r
            rt = jnp.transpose(r)
            gate = dot(xb, weight(g * COLS, COLS))
            inner = dot(xb, weight(WIDE + g * COLS, COLS))
            inner_out[:, cut] = inner
            ext[8 : BLOCK + 8, cut] = inner
            zv = prm[g, 4:5, :] + sum(prm[g, j : j + 1, :] * ext[5 + j : 5 + j + BLOCK, cut] for j in range(4))
            z_out[:, cut] = zv
            xv = zv * sigmoid(zv)
            last = r[BLOCK - 1 : BLOCK, :]
            w = xv * spread(dt, ones)
            grow = spread(jnp.exp2(r), ones)
            tail = spread(jnp.exp2(last - r), ones)
            skip = spread(prm[g, 8:16, 0:128], ones)[0:1, :]
            wl = w.astype(BF16)
            h = state[:, cut]
            h_out[0, g] = h
            parts = []
            for p in range(HEADS // 2):
                halves = []
                for n in (2 * p, 2 * p + 1):
                    gap = jnp.minimum(r[:, n : n + 1] - rt[n : n + 1, :], 0.0)
                    halves.append(dot((scores * jnp.exp2(gap)).astype(BF16), wl[:, 128 * p : 128 * (p + 1)]))
                parts.append(jnp.where(left, halves[0], halves[1]))
            yv = jnp.concatenate(parts, axis=1) + grow * dot(c, h.astype(BF16)) + skip * xv
            y_out[:, cut] = yv
            state[:, cut] = grow[BLOCK - 1 : BLOCK, :] * h + dot_tn(b, (tail * w).astype(BF16))
            sig = sigmoid(gate)
            act = gate * sig
            gp = yv * act
            here_now = pl.ds(pl.multiple_of(i * BLOCK, BLOCK), BLOCK)
            gps[here_now, cut] = gp
            acts[here_now, cut] = act
            slopes[here_now, cut] = yv * (sig + act * (1.0 - sig))
            sq = gp * gp
            total = total + (sq[:, 0:128] + sq[:, 128:256] + sq[:, 256:384])
        stat[pl.ds(i, 1), :] = token_row(total)

    @pl.when(i == BLOCKS)
    def _():
        own().wait()
        arrive(oc)
        leave(4).start()

    @pl.when(i == BLOCKS + 1)
    def _():
        arrive(c1)

    @pl.when(i == 2 * BLOCKS - 1)
    def _():
        for copy in c2:
            copy.arrived()

    @pl.when(i >= BLOCKS)
    def _():
        t = i - BLOCKS
        block = lax.rem(z + t + lax.div(t, 2) - 2 * lax.div(t, 3), 4)
        at = pl.ds(pl.multiple_of(block * BLOCK, BLOCK), BLOCK)
        cb = cots[at, :]
        turned = jnp.transpose(cb).reshape(2, 4, 2, 96, BLOCK)
        for core in range(2):
            turned_c[core, :, :, :, at] = turned[:, :, core]
        gm = dot(cb, wout[...].reshape(D, WIDE))
        gms[at, :] = gm
        gain = jnp.concatenate([prm[0, 5:6, :], prm[1, 5:6, :]], axis=1)
        stat[pl.ds(BLOCKS + block, 1), :] = token_row(gm * gain * gps[at, :])

    @pl.when(i == 2 * BLOCKS - 1)
    def _():
        for copy in q:
            copy.start()
        slots[z] = stat[...]
        for copy in q:
            copy.arrived()
            copy.left()
        sums = (slots[0] + slots[1]) + (slots[2] + slots[3])
        root = lax.rsqrt(sums[0:4, :] * (1.0 / INNER) + EPS)
        stat[0:4, :] = root
        stat[4:8, :] = root * root * root * (sums[4:8, :] * (1.0 / INNER))
        columns = jnp.transpose(stat[...])
        gain = jnp.concatenate([prm[0, 5:6, :], prm[1, 5:6, :]], axis=1)
        leave(5).start()
        gain_grad = jnp.zeros((1, WIDE), F32)
        moved = []
        for k in range(BLOCKS):
            at = slice(k * BLOCK, (k + 1) * BLOCK)
            gp, gm = gps[at, :], gms[at, :]
            normal = gp * columns[:, k : k + 1]
            gain_grad = gain_grad + jnp.sum(gm * normal, axis=0, keepdims=True)
            mixed[at, :] = (normal * gain).astype(BF16)
            gated = (gm * gain) * columns[:, k : k + 1] - gp * columns[:, BLOCKS + k : BLOCKS + k + 1]
            gms[at, :] = gated * acts[at, :]
            gg[at, :] = (gated * slopes[at, :]).astype(BF16)
            block = pl.ds(k * BLOCK, BLOCK)
            for src, dst in ((mixed, mixed_out), (gms, gs_out), (gg, gg_out)):
                moved.append(pltpu.make_async_copy(src.at[block], dst.at[block], local.at[14 + len(moved)]))
                moved[-1].start()
        gains_out[...] = jnp.concatenate([gain_grad, jnp.zeros((7, WIDE), F32)], axis=0)
        for copy in c1 + c2 + q + o1 + o2 + o3 + o4 + oc:
            copy.left()
        for copy in moved:
            copy.wait()
        for n in range(len(pairs)):
            leave(n).wait()


def run_front(*args):
    first = lambda k: jnp.minimum(k, BLOCKS - 1)
    keep = lambda *s: pl.BlockSpec(s, lambda k: (0,) * len(s))
    block = lambda n: pl.BlockSpec((BLOCK, n), lambda k: (first(k), 0))
    small = lambda: pl.BlockSpec((GROUPS, BLOCK, 128), lambda k: (0, first(k), 0))
    wide = SHAPE((LEN, WIDE), F32)
    narrow = SHAPE((GROUPS, LEN, 128), F32)
    bf = lambda *s: pltpu.VMEM(s, BF16)
    f32 = lambda *s: pltpu.VMEM(s, F32)
    return pl.pallas_call(
        front_kernel,
        grid=(2 * BLOCKS,),
        out_shape=[
            wide,
            wide,
            wide,
            SHAPE((BLOCKS, GROUPS, STATE, COLS), F32),
            narrow,
            narrow,
            narrow,
            SHAPE((LEN, 256), BF16),
            SHAPE((LEN, 256), F32),
            SHAPE((LEN, 256), F32),
            SHAPE((2, 2, 4, 96, LEN), BF16),
            SHAPE((8, WIDE), F32),
            SHAPE((LEN, WIDE), BF16),
            wide,
            SHAPE((LEN, WIDE), BF16),
            SHAPE((2, 2, 4, 96, LEN), BF16),
            SHAPE((LEN, D), BF16),
            SHAPE((2, 4, 2, 96, PROJ), BF16),
            SHAPE((2, 4, 2, 96, WIDE), BF16),
            SHAPE((2, 4, 2, 96, 256), BF16),
            SHAPE((GROUPS, 16, COLS), F32),
        ],
        in_specs=[ANY, VMEM, ANY, ANY, ANY, ANY] + [VMEM] * 9 + [ANY],
        out_specs=[
            block(WIDE),
            block(WIDE),
            block(WIDE),
            pl.BlockSpec((1, GROUPS, STATE, COLS), lambda k: (first(k), 0, 0, 0)),
            small(),
            small(),
            small(),
            block(256),
            block(256),
            block(256),
            pl.BlockSpec((2, 2, 4, 96, BLOCK), lambda k: (0, 0, 0, 0, first(k))),
            keep(8, WIDE),
        ]
        + [ANY] * 9,
        scratch_shapes=[
            bf(LEN, D),
            bf(2, 4, 2, 96, PROJ),
            bf(2, 4, 2, 96, WIDE),
            bf(2, 4, 2, 96, 256),
            f32(GROUPS, 16, COLS),
            bf(256, D),
            bf(96, 128),
            f32(128, 128),
            f32(16, COLS),
            bf(LEN, D),
            f32(LEN, WIDE),
            f32(LEN, WIDE),
            f32(LEN, WIDE),
            f32(LEN, WIDE),
            bf(LEN, WIDE),
            bf(LEN, WIDE),
            bf(2, 2, 4, 96, LEN),
            f32(BLOCK + 8, WIDE),
            f32(BLOCK + 8, 256),
            f32(STATE, WIDE),
            f32(8, BLOCK),
            f32(4, 8, BLOCK),
        ]
        + sems(96)
        + [pltpu.SemaphoreType.DMA((26,))],
        compiler_params=pltpu.CompilerParams(collective_id=1, has_side_effects=True, vmem_limit_bytes=ROOM),
        name="front",
    )(*args)


def backward_kernel(
    gs_in, inner, zin, y, hin, prm, bc, dt, r, u, gains, mixed, wout, cot_t, gg, normed_t, tokens,
    cat_out, dbc_out, acc, branch_out, wout_out, wgate_out,
    ext, dstate, dst, dbc, held, got, away, mv, wv, cv, gv, nv, ownb, g0, g1, g2, g3, s1, s2, s3, t1, t2, t3, send, recv, local,
):
    k = pl.program_id(0)
    net = Net(send, recv)
    cc, z = net.at["c"], net.at["z"]
    cross = [net.plan(lambda n=n: away.at[n], lambda n=n: got.at[n], "c") for n in range(2)]
    token = TokenSum(net, (g0, g1, g2, g3))
    rings = (GridSum(net, "y", held.at[0], ((0, COLS),), (s1, s2, s3)), GridSum(net, "x", held.at[1], ((0, COLS),), (t1, t2, t3)))

    @pl.when(k == 0)
    def _():
        loads = [pltpu.make_async_copy(src, dst, local.at[n]) for n, (src, dst) in enumerate(((mixed, mv), (wout, wv), (cot_t, cv), (gg, gv), (normed_t, nv)))]
        for copy in loads:
            copy.start()
        net.barrier([("z", 1), ("z", -1)] + [(a, s) for a in ("x", "y") for s in (1, -1, 2)] + [("c", 1)])
        loads[0].wait()
        loads[1].wait()
        branch = lambda place: dot_nt(mv[pl.ds(pl.multiple_of(place * 256, 256), 256), :], wv[...])
        grads = lambda left, right, core: dot(left[core].reshape(8 * 96, LEN), right[...]).astype(BF16).reshape(2, 4, 96, WIDE)
        g0[...] = branch(net.near("z", 2)).astype(BF16)
        token.step1()
        loads[2].wait()
        away[0] = grads(cv, mv, net.other)
        cross[0].start()
        loads[3].wait()
        loads[4].wait()
        away[1] = grads(nv, gv, net.other)
        cross[1].start()
        g2[0] = branch(net.near("z", 1)).astype(BF16)
        g2[1] = branch(net.near("z", -1)).astype(BF16)
        ownb[...] = branch(z)
        held[0] = grads(cv, mv, cc)
        held[1] = grads(nv, gv, cc)
        acc[...] = jnp.zeros_like(acc)
        for g in range(GROUPS):
            acc[g, 5:6, :] = gains[0:1, g * COLS : (g + 1) * COLS]
        ext[BLOCK : BLOCK + 8, :] = jnp.zeros((8, WIDE), F32)
        dstate[...] = jnp.zeros_like(dstate)

    @pl.when(k > 0)
    def _():
        ext[BLOCK : BLOCK + 8, :] = ext[0:8, :]

    b, c = bc[:, :STATE], bc[:, STATE:]
    valid = iota((BLOCK, BLOCK), 1) >= iota((BLOCK, BLOCK), 0)
    scores = jnp.where(valid, dot_nt(b, c), 0.0)
    ones, fold = expander(), reducer()
    left = iota((BLOCK, 128), 1) < 64
    suffix, prefix = upper(), lower(strict=True)
    dst[...] = jnp.zeros_like(dst)
    dbc[...] = jnp.zeros_like(dbc)
    for g in range(GROUPS):
        if g == 0:

            @pl.when(k == 1)
            def _():
                token.step2()

            @pl.when(k == 3)
            def _():
                for ring in rings:
                    ring.step2()

        else:

            @pl.when(k == 0)
            def _():
                for n in range(2):
                    cross[n].arrived()
                    held[n] += got[n]
                    rings[n].step1()

        cut = slice(g * COLS, (g + 1) * COLS)
        yv = y[:, cut]
        gs = gs_in[:, cut]
        xi = inner[:, cut]
        zv = zin[:, cut]
        zs = sigmoid(zv)
        xv = zv * zs
        rv = r[g]
        rt = jnp.transpose(rv)
        last = rv[BLOCK - 1 : BLOCK, :]
        dte = spread(dt[g], ones)
        grow = spread(jnp.exp2(rv), ones)
        tail = spread(jnp.exp2(last - rv), ones)
        skip = spread(prm[g, 8:16, 0:128], ones)[0:1, :]
        w = xv * dte
        wl = w.astype(BF16)
        gl = gs.astype(BF16)
        h = hin[0, g]
        dh = dstate[:, cut]
        dhl = dh.astype(BF16)
        parts = []
        for p in range(HEADS // 2):
            halves = []
            pair = slice(128 * p, 128 * (p + 1))
            wp, gpair = wl[:, pair], gl[:, pair]
            zero = jnp.zeros_like(wp)
            w_low = pltpu.roll(w[:, pair] - wp.astype(F32), 64, 1).astype(BF16)
            g_low = (gs[:, pair] - gpair.astype(F32)).astype(BF16)
            g_turn = pltpu.roll(gpair.astype(F32), 64, 1).astype(BF16)
            for n in (2 * p, 2 * p + 1):
                decay = jnp.exp2(jnp.minimum(rt[n : n + 1, :] - rv[:, n : n + 1], 0.0))
                halves.append(dot((scores * decay).astype(BF16), gpair))
                pick = (lambda a, b: jnp.where(left, a, b)) if n % 2 == 0 else (lambda a, b: jnp.where(left, b, a))
                one = jnp.concatenate([pick(wp, w_low), pick(wp, zero)], axis=1)
                two = jnp.concatenate([pick(gpair, g_turn), g_low], axis=1)
                dst[...] += dot_nt(one, two) * decay
            parts.append(jnp.where(left, halves[0], halves[1]))
        dwi = jnp.concatenate(parts, axis=1)
        dws = tail * dot(b, dhl)
        dw = dwi + dws
        skipgrad = gs * xv
        diff = folded(gl.astype(F32) * (yv - skip * xv) - wl.astype(F32) * dwi, fold)
        zsum = folded(w * dws, fold)
        const = folded(jnp.sum(h * dh, axis=0, keepdims=True) * grow[BLOCK - 1 : BLOCK, :] + jnp.zeros((8, COLS), F32), fold)
        da = dot_right(suffix, diff, 3) + dot_right(prefix, zsum, 3) + const[0:1, :]
        rate = -jnp.exp(prm[g, 7:8, 0:128])
        dstep = (folded(xv * dw, fold) + rate * da) * sigmoid(u[g])
        cat_out[:, WIDE + 128 * g : WIDE + 128 * (g + 1)] = dstep.astype(BF16)
        gx = (grow * gs).astype(BF16)
        dbc[:, STATE:] += dot_nt(gx, h.astype(BF16))
        dbc[:, :STATE] += dot_nt((tail * w).astype(BF16), dhl)
        dstate[:, cut] = grow[BLOCK - 1 : BLOCK, :] * dh + dot_tn(c, gx)
        dx = dte * dw + skip * gs
        dz = dx * (zs * (1.0 + zv * (1.0 - zs)))
        ext[0:BLOCK, cut] = dz
        gi = jnp.zeros((BLOCK, COLS), F32)
        for j in range(4):
            moved = ext[3 - j : 3 - j + BLOCK, cut]
            gi = gi + prm[g, j : j + 1, :] * moved
            acc[g, j : j + 1, :] += jnp.sum(xi * moved, axis=0, keepdims=True)
        cat_out[:, cut] = gi.astype(BF16)
        acc[g, 4:5, :] += jnp.sum(dz, axis=0, keepdims=True)
        acc[g, 6:7, 0:128] += jnp.sum(dstep, axis=0, keepdims=True)
        acc[g, 7:8, 0:128] += jnp.sum(da * dt[g], axis=0, keepdims=True) * rate
        acc[g, 8:9, 0:128] += folded(jnp.sum(skipgrad, axis=0, keepdims=True) + jnp.zeros((8, COLS), F32), fold)[0:1, :]
    ds = jnp.where(valid, dst[...], 0.0).astype(BF16)
    dbc_out[:, STATE:] = (dbc[:, STATE:] + dot_tn(ds, b)).astype(BF16)
    dbc_out[:, :STATE] = (dbc[:, :STATE] + dot(ds, c)).astype(BF16)

    @pl.when(k == BLOCKS - 1)
    def _():
        rings[0].step3(wout_out)
        rings[1].step3(wgate_out)
        branch_out[...] = (tokens[...].astype(F32) + (ownb[...] + token.step3())).astype(BF16)
        for copy in net.copies:
            copy.left()


def run_backward(*args):
    rev = lambda k: BLOCKS - 1 - k
    cols = lambda n: pl.BlockSpec((BLOCK, n), lambda k: (rev(k), 0))
    small = lambda: pl.BlockSpec((GROUPS, BLOCK, 128), lambda k: (0, rev(k), 0))
    keep = lambda *s: pl.BlockSpec(s, lambda k: (0,) * len(s))
    bf = lambda *s: pltpu.VMEM(s, BF16)
    f32 = lambda *s: pltpu.VMEM(s, F32)
    return pl.pallas_call(
        backward_kernel,
        grid=(BLOCKS,),
        out_shape=[
            SHAPE((LEN, MORE), BF16),
            SHAPE((LEN, 256), BF16),
            SHAPE((GROUPS, 16, COLS), F32),
            SHAPE((256, D), BF16),
            SHAPE((96, COLS), F32),
            SHAPE((96, COLS), F32),
        ],
        in_specs=[cols(WIDE)] * 4
        + [
            pl.BlockSpec((1, GROUPS, STATE, COLS), lambda k: (rev(k), 0, 0, 0)),
            keep(GROUPS, 16, COLS),
            cols(256),
            small(),
            small(),
            small(),
            keep(8, WIDE),
        ]
        + [ANY] * 5
        + [keep(256, D)],
        out_specs=[cols(MORE), cols(256), keep(GROUPS, 16, COLS), keep(256, D), keep(96, COLS), keep(96, COLS)],
        scratch_shapes=[
            f32(BLOCK + 8, WIDE),
            f32(STATE, WIDE),
            f32(BLOCK, BLOCK),
            f32(BLOCK, 256),
            bf(2, 2, 4, 96, WIDE),
            bf(2, 2, 4, 96, WIDE),
            bf(2, 2, 4, 96, WIDE),
            bf(LEN, WIDE),
            bf(D, WIDE),
            bf(2, 2, 4, 96, LEN),
            bf(LEN, WIDE),
            bf(2, 2, 4, 96, LEN),
            f32(256, D),
        ]
        + token_scratch()
        + grid_scratch("y", COLS)
        + grid_scratch("x", COLS)
        + sems(24)
        + [pltpu.SemaphoreType.DMA((5,))],
        compiler_params=pltpu.CompilerParams(collective_id=2, has_side_effects=True, vmem_limit_bytes=ROOM),
        name="backward",
    )(*args)


def tail_kernel(
    gg, cat, wx, normed_t, normed, dbc, zbc, bc_in, acc, wbc, tokens, cot, gain, conv,
    tokens_out, inner_out, bc_out, small_out,
    ggv, catv, wxv, ntv, nv, mine, slots, zv, xi, wv, xv, ov, ext, gnbc, ownb, held, got, away, dbw, heldb, gotb, small, sp0, sp1, sp2, sp3, bz, by,
    g0, g1, g2, g3, a1, a2, a3, b1, b2, b3, c1, c2, c3, send, recv, local,
):
    net = Net(send, recv)
    at = net.at
    yh, cx, cc, z, y = at["yh"], at["x"], at["c"], at["z"], at["y"]
    pairs = (
        (gg, ggv),
        (cat, catv),
        (wx, wxv),
        (normed, nv),
        (normed_t, ntv),
        (rows(zbc, z * 256, 256), zv.at[pl.ds(0, 256)]),
        (rows(zbc, lax.rem(z * 256 + 256, LEN), 16), zv.at[pl.ds(256, 16)]),
        (rows(bc_in, z * 256, 256), xi),
        (wbc, wv),
        (tokens, xv),
        (cot, ov),
    )
    loads = [pltpu.make_async_copy(src, dst, local.at[i]) for i, (src, dst) in enumerate(pairs)]
    for copy in loads:
        copy.start()
    token = TokenSum(net, (g0, g1, g2, g3))
    spans = ((0, COLS), (WIDE, 128))
    rings = (GridSum(net, "x", held, spans, (a1, a2, a3), (0, 48)), GridSum(net, "y", held, spans, (b1, b2, b3), (48, 48)))
    ring_bc = GridSum(net, "x", heldb, ((0, 128),), (c1, c2, c3))
    mine[0:LEN, :] = dbc[...]
    mine[LEN : LEN + 16, :] = jnp.zeros((16, 256), BF16)
    slots[z] = mine[pl.ds(pl.multiple_of(z * 256, 16), 272), :]
    net.barrier([(a, s) for a in ("z", "x", "y") for s in (1, -1, 2)] + [("c", 1)])
    swap = [net.start(rows(mine, net.near("z", s) * 256, 272), slots.at[z], "z", s) for s in (1, -1, 2)]
    gain_row = gain[...].reshape(1, D)
    norm_part = jnp.zeros((1, D), F32)

    def block(place):
        cut = pl.ds(pl.multiple_of(place * 256, 256), 256)
        got = dot_nt(ggv[cut, :], wxv[:, 0:WIDE]) + dot_nt(catv[cut, :], wxv[:, WIDE:])
        return got, jnp.sum(got * nv[cut, :].astype(F32), axis=0, keepdims=True)

    for copy in loads[:4]:
        copy.wait()
    out, part = block(net.near("z", 2))
    norm_part = norm_part + part
    g0[...] = out.astype(BF16)
    token.step1()
    grads = lambda core: dot(ntv[core].reshape(8 * 96, LEN), catv[...]).astype(BF16).reshape(2, 4, 96, MORE)
    loads[4].wait()
    away[...] = grads(net.other)
    cross = net.start(away, got, "c")
    for copy in loads[5:]:
        copy.wait()
    arrive(swap)
    total = (slots[0].astype(F32) + slots[1].astype(F32)) + (slots[2].astype(F32) + slots[3].astype(F32))
    sig = sigmoid(zv[...])
    dz = total * (sig * (1.0 + zv[...] * (1.0 - sig)))
    ext[...] = jnp.where(iota((272, 256), 0) + z * 256 < LEN, dz, 0.0)
    gbc = jnp.zeros((256, 256), F32)
    small[0:16, :] = acc[0]
    small[16:32, :] = acc[1]
    small[32:48, :] = jnp.zeros((16, COLS), F32)
    for j in range(4):
        moved = ext[3 - j : 3 - j + 256, :]
        gbc = gbc + conv[j : j + 1, :] * moved
        small[36 + j : 37 + j, 0:256] = jnp.sum(xi[...] * moved, axis=0, keepdims=True)
    small[40:41, 0:256] = jnp.sum(ext[0:256, :], axis=0, keepdims=True)
    gbc = gbc.astype(BF16)
    own = pl.ds(pl.multiple_of(z * 256, 256), 256)
    for core in range(2):
        dbw[core] = dot(ntv[core, :, :, :, own].reshape(8 * 96, 256), gbc).astype(BF16).reshape(2, 4, 96, 256)
    crossb = net.start(dbw.at[net.other], gotb, "c")
    gnbc[...] = dot_nt(gbc, wv[...])
    norm_part = norm_part + jnp.sum(gnbc[...] * nv[own, :].astype(F32), axis=0, keepdims=True)
    held[...] = grads(cc)
    cross.arrived()
    held[...] += got[...]
    for ring in rings:
        ring.step1()
    crossb.arrived()
    heldb[...] = dbw[cc] + gotb[...]
    ring_bc.step1()
    for p, step in HALVES:
        out, part = block(net.near("z", step))
        norm_part = norm_part + part
        g2[p] = out.astype(BF16)
    token.step2()
    out, part = block(z)
    norm_part = (norm_part + part) / gain_row
    ownb[...] = out + gnbc[...]
    for k in range(4):
        small[32 + k : 33 + k, :] = norm_part[:, k * COLS : (k + 1) * COLS]
    sp1[cx] = small[...]
    q = net.around(sp1.at[cx], sp1.at[cx], "x")
    ring_bc.step2()
    v = xv[...].astype(F32)
    root = lax.rsqrt(jnp.mean(v * v, axis=1, keepdims=True) + EPS)
    arrive(q)
    sp2[y] = (sp1[0] + sp1[1]) + (sp1[2] + sp1[3])
    q = net.around(sp2.at[y], sp2.at[y], "y")
    ring_bc.step3(by.at[yh])
    qb = [net.start(by.at[yh], by.at[yh], "y", 2)]
    for ring in rings:
        ring.step2()
    arrive(q)
    sp3[cc] = (sp2[0] + sp2[1]) + (sp2[2] + sp2[3])
    q = [net.start(sp3.at[cc], sp3.at[cc], "c")]
    arrive(qb)
    bz[z, :, 0:128] = by[0]
    bz[z, :, 128:256] = by[1]
    qb = net.around(bz.at[z], bz.at[z], "z")
    arrive(q)
    small[...] = sp3[0] + sp3[1]
    sp0[z] = small[32:48, :]
    q = net.around(sp0.at[z], sp0.at[z], "z")
    small_out[0:32, :] = small[0:32, :]
    for ring in rings:
        ring.step3(inner_out)
    g = token.step3() + ownb[...]
    scaled = g * gain_row
    tokens_out[...] = ov[...].astype(F32) + root * scaled - v * (root * root * root) * jnp.mean(scaled * v, axis=1, keepdims=True)
    arrive(qb)
    bc_out[...] = (bz[0] + bz[1]) + (bz[2] + bz[3])
    arrive(q)
    small_out[32:48, :] = (sp0[0] + sp0[1]) + (sp0[2] + sp0[3])
    net.finish()


def run_tail(*args):
    bf = lambda *s: pltpu.VMEM(s, BF16)
    f32 = lambda *s: pltpu.VMEM(s, F32)
    return pl.pallas_call(
        tail_kernel,
        out_shape=[
            SHAPE((256, D), F32),
            SHAPE((96, COLS + 128), F32),
            SHAPE((96, 256), F32),
            SHAPE((48, COLS), F32),
        ],
        in_specs=[ANY] * 5 + [VMEM, ANY, ANY, VMEM, ANY, ANY, ANY, VMEM, VMEM],
        out_specs=[VMEM] * 4,
        scratch_shapes=[
            bf(LEN, WIDE),
            bf(LEN, MORE),
            bf(D, PROJ),
            bf(2, 2, 4, 96, LEN),
            bf(LEN, D),
            bf(LEN + 16, 256),
            bf(4, 272, 256),
            f32(272, 256),
            f32(256, 256),
            bf(D, 256),
            bf(256, D),
            bf(256, D),
            f32(272, 256),
            f32(256, D),
            f32(256, D),
            bf(2, 4, 96, MORE),
            bf(2, 4, 96, MORE),
            bf(2, 4, 96, MORE),
            bf(2, 2, 4, 96, 256),
            bf(2, 4, 96, 256),
            bf(2, 4, 96, 256),
            f32(48, COLS),
            f32(4, 16, COLS),
            f32(4, 48, COLS),
            f32(4, 48, COLS),
            f32(2, 48, COLS),
            f32(4, 96, 256),
            f32(2, 96, 128),
        ]
        + token_scratch()
        + grid_scratch("x", COLS + 128, 48)
        + grid_scratch("y", COLS + 128, 48)
        + grid_scratch("x", 128)
        + sems(64)
        + [pltpu.SemaphoreType.DMA((11,))],
        compiler_params=pltpu.CompilerParams(collective_id=3, has_side_effects=True, vmem_limit_bytes=ROOM),
        name="tail",
    )(*args)


def finish_kernel(tokens, branch, inner, bc, small, gate, wout, tokens_out, branch_out, inner_out, bc_out, gate_out, wout_out, step_out, norm, conv, bias, conv_bc, bias_bc, step_bias, decay, skip, gain, tv, rv, iv, cv, gv, wv, sem):
    trips = (
        (tokens, tv, tokens_out),
        (branch, rv, branch_out),
        (inner.at[:, pl.ds(0, COLS)], iv, inner_out),
        (bc, cv, bc_out),
        (gate, gv, gate_out),
        (wout, wv, wout_out),
    )
    reads = [pltpu.make_async_copy(src, via, sem.at[i]) for i, (src, via, dst) in enumerate(trips)]
    copies = [pltpu.make_async_copy(via, dst, sem.at[len(trips) + i]) for i, (src, via, dst) in enumerate(trips)]
    for copy in reads:
        copy.start()
    for read, copy in zip(reads, copies):
        read.wait()
        copy.start()
    step_out[...] = jnp.transpose(jnp.concatenate([inner[:, COLS:], jnp.zeros((32, 128), F32)], axis=0))[0:HEADS, 0:96]
    for k in range(4):
        norm[:, k * COLS : (k + 1) * COLS] = small[32 + k : 33 + k, :]
    conv_bc[...] = small[36:40, 0:256]
    bias_bc[...] = small[40:41, 0:256]
    mine = small[pl.ds(pl.multiple_of(lax.axis_index("yh") * 16, 8), 16), :]
    conv[...] = mine[0:4, :]
    bias[...] = mine[4:5, :]
    gain[...] = mine[5:6, :]
    step_bias[...] = mine[6:7, 0:HEADS]
    decay[...] = mine[7:8, 0:HEADS]
    skip[...] = mine[8:9, 0:HEADS]
    for copy in copies:
        copy.wait()


def run_finish(*args):
    f32 = lambda *s: SHAPE(s, F32)
    return pl.pallas_call(
        finish_kernel,
        out_shape=[
            f32(256, D),
            SHAPE((256, D), BF16),
            f32(96, COLS),
            f32(96, 256),
            f32(96, COLS),
            f32(96, COLS),
            f32(HEADS, 96),
            f32(1, D),
            f32(4, COLS),
            f32(1, COLS),
            f32(4, 256),
            f32(1, 256),
            f32(1, HEADS),
            f32(1, HEADS),
            f32(1, HEADS),
            f32(1, COLS),
        ],
        in_specs=[ANY, ANY, VMEM, ANY, VMEM, ANY, ANY],
        out_specs=[ANY] * 6 + [VMEM] * 10,
        scratch_shapes=[
            pltpu.VMEM((256, D), F32),
            pltpu.VMEM((256, D), BF16),
            pltpu.VMEM((96, COLS), F32),
            pltpu.VMEM((96, 256), F32),
            pltpu.VMEM((96, COLS), F32),
            pltpu.VMEM((96, COLS), F32),
            pltpu.SemaphoreType.DMA((12,)),
        ],
        compiler_params=pltpu.CompilerParams(vmem_limit_bytes=ROOM),
        name="finish",
    )(*args)


def shards(tokens, norm_gain, w_gate, w_inner, w_bc, w_step, conv_inner, bias_inner, conv_bc, bias_bc, step_bias, decay_log, skip_gain, gate_gain, w_out, cotangent):
    (
        inner, zin, y, hin, dt, r, u, bc, bc_in, zbc, normed_t, gains, mixed, gs, gg, cot_t, normed, wx, wout, wbc, prm,
    ) = run_front(
        tokens, norm_gain, w_gate, w_inner, w_out, w_bc, w_step.T, conv_inner, bias_inner, gate_gain, step_bias, decay_log,
        skip_gain, conv_bc, bias_bc, cotangent,
    )
    wx, wout, wbc = wx.reshape(D, PROJ), wout.reshape(D, WIDE), wbc.reshape(D, 256)
    cat, dbc, acc, output, wout_grad, gate_grad = run_backward(
        gs, inner, zin, y, hin, prm, bc, dt, r, u, gains, mixed, wout, cot_t, gg, normed_t, tokens
    )
    tokens_grad, inner_grad, bc_grad, small = run_tail(
        gg, cat, wx, normed_t, normed, dbc, zbc, bc_in, acc, wbc, tokens, cotangent, norm_gain, conv_bc
    )
    (
        tokens_grad, output, inner_grad, bc_grad, gate_grad, wout_grad, step_grad,
        norm, conv, bias, conv_bc_grad, bias_bc_grad, step_bias_grad, decay, skip, gate_gain_grad,
    ) = run_finish(tokens_grad, output, inner_grad, bc_grad, small, gate_grad, wout_grad)
    flat = lambda v: v.reshape(-1)
    return (
        output, tokens_grad, flat(norm), gate_grad, inner_grad, bc_grad, step_grad.T, conv, flat(bias), conv_bc_grad,
        flat(bias_bc_grad), flat(step_bias_grad), flat(decay), flat(skip), flat(gate_gain_grad), wout_grad,
    )


def solution(mesh):
    fine = Mesh(mesh.devices.reshape(2, 4, 2, 2, 4), AXES)
    dp, tensor = ("yl", "x", "c"), ("yh", "z")
    tokens, weight = P(dp + tensor, None), P(dp, tensor)
    heads, shared = P(tensor), P()
    return jax.shard_map(
        shards,
        mesh=fine,
        in_specs=(
            tokens, shared, weight, weight, P(dp, None), weight, P(None, tensor), heads,
            shared, shared, heads, heads, heads, heads, weight, tokens,
        ),
        out_specs=(
            tokens, tokens, shared, weight, weight, P(dp, None), weight, P(None, tensor), heads,
            shared, shared, heads, heads, heads, heads, weight,
        ),
        check_vma=False,
    )
```

```python
import jax
import jax.numpy as jnp
from jax import lax
from jax.experimental import pallas as pl
from jax.experimental.pallas import tpu as pltpu
from jax.sharding import Mesh
from jax.sharding import PartitionSpec as P

D = 1536
LEN = 1024
INNER = 3072
STATE = 128
BLOCK = 256
BLOCKS = LEN // BLOCK
GROUPS = 2
HEADS = 6
COLS = HEADS * 64
WIDE = GROUPS * COLS
STEPS = 2 * WIDE
PROJ = STEPS + GROUPS * 128
MORE = PROJ - WIDE
LOG2E = 1.4426950408889634
EPS = 1e-05
F32 = jnp.float32
BF16 = jnp.bfloat16
MESH = pl.DeviceIdType.MESH
AXES = ("yl", "x", "c", "yh", "z")
ANY = pl.BlockSpec(memory_space=pl.ANY)
VMEM = pl.BlockSpec(memory_space=pltpu.VMEM)
SHAPE = jax.ShapeDtypeStruct
ROOM = 60 * 2**20


def dot(a, b):
    return jnp.dot(a, b, preferred_element_type=F32)


def dot_nt(a, b):
    return lax.dot_general(a, b, (((1,), (1,)), ((), ())), preferred_element_type=F32)


def dot_tn(a, b):
    return lax.dot_general(a, b, (((0,), (0,)), ((), ())), preferred_element_type=F32)


def pieces(v, n):
    out = []
    for _ in range(n):
        hi = v.astype(BF16)
        out.append(hi)
        v = v - hi.astype(F32)
    return out


def dot_left(v, ones, n):
    return sum(dot(p, ones) for p in pieces(v, n))


def spread(v, ones):
    hi = v.astype(BF16).astype(F32)
    low = pltpu.roll(v - hi, 64, 1)
    return dot(jnp.where(iota(v.shape, 1) < 64, hi, low).astype(BF16), ones)


def folded(v, ones):
    hi = v.astype(BF16)
    low = (v - hi.astype(F32)).astype(BF16)
    return dot(hi, ones) + dot(low, ones)


def dot_right(ones, v, n):
    return sum(dot(ones, p) for p in pieces(v, n))


def iota(shape, axis):
    return lax.broadcasted_iota(jnp.int32, shape, axis)


def expander():
    row, col = iota((128, COLS), 0), iota((128, COLS), 1)
    return ((row & 63) == lax.shift_right_logical(col, 6)).astype(BF16)


def reducer():
    row, col = iota((COLS, 128), 0), iota((COLS, 128), 1)
    return (col == lax.shift_right_logical(row, 6)).astype(BF16)


def sigmoid(v):
    return 0.5 * jnp.tanh(0.5 * v) + 0.5


def lower(strict=False):
    row, col = iota((BLOCK, BLOCK), 0), iota((BLOCK, BLOCK), 1)
    return ((row > col) if strict else (row >= col)).astype(BF16)


def upper():
    return (iota((BLOCK, BLOCK), 0) <= iota((BLOCK, BLOCK), 1)).astype(BF16)


def token_row(v):
    v = sum(v[:, 128 * i : 128 * (i + 1)] for i in range(v.shape[1] // 128))
    ones = jnp.ones((8, 128), BF16)
    return sum(dot_nt(ones, p) for p in pieces(v, 3))[0:1, :]


class Net:
    def __init__(self, send, recv):
        self.send, self.recv, self.copies = send, recv, []
        self.at = {name: lax.axis_index(name) for name in AXES}
        self.at["y"] = self.at["yh"] * 2 + self.at["yl"]
        self.places = {(a, s): lax.rem(self.at[a] + s + 4, 4) for a in ("x", "y", "z") for s in (1, -1, 2)}
        self.other = 1 - self.at["c"]
        self.targets = {("c", 1): {"c": self.other}}
        for (a, s), place in self.places.items():
            self.targets[a, s] = {"yh": place // 2, "yl": lax.rem(place, 2)} if a == "y" else {a: place}

    def near(self, axis, step):
        return self.places[axis, step]

    def plan(self, src, dst, axis, step=1):
        copy = Copy(self, len(self.copies), src, dst, self.targets[axis, step])
        self.copies.append(copy)
        return copy

    def start(self, src, dst, axis, step=1):
        return self.plan(lambda: src, lambda: dst, axis, step).start()

    def around(self, src, dst, axis):
        return [self.start(src, dst, axis, step) for step in (1, -1, 2)]

    def barrier(self, peers):
        here = pltpu.get_barrier_semaphore()
        for peer in peers:
            pl.semaphore_signal(here, inc=1, device_id=self.targets[peer], device_id_type=MESH)
        pl.semaphore_wait(here, len(peers))

    def finish(self):
        for copy in self.copies:
            copy.arrived()
        for copy in self.copies:
            copy.left()


class Copy:
    def __init__(self, net, index, src, dst, target):
        self.net, self.index, self.src, self.dst, self.target = net, index, src, dst, target
        self.here, self.gone = False, False

    def made(self):
        return pltpu.make_async_remote_copy(
            src_ref=self.src(),
            dst_ref=self.dst(),
            send_sem=self.net.send.at[self.index],
            recv_sem=self.net.recv.at[self.index],
            device_id=self.target,
            device_id_type=MESH,
        )

    def start(self):
        self.made().start()
        return self

    def arrived(self):
        if not self.here:
            self.here = True
            self.made().wait_recv()

    def left(self):
        if not self.gone:
            self.gone = True
            self.made().wait_send()


def sems(n):
    return [pltpu.SemaphoreType.DMA((n,)), pltpu.SemaphoreType.DMA((n,))]


def rows(ref, first, count):
    return ref.at[pl.ds(pl.multiple_of(first, 16), count)]


def lanes(first, count):
    return pl.ds(pl.multiple_of(first, 128), count)


def arrive(copies):
    for copy in copies:
        copy.arrived()


HALVES = ((0, 1), (1, -1))


class GridSum:
    def __init__(self, net, first, held, spans, scratch, cut=(0, 96)):
        self.net, self.first, self.held, self.spans = net, first, held, spans
        self.land, self.mid, self.last = scratch
        self.rows = pl.ds(*cut)
        self.one, self.two = [], []
        for slot, step in enumerate((2, 1, -1)):
            if first == "x":
                self.plan(self.one, lambda step=step: held.at[:, net.near("x", step), self.rows], lambda slot=slot: self.land.at[slot], "x", step)
            else:
                self.plan(self.two, lambda step=step: self.mid.at[net.near("x", step)], lambda slot=slot: self.last.at[slot], "x", step)
            lane = 0
            for base, n in spans:
                there = lambda step=step, base=base, n=n: lanes(base + (net.near("y", step) // 2) * n, n)
                if first == "x":
                    src = lambda step=step, there=there: self.mid.at[lax.rem(net.near("y", step), 2), :, there()]
                    self.plan(self.two, src, lambda slot=slot, lane=lane, n=n: self.last.at[slot, :, pl.ds(lane, n)], "y", step)
                else:
                    src = lambda step=step, there=there: held.at[lax.rem(net.near("y", step), 2), :, self.rows, there()]
                    self.plan(self.one, src, lambda slot=slot, lane=lane, n=n: self.land.at[slot, :, :, pl.ds(lane, n)], "y", step)
                lane += n

    def plan(self, to, src, dst, axis, step):
        to.append(self.net.plan(src, dst, axis, step))

    def step1(self):
        for copy in self.one:
            copy.start()

    def step2(self):
        arrive(self.one)
        at = self.net.at
        if self.first == "x":
            self.mid[...] = self.total(self.held[:, at["x"], self.rows], self.land, slice(None)).astype(BF16)
        else:
            lane = 0
            for base, n in self.spans:
                cut = slice(lane, lane + n)
                own = self.held[at["yl"], :, self.rows, lanes(base + at["yh"] * n, n)]
                self.mid[:, :, cut] = self.total(own, self.land, cut).astype(BF16)
                lane += n
        for copy in self.two:
            copy.start()

    def total(self, own, others, cut):
        return (own.astype(F32) + others[0, ..., cut].astype(F32)) + (others[1, ..., cut].astype(F32) + others[2, ..., cut].astype(F32))

    def step3(self, out):
        arrive(self.two)
        at = self.net.at
        if self.first == "y":
            out[self.rows, :] = self.total(self.mid[at["x"]], self.last, slice(None))
            return
        lane = 0
        for base, n in self.spans:
            cut = slice(lane, lane + n)
            out[self.rows, cut] = self.total(self.mid[at["yl"], :, lanes(base + at["yh"] * n, n)], self.last, cut)
            lane += n


def grid_scratch(first, width, count=96):
    blocks, wide = (2, 2 * width) if first == "x" else (4, width)
    return [pltpu.VMEM(s, BF16) for s in ((3, blocks, count, wide), (blocks, count, wide), (3, count, width))]


class TokenSum:
    def __init__(self, net, scratch):
        self.net, self.far, self.half, self.fold, self.whole = net, *scratch
        self.one = [
            net.plan(lambda p=p: self.far.at[pl.ds(128 * p, 128)], lambda p=p: self.half.at[p], "z", step) for p, step in HALVES
        ]
        half = lambda ref, p, n: ref.at[p, pl.ds(128 * n, 128)]
        self.ready = [net.plan(lambda p=p: half(self.fold, p, 1 - p), lambda p=p: half(self.whole, p, 1 - p), "z", step) for p, step in HALVES]
        self.added = [net.plan(lambda p=p: half(self.fold, p, p), lambda p=p: half(self.whole, p, p), "z", step) for p, step in HALVES]

    def step1(self):
        for copy in self.one:
            copy.start()

    def folded(self, p):
        self.ready[p].start()

    def step2(self):
        arrive(self.one)
        for p, _ in HALVES:
            self.fold[p, 128 * p : 128 * p + 128, :] += self.half[p]
            self.added[p].start()

    def step3(self):
        arrive(self.ready + self.added)
        return self.whole[0].astype(F32) + self.whole[1].astype(F32)


def token_scratch():
    return [pltpu.VMEM((256, D), BF16), pltpu.VMEM((2, 128, D), BF16), pltpu.VMEM((2, 256, D), BF16), pltpu.VMEM((2, 256, D), BF16)]


def front_kernel(
    x, gain, w_gate, w_inner, w_out, w_bc, w_step, conv, bias, gate_gain, step_bias, decay_log, skip_gain, conv_bc, bias_bc, cot,
    inner_out, z_out, y_out, h_out, dt_out, r_out, u_out, bc_out, bcin_out, zbc_out, normed_t, gains_out,
    mixed_out, gs_out, gg_out, cot_t, normed_out, wx_out, wout_out, wbc_out, prm_out,
    normed, wx, wout, wbc, prm, xv, stepv, stept, pk,
    cots, gps, acts, slopes, gms, mixed, gg, turned_c, ext, extbc, state, stat, slots, send, recv, local,
):
    i = pl.program_id(0)
    net = Net(send, recv)
    at = net.at
    yh, cx, cc, z, y = at["yh"], at["x"], at["c"], at["z"], at["y"]
    own_rows = lambda ref: rows(ref, z * 256, 256)
    order = ((0, 1), (1, -1), (1, 1), (0, -1))
    part = lambda ref, p, s: rows(ref, net.near("z", -s) * 256 + 128 * p, 128)
    c1 = [
        net.plan(lambda p=p: cot.at[pl.ds(128 * p, 128)], lambda p=p: rows(cots, z * 256 + 128 * p, 128), "z", s) for p, s in order
    ]
    c2 = [net.plan(lambda p=p, s=s: part(cots, p, s), lambda p=p, s=s: part(cots, p, s), "z", s) for p, s in HALVES]
    q = [net.plan(lambda: stat, lambda: slots.at[z], "z", step) for step in (1, -1, 2)]
    spot_o = lambda xx, cut=pl.ds(0, 96): wout.at[at["yl"], xx, cc, cut, lanes(yh * COLS, COLS)]
    line_o = lambda yy, cut=pl.ds(0, 96): wout.at[lax.rem(yy, 2), :, cc, cut, lanes((yy // 2) * COLS, COLS)]
    same = lambda ref, axis, step=1: net.plan(ref, ref, axis, step)
    o1 = [net.plan(lambda: w_out, lambda: spot_o(cx), "x", step) for _, step in HALVES]
    o2 = [same(lambda p=p, s=s: spot_o(net.near("x", -s), pl.ds(48 * p, 48)), "x", s) for p, s in HALVES]
    o3 = [same(lambda: line_o(y), "y", step) for _, step in HALVES]
    o4 = [same(lambda p=p, s=s: line_o(net.near("y", -s), pl.ds(48 * p, 48)), "y", s) for p, s in HALVES]
    oc = [same(lambda: line_o(y), "c")] + [same(lambda s=s: line_o(net.near("y", s)), "c") for s in (1, -1, 2)]
    own = lambda: pltpu.make_async_copy(cot, own_rows(cots), local.at[0])
    pairs = ((normed, normed_out), (wx, wx_out), (wbc, wbc_out), (prm, prm_out), (wout, wout_out), (turned_c, cot_t))
    leave = lambda n: pltpu.make_async_copy(*pairs[n], local.at[1 + n])

    @pl.when(i == 0)
    def _():
        load = pltpu.make_async_copy(x, xv, local.at[7])
        load.start()
        own().start()
        stept[...] = jnp.zeros_like(stept)
        stept[0:HEADS, 0:96] = w_step[...].astype(F32)
        stepv[...] = jnp.transpose(stept[...])[0:96, :].astype(BF16)
        pk[...] = jnp.zeros_like(pk)
        pk[0:4, :] = conv[...]
        pk[4:5, :] = bias[...].reshape(1, COLS)
        pk[5:6, :] = gate_gain[...].reshape(1, COLS)
        pk[6:7, 0:HEADS] = step_bias[...].reshape(1, HEADS)
        pk[7:8, 0:HEADS] = decay_log[...].reshape(1, HEADS)
        pk[8:9, 0:HEADS] = skip_gain[...].reshape(1, HEADS)
        net.barrier([("z", 1), ("z", -1), ("z", 2), ("x", 1), ("x", -1), ("y", 1), ("y", -1), ("y", 2), ("c", 1)])
        first = {
            "x": ((w_gate, wx, 0, COLS), (w_bc.at[:, lanes(yh * 128, 128)], wbc, 0, 128)),
            "y": ((w_inner, wx, WIDE, COLS), (stepv, wx, STEPS, 128)),
        }
        then = {"x": "y", "y": "x"}
        done = []

        def go(src, dst, axis, step=1):
            done.append(net.start(src, dst, axis, step))
            return done[-1]

        def spot(ref, base, n, yy, xx, cut=pl.ds(0, 96)):
            return ref.at[lax.rem(yy, 2), xx, cc, cut, lanes(base + (yy // 2) * n, n)]

        def line(axis, ref, base, n, place, cut=pl.ds(0, 96)):
            if axis == "x":
                return ref.at[lax.rem(place, 2), :, cc, cut, lanes(base + (place // 2) * n, n)]
            return ref.at[:, place, cc, cut, lanes(base, 2 * n)]

        sent = {"x": [], "y": []}
        for axis in ("x", "y"):
            for src, ref, base, n in first[axis]:
                sent[axis].append([go(src, spot(ref, base, n, y, cx), axis, step) for _, step in HALVES])
        load.wait()
        v = xv[...].astype(F32)
        root = lax.rsqrt(jnp.mean(v * v, axis=1, keepdims=True) + EPS)
        normed[pl.ds(pl.multiple_of(z * 256, 256), 256), :] = (v * root * gain[...].reshape(1, D)).astype(BF16)
        zs = {}
        for p, s in order:
            here = rows(normed, z * 256 + 128 * p, 128)
            zs[p, s] = go(here, here, "z", s)
        mine = [
            pltpu.make_async_copy(src, spot(ref, base, n, y, cx), local.at[8 + k])
            for k, (src, ref, base, n) in enumerate(first["x"] + first["y"])
        ]
        mine.append(pltpu.make_async_copy(pk, prm.at[yh], local.at[12]))
        mine.append(pltpu.make_async_copy(w_out, spot_o(cx), local.at[13]))
        for copy in mine:
            copy.start()
        for copy in o1:
            copy.start()
        for axis in ("x", "y"):
            for src, ref, base, n in first[axis]:
                go(src, spot(ref, base, n, y, cx), "c")
        go(pk, prm.at[yh], "y", 2)
        second = {"x": [], "y": []}
        for axis in ("x", "y"):
            for (src, ref, base, n), copies in zip(first[axis], sent[axis]):
                for (p, s), copy in zip(HALVES, copies):
                    copy.arrived()
                    cut = pl.ds(48 * p, 48)
                    here = spot(ref, base, n, y, net.near("x", -s), cut) if axis == "x" else spot(ref, base, n, net.near("y", -s), cx, cut)
                    second[axis].append(go(here, here, axis, s))
        for copy in mine:
            copy.wait()
        third = {"x": [], "y": []}
        for axis in ("x", "y"):
            arrive(second[axis])
            for src, ref, base, n in first[axis]:
                here = line(axis, ref, base, n, at[then[axis]])
                third[axis].append([go(here, here, then[axis], s) for _, s in HALVES])
        for copy, start in zip(o1, o2):
            copy.arrived()
            start.start()
        for axis in ("x", "y"):
            for src, ref, base, n in first[axis]:
                for s in (1, -1, 2):
                    here = spot(ref, base, n, y, net.near("x", s)) if axis == "x" else spot(ref, base, n, net.near("y", s), cx)
                    go(here, here, "c")
        for p, s in HALVES:
            zs[p, s].arrived()
            here = part(normed, p, s)
            go(here, here, "z", s)
        for copy in c1:
            copy.start()
        fourth = {"x": [], "y": []}
        for axis in ("x", "y"):
            for (src, ref, base, n), copies in zip(first[axis], third[axis]):
                for (p, s), copy in zip(HALVES, copies):
                    copy.arrived()
                    place = net.near(then[axis], -s)
                    here = line(axis, ref, base, n, place, pl.ds(48 * p, 48))
                    fourth[axis].append(go(here, here, then[axis], s))
                    here = line(axis, ref, base, n, place)
                    go(here, here, "c")
        arrive(o2)
        for copy in o3:
            copy.start()
        for axis in ("x", "y"):
            arrive(fourth[axis])
            for src, ref, base, n in first[axis]:
                here = line(axis, ref, base, n, net.near(then[axis], 2))
                go(here, here, "c")
        for copy in done:
            copy.arrived()
        for copy in done:
            copy.left()
        for n in range(4):
            leave(n).start()
        ext[0:8, :] = jnp.zeros((8, WIDE), F32)
        extbc[0:8, :] = jnp.zeros((8, 256), F32)
        state[...] = jnp.zeros_like(state)

    @pl.when((i > 0) & (i < BLOCKS))
    def _():
        ext[0:8, :] = ext[BLOCK : BLOCK + 8, :]
        extbc[0:8, :] = extbc[BLOCK : BLOCK + 8, :]

    @pl.when(i == 2)
    def _():
        for copy, start in zip(c1[:2], c2):
            copy.arrived()
            start.start()
        for copy, start in zip(o3, o4):
            copy.arrived()
            start.start()
        for copy in oc[:3]:
            copy.start()

    @pl.when(i < BLOCKS)
    def _():
        xb = normed[pl.ds(pl.multiple_of(i * BLOCK, BLOCK), BLOCK), :]
        turned = jnp.transpose(xb).reshape(2, 4, 2, 96, BLOCK)
        for core in range(2):
            normed_t[core] = turned[:, :, core]
        bc_in = dot(xb, wbc[...].reshape(D, 256))
        bcin_out[...] = bc_in
        extbc[8 : BLOCK + 8, :] = bc_in
        zb = bias_bc[...].reshape(1, 256) + sum(conv_bc[j : j + 1, :] * extbc[5 + j : 5 + j + BLOCK, :] for j in range(4))
        zbc_out[...] = zb
        bc = (zb * sigmoid(zb)).astype(BF16)
        bc_out[...] = bc
        b, c = bc[:, :STATE], bc[:, STATE:]
        scores = jnp.where(iota((BLOCK, BLOCK), 0) >= iota((BLOCK, BLOCK), 1), dot_nt(c, b), 0.0)
        tri, ones = lower(), expander()
        left = iota((BLOCK, 128), 1) < 64
        weight = lambda first, n: wx[:, :, :, :, first : first + n].reshape(D, n)
        steps = dot(xb, weight(STEPS, 256))
        total = jnp.zeros((BLOCK, 128), F32)
        for g in range(GROUPS):
            if g == 1:

                @pl.when(i == BLOCKS - 1)
                def _():
                    arrive(o4)
                    oc[3].start()

            cut = slice(g * COLS, (g + 1) * COLS)
            u = steps[:, 128 * g : 128 * (g + 1)] + prm[g, 6:7, 0:128]
            dt = jnp.maximum(u, 0.0) + jnp.log(1.0 + jnp.exp(-jnp.abs(u)))
            rate = -jnp.exp(prm[g, 7:8, 0:128]) * LOG2E
            r = dot_right(tri, dt * rate, 3)
            u_out[g] = u
            dt_out[g] = dt
            r_out[g] = r
            rt = jnp.transpose(r)
            gate = dot(xb, weight(g * COLS, COLS))
            inner = dot(xb, weight(WIDE + g * COLS, COLS))
            inner_out[:, cut] = inner
            ext[8 : BLOCK + 8, cut] = inner
            zv = prm[g, 4:5, :] + sum(prm[g, j : j + 1, :] * ext[5 + j : 5 + j + BLOCK, cut] for j in range(4))
            z_out[:, cut] = zv
            xv = zv * sigmoid(zv)
            last = r[BLOCK - 1 : BLOCK, :]
            w = xv * spread(dt, ones)
            grow = spread(jnp.exp2(r), ones)
            tail = spread(jnp.exp2(last - r), ones)
            skip = spread(prm[g, 8:16, 0:128], ones)[0:1, :]
            wl = w.astype(BF16)
            h = state[:, cut]
            h_out[0, g] = h
            parts = []
            for p in range(HEADS // 2):
                halves = []
                for n in (2 * p, 2 * p + 1):
                    gap = jnp.minimum(r[:, n : n + 1] - rt[n : n + 1, :], 0.0)
                    halves.append(dot((scores * jnp.exp2(gap)).astype(BF16), wl[:, 128 * p : 128 * (p + 1)]))
                parts.append(jnp.where(left, halves[0], halves[1]))
            yv = jnp.concatenate(parts, axis=1) + grow * dot(c, h.astype(BF16)) + skip * xv
            y_out[:, cut] = yv
            state[:, cut] = grow[BLOCK - 1 : BLOCK, :] * h + dot_tn(b, (tail * w).astype(BF16))
            sig = sigmoid(gate)
            act = gate * sig
            gp = yv * act
            here_now = pl.ds(pl.multiple_of(i * BLOCK, BLOCK), BLOCK)
            gps[here_now, cut] = gp
            acts[here_now, cut] = act
            slopes[here_now, cut] = yv * (sig + act * (1.0 - sig))
            sq = gp * gp
            total = total + (sq[:, 0:128] + sq[:, 128:256] + sq[:, 256:384])
        stat[pl.ds(i, 1), :] = token_row(total)

    @pl.when(i == BLOCKS)
    def _():
        own().wait()
        arrive(oc)
        leave(4).start()

    @pl.when(i == BLOCKS + 1)
    def _():
        arrive(c1)

    @pl.when(i == 2 * BLOCKS - 1)
    def _():
        for copy in c2:
            copy.arrived()

    @pl.when(i >= BLOCKS)
    def _():
        t = i - BLOCKS
        block = lax.rem(z + t + lax.div(t, 2) - 2 * lax.div(t, 3), 4)
        at = pl.ds(pl.multiple_of(block * BLOCK, BLOCK), BLOCK)
        cb = cots[at, :]
        turned = jnp.transpose(cb).reshape(2, 4, 2, 96, BLOCK)
        for core in range(2):
            turned_c[core, :, :, :, at] = turned[:, :, core]
        gm = dot(cb, wout[...].reshape(D, WIDE))
        gms[at, :] = gm
        gain = jnp.concatenate([prm[0, 5:6, :], prm[1, 5:6, :]], axis=1)
        stat[pl.ds(BLOCKS + block, 1), :] = token_row(gm * gain * gps[at, :])

    @pl.when(i == 2 * BLOCKS - 1)
    def _():
        for copy in q:
            copy.start()
        slots[z] = stat[...]
        for copy in q:
            copy.arrived()
            copy.left()
        sums = (slots[0] + slots[1]) + (slots[2] + slots[3])
        root = lax.rsqrt(sums[0:4, :] * (1.0 / INNER) + EPS)
        stat[0:4, :] = root
        stat[4:8, :] = root * root * root * (sums[4:8, :] * (1.0 / INNER))
        columns = jnp.transpose(stat[...])
        gain = jnp.concatenate([prm[0, 5:6, :], prm[1, 5:6, :]], axis=1)
        leave(5).start()
        gain_grad = jnp.zeros((1, WIDE), F32)
        moved = []
        for k in range(BLOCKS):
            at = slice(k * BLOCK, (k + 1) * BLOCK)
            gp, gm = gps[at, :], gms[at, :]
            normal = gp * columns[:, k : k + 1]
            gain_grad = gain_grad + jnp.sum(gm * normal, axis=0, keepdims=True)
            mixed[at, :] = (normal * gain).astype(BF16)
            gated = (gm * gain) * columns[:, k : k + 1] - gp * columns[:, BLOCKS + k : BLOCKS + k + 1]
            gms[at, :] = gated * acts[at, :]
            gg[at, :] = (gated * slopes[at, :]).astype(BF16)
            block = pl.ds(k * BLOCK, BLOCK)
            for src, dst in ((mixed, mixed_out), (gms, gs_out), (gg, gg_out)):
                moved.append(pltpu.make_async_copy(src.at[block], dst.at[block], local.at[14 + len(moved)]))
                moved[-1].start()
        gains_out[...] = jnp.concatenate([gain_grad, jnp.zeros((7, WIDE), F32)], axis=0)
        for copy in c1 + c2 + q + o1 + o2 + o3 + o4 + oc:
            copy.left()
        for copy in moved:
            copy.wait()
        for n in range(len(pairs)):
            leave(n).wait()


def run_front(*args):
    first = lambda k: jnp.minimum(k, BLOCKS - 1)
    keep = lambda *s: pl.BlockSpec(s, lambda k: (0,) * len(s))
    block = lambda n: pl.BlockSpec((BLOCK, n), lambda k: (first(k), 0))
    small = lambda: pl.BlockSpec((GROUPS, BLOCK, 128), lambda k: (0, first(k), 0))
    wide = SHAPE((LEN, WIDE), F32)
    narrow = SHAPE((GROUPS, LEN, 128), F32)
    bf = lambda *s: pltpu.VMEM(s, BF16)
    f32 = lambda *s: pltpu.VMEM(s, F32)
    return pl.pallas_call(
        front_kernel,
        grid=(2 * BLOCKS,),
        out_shape=[
            wide,
            wide,
            wide,
            SHAPE((BLOCKS, GROUPS, STATE, COLS), F32),
            narrow,
            narrow,
            narrow,
            SHAPE((LEN, 256), BF16),
            SHAPE((LEN, 256), F32),
            SHAPE((LEN, 256), F32),
            SHAPE((2, 2, 4, 96, LEN), BF16),
            SHAPE((8, WIDE), F32),
            SHAPE((LEN, WIDE), BF16),
            wide,
            SHAPE((LEN, WIDE), BF16),
            SHAPE((2, 2, 4, 96, LEN), BF16),
            SHAPE((LEN, D), BF16),
            SHAPE((2, 4, 2, 96, PROJ), BF16),
            SHAPE((2, 4, 2, 96, WIDE), BF16),
            SHAPE((2, 4, 2, 96, 256), BF16),
            SHAPE((GROUPS, 16, COLS), F32),
        ],
        in_specs=[ANY, VMEM, ANY, ANY, ANY, ANY] + [VMEM] * 9 + [ANY],
        out_specs=[
            block(WIDE),
            block(WIDE),
            block(WIDE),
            pl.BlockSpec((1, GROUPS, STATE, COLS), lambda k: (first(k), 0, 0, 0)),
            small(),
            small(),
            small(),
            block(256),
            block(256),
            block(256),
            pl.BlockSpec((2, 2, 4, 96, BLOCK), lambda k: (0, 0, 0, 0, first(k))),
            keep(8, WIDE),
        ]
        + [ANY] * 9,
        scratch_shapes=[
            bf(LEN, D),
            bf(2, 4, 2, 96, PROJ),
            bf(2, 4, 2, 96, WIDE),
            bf(2, 4, 2, 96, 256),
            f32(GROUPS, 16, COLS),
            bf(256, D),
            bf(96, 128),
            f32(128, 128),
            f32(16, COLS),
            bf(LEN, D),
            f32(LEN, WIDE),
            f32(LEN, WIDE),
            f32(LEN, WIDE),
            f32(LEN, WIDE),
            bf(LEN, WIDE),
            bf(LEN, WIDE),
            bf(2, 2, 4, 96, LEN),
            f32(BLOCK + 8, WIDE),
            f32(BLOCK + 8, 256),
            f32(STATE, WIDE),
            f32(8, BLOCK),
            f32(4, 8, BLOCK),
        ]
        + sems(96)
        + [pltpu.SemaphoreType.DMA((26,))],
        compiler_params=pltpu.CompilerParams(collective_id=1, has_side_effects=True, vmem_limit_bytes=ROOM),
        name="front",
    )(*args)


def backward_kernel(
    gs_in, inner, zin, y, hin, prm, bc, dt, r, u, gains, mixed, wout, cot_t, gg, normed_t, tokens, zbc, bc_in, conv_bc,
    cat_out, acc, acc_bc, branch_out, wout_out, wgate_out,
    ext, extbc, dstate, dst, dbc, held, got, away, mv, wv, cv, gv, nv, ownb, g0, g1, g2, g3, s1, s2, s3, t1, t2, t3, send, recv, local,
):
    k = pl.program_id(0)
    net = Net(send, recv)
    cc, z = net.at["c"], net.at["z"]
    cross = [net.plan(lambda n=n: away.at[n], lambda n=n: got.at[n], "c") for n in range(2)]
    token = TokenSum(net, (g0, g1, g2, g3))
    rings = (GridSum(net, "y", held.at[0], ((0, COLS),), (s1, s2, s3)), GridSum(net, "x", held.at[1], ((0, COLS),), (t1, t2, t3)))

    @pl.when(k == 0)
    def _():
        loads = [pltpu.make_async_copy(src, dst, local.at[n]) for n, (src, dst) in enumerate(((mixed, mv), (wout, wv), (cot_t, cv), (gg, gv), (normed_t, nv)))]
        for copy in loads:
            copy.start()
        net.barrier([("z", 1), ("z", -1)] + [(a, s) for a in ("x", "y") for s in (1, -1, 2)] + [("c", 1)])
        loads[0].wait()
        loads[1].wait()
        branch = lambda place: dot_nt(mv[pl.ds(pl.multiple_of(place * 256, 256), 256), :], wv[...])
        grads = lambda left, right, core: dot(left[core].reshape(8 * 96, LEN), right[...]).astype(BF16).reshape(2, 4, 96, WIDE)
        g0[...] = branch(net.near("z", 2)).astype(BF16)
        token.step1()
        loads[2].wait()
        away[0] = grads(cv, mv, net.other)
        cross[0].start()
        loads[3].wait()
        loads[4].wait()
        away[1] = grads(nv, gv, net.other)
        cross[1].start()
        for p, step in HALVES:
            g2[p] = branch(net.near("z", step)).astype(BF16)
            token.folded(p)
        ownb[...] = branch(z)
        held[0] = grads(cv, mv, cc)
        held[1] = grads(nv, gv, cc)
        acc[...] = jnp.zeros_like(acc)
        acc_bc[...] = jnp.zeros_like(acc_bc)
        extbc[BLOCK : BLOCK + 8, :] = jnp.zeros((8, 256), F32)
        for g in range(GROUPS):
            acc[g, 5:6, :] = gains[0:1, g * COLS : (g + 1) * COLS]
        ext[BLOCK : BLOCK + 8, :] = jnp.zeros((8, WIDE), F32)
        dstate[...] = jnp.zeros_like(dstate)

    @pl.when(k > 0)
    def _():
        ext[BLOCK : BLOCK + 8, :] = ext[0:8, :]
        extbc[BLOCK : BLOCK + 8, :] = extbc[0:8, :]

    b, c = bc[:, :STATE], bc[:, STATE:]
    valid = iota((BLOCK, BLOCK), 1) >= iota((BLOCK, BLOCK), 0)
    scores = jnp.where(valid, dot_nt(b, c), 0.0)
    ones, fold = expander(), reducer()
    left = iota((BLOCK, 128), 1) < 64
    suffix, prefix = upper(), lower(strict=True)
    dst[...] = jnp.zeros_like(dst)
    dbc[...] = jnp.zeros_like(dbc)
    for g in range(GROUPS):
        if g == 0:

            @pl.when(k == 1)
            def _():
                token.step2()

            @pl.when(k == 3)
            def _():
                for ring in rings:
                    ring.step2()

        else:

            @pl.when(k == 0)
            def _():
                for n in range(2):
                    cross[n].arrived()
                    held[n] += got[n]
                    rings[n].step1()

        cut = slice(g * COLS, (g + 1) * COLS)
        yv = y[:, cut]
        gs = gs_in[:, cut]
        xi = inner[:, cut]
        zv = zin[:, cut]
        zs = sigmoid(zv)
        xv = zv * zs
        rv = r[g]
        rt = jnp.transpose(rv)
        last = rv[BLOCK - 1 : BLOCK, :]
        dte = spread(dt[g], ones)
        grow = spread(jnp.exp2(rv), ones)
        tail = spread(jnp.exp2(last - rv), ones)
        skip = spread(prm[g, 8:16, 0:128], ones)[0:1, :]
        w = xv * dte
        wl = w.astype(BF16)
        gl = gs.astype(BF16)
        h = hin[0, g]
        dh = dstate[:, cut]
        dhl = dh.astype(BF16)
        parts = []
        for p in range(HEADS // 2):
            halves = []
            pair = slice(128 * p, 128 * (p + 1))
            wp, gpair = wl[:, pair], gl[:, pair]
            zero = jnp.zeros_like(wp)
            w_low = pltpu.roll(w[:, pair] - wp.astype(F32), 64, 1).astype(BF16)
            g_low = (gs[:, pair] - gpair.astype(F32)).astype(BF16)
            g_turn = pltpu.roll(gpair.astype(F32), 64, 1).astype(BF16)
            for n in (2 * p, 2 * p + 1):
                decay = jnp.exp2(jnp.minimum(rt[n : n + 1, :] - rv[:, n : n + 1], 0.0))
                halves.append(dot((scores * decay).astype(BF16), gpair))
                pick = (lambda a, b: jnp.where(left, a, b)) if n % 2 == 0 else (lambda a, b: jnp.where(left, b, a))
                one = jnp.concatenate([pick(wp, w_low), pick(wp, zero)], axis=1)
                two = jnp.concatenate([pick(gpair, g_turn), g_low], axis=1)
                dst[...] += dot_nt(one, two) * decay
            parts.append(jnp.where(left, halves[0], halves[1]))
        dwi = jnp.concatenate(parts, axis=1)
        dws = tail * dot(b, dhl)
        dw = dwi + dws
        skipgrad = gs * xv
        diff = folded(gl.astype(F32) * (yv - skip * xv) - wl.astype(F32) * dwi, fold)
        zsum = folded(w * dws, fold)
        const = folded(jnp.sum(h * dh, axis=0, keepdims=True) * grow[BLOCK - 1 : BLOCK, :] + jnp.zeros((8, COLS), F32), fold)
        da = dot_right(suffix, diff, 3) + dot_right(prefix, zsum, 3) + const[0:1, :]
        rate = -jnp.exp(prm[g, 7:8, 0:128])
        dstep = (folded(xv * dw, fold) + rate * da) * sigmoid(u[g])
        cat_out[:, WIDE + 128 * g : WIDE + 128 * (g + 1)] = dstep.astype(BF16)
        gx = (grow * gs).astype(BF16)
        dbc[:, STATE:] += dot_nt(gx, h.astype(BF16))
        dbc[:, :STATE] += dot_nt((tail * w).astype(BF16), dhl)
        dstate[:, cut] = grow[BLOCK - 1 : BLOCK, :] * dh + dot_tn(c, gx)
        dx = dte * dw + skip * gs
        dz = dx * (zs * (1.0 + zv * (1.0 - zs)))
        ext[0:BLOCK, cut] = dz
        gi = jnp.zeros((BLOCK, COLS), F32)
        for j in range(4):
            moved = ext[3 - j : 3 - j + BLOCK, cut]
            gi = gi + prm[g, j : j + 1, :] * moved
            acc[g, j : j + 1, :] += jnp.sum(xi * moved, axis=0, keepdims=True)
        cat_out[:, cut] = gi.astype(BF16)
        acc[g, 4:5, :] += jnp.sum(dz, axis=0, keepdims=True)
        acc[g, 6:7, 0:128] += jnp.sum(dstep, axis=0, keepdims=True)
        acc[g, 7:8, 0:128] += jnp.sum(da * dt[g], axis=0, keepdims=True) * rate
        acc[g, 8:9, 0:128] += folded(jnp.sum(skipgrad, axis=0, keepdims=True) + jnp.zeros((8, COLS), F32), fold)[0:1, :]
    ds = jnp.where(valid, dst[...], 0.0).astype(BF16)
    dbc[:, STATE:] += dot_tn(ds, b)
    dbc[:, :STATE] += dot(ds, c)
    zb = zbc[...]
    sig = sigmoid(zb)
    dz = dbc[...] * (sig + zb * sig * (1.0 - sig))
    extbc[0:BLOCK, :] = dz
    bi = bc_in[...]
    gi = jnp.zeros((BLOCK, 256), F32)
    for j in range(4):
        moved = extbc[3 - j : 3 - j + BLOCK, :]
        gi = gi + conv_bc[j : j + 1, :] * moved
        acc_bc[j : j + 1, :] += jnp.sum(bi * moved, axis=0, keepdims=True)
    acc_bc[4:5, :] += jnp.sum(dz, axis=0, keepdims=True)
    cat_out[:, MORE:] = gi.astype(BF16)

    @pl.when(k == BLOCKS - 1)
    def _():
        rings[0].step3(wout_out)
        rings[1].step3(wgate_out)
        branch_out[...] = (tokens[...].astype(F32) + (ownb[...] + token.step3())).astype(BF16)
        for copy in net.copies:
            copy.left()


def run_backward(*args):
    rev = lambda k: BLOCKS - 1 - k
    cols = lambda n: pl.BlockSpec((BLOCK, n), lambda k: (rev(k), 0))
    small = lambda: pl.BlockSpec((GROUPS, BLOCK, 128), lambda k: (0, rev(k), 0))
    keep = lambda *s: pl.BlockSpec(s, lambda k: (0,) * len(s))
    bf = lambda *s: pltpu.VMEM(s, BF16)
    f32 = lambda *s: pltpu.VMEM(s, F32)
    return pl.pallas_call(
        backward_kernel,
        grid=(BLOCKS,),
        out_shape=[
            SHAPE((LEN, MORE + 256), BF16),
            SHAPE((GROUPS, 16, COLS), F32),
            SHAPE((8, 256), F32),
            SHAPE((256, D), BF16),
            SHAPE((96, COLS), F32),
            SHAPE((96, COLS), F32),
        ],
        in_specs=[cols(WIDE)] * 4
        + [
            pl.BlockSpec((1, GROUPS, STATE, COLS), lambda k: (rev(k), 0, 0, 0)),
            keep(GROUPS, 16, COLS),
            cols(256),
            small(),
            small(),
            small(),
            keep(8, WIDE),
        ]
        + [ANY] * 5
        + [keep(256, D), cols(256), cols(256), keep(4, 256)],
        out_specs=[cols(MORE + 256), keep(GROUPS, 16, COLS), keep(8, 256), keep(256, D), keep(96, COLS), keep(96, COLS)],
        scratch_shapes=[
            f32(BLOCK + 8, WIDE),
            f32(BLOCK + 8, 256),
            f32(STATE, WIDE),
            f32(BLOCK, BLOCK),
            f32(BLOCK, 256),
            bf(2, 2, 4, 96, WIDE),
            bf(2, 2, 4, 96, WIDE),
            bf(2, 2, 4, 96, WIDE),
            bf(LEN, WIDE),
            bf(D, WIDE),
            bf(2, 2, 4, 96, LEN),
            bf(LEN, WIDE),
            bf(2, 2, 4, 96, LEN),
            f32(256, D),
        ]
        + token_scratch()
        + grid_scratch("y", COLS)
        + grid_scratch("x", COLS)
        + sems(26)
        + [pltpu.SemaphoreType.DMA((5,))],
        compiler_params=pltpu.CompilerParams(collective_id=2, has_side_effects=True, vmem_limit_bytes=ROOM),
        name="backward",
    )(*args)


def tail_kernel(
    gg, cat, wx, normed_t, normed, acc, acc_bc, wbc, gain,
    tokens_out, inner_out, bc_out, small_out,
    ggv, catv, wxv, ntv, nv, wv, ownb, held, got, away, dbw, heldb, gotb, small, sp0, sp1, sp2, sp3, bz, by,
    g0, g1, g2, g3, a1, a2, a3, b1, b2, b3, c1, c2, c3, send, recv, local,
):
    net = Net(send, recv)
    at = net.at
    yh, cx, cc, z, y = at["yh"], at["x"], at["c"], at["z"], at["y"]
    pairs = ((cat, catv), (gg, ggv), (wx, wxv), (wbc, wv), (normed, nv), (normed_t, ntv))
    loads = [pltpu.make_async_copy(src, dst, local.at[i]) for i, (src, dst) in enumerate(pairs)]
    for copy in loads:
        copy.start()
    token = TokenSum(net, (g0, g1, g2, g3))
    spans = ((0, COLS), (WIDE, 128))
    rings = (GridSum(net, "x", held, spans, (a1, a2, a3), (0, 48)), GridSum(net, "y", held, spans, (b1, b2, b3), (48, 48)))
    ring_bc = GridSum(net, "x", heldb, ((0, 128),), (c1, c2, c3))
    net.barrier([(a, s) for a in ("z", "x", "y") for s in (1, -1, 2)] + [("c", 1)])

    def block(place):
        cut = pl.ds(pl.multiple_of(place * 256, 256), 256)
        return dot_nt(ggv[cut, :], wxv[:, 0:WIDE]) + dot_nt(catv[cut, 0:MORE], wxv[:, WIDE:]) + dot_nt(catv[cut, MORE:], wv[...])

    def of_norm(place, grad):
        cut = pl.ds(pl.multiple_of(place * 256, 256), 256)
        return jnp.sum(grad * nv[cut, :].astype(F32), axis=0, keepdims=True)

    for copy in loads[:4]:
        copy.wait()
    far = block(net.near("z", 2))
    g0[...] = far.astype(BF16)
    token.step1()
    loads[4].wait()
    norm_part = of_norm(net.near("z", 2), far)
    for p, step in HALVES:
        out = block(net.near("z", step))
        g2[p] = out.astype(BF16)
        norm_part = norm_part + of_norm(net.near("z", step), out)
    ownb[...] = block(z)
    norm_part = (norm_part + of_norm(z, ownb[...])) / gain[...].reshape(1, D)
    small[0:16, :] = acc[0]
    small[16:32, :] = acc[1]
    small[32:48, :] = jnp.zeros((16, COLS), F32)
    for k in range(4):
        small[32 + k : 33 + k, :] = norm_part[:, k * COLS : (k + 1) * COLS]
    small[36:41, 0:256] = acc_bc[0:5, :]
    sp0[z] = small[32:48, :]
    q = net.around(sp0.at[z], sp0.at[z], "z")
    for p, _ in HALVES:
        token.folded(p)
    loads[5].wait()
    grads = lambda core, cut, n: dot(ntv[core].reshape(8 * 96, LEN), catv[:, cut]).astype(BF16).reshape(2, 4, 96, n)
    for core in range(2):
        dbw[core] = grads(core, slice(MORE, MORE + 256), 256)
    crossb = net.start(dbw.at[net.other], gotb, "c")
    away[...] = grads(net.other, slice(0, MORE), MORE)
    cross = net.start(away, got, "c")
    crossb.arrived()
    heldb[...] = dbw[cc] + gotb[...]
    ring_bc.step1()
    held[...] = grads(cc, slice(0, MORE), MORE)
    cross.arrived()
    held[...] += got[...]
    arrive(q)
    sp1[cx, 0:32, :] = small[0:32, :]
    sp1[cx, 32:48, :] = (sp0[0] + sp0[1]) + (sp0[2] + sp0[3])
    q = net.around(sp1.at[cx], sp1.at[cx], "x")
    ring_bc.step2()
    for ring in rings:
        ring.step1()
    token.step2()
    arrive(q)
    sp2[y] = (sp1[0] + sp1[1]) + (sp1[2] + sp1[3])
    q = net.around(sp2.at[y], sp2.at[y], "y")
    ring_bc.step3(by.at[yh])
    qb = [net.start(by.at[yh], by.at[yh], "y", 2)]
    for ring in rings:
        ring.step2()
    arrive(qb)
    bz[z, :, 0:128] = by[0]
    bz[z, :, 128:256] = by[1]
    qb = net.around(bz.at[z], bz.at[z], "z")
    arrive(q)
    sp3[cc] = (sp2[0] + sp2[1]) + (sp2[2] + sp2[3])
    q = [net.start(sp3.at[cc], sp3.at[cc], "c")]
    for ring in rings:
        ring.step3(inner_out)
    arrive(q)
    small_out[...] = sp3[0] + sp3[1]
    tokens_out[...] = token.step3() + ownb[...]
    arrive(qb)
    bc_out[...] = (bz[0] + bz[1]) + (bz[2] + bz[3])
    net.finish()


def run_tail(*args):
    bf = lambda *s: pltpu.VMEM(s, BF16)
    f32 = lambda *s: pltpu.VMEM(s, F32)
    return pl.pallas_call(
        tail_kernel,
        out_shape=[
            SHAPE((256, D), F32),
            SHAPE((96, COLS + 128), F32),
            SHAPE((96, 256), F32),
            SHAPE((48, COLS), F32),
        ],
        in_specs=[ANY] * 5 + [VMEM, VMEM, ANY, VMEM],
        out_specs=[VMEM] * 4,
        scratch_shapes=[
            bf(LEN, WIDE),
            bf(LEN, MORE + 256),
            bf(D, PROJ),
            bf(2, 2, 4, 96, LEN),
            bf(LEN, D),
            bf(D, 256),
            f32(256, D),
            bf(2, 4, 96, MORE),
            bf(2, 4, 96, MORE),
            bf(2, 4, 96, MORE),
            bf(2, 2, 4, 96, 256),
            bf(2, 4, 96, 256),
            bf(2, 4, 96, 256),
            f32(48, COLS),
            f32(4, 16, COLS),
            f32(4, 48, COLS),
            f32(4, 48, COLS),
            f32(2, 48, COLS),
            f32(4, 96, 256),
            f32(2, 96, 128),
        ]
        + token_scratch()
        + grid_scratch("x", COLS + 128, 48)
        + grid_scratch("y", COLS + 128, 48)
        + grid_scratch("x", 128)
        + sems(64)
        + [pltpu.SemaphoreType.DMA((6,))],
        compiler_params=pltpu.CompilerParams(collective_id=3, has_side_effects=True, vmem_limit_bytes=ROOM),
        name="tail",
    )(*args)


def finish_kernel(grad, tokens, cot, branch, norm_gain, inner, bc, small, gate, wout, tokens_out, branch_out, inner_out, bc_out, gate_out, wout_out, step_out, norm, conv, bias, conv_bc, bias_bc, step_bias, decay, skip, gain):
    v = tokens[...].astype(F32)
    root = lax.rsqrt(jnp.mean(v * v, axis=1, keepdims=True) + EPS)
    scaled = grad[...] * norm_gain[...].reshape(1, D)
    tokens_out[...] = cot[...].astype(F32) + root * scaled - v * (root * root * root) * jnp.mean(scaled * v, axis=1, keepdims=True)
    branch_out[...] = branch[...]

    @pl.when(pl.program_id(0) == 0)
    def _():
        inner_out[...] = inner[:, :COLS]
        bc_out[...] = bc[...]
        gate_out[...] = gate[...]
        wout_out[...] = wout[...]
        step_out[...] = jnp.transpose(jnp.concatenate([inner[:, COLS:], jnp.zeros((32, 128), F32)], axis=0))[0:HEADS, 0:96]
        norm[...] = jnp.concatenate([small[32 + k : 33 + k, :] for k in range(4)], axis=1).reshape(D)
        conv_bc[...] = small[36:40, 0:256]
        bias_bc[...] = small[40:41, 0:256].reshape(256)
        mine = small[pl.ds(pl.multiple_of(lax.axis_index("yh") * 16, 8), 16), :]
        conv[...] = mine[0:4, :]
        bias[...] = mine[4:5, :].reshape(COLS)
        gain[...] = mine[5:6, :].reshape(COLS)
        step_bias[...] = mine[6:7, 0:HEADS].reshape(HEADS)
        decay[...] = mine[7:8, 0:HEADS].reshape(HEADS)
        skip[...] = mine[8:9, 0:HEADS].reshape(HEADS)


def run_finish(*args):
    f32 = lambda *s: SHAPE(s, F32)
    strip = lambda: pl.BlockSpec((64, D), lambda k: (k, 0))
    whole = lambda *s: pl.BlockSpec(s, lambda k: (0,) * len(s))
    shapes = (
        (96, COLS), (96, 256), (96, COLS), (96, COLS), (HEADS, 96), (D,), (4, COLS), (COLS,), (4, 256), (256,), (HEADS,), (HEADS,), (HEADS,), (COLS,),
    )
    return pl.pallas_call(
        finish_kernel,
        grid=(4,),
        out_shape=[f32(256, D), SHAPE((256, D), BF16)] + [f32(*s) for s in shapes],
        in_specs=[strip(), strip(), strip(), strip()]
        + [whole(*s) for s in ((D,), (96, COLS + 128), (96, 256), (48, COLS), (96, COLS), (96, COLS))],
        out_specs=[strip(), strip()] + [whole(*s) for s in shapes],
        compiler_params=pltpu.CompilerParams(vmem_limit_bytes=ROOM),
        name="finish",
    )(*args)


def shards(tokens, norm_gain, w_gate, w_inner, w_bc, w_step, conv_inner, bias_inner, conv_bc, bias_bc, step_bias, decay_log, skip_gain, gate_gain, w_out, cotangent):
    (
        inner, zin, y, hin, dt, r, u, bc, bc_in, zbc, normed_t, gains, mixed, gs, gg, cot_t, normed, wx, wout, wbc, prm,
    ) = run_front(
        tokens, norm_gain, w_gate, w_inner, w_out, w_bc, w_step.T, conv_inner, bias_inner, gate_gain, step_bias, decay_log,
        skip_gain, conv_bc, bias_bc, cotangent,
    )
    wx, wout, wbc = wx.reshape(D, PROJ), wout.reshape(D, WIDE), wbc.reshape(D, 256)
    cat, acc, acc_bc, output, wout_grad, gate_grad = run_backward(
        gs, inner, zin, y, hin, prm, bc, dt, r, u, gains, mixed, wout, cot_t, gg, normed_t, tokens, zbc, bc_in, conv_bc
    )
    grad, inner_grad, bc_grad, small = run_tail(gg, cat, wx, normed_t, normed, acc, acc_bc, wbc, norm_gain)
    (
        tokens_grad, output, inner_grad, bc_grad, gate_grad, wout_grad, step_grad,
        norm, conv, bias, conv_bc_grad, bias_bc_grad, step_bias_grad, decay, skip, gate_gain_grad,
    ) = run_finish(grad, tokens, cotangent, output, norm_gain, inner_grad, bc_grad, small, gate_grad, wout_grad)
    return (
        output, tokens_grad, norm, gate_grad, inner_grad, bc_grad, step_grad.T, conv, bias, conv_bc_grad,
        bias_bc_grad, step_bias_grad, decay, skip, gate_gain_grad, wout_grad,
    )


def solution(mesh):
    fine = Mesh(mesh.devices.reshape(2, 4, 2, 2, 4), AXES)
    dp, tensor = ("yl", "x", "c"), ("yh", "z")
    tokens, weight = P(dp + tensor, None), P(dp, tensor)
    heads, shared = P(tensor), P()
    return jax.shard_map(
        shards,
        mesh=fine,
        in_specs=(
            tokens, shared, weight, weight, P(dp, None), weight, P(None, tensor), heads,
            shared, shared, heads, heads, heads, heads, weight, tokens,
        ),
        out_specs=(
            tokens, tokens, shared, weight, weight, P(dp, None), weight, P(None, tensor), heads,
            shared, shared, heads, heads, heads, heads, weight,
        ),
        check_vma=False,
    )
```

```python
import jax
import jax.numpy as jnp
from jax import lax
from jax.experimental import pallas as pl
from jax.experimental.pallas import tpu as pltpu
from jax.sharding import Mesh
from jax.sharding import PartitionSpec as P

D = 1536
LEN = 1024
INNER = 3072
STATE = 128
BLOCK = 256
BLOCKS = LEN // BLOCK
GROUPS = 2
HEADS = 6
COLS = HEADS * 64
WIDE = GROUPS * COLS
STEPS = 2 * WIDE
PROJ = STEPS + GROUPS * 128
MORE = PROJ - WIDE
LOG2E = 1.4426950408889634
EPS = 1e-05
F32 = jnp.float32
BF16 = jnp.bfloat16
MESH = pl.DeviceIdType.MESH
AXES = ("yl", "x", "c", "yh", "z")
ANY = pl.BlockSpec(memory_space=pl.ANY)
VMEM = pl.BlockSpec(memory_space=pltpu.VMEM)
SHAPE = jax.ShapeDtypeStruct
ROOM = 60 * 2**20


def dot(a, b):
    return jnp.dot(a, b, preferred_element_type=F32)


def dot_nt(a, b):
    return lax.dot_general(a, b, (((1,), (1,)), ((), ())), preferred_element_type=F32)


def dot_tn(a, b):
    return lax.dot_general(a, b, (((0,), (0,)), ((), ())), preferred_element_type=F32)


def pieces(v, n):
    out = []
    for _ in range(n):
        hi = v.astype(BF16)
        out.append(hi)
        v = v - hi.astype(F32)
    return out


def dot_left(v, ones, n):
    return sum(dot(p, ones) for p in pieces(v, n))


def spread(v, ones):
    hi = v.astype(BF16).astype(F32)
    low = pltpu.roll(v - hi, 64, 1)
    return dot(jnp.where(iota(v.shape, 1) < 64, hi, low).astype(BF16), ones)


def folded(v, ones):
    hi = v.astype(BF16)
    low = (v - hi.astype(F32)).astype(BF16)
    return dot(hi, ones) + dot(low, ones)


def dot_right(ones, v, n):
    return sum(dot(ones, p) for p in pieces(v, n))


def iota(shape, axis):
    return lax.broadcasted_iota(jnp.int32, shape, axis)


def expander():
    row, col = iota((128, COLS), 0), iota((128, COLS), 1)
    return ((row & 63) == lax.shift_right_logical(col, 6)).astype(BF16)


def reducer():
    row, col = iota((COLS, 128), 0), iota((COLS, 128), 1)
    return (col == lax.shift_right_logical(row, 6)).astype(BF16)


def sigmoid(v):
    return 0.5 * jnp.tanh(0.5 * v) + 0.5


def lower(strict=False):
    row, col = iota((BLOCK, BLOCK), 0), iota((BLOCK, BLOCK), 1)
    return ((row > col) if strict else (row >= col)).astype(BF16)


def upper():
    return (iota((BLOCK, BLOCK), 0) <= iota((BLOCK, BLOCK), 1)).astype(BF16)


def token_row(v):
    v = sum(v[:, 128 * i : 128 * (i + 1)] for i in range(v.shape[1] // 128))
    ones = jnp.ones((8, 128), BF16)
    return sum(dot_nt(ones, p) for p in pieces(v, 3))[0:1, :]


class Net:
    def __init__(self, send, recv):
        self.send, self.recv, self.copies = send, recv, []
        self.at = {name: lax.axis_index(name) for name in AXES}
        self.at["y"] = self.at["yh"] * 2 + self.at["yl"]
        self.places = {(a, s): lax.rem(self.at[a] + s + 4, 4) for a in ("x", "y", "z") for s in (1, -1, 2)}
        self.other = 1 - self.at["c"]
        self.targets = {("c", 1): {"c": self.other}}
        for (a, s), place in self.places.items():
            self.targets[a, s] = {"yh": place // 2, "yl": lax.rem(place, 2)} if a == "y" else {a: place}

    def near(self, axis, step):
        return self.places[axis, step]

    def plan(self, src, dst, axis, step=1):
        copy = Copy(self, len(self.copies), src, dst, self.targets[axis, step])
        self.copies.append(copy)
        return copy

    def start(self, src, dst, axis, step=1):
        return self.plan(lambda: src, lambda: dst, axis, step).start()

    def around(self, src, dst, axis):
        return [self.start(src, dst, axis, step) for step in (1, -1, 2)]

    def greet(self, peers):
        here, self.peers = pltpu.get_barrier_semaphore(), len(peers)
        for peer in peers:
            pl.semaphore_signal(here, inc=1, device_id=self.targets[peer], device_id_type=MESH)

    def met(self):
        pl.semaphore_wait(pltpu.get_barrier_semaphore(), self.peers)

    def finish(self):
        for copy in self.copies:
            copy.arrived()
        for copy in self.copies:
            copy.left()


class Copy:
    def __init__(self, net, index, src, dst, target):
        self.net, self.index, self.src, self.dst, self.target = net, index, src, dst, target
        self.here, self.gone = False, False

    def made(self):
        return pltpu.make_async_remote_copy(
            src_ref=self.src(),
            dst_ref=self.dst(),
            send_sem=self.net.send.at[self.index],
            recv_sem=self.net.recv.at[self.index],
            device_id=self.target,
            device_id_type=MESH,
        )

    def start(self):
        self.made().start()
        return self

    def arrived(self):
        if not self.here:
            self.here = True
            self.made().wait_recv()

    def left(self):
        if not self.gone:
            self.gone = True
            self.made().wait_send()


def sems(n):
    return [pltpu.SemaphoreType.DMA((n,)), pltpu.SemaphoreType.DMA((n,))]


def rows(ref, first, count):
    return ref.at[pl.ds(pl.multiple_of(first, 16), count)]


def lanes(first, count):
    return pl.ds(pl.multiple_of(first, 128), count)


def arrive(copies):
    for copy in copies:
        copy.arrived()


HALVES = ((0, 1), (1, -1))


class GridSum:
    def __init__(self, net, first, held, spans, scratch, cut=(0, 96)):
        self.net, self.first, self.held, self.spans = net, first, held, spans
        self.land, self.mid, self.last = scratch
        self.rows = pl.ds(*cut)
        self.one, self.two = [], []
        for slot, step in enumerate((2, 1, -1)):
            if first == "x":
                self.plan(self.one, lambda step=step: held.at[:, net.near("x", step), self.rows], lambda slot=slot: self.land.at[slot], "x", step)
            else:
                self.plan(self.two, lambda step=step: self.mid.at[net.near("x", step)], lambda slot=slot: self.last.at[slot], "x", step)
            lane = 0
            for base, n in spans:
                there = lambda step=step, base=base, n=n: lanes(base + (net.near("y", step) // 2) * n, n)
                if first == "x":
                    src = lambda step=step, there=there: self.mid.at[lax.rem(net.near("y", step), 2), :, there()]
                    self.plan(self.two, src, lambda slot=slot, lane=lane, n=n: self.last.at[slot, :, pl.ds(lane, n)], "y", step)
                else:
                    src = lambda step=step, there=there: held.at[lax.rem(net.near("y", step), 2), :, self.rows, there()]
                    self.plan(self.one, src, lambda slot=slot, lane=lane, n=n: self.land.at[slot, :, :, pl.ds(lane, n)], "y", step)
                lane += n

    def plan(self, to, src, dst, axis, step):
        to.append(self.net.plan(src, dst, axis, step))

    def step1(self):
        for copy in self.one:
            copy.start()

    def step2(self):
        arrive(self.one)
        at = self.net.at
        if self.first == "x":
            self.mid[...] = self.total(self.held[:, at["x"], self.rows], self.land, slice(None)).astype(BF16)
        else:
            lane = 0
            for base, n in self.spans:
                cut = slice(lane, lane + n)
                own = self.held[at["yl"], :, self.rows, lanes(base + at["yh"] * n, n)]
                self.mid[:, :, cut] = self.total(own, self.land, cut).astype(BF16)
                lane += n
        for copy in self.two:
            copy.start()

    def total(self, own, others, cut):
        return (own.astype(F32) + others[0, ..., cut].astype(F32)) + (others[1, ..., cut].astype(F32) + others[2, ..., cut].astype(F32))

    def step3(self, out):
        arrive(self.two)
        at = self.net.at
        if self.first == "y":
            out[self.rows, :] = self.total(self.mid[at["x"]], self.last, slice(None))
            return
        lane = 0
        for base, n in self.spans:
            cut = slice(lane, lane + n)
            out[self.rows, cut] = self.total(self.mid[at["yl"], :, lanes(base + at["yh"] * n, n)], self.last, cut)
            lane += n


def grid_scratch(first, width, count=96):
    blocks, wide = (2, 2 * width) if first == "x" else (4, width)
    return [pltpu.VMEM(s, BF16) for s in ((3, blocks, count, wide), (blocks, count, wide), (3, count, width))]


class TokenSum:
    def __init__(self, net, scratch):
        self.net, self.far, self.half, self.fold, self.whole = net, *scratch
        self.one = [
            net.plan(lambda p=p: self.far.at[pl.ds(128 * p, 128)], lambda p=p: self.half.at[p], "z", step) for p, step in HALVES
        ]
        half = lambda ref, p, n: ref.at[p, pl.ds(128 * n, 128)]
        self.ready = [net.plan(lambda p=p: half(self.fold, p, 1 - p), lambda p=p: half(self.whole, p, 1 - p), "z", step) for p, step in HALVES]
        self.added = [net.plan(lambda p=p: half(self.fold, p, p), lambda p=p: half(self.whole, p, p), "z", step) for p, step in HALVES]

    def step1(self):
        for copy in self.one:
            copy.start()

    def folded(self, p):
        self.ready[p].start()

    def step2(self):
        arrive(self.one)
        for p, _ in HALVES:
            self.fold[p, 128 * p : 128 * p + 128, :] += self.half[p]
            self.added[p].start()

    def step3(self):
        arrive(self.ready + self.added)
        return self.whole[0].astype(F32) + self.whole[1].astype(F32)


def token_scratch():
    return [pltpu.VMEM((256, D), BF16), pltpu.VMEM((2, 128, D), BF16), pltpu.VMEM((2, 256, D), BF16), pltpu.VMEM((2, 256, D), BF16)]


def front_kernel(
    x, gain, w_gate, w_inner, w_out, w_bc, w_step, conv, bias, gate_gain, step_bias, decay_log, skip_gain, conv_bc, bias_bc, cot,
    inner_out, z_out, y_out, h_out, dt_out, r_out, u_out, bc_out, bcin_out, zbc_out, normed_t, gains_out,
    mixed_out, gs_out, gg_out, cot_t, normed_out, wx_out, wout_out, wbc_out, prm_out,
    normed, wx, wout, wbc, prm, xv, stepv, stept, pk,
    cots, gps, acts, slopes, gms, mixed, gg, turned_c, ext, extbc, state, stat, slots, send, recv, local,
):
    i = pl.program_id(0)
    net = Net(send, recv)
    at = net.at
    yh, cx, cc, z, y = at["yh"], at["x"], at["c"], at["z"], at["y"]
    own_rows = lambda ref: rows(ref, z * 256, 256)
    order = ((0, 1), (1, -1), (1, 1), (0, -1))
    part = lambda ref, p, s: rows(ref, net.near("z", -s) * 256 + 128 * p, 128)
    c1 = [
        net.plan(lambda p=p: cot.at[pl.ds(128 * p, 128)], lambda p=p: rows(cots, z * 256 + 128 * p, 128), "z", s) for p, s in order
    ]
    c2 = [net.plan(lambda p=p, s=s: part(cots, p, s), lambda p=p, s=s: part(cots, p, s), "z", s) for p, s in HALVES]
    q = [net.plan(lambda: stat, lambda: slots.at[z], "z", step) for step in (1, -1, 2)]
    spot_o = lambda xx, cut=pl.ds(0, 96): wout.at[at["yl"], xx, cc, cut, lanes(yh * COLS, COLS)]
    line_o = lambda yy, cut=pl.ds(0, 96): wout.at[lax.rem(yy, 2), :, cc, cut, lanes((yy // 2) * COLS, COLS)]
    same = lambda ref, axis, step=1: net.plan(ref, ref, axis, step)
    o1 = [net.plan(lambda: w_out, lambda: spot_o(cx), "x", step) for _, step in HALVES]
    o2 = [same(lambda p=p, s=s: spot_o(net.near("x", -s), pl.ds(48 * p, 48)), "x", s) for p, s in HALVES]
    o3 = [same(lambda: line_o(y), "y", step) for _, step in HALVES]
    o4 = [same(lambda p=p, s=s: line_o(net.near("y", -s), pl.ds(48 * p, 48)), "y", s) for p, s in HALVES]
    oc = [same(lambda: line_o(y), "c")] + [same(lambda s=s: line_o(net.near("y", s)), "c") for s in (1, -1, 2)]
    own = lambda: pltpu.make_async_copy(cot, own_rows(cots), local.at[0])
    pairs = ((normed, normed_out), (wx, wx_out), (wbc, wbc_out), (prm, prm_out), (wout, wout_out), (turned_c, cot_t))
    leave = lambda n: pltpu.make_async_copy(*pairs[n], local.at[1 + n])

    @pl.when(i == 0)
    def _():
        load = pltpu.make_async_copy(x, xv, local.at[7])
        load.start()
        net.greet([("z", 1), ("z", -1), ("z", 2), ("x", 1), ("x", -1), ("y", 1), ("y", -1), ("y", 2), ("c", 1)])
        own().start()
        stept[...] = jnp.zeros_like(stept)
        stept[0:HEADS, 0:96] = w_step[...].astype(F32)
        stepv[...] = jnp.transpose(stept[...])[0:96, :].astype(BF16)
        pk[...] = jnp.zeros_like(pk)
        pk[0:4, :] = conv[...]
        pk[4:5, :] = bias[...].reshape(1, COLS)
        pk[5:6, :] = gate_gain[...].reshape(1, COLS)
        pk[6:7, 0:HEADS] = step_bias[...].reshape(1, HEADS)
        pk[7:8, 0:HEADS] = decay_log[...].reshape(1, HEADS)
        pk[8:9, 0:HEADS] = skip_gain[...].reshape(1, HEADS)
        first = {
            "x": ((w_gate, wx, 0, COLS), (w_bc.at[:, lanes(yh * 128, 128)], wbc, 0, 128)),
            "y": ((w_inner, wx, WIDE, COLS), (stepv, wx, STEPS, 128)),
        }
        then = {"x": "y", "y": "x"}
        done = []

        def go(src, dst, axis, step=1):
            done.append(net.start(src, dst, axis, step))
            return done[-1]

        def spot(ref, base, n, yy, xx, cut=pl.ds(0, 96)):
            return ref.at[lax.rem(yy, 2), xx, cc, cut, lanes(base + (yy // 2) * n, n)]

        def line(axis, ref, base, n, place, cut=pl.ds(0, 96)):
            if axis == "x":
                return ref.at[lax.rem(place, 2), :, cc, cut, lanes(base + (place // 2) * n, n)]
            return ref.at[:, place, cc, cut, lanes(base, 2 * n)]

        load.wait()
        v = xv[...].astype(F32)
        root = lax.rsqrt(jnp.mean(v * v, axis=1, keepdims=True) + EPS)
        normed[pl.ds(pl.multiple_of(z * 256, 256), 256), :] = (v * root * gain[...].reshape(1, D)).astype(BF16)
        net.met()
        zs = {}
        for p, s in order:
            here = rows(normed, z * 256 + 128 * p, 128)
            zs[p, s] = go(here, here, "z", s)
        sent = {"x": [], "y": []}
        for axis in ("x", "y"):
            for src, ref, base, n in first[axis]:
                sent[axis].append([go(src, spot(ref, base, n, y, cx), axis, step) for _, step in HALVES])
        mine = [
            pltpu.make_async_copy(src, spot(ref, base, n, y, cx), local.at[8 + k])
            for k, (src, ref, base, n) in enumerate(first["x"] + first["y"])
        ]
        mine.append(pltpu.make_async_copy(pk, prm.at[yh], local.at[12]))
        mine.append(pltpu.make_async_copy(w_out, spot_o(cx), local.at[13]))
        for copy in mine:
            copy.start()
        for copy in o1:
            copy.start()
        for axis in ("x", "y"):
            for src, ref, base, n in first[axis]:
                go(src, spot(ref, base, n, y, cx), "c")
        go(pk, prm.at[yh], "y", 2)
        second = {"x": [], "y": []}
        for axis in ("x", "y"):
            for (src, ref, base, n), copies in zip(first[axis], sent[axis]):
                for (p, s), copy in zip(HALVES, copies):
                    copy.arrived()
                    cut = pl.ds(48 * p, 48)
                    here = spot(ref, base, n, y, net.near("x", -s), cut) if axis == "x" else spot(ref, base, n, net.near("y", -s), cx, cut)
                    second[axis].append(go(here, here, axis, s))
        for copy in mine:
            copy.wait()
        third = {"x": [], "y": []}
        for axis in ("x", "y"):
            arrive(second[axis])
            for src, ref, base, n in first[axis]:
                here = line(axis, ref, base, n, at[then[axis]])
                third[axis].append([go(here, here, then[axis], s) for _, s in HALVES])
        for copy, start in zip(o1, o2):
            copy.arrived()
            start.start()
        for axis in ("x", "y"):
            for src, ref, base, n in first[axis]:
                for s in (1, -1, 2):
                    here = spot(ref, base, n, y, net.near("x", s)) if axis == "x" else spot(ref, base, n, net.near("y", s), cx)
                    go(here, here, "c")
        for p, s in HALVES:
            zs[p, s].arrived()
            here = part(normed, p, s)
            go(here, here, "z", s)
        for copy in c1:
            copy.start()
        fourth = {"x": [], "y": []}
        for axis in ("x", "y"):
            for (src, ref, base, n), copies in zip(first[axis], third[axis]):
                for (p, s), copy in zip(HALVES, copies):
                    copy.arrived()
                    place = net.near(then[axis], -s)
                    here = line(axis, ref, base, n, place, pl.ds(48 * p, 48))
                    fourth[axis].append(go(here, here, then[axis], s))
                    here = line(axis, ref, base, n, place)
                    go(here, here, "c")
        arrive(o2)
        for copy in o3:
            copy.start()
        for axis in ("x", "y"):
            arrive(fourth[axis])
            for src, ref, base, n in first[axis]:
                here = line(axis, ref, base, n, net.near(then[axis], 2))
                go(here, here, "c")
        for copy in done:
            copy.arrived()
        for copy in done:
            copy.left()
        for n in range(4):
            leave(n).start()
        ext[0:8, :] = jnp.zeros((8, WIDE), F32)
        extbc[0:8, :] = jnp.zeros((8, 256), F32)
        state[...] = jnp.zeros_like(state)

    @pl.when((i > 0) & (i < BLOCKS))
    def _():
        ext[0:8, :] = ext[BLOCK : BLOCK + 8, :]
        extbc[0:8, :] = extbc[BLOCK : BLOCK + 8, :]

    @pl.when(i == 2)
    def _():
        for copy, start in zip(c1[:2], c2):
            copy.arrived()
            start.start()
        for copy, start in zip(o3, o4):
            copy.arrived()
            start.start()
        for copy in oc[:3]:
            copy.start()

    @pl.when(i < BLOCKS)
    def _():
        xb = normed[pl.ds(pl.multiple_of(i * BLOCK, BLOCK), BLOCK), :]
        turned = jnp.transpose(xb).reshape(2, 4, 2, 96, BLOCK)
        for core in range(2):
            normed_t[core] = turned[:, :, core]
        bc_in = dot(xb, wbc[...].reshape(D, 256))
        bcin_out[...] = bc_in
        extbc[8 : BLOCK + 8, :] = bc_in
        zb = bias_bc[...].reshape(1, 256) + sum(conv_bc[j : j + 1, :] * extbc[5 + j : 5 + j + BLOCK, :] for j in range(4))
        zbc_out[...] = zb
        bc = (zb * sigmoid(zb)).astype(BF16)
        bc_out[...] = bc
        b, c = bc[:, :STATE], bc[:, STATE:]
        scores = jnp.where(iota((BLOCK, BLOCK), 0) >= iota((BLOCK, BLOCK), 1), dot_nt(c, b), 0.0)
        tri, ones = lower(), expander()
        left = iota((BLOCK, 128), 1) < 64
        weight = lambda first, n: wx[:, :, :, :, first : first + n].reshape(D, n)
        steps = dot(xb, weight(STEPS, 256))
        total = jnp.zeros((BLOCK, 128), F32)
        for g in range(GROUPS):
            if g == 1:

                @pl.when(i == BLOCKS - 1)
                def _():
                    arrive(o4)
                    oc[3].start()

            cut = slice(g * COLS, (g + 1) * COLS)
            u = steps[:, 128 * g : 128 * (g + 1)] + prm[g, 6:7, 0:128]
            dt = jnp.maximum(u, 0.0) + jnp.log(1.0 + jnp.exp(-jnp.abs(u)))
            rate = -jnp.exp(prm[g, 7:8, 0:128]) * LOG2E
            r = dot_right(tri, dt * rate, 3)
            u_out[g] = u
            dt_out[g] = dt
            r_out[g] = r
            rt = jnp.transpose(r)
            gate = dot(xb, weight(g * COLS, COLS))
            inner = dot(xb, weight(WIDE + g * COLS, COLS))
            inner_out[:, cut] = inner
            ext[8 : BLOCK + 8, cut] = inner
            zv = prm[g, 4:5, :] + sum(prm[g, j : j + 1, :] * ext[5 + j : 5 + j + BLOCK, cut] for j in range(4))
            z_out[:, cut] = zv
            xv = zv * sigmoid(zv)
            last = r[BLOCK - 1 : BLOCK, :]
            w = xv * spread(dt, ones)
            grow = spread(jnp.exp2(r), ones)
            tail = spread(jnp.exp2(last - r), ones)
            skip = spread(prm[g, 8:16, 0:128], ones)[0:1, :]
            wl = w.astype(BF16)
            h = state[:, cut]
            h_out[0, g] = h
            parts = []
            for p in range(HEADS // 2):
                halves = []
                for n in (2 * p, 2 * p + 1):
                    gap = jnp.minimum(r[:, n : n + 1] - rt[n : n + 1, :], 0.0)
                    halves.append(dot((scores * jnp.exp2(gap)).astype(BF16), wl[:, 128 * p : 128 * (p + 1)]))
                parts.append(jnp.where(left, halves[0], halves[1]))
            yv = jnp.concatenate(parts, axis=1) + grow * dot(c, h.astype(BF16)) + skip * xv
            y_out[:, cut] = yv
            state[:, cut] = grow[BLOCK - 1 : BLOCK, :] * h + dot_tn(b, (tail * w).astype(BF16))
            sig = sigmoid(gate)
            act = gate * sig
            gp = yv * act
            here_now = pl.ds(pl.multiple_of(i * BLOCK, BLOCK), BLOCK)
            gps[here_now, cut] = gp
            acts[here_now, cut] = act
            slopes[here_now, cut] = yv * (sig + act * (1.0 - sig))
            sq = gp * gp
            total = total + (sq[:, 0:128] + sq[:, 128:256] + sq[:, 256:384])
        stat[pl.ds(i, 1), :] = token_row(total)

    @pl.when(i == BLOCKS)
    def _():
        own().wait()
        arrive(oc)
        leave(4).start()

    @pl.when(i == BLOCKS + 1)
    def _():
        arrive(c1)

    @pl.when(i == 2 * BLOCKS - 1)
    def _():
        for copy in c2:
            copy.arrived()

    @pl.when(i >= BLOCKS)
    def _():
        t = i - BLOCKS
        block = lax.rem(z + t + lax.div(t, 2) - 2 * lax.div(t, 3), 4)
        at = pl.ds(pl.multiple_of(block * BLOCK, BLOCK), BLOCK)
        cb = cots[at, :]
        turned = jnp.transpose(cb).reshape(2, 4, 2, 96, BLOCK)
        for core in range(2):
            turned_c[core, :, :, :, at] = turned[:, :, core]
        gm = dot(cb, wout[...].reshape(D, WIDE))
        gms[at, :] = gm
        gain = jnp.concatenate([prm[0, 5:6, :], prm[1, 5:6, :]], axis=1)
        stat[pl.ds(BLOCKS + block, 1), :] = token_row(gm * gain * gps[at, :])

    @pl.when(i == 2 * BLOCKS - 1)
    def _():
        for copy in q:
            copy.start()
        slots[z] = stat[...]
        for copy in q:
            copy.arrived()
            copy.left()
        sums = (slots[0] + slots[1]) + (slots[2] + slots[3])
        root = lax.rsqrt(sums[0:4, :] * (1.0 / INNER) + EPS)
        stat[0:4, :] = root
        stat[4:8, :] = root * root * root * (sums[4:8, :] * (1.0 / INNER))
        columns = jnp.transpose(stat[...])
        gain = jnp.concatenate([prm[0, 5:6, :], prm[1, 5:6, :]], axis=1)
        leave(5).start()
        gain_grad = jnp.zeros((1, WIDE), F32)
        moved = []
        for k in range(BLOCKS):
            at = slice(k * BLOCK, (k + 1) * BLOCK)
            gp, gm = gps[at, :], gms[at, :]
            normal = gp * columns[:, k : k + 1]
            gain_grad = gain_grad + jnp.sum(gm * normal, axis=0, keepdims=True)
            mixed[at, :] = (normal * gain).astype(BF16)
            gated = (gm * gain) * columns[:, k : k + 1] - gp * columns[:, BLOCKS + k : BLOCKS + k + 1]
            gms[at, :] = gated * acts[at, :]
            gg[at, :] = (gated * slopes[at, :]).astype(BF16)
            block = pl.ds(k * BLOCK, BLOCK)
            for src, dst in ((mixed, mixed_out), (gms, gs_out), (gg, gg_out)):
                moved.append(pltpu.make_async_copy(src.at[block], dst.at[block], local.at[14 + len(moved)]))
                moved[-1].start()
        gains_out[...] = jnp.concatenate([gain_grad, jnp.zeros((7, WIDE), F32)], axis=0)
        for copy in c1 + c2 + q + o1 + o2 + o3 + o4 + oc:
            copy.left()
        for copy in moved:
            copy.wait()
        for n in range(len(pairs)):
            leave(n).wait()


def run_front(*args):
    first = lambda k: jnp.minimum(k, BLOCKS - 1)
    keep = lambda *s: pl.BlockSpec(s, lambda k: (0,) * len(s))
    block = lambda n: pl.BlockSpec((BLOCK, n), lambda k: (first(k), 0))
    small = lambda: pl.BlockSpec((GROUPS, BLOCK, 128), lambda k: (0, first(k), 0))
    wide = SHAPE((LEN, WIDE), F32)
    narrow = SHAPE((GROUPS, LEN, 128), F32)
    bf = lambda *s: pltpu.VMEM(s, BF16)
    f32 = lambda *s: pltpu.VMEM(s, F32)
    return pl.pallas_call(
        front_kernel,
        grid=(2 * BLOCKS,),
        out_shape=[
            wide,
            wide,
            wide,
            SHAPE((BLOCKS, GROUPS, STATE, COLS), F32),
            narrow,
            narrow,
            narrow,
            SHAPE((LEN, 256), BF16),
            SHAPE((LEN, 256), F32),
            SHAPE((LEN, 256), F32),
            SHAPE((2, 2, 4, 96, LEN), BF16),
            SHAPE((8, WIDE), F32),
            SHAPE((LEN, WIDE), BF16),
            wide,
            SHAPE((LEN, WIDE), BF16),
            SHAPE((2, 2, 4, 96, LEN), BF16),
            SHAPE((LEN, D), BF16),
            SHAPE((2, 4, 2, 96, PROJ), BF16),
            SHAPE((2, 4, 2, 96, WIDE), BF16),
            SHAPE((2, 4, 2, 96, 256), BF16),
            SHAPE((GROUPS, 16, COLS), F32),
        ],
        in_specs=[ANY, VMEM, ANY, ANY, ANY, ANY] + [VMEM] * 9 + [ANY],
        out_specs=[
            block(WIDE),
            block(WIDE),
            block(WIDE),
            pl.BlockSpec((1, GROUPS, STATE, COLS), lambda k: (first(k), 0, 0, 0)),
            small(),
            small(),
            small(),
            block(256),
            block(256),
            block(256),
            pl.BlockSpec((2, 2, 4, 96, BLOCK), lambda k: (0, 0, 0, 0, first(k))),
            keep(8, WIDE),
        ]
        + [ANY] * 9,
        scratch_shapes=[
            bf(LEN, D),
            bf(2, 4, 2, 96, PROJ),
            bf(2, 4, 2, 96, WIDE),
            bf(2, 4, 2, 96, 256),
            f32(GROUPS, 16, COLS),
            bf(256, D),
            bf(96, 128),
            f32(128, 128),
            f32(16, COLS),
            bf(LEN, D),
            f32(LEN, WIDE),
            f32(LEN, WIDE),
            f32(LEN, WIDE),
            f32(LEN, WIDE),
            bf(LEN, WIDE),
            bf(LEN, WIDE),
            bf(2, 2, 4, 96, LEN),
            f32(BLOCK + 8, WIDE),
            f32(BLOCK + 8, 256),
            f32(STATE, WIDE),
            f32(8, BLOCK),
            f32(4, 8, BLOCK),
        ]
        + sems(96)
        + [pltpu.SemaphoreType.DMA((26,))],
        compiler_params=pltpu.CompilerParams(collective_id=1, has_side_effects=True, vmem_limit_bytes=ROOM),
        name="front",
    )(*args)


def later(v, after, step):
    turned = pltpu.roll(v, BLOCK - step, 0)
    ends = jnp.where(iota(after.shape, 0) < 8 - step, turned[BLOCK - 8 :, :], pltpu.roll(after, 8 - step, 0))
    return jnp.concatenate([turned[: BLOCK - 8, :], ends], axis=0)


def backward_kernel(
    gs_in, inner, zin, y, hin, prm, bc, dt, r, u, gains, mixed, wout, cot_t, gg, normed_t, tokens, zbc, bc_in, conv_bc,
    cat_out, acc, acc_bc, branch_out, wout_out, wgate_out,
    ext, extbc, dstate, dst, dbc, held, got, away, mv, wv, cv, gv, nv, ownb, g0, g1, g2, g3, s1, s2, s3, t1, t2, t3, send, recv, local,
):
    k = pl.program_id(0)
    net = Net(send, recv)
    cc, z = net.at["c"], net.at["z"]
    cross = [net.plan(lambda n=n: away.at[n], lambda n=n: got.at[n], "c") for n in range(2)]
    token = TokenSum(net, (g0, g1, g2, g3))
    rings = (GridSum(net, "y", held.at[0], ((0, COLS),), (s1, s2, s3)), GridSum(net, "x", held.at[1], ((0, COLS),), (t1, t2, t3)))

    @pl.when(k == 0)
    def _():
        net.greet([("z", 1), ("z", -1)] + [(a, s) for a in ("x", "y") for s in (1, -1, 2)] + [("c", 1)])
        loads = [pltpu.make_async_copy(src, dst, local.at[n]) for n, (src, dst) in enumerate(((mixed, mv), (wout, wv), (cot_t, cv), (gg, gv), (normed_t, nv)))]
        for copy in loads:
            copy.start()
        loads[0].wait()
        loads[1].wait()
        branch = lambda place: dot_nt(mv[pl.ds(pl.multiple_of(place * 256, 256), 256), :], wv[...])
        grads = lambda left, right, core: dot(left[core].reshape(8 * 96, LEN), right[...]).astype(BF16).reshape(2, 4, 96, WIDE)
        g0[...] = branch(net.near("z", 2)).astype(BF16)
        net.met()
        token.step1()
        for p, step in HALVES:
            g2[p] = branch(net.near("z", step)).astype(BF16)
            token.folded(p)
        ownb[...] = branch(z)
        loads[2].wait()
        away[0] = grads(cv, mv, net.other)
        cross[0].start()
        loads[3].wait()
        loads[4].wait()
        away[1] = grads(nv, gv, net.other)
        cross[1].start()
        held[0] = grads(cv, mv, cc)
        held[1] = grads(nv, gv, cc)
        acc[...] = jnp.zeros_like(acc)
        acc_bc[...] = jnp.zeros_like(acc_bc)
        extbc[BLOCK : BLOCK + 8, :] = jnp.zeros((8, 256), F32)
        for g in range(GROUPS):
            acc[g, 5:6, :] = gains[0:1, g * COLS : (g + 1) * COLS]
        ext[BLOCK : BLOCK + 8, :] = jnp.zeros((8, WIDE), F32)
        dstate[...] = jnp.zeros_like(dstate)

    @pl.when(k > 0)
    def _():
        ext[BLOCK : BLOCK + 8, :] = ext[0:8, :]
        extbc[BLOCK : BLOCK + 8, :] = extbc[0:8, :]

    b, c = bc[:, :STATE], bc[:, STATE:]
    valid = iota((BLOCK, BLOCK), 1) >= iota((BLOCK, BLOCK), 0)
    scores = jnp.where(valid, dot_nt(b, c), 0.0)
    ones, fold = expander(), reducer()
    left = iota((BLOCK, 128), 1) < 64
    suffix, prefix = upper(), lower(strict=True)
    dst[...] = jnp.zeros_like(dst)
    dbc[...] = jnp.zeros_like(dbc)
    for g in range(GROUPS):
        if g == 0:

            @pl.when(k == 1)
            def _():
                token.step2()

            @pl.when(k == 3)
            def _():
                for ring in rings:
                    ring.step2()

        else:

            @pl.when(k == 0)
            def _():
                for n in range(2):
                    cross[n].arrived()
                    held[n] += got[n]
                    rings[n].step1()

        cut = slice(g * COLS, (g + 1) * COLS)
        yv = y[:, cut]
        gs = gs_in[:, cut]
        xi = inner[:, cut]
        zv = zin[:, cut]
        zs = sigmoid(zv)
        xv = zv * zs
        rv = r[g]
        rt = jnp.transpose(rv)
        last = rv[BLOCK - 1 : BLOCK, :]
        dte = spread(dt[g], ones)
        grow = spread(jnp.exp2(rv), ones)
        tail = spread(jnp.exp2(last - rv), ones)
        skip = spread(prm[g, 8:16, 0:128], ones)[0:1, :]
        w = xv * dte
        wl = w.astype(BF16)
        gl = gs.astype(BF16)
        h = hin[0, g]
        dh = dstate[:, cut]
        dhl = dh.astype(BF16)
        parts = []
        for p in range(HEADS // 2):
            halves = []
            pair = slice(128 * p, 128 * (p + 1))
            wp, gpair = wl[:, pair], gl[:, pair]
            zero = jnp.zeros_like(wp)
            w_low = pltpu.roll(w[:, pair] - wp.astype(F32), 64, 1).astype(BF16)
            g_low = (gs[:, pair] - gpair.astype(F32)).astype(BF16)
            g_turn = pltpu.roll(gpair.astype(F32), 64, 1).astype(BF16)
            for n in (2 * p, 2 * p + 1):
                decay = jnp.exp2(jnp.minimum(rt[n : n + 1, :] - rv[:, n : n + 1], 0.0))
                halves.append(dot((scores * decay).astype(BF16), gpair))
                pick = (lambda a, b: jnp.where(left, a, b)) if n % 2 == 0 else (lambda a, b: jnp.where(left, b, a))
                one = jnp.concatenate([pick(wp, w_low), pick(wp, zero)], axis=1)
                two = jnp.concatenate([pick(gpair, g_turn), g_low], axis=1)
                dst[...] += dot_nt(one, two) * decay
            parts.append(jnp.where(left, halves[0], halves[1]))
        dwi = jnp.concatenate(parts, axis=1)
        dws = tail * dot(b, dhl)
        dw = dwi + dws
        skipgrad = gs * xv
        diff = folded(gl.astype(F32) * (yv - skip * xv) - wl.astype(F32) * dwi, fold)
        zsum = dot((w * dws).astype(BF16), fold)
        const = folded(jnp.sum(h * dh, axis=0, keepdims=True) * grow[BLOCK - 1 : BLOCK, :] + jnp.zeros((8, COLS), F32), fold)
        da = dot_right(suffix, diff, 3) + dot_right(prefix, zsum, 3) + const[0:1, :]
        rate = -jnp.exp(prm[g, 7:8, 0:128])
        dstep = (dot((xv * dw).astype(BF16), fold) + rate * da) * sigmoid(u[g])
        cat_out[:, WIDE + 128 * g : WIDE + 128 * (g + 1)] = dstep.astype(BF16)
        gx = (grow * gs).astype(BF16)
        dbc[:, STATE:] += dot_nt(gx, h.astype(BF16))
        dbc[:, :STATE] += dot_nt((tail * w).astype(BF16), dhl)
        dstate[:, cut] = grow[BLOCK - 1 : BLOCK, :] * dh + dot_tn(c, gx)
        dx = dte * dw + skip * gs
        dz = dx * (zs * (1.0 + zv * (1.0 - zs)))
        after = ext[BLOCK : BLOCK + 8, cut]
        ext[0:8, cut] = dz[0:8, :]
        gi = jnp.zeros((BLOCK, COLS), F32)
        for j in range(4):
            moved = dz if j == 3 else later(dz, after, 3 - j)
            gi = gi + prm[g, j : j + 1, :] * moved
            acc[g, j : j + 1, :] += jnp.sum(xi * moved, axis=0, keepdims=True)
        cat_out[:, cut] = gi.astype(BF16)
        acc[g, 4:5, :] += jnp.sum(dz, axis=0, keepdims=True)
        acc[g, 6:7, 0:128] += jnp.sum(dstep, axis=0, keepdims=True)
        acc[g, 7:8, 0:128] += jnp.sum(da * dt[g], axis=0, keepdims=True) * rate
        acc[g, 8:9, 0:128] += folded(jnp.sum(skipgrad, axis=0, keepdims=True) + jnp.zeros((8, COLS), F32), fold)[0:1, :]
    ds = jnp.where(valid, dst[...], 0.0).astype(BF16)
    dbc[:, STATE:] += dot_tn(ds, b)
    dbc[:, :STATE] += dot(ds, c)
    zb = zbc[...]
    sig = sigmoid(zb)
    dz = dbc[...] * (sig + zb * sig * (1.0 - sig))
    extbc[0:BLOCK, :] = dz
    bi = bc_in[...]
    gi = jnp.zeros((BLOCK, 256), F32)
    for j in range(4):
        moved = extbc[3 - j : 3 - j + BLOCK, :]
        gi = gi + conv_bc[j : j + 1, :] * moved
        acc_bc[j : j + 1, :] += jnp.sum(bi * moved, axis=0, keepdims=True)
    acc_bc[4:5, :] += jnp.sum(dz, axis=0, keepdims=True)
    cat_out[:, MORE:] = gi.astype(BF16)

    @pl.when(k == BLOCKS - 1)
    def _():
        rings[0].step3(wout_out)
        rings[1].step3(wgate_out)
        branch_out[...] = (tokens[...].astype(F32) + (ownb[...] + token.step3())).astype(BF16)
        for copy in net.copies:
            copy.left()


def run_backward(*args):
    rev = lambda k: BLOCKS - 1 - k
    cols = lambda n: pl.BlockSpec((BLOCK, n), lambda k: (rev(k), 0))
    small = lambda: pl.BlockSpec((GROUPS, BLOCK, 128), lambda k: (0, rev(k), 0))
    keep = lambda *s: pl.BlockSpec(s, lambda k: (0,) * len(s))
    bf = lambda *s: pltpu.VMEM(s, BF16)
    f32 = lambda *s: pltpu.VMEM(s, F32)
    return pl.pallas_call(
        backward_kernel,
        grid=(BLOCKS,),
        out_shape=[
            SHAPE((LEN, MORE + 256), BF16),
            SHAPE((GROUPS, 16, COLS), F32),
            SHAPE((8, 256), F32),
            SHAPE((256, D), BF16),
            SHAPE((96, COLS), F32),
            SHAPE((96, COLS), F32),
        ],
        in_specs=[cols(WIDE)] * 4
        + [
            pl.BlockSpec((1, GROUPS, STATE, COLS), lambda k: (rev(k), 0, 0, 0)),
            keep(GROUPS, 16, COLS),
            cols(256),
            small(),
            small(),
            small(),
            keep(8, WIDE),
        ]
        + [ANY] * 5
        + [keep(256, D), cols(256), cols(256), keep(4, 256)],
        out_specs=[cols(MORE + 256), keep(GROUPS, 16, COLS), keep(8, 256), keep(256, D), keep(96, COLS), keep(96, COLS)],
        scratch_shapes=[
            f32(BLOCK + 8, WIDE),
            f32(BLOCK + 8, 256),
            f32(STATE, WIDE),
            f32(BLOCK, BLOCK),
            f32(BLOCK, 256),
            bf(2, 2, 4, 96, WIDE),
            bf(2, 2, 4, 96, WIDE),
            bf(2, 2, 4, 96, WIDE),
            bf(LEN, WIDE),
            bf(D, WIDE),
            bf(2, 2, 4, 96, LEN),
            bf(LEN, WIDE),
            bf(2, 2, 4, 96, LEN),
            f32(256, D),
        ]
        + token_scratch()
        + grid_scratch("y", COLS)
        + grid_scratch("x", COLS)
        + sems(26)
        + [pltpu.SemaphoreType.DMA((5,))],
        compiler_params=pltpu.CompilerParams(collective_id=2, has_side_effects=True, vmem_limit_bytes=ROOM),
        name="backward",
    )(*args)


def tail_kernel(
    gg, cat, wx, normed_t, normed, acc, acc_bc, wbc, gain,
    tokens_out, inner_out, bc_out, small_out,
    far_gg, far_cat, ggv, catv, wxv, ntv, nv, wv, ownb, held, got, away, dbw, heldb, gotb, small, sp0, sp1, sp2, sp3, bz, by,
    g0, g1, g2, g3, a1, a2, a3, b1, b2, b3, c1, c2, c3, send, recv, local,
):
    net = Net(send, recv)
    at = net.at
    yh, cx, cc, z, y = at["yh"], at["x"], at["c"], at["z"], at["y"]
    net.greet([(a, s) for a in ("z", "x", "y") for s in (1, -1, 2)] + [("c", 1)])
    far_rows = lambda ref: rows(ref, net.near("z", 2) * 256, 256)
    pairs = ((far_rows(cat), far_cat), (far_rows(gg), far_gg), (wx, wxv), (wbc, wv), (cat, catv), (gg, ggv), (normed_t, ntv), (normed, nv))
    loads = [pltpu.make_async_copy(src, dst, local.at[i]) for i, (src, dst) in enumerate(pairs)]
    for copy in loads:
        copy.start()
    token = TokenSum(net, (g0, g1, g2, g3))
    spans = ((0, COLS), (WIDE, 128))
    rings = (GridSum(net, "x", held, spans, (a1, a2, a3), (0, 48)), GridSum(net, "y", held, spans, (b1, b2, b3), (48, 48)))
    ring_bc = GridSum(net, "x", heldb, ((0, 128),), (c1, c2, c3))

    def product(gates, others):
        return dot_nt(gates, wxv[:, 0:WIDE]) + dot_nt(others[:, 0:MORE], wxv[:, WIDE:]) + dot_nt(others[:, MORE:], wv[...])

    def block(place):
        cut = pl.ds(pl.multiple_of(place * 256, 256), 256)
        return product(ggv[cut, :], catv[cut, :])

    def of_norm(place, grad):
        cut = pl.ds(pl.multiple_of(place * 256, 256), 256)
        return jnp.sum(grad * nv[cut, :].astype(F32), axis=0, keepdims=True)

    for copy in loads[:4]:
        copy.wait()
    far = product(far_gg[...], far_cat[...])
    g0[...] = far.astype(BF16)
    net.met()
    token.step1()
    for copy in loads[4:7]:
        copy.wait()
    grads = lambda core, cut, n: dot(ntv[core].reshape(8 * 96, LEN), catv[:, cut]).astype(BF16).reshape(2, 4, 96, n)
    for core in range(2):
        dbw[core] = grads(core, slice(MORE, MORE + 256), 256)
    crossb = net.start(dbw.at[net.other], gotb, "c")
    loads[7].wait()
    norm_part = of_norm(net.near("z", 2), far)
    for p, step in HALVES:
        out = block(net.near("z", step))
        g2[p] = out.astype(BF16)
        norm_part = norm_part + of_norm(net.near("z", step), out)
        if p == 0:
            crossb.arrived()
            heldb[...] = dbw[cc] + gotb[...]
            ring_bc.step1()
    ownb[...] = block(z)
    norm_part = (norm_part + of_norm(z, ownb[...])) / gain[...].reshape(1, D)
    small[0:16, :] = acc[0]
    small[16:32, :] = acc[1]
    small[32:48, :] = jnp.zeros((16, COLS), F32)
    for k in range(4):
        small[32 + k : 33 + k, :] = norm_part[:, k * COLS : (k + 1) * COLS]
    small[36:41, 0:256] = acc_bc[0:5, :]
    sp0[z] = small[32:48, :]
    q = net.around(sp0.at[z], sp0.at[z], "z")
    for p, _ in HALVES:
        token.folded(p)
    ring_bc.step2()
    away[...] = grads(net.other, slice(0, MORE), MORE)
    cross = net.start(away, got, "c")
    held[...] = grads(cc, slice(0, MORE), MORE)
    cross.arrived()
    held[...] += got[...]
    ring_bc.step3(by.at[yh])
    qb = [net.start(by.at[yh], by.at[yh], "y", 2)]
    arrive(q)
    sp1[cx, 0:32, :] = small[0:32, :]
    sp1[cx, 32:48, :] = (sp0[0] + sp0[1]) + (sp0[2] + sp0[3])
    q = net.around(sp1.at[cx], sp1.at[cx], "x")
    for ring in rings:
        ring.step1()
    token.step2()
    arrive(qb)
    bz[z, :, 0:128] = by[0].astype(BF16)
    bz[z, :, 128:256] = by[1].astype(BF16)
    qb = net.around(bz.at[z], bz.at[z], "z")
    arrive(q)
    sp2[y] = (sp1[0] + sp1[1]) + (sp1[2] + sp1[3])
    q = net.around(sp2.at[y], sp2.at[y], "y")
    for ring in rings:
        ring.step2()
    arrive(q)
    sp3[cc] = (sp2[0] + sp2[1]) + (sp2[2] + sp2[3])
    q = [net.start(sp3.at[cc], sp3.at[cc], "c")]
    for ring in rings:
        ring.step3(inner_out)
    arrive(q)
    small_out[...] = sp3[0] + sp3[1]
    tokens_out[...] = token.step3() + ownb[...]
    arrive(qb)
    bc_out[...] = (bz[0].astype(F32) + bz[1].astype(F32)) + (bz[2].astype(F32) + bz[3].astype(F32))
    net.finish()


def run_tail(*args):
    bf = lambda *s: pltpu.VMEM(s, BF16)
    f32 = lambda *s: pltpu.VMEM(s, F32)
    return pl.pallas_call(
        tail_kernel,
        out_shape=[
            SHAPE((256, D), F32),
            SHAPE((96, COLS + 128), F32),
            SHAPE((96, 256), F32),
            SHAPE((48, COLS), F32),
        ],
        in_specs=[ANY] * 5 + [VMEM, VMEM, ANY, VMEM],
        out_specs=[VMEM] * 4,
        scratch_shapes=[
            bf(256, WIDE),
            bf(256, MORE + 256),
            bf(LEN, WIDE),
            bf(LEN, MORE + 256),
            bf(D, PROJ),
            bf(2, 2, 4, 96, LEN),
            bf(LEN, D),
            bf(D, 256),
            f32(256, D),
            bf(2, 4, 96, MORE),
            bf(2, 4, 96, MORE),
            bf(2, 4, 96, MORE),
            bf(2, 2, 4, 96, 256),
            bf(2, 4, 96, 256),
            bf(2, 4, 96, 256),
            f32(48, COLS),
            f32(4, 16, COLS),
            f32(4, 48, COLS),
            f32(4, 48, COLS),
            f32(2, 48, COLS),
            bf(4, 96, 256),
            f32(2, 96, 128),
        ]
        + token_scratch()
        + grid_scratch("x", COLS + 128, 48)
        + grid_scratch("y", COLS + 128, 48)
        + grid_scratch("x", 128)
        + sems(64)
        + [pltpu.SemaphoreType.DMA((8,))],
        compiler_params=pltpu.CompilerParams(collective_id=3, has_side_effects=True, vmem_limit_bytes=ROOM),
        name="tail",
    )(*args)


def finish_kernel(grad, tokens, cot, branch, norm_gain, inner, bc, small, gate, wout, tokens_out, branch_out, inner_out, bc_out, gate_out, wout_out, step_out, norm, conv, bias, conv_bc, bias_bc, step_bias, decay, skip, gain):
    v = tokens[...].astype(F32)
    root = lax.rsqrt(jnp.mean(v * v, axis=1, keepdims=True) + EPS)
    scaled = grad[...] * norm_gain[...].reshape(1, D)
    tokens_out[...] = cot[...].astype(F32) + root * scaled - v * (root * root * root) * jnp.mean(scaled * v, axis=1, keepdims=True)
    branch_out[...] = branch[...]

    @pl.when(pl.program_id(0) == 0)
    def _():
        inner_out[...] = inner[:, :COLS]
        bc_out[...] = bc[...]
        gate_out[...] = gate[...]
        wout_out[...] = wout[...]
        step_out[...] = jnp.transpose(jnp.concatenate([inner[:, COLS:], jnp.zeros((32, 128), F32)], axis=0))[0:HEADS, 0:96]
        norm[...] = jnp.concatenate([small[32 + k : 33 + k, :] for k in range(4)], axis=1).reshape(D)
        conv_bc[...] = small[36:40, 0:256]
        bias_bc[...] = small[40:41, 0:256].reshape(256)
        mine = small[pl.ds(pl.multiple_of(lax.axis_index("yh") * 16, 8), 16), :]
        conv[...] = mine[0:4, :]
        bias[...] = mine[4:5, :].reshape(COLS)
        gain[...] = mine[5:6, :].reshape(COLS)
        step_bias[...] = mine[6:7, 0:HEADS].reshape(HEADS)
        decay[...] = mine[7:8, 0:HEADS].reshape(HEADS)
        skip[...] = mine[8:9, 0:HEADS].reshape(HEADS)


def run_finish(*args):
    f32 = lambda *s: SHAPE(s, F32)
    strip = lambda: pl.BlockSpec((64, D), lambda k: (k, 0))
    whole = lambda *s: pl.BlockSpec(s, lambda k: (0,) * len(s))
    shapes = (
        (96, COLS), (96, 256), (96, COLS), (96, COLS), (HEADS, 96), (D,), (4, COLS), (COLS,), (4, 256), (256,), (HEADS,), (HEADS,), (HEADS,), (COLS,),
    )
    return pl.pallas_call(
        finish_kernel,
        grid=(4,),
        out_shape=[f32(256, D), SHAPE((256, D), BF16)] + [f32(*s) for s in shapes],
        in_specs=[strip(), strip(), strip(), strip()]
        + [whole(*s) for s in ((D,), (96, COLS + 128), (96, 256), (48, COLS), (96, COLS), (96, COLS))],
        out_specs=[strip(), strip()] + [whole(*s) for s in shapes],
        compiler_params=pltpu.CompilerParams(vmem_limit_bytes=ROOM),
        name="finish",
    )(*args)


def shards(tokens, norm_gain, w_gate, w_inner, w_bc, w_step, conv_inner, bias_inner, conv_bc, bias_bc, step_bias, decay_log, skip_gain, gate_gain, w_out, cotangent):
    (
        inner, zin, y, hin, dt, r, u, bc, bc_in, zbc, normed_t, gains, mixed, gs, gg, cot_t, normed, wx, wout, wbc, prm,
    ) = run_front(
        tokens, norm_gain, w_gate, w_inner, w_out, w_bc, w_step.T, conv_inner, bias_inner, gate_gain, step_bias, decay_log,
        skip_gain, conv_bc, bias_bc, cotangent,
    )
    wx, wout, wbc = wx.reshape(D, PROJ), wout.reshape(D, WIDE), wbc.reshape(D, 256)
    cat, acc, acc_bc, output, wout_grad, gate_grad = run_backward(
        gs, inner, zin, y, hin, prm, bc, dt, r, u, gains, mixed, wout, cot_t, gg, normed_t, tokens, zbc, bc_in, conv_bc
    )
    grad, inner_grad, bc_grad, small = run_tail(gg, cat, wx, normed_t, normed, acc, acc_bc, wbc, norm_gain)
    (
        tokens_grad, output, inner_grad, bc_grad, gate_grad, wout_grad, step_grad,
        norm, conv, bias, conv_bc_grad, bias_bc_grad, step_bias_grad, decay, skip, gate_gain_grad,
    ) = run_finish(grad, tokens, cotangent, output, norm_gain, inner_grad, bc_grad, small, gate_grad, wout_grad)
    return (
        output, tokens_grad, norm, gate_grad, inner_grad, bc_grad, step_grad.T, conv, bias, conv_bc_grad,
        bias_bc_grad, step_bias_grad, decay, skip, gate_gain_grad, wout_grad,
    )


def solution(mesh):
    fine = Mesh(mesh.devices.reshape(2, 4, 2, 2, 4), AXES)
    dp, tensor = ("yl", "x", "c"), ("yh", "z")
    tokens, weight = P(dp + tensor, None), P(dp, tensor)
    heads, shared = P(tensor), P()
    return jax.shard_map(
        shards,
        mesh=fine,
        in_specs=(
            tokens, shared, weight, weight, P(dp, None), weight, P(None, tensor), heads,
            shared, shared, heads, heads, heads, heads, weight, tokens,
        ),
        out_specs=(
            tokens, tokens, shared, weight, weight, P(dp, None), weight, P(None, tensor), heads,
            shared, shared, heads, heads, heads, heads, weight,
        ),
        check_vma=False,
    )
```

```python
import jax
import jax.numpy as jnp
from jax import lax
from jax.experimental import pallas as pl
from jax.experimental.pallas import tpu as pltpu
from jax.sharding import Mesh
from jax.sharding import PartitionSpec as P

D = 1536
LEN = 1024
INNER = 3072
STATE = 128
BLOCK = 256
BLOCKS = LEN // BLOCK
GROUPS = 2
HEADS = 6
COLS = HEADS * 64
WIDE = GROUPS * COLS
STEPS = 2 * WIDE
PROJ = STEPS + GROUPS * 128
MORE = PROJ - WIDE
LOG2E = 1.4426950408889634
EPS = 1e-05
F32 = jnp.float32
BF16 = jnp.bfloat16
MESH = pl.DeviceIdType.MESH
AXES = ("yl", "x", "c", "yh", "z")
ANY = pl.BlockSpec(memory_space=pl.ANY)
VMEM = pl.BlockSpec(memory_space=pltpu.VMEM)
SHAPE = jax.ShapeDtypeStruct
ROOM = 60 * 2**20


def dot(a, b):
    return jnp.dot(a, b, preferred_element_type=F32)


def dot_nt(a, b):
    return lax.dot_general(a, b, (((1,), (1,)), ((), ())), preferred_element_type=F32)


def dot_tn(a, b):
    return lax.dot_general(a, b, (((0,), (0,)), ((), ())), preferred_element_type=F32)


def pieces(v, n):
    out = []
    for _ in range(n):
        hi = v.astype(BF16)
        out.append(hi)
        v = v - hi.astype(F32)
    return out


def dot_left(v, ones, n):
    return sum(dot(p, ones) for p in pieces(v, n))


def spread(v, ones):
    hi = v.astype(BF16).astype(F32)
    low = pltpu.roll(v - hi, 64, 1)
    return dot(jnp.where(iota(v.shape, 1) < 64, hi, low).astype(BF16), ones)


def folded(v, ones):
    hi = v.astype(BF16)
    low = (v - hi.astype(F32)).astype(BF16)
    return dot(hi, ones) + dot(low, ones)


def dot_right(ones, v, n):
    return sum(dot(ones, p) for p in pieces(v, n))


def iota(shape, axis):
    return lax.broadcasted_iota(jnp.int32, shape, axis)


def expander():
    row, col = iota((128, COLS), 0), iota((128, COLS), 1)
    return ((row & 63) == lax.shift_right_logical(col, 6)).astype(BF16)


def reducer():
    row, col = iota((COLS, 128), 0), iota((COLS, 128), 1)
    return (col == lax.shift_right_logical(row, 6)).astype(BF16)


def sigmoid(v):
    return 0.5 * jnp.tanh(0.5 * v) + 0.5


def lower(strict=False):
    row, col = iota((BLOCK, BLOCK), 0), iota((BLOCK, BLOCK), 1)
    return ((row > col) if strict else (row >= col)).astype(BF16)


def upper():
    return (iota((BLOCK, BLOCK), 0) <= iota((BLOCK, BLOCK), 1)).astype(BF16)


def token_row(v):
    v = sum(v[:, 128 * i : 128 * (i + 1)] for i in range(v.shape[1] // 128))
    ones = jnp.ones((8, 128), BF16)
    return sum(dot_nt(ones, p) for p in pieces(v, 3))[0:1, :]


class Net:
    def __init__(self, send, recv):
        self.send, self.recv, self.copies = send, recv, []
        self.at = {name: lax.axis_index(name) for name in AXES}
        self.at["y"] = self.at["yh"] * 2 + self.at["yl"]
        self.places = {(a, s): lax.rem(self.at[a] + s + 4, 4) for a in ("x", "y", "z") for s in (1, -1, 2)}
        self.other = 1 - self.at["c"]
        self.targets = {("c", 1): {"c": self.other}}
        for (a, s), place in self.places.items():
            self.targets[a, s] = {"yh": place // 2, "yl": lax.rem(place, 2)} if a == "y" else {a: place}

    def near(self, axis, step):
        return self.places[axis, step]

    def plan(self, src, dst, axis, step=1):
        copy = Copy(self, len(self.copies), src, dst, self.targets[axis, step])
        self.copies.append(copy)
        return copy

    def start(self, src, dst, axis, step=1):
        return self.plan(lambda: src, lambda: dst, axis, step).start()

    def around(self, src, dst, axis):
        return [self.start(src, dst, axis, step) for step in (1, -1, 2)]

    def greet(self, peers):
        here, self.peers = pltpu.get_barrier_semaphore(), len(peers)
        for peer in peers:
            pl.semaphore_signal(here, inc=1, device_id=self.targets[peer], device_id_type=MESH)

    def met(self):
        pl.semaphore_wait(pltpu.get_barrier_semaphore(), self.peers)

    def finish(self):
        for copy in self.copies:
            copy.arrived()
        for copy in self.copies:
            copy.left()


class Copy:
    def __init__(self, net, index, src, dst, target):
        self.net, self.index, self.src, self.dst, self.target = net, index, src, dst, target
        self.here, self.gone = False, False

    def made(self):
        return pltpu.make_async_remote_copy(
            src_ref=self.src(),
            dst_ref=self.dst(),
            send_sem=self.net.send.at[self.index],
            recv_sem=self.net.recv.at[self.index],
            device_id=self.target,
            device_id_type=MESH,
        )

    def start(self):
        self.made().start()
        return self

    def arrived(self):
        if not self.here:
            self.here = True
            self.made().wait_recv()

    def left(self):
        if not self.gone:
            self.gone = True
            self.made().wait_send()


def sems(n):
    return [pltpu.SemaphoreType.DMA((n,)), pltpu.SemaphoreType.DMA((n,))]


def rows(ref, first, count):
    return ref.at[pl.ds(pl.multiple_of(first, 16), count)]


def lanes(first, count):
    return pl.ds(pl.multiple_of(first, 128), count)


def arrive(copies):
    for copy in copies:
        copy.arrived()


HALVES = ((0, 1), (1, -1))


class GridSum:
    def __init__(self, net, first, held, spans, scratch, cut=(0, 96)):
        self.net, self.first, self.held, self.spans = net, first, held, spans
        self.land, self.mid, self.last = scratch
        self.rows = pl.ds(*cut)
        self.one, self.two = [], []
        for slot, step in enumerate((2, 1, -1)):
            if first == "x":
                self.plan(self.one, lambda step=step: held.at[:, net.near("x", step), self.rows], lambda slot=slot: self.land.at[slot], "x", step)
            else:
                self.plan(self.two, lambda step=step: self.mid.at[net.near("x", step)], lambda slot=slot: self.last.at[slot], "x", step)
            lane = 0
            for base, n in spans:
                there = lambda step=step, base=base, n=n: lanes(base + (net.near("y", step) // 2) * n, n)
                if first == "x":
                    src = lambda step=step, there=there: self.mid.at[lax.rem(net.near("y", step), 2), :, there()]
                    self.plan(self.two, src, lambda slot=slot, lane=lane, n=n: self.last.at[slot, :, pl.ds(lane, n)], "y", step)
                else:
                    src = lambda step=step, there=there: held.at[lax.rem(net.near("y", step), 2), :, self.rows, there()]
                    self.plan(self.one, src, lambda slot=slot, lane=lane, n=n: self.land.at[slot, :, :, pl.ds(lane, n)], "y", step)
                lane += n

    def plan(self, to, src, dst, axis, step):
        to.append(self.net.plan(src, dst, axis, step))

    def step1(self):
        for copy in self.one:
            copy.start()

    def step2(self):
        arrive(self.one)
        at = self.net.at
        if self.first == "x":
            self.mid[...] = self.total(self.held[:, at["x"], self.rows], self.land, slice(None)).astype(BF16)
        else:
            lane = 0
            for base, n in self.spans:
                cut = slice(lane, lane + n)
                own = self.held[at["yl"], :, self.rows, lanes(base + at["yh"] * n, n)]
                self.mid[:, :, cut] = self.total(own, self.land, cut).astype(BF16)
                lane += n
        for copy in self.two:
            copy.start()

    def total(self, own, others, cut):
        return (own.astype(F32) + others[0, ..., cut].astype(F32)) + (others[1, ..., cut].astype(F32) + others[2, ..., cut].astype(F32))

    def step3(self, out):
        arrive(self.two)
        at = self.net.at
        if self.first == "y":
            out[self.rows, :] = self.total(self.mid[at["x"]], self.last, slice(None))
            return
        lane = 0
        for base, n in self.spans:
            cut = slice(lane, lane + n)
            out[self.rows, cut] = self.total(self.mid[at["yl"], :, lanes(base + at["yh"] * n, n)], self.last, cut)
            lane += n


def grid_scratch(first, width, count=96):
    blocks, wide = (2, 2 * width) if first == "x" else (4, width)
    return [pltpu.VMEM(s, BF16) for s in ((3, blocks, count, wide), (blocks, count, wide), (3, count, width))]


class TokenSum:
    def __init__(self, net, scratch):
        self.net, self.far, self.half, self.fold, self.whole = net, *scratch
        self.one = [
            net.plan(lambda p=p: self.far.at[pl.ds(128 * p, 128)], lambda p=p: self.half.at[p], "z", step) for p, step in HALVES
        ]
        half = lambda ref, p, n: ref.at[p, pl.ds(128 * n, 128)]
        self.ready = [net.plan(lambda p=p: half(self.fold, p, 1 - p), lambda p=p: half(self.whole, p, 1 - p), "z", step) for p, step in HALVES]
        self.added = [net.plan(lambda p=p: half(self.fold, p, p), lambda p=p: half(self.whole, p, p), "z", step) for p, step in HALVES]

    def step1(self):
        for copy in self.one:
            copy.start()

    def folded(self, p):
        self.ready[p].start()

    def step2(self):
        arrive(self.one)
        for p, _ in HALVES:
            self.fold[p, 128 * p : 128 * p + 128, :] += self.half[p]
            self.added[p].start()

    def step3(self):
        arrive(self.ready + self.added)
        return self.whole[0].astype(F32) + self.whole[1].astype(F32)


def token_scratch():
    return [pltpu.VMEM((256, D), BF16), pltpu.VMEM((2, 128, D), BF16), pltpu.VMEM((2, 256, D), BF16), pltpu.VMEM((2, 256, D), BF16)]


def earlier(v, before, step):
    if step == 0:
        return v
    turned = pltpu.roll(v, step, 0)
    starts = jnp.where(iota(before.shape, 0) < step, pltpu.roll(before, step, 0), turned[0:8, :])
    return jnp.concatenate([starts, turned[8:, :]], axis=0)


def front_kernel(
    x, gain, w_gate, w_inner, w_out, w_bc, w_step, conv, bias, gate_gain, step_bias, decay_log, skip_gain, conv_bc, bias_bc, cot,
    inner_out, z_out, y_out, h_out, dt_out, r_out, bc_out, bcin_out, zbc_out, normed_t, gains_out,
    mixed_out, gs_out, gg_out, cot_t, normed_out, wx_out, wout_out, wbc_out, prm_out,
    normed, wx, wout, wbc, prm, xv, stepv, stept, pk,
    cots, gps, acts, slopes, gms, mixed, gg, turned_c, ext, extbc, state, stat, cross, slots, slots_c, send, recv, local,
):
    i = pl.program_id(0)
    net = Net(send, recv)
    at = net.at
    yh, cx, cc, z, y = at["yh"], at["x"], at["c"], at["z"], at["y"]
    own_rows = lambda ref: rows(ref, z * 256, 256)
    order = ((0, 1), (1, -1), (1, 1), (0, -1))
    part = lambda ref, p, s: rows(ref, net.near("z", -s) * 256 + 128 * p, 128)
    c1 = [
        net.plan(lambda p=p: cot.at[pl.ds(128 * p, 128)], lambda p=p: rows(cots, z * 256 + 128 * p, 128), "z", s) for p, s in order
    ]
    c2 = [net.plan(lambda p=p, s=s: part(cots, p, s), lambda p=p, s=s: part(cots, p, s), "z", s) for p, s in HALVES]
    q = [net.plan(lambda: stat, lambda: slots.at[z], "z", step) for step in (1, -1, 2)]
    qc = [net.plan(lambda: cross, lambda: slots_c.at[z], "z", step) for step in (1, -1, 2)]
    spot_o = lambda xx, cut=pl.ds(0, 96): wout.at[at["yl"], xx, cc, cut, lanes(yh * COLS, COLS)]
    line_o = lambda yy, cut=pl.ds(0, 96): wout.at[lax.rem(yy, 2), :, cc, cut, lanes((yy // 2) * COLS, COLS)]
    same = lambda ref, axis, step=1: net.plan(ref, ref, axis, step)
    o1 = [net.plan(lambda: w_out, lambda: spot_o(cx), "x", step) for _, step in HALVES]
    o2 = [same(lambda p=p, s=s: spot_o(net.near("x", -s), pl.ds(48 * p, 48)), "x", s) for p, s in HALVES]
    o3 = [same(lambda: line_o(y), "y", step) for _, step in HALVES]
    o4 = [same(lambda p=p, s=s: line_o(net.near("y", -s), pl.ds(48 * p, 48)), "y", s) for p, s in HALVES]
    oc = [same(lambda: line_o(y), "c")] + [same(lambda s=s: line_o(net.near("y", s)), "c") for s in (1, -1, 2)]
    own = lambda: pltpu.make_async_copy(cot, own_rows(cots), local.at[0])
    pairs = ((normed, normed_out), (wx, wx_out), (wbc, wbc_out), (prm, prm_out), (wout, wout_out))
    leave = lambda n: pltpu.make_async_copy(*pairs[n], local.at[1 + n])

    @pl.when(i == 0)
    def _():
        load = pltpu.make_async_copy(x, xv, local.at[7])
        load.start()
        net.greet([("z", 1), ("z", -1), ("z", 2), ("x", 1), ("x", -1), ("y", 1), ("y", -1), ("y", 2), ("c", 1)])
        own().start()
        stept[...] = jnp.zeros_like(stept)
        stept[0:HEADS, 0:96] = w_step[...].astype(F32)
        stepv[...] = jnp.transpose(stept[...])[0:96, :].astype(BF16)
        pk[...] = jnp.zeros_like(pk)
        pk[0:4, :] = conv[...]
        pk[4:5, :] = bias[...].reshape(1, COLS)
        pk[5:6, :] = gate_gain[...].reshape(1, COLS)
        pk[6:7, 0:HEADS] = step_bias[...].reshape(1, HEADS)
        pk[7:8, 0:HEADS] = decay_log[...].reshape(1, HEADS)
        pk[8:9, 0:HEADS] = skip_gain[...].reshape(1, HEADS)
        first = {
            "x": ((w_gate, wx, 0, COLS), (w_bc.at[:, lanes(yh * 128, 128)], wbc, 0, 128)),
            "y": ((w_inner, wx, WIDE, COLS), (stepv, wx, STEPS, 128)),
        }
        then = {"x": "y", "y": "x"}
        done = []

        def go(src, dst, axis, step=1):
            done.append(net.start(src, dst, axis, step))
            return done[-1]

        def spot(ref, base, n, yy, xx, cut=pl.ds(0, 96)):
            return ref.at[lax.rem(yy, 2), xx, cc, cut, lanes(base + (yy // 2) * n, n)]

        def line(axis, ref, base, n, place, cut=pl.ds(0, 96)):
            if axis == "x":
                return ref.at[lax.rem(place, 2), :, cc, cut, lanes(base + (place // 2) * n, n)]
            return ref.at[:, place, cc, cut, lanes(base, 2 * n)]

        load.wait()
        v = xv[...].astype(F32)
        root = lax.rsqrt(jnp.mean(v * v, axis=1, keepdims=True) + EPS)
        normed[pl.ds(pl.multiple_of(z * 256, 256), 256), :] = (v * root * gain[...].reshape(1, D)).astype(BF16)
        net.met()
        zs = {}
        for p, s in order:
            here = rows(normed, z * 256 + 128 * p, 128)
            zs[p, s] = go(here, here, "z", s)
        sent = {"x": [], "y": []}
        for axis in ("x", "y"):
            for src, ref, base, n in first[axis]:
                sent[axis].append([go(src, spot(ref, base, n, y, cx), axis, step) for _, step in HALVES])
        mine = [
            pltpu.make_async_copy(src, spot(ref, base, n, y, cx), local.at[8 + k])
            for k, (src, ref, base, n) in enumerate(first["x"] + first["y"])
        ]
        mine.append(pltpu.make_async_copy(pk, prm.at[yh], local.at[12]))
        mine.append(pltpu.make_async_copy(w_out, spot_o(cx), local.at[13]))
        for copy in mine:
            copy.start()
        for copy in o1:
            copy.start()
        for axis in ("x", "y"):
            for src, ref, base, n in first[axis]:
                go(src, spot(ref, base, n, y, cx), "c")
        go(pk, prm.at[yh], "y", 2)
        second = {"x": [], "y": []}
        for axis in ("x", "y"):
            for (src, ref, base, n), copies in zip(first[axis], sent[axis]):
                for (p, s), copy in zip(HALVES, copies):
                    copy.arrived()
                    cut = pl.ds(48 * p, 48)
                    here = spot(ref, base, n, y, net.near("x", -s), cut) if axis == "x" else spot(ref, base, n, net.near("y", -s), cx, cut)
                    second[axis].append(go(here, here, axis, s))
        for copy in mine:
            copy.wait()
        third = {"x": [], "y": []}
        for axis in ("x", "y"):
            arrive(second[axis])
            for src, ref, base, n in first[axis]:
                here = line(axis, ref, base, n, at[then[axis]])
                third[axis].append([go(here, here, then[axis], s) for _, s in HALVES])
        for copy, start in zip(o1, o2):
            copy.arrived()
            start.start()
        for axis in ("x", "y"):
            for src, ref, base, n in first[axis]:
                for s in (1, -1, 2):
                    here = spot(ref, base, n, y, net.near("x", s)) if axis == "x" else spot(ref, base, n, net.near("y", s), cx)
                    go(here, here, "c")
        for p, s in HALVES:
            zs[p, s].arrived()
            here = part(normed, p, s)
            go(here, here, "z", s)
        for copy in c1:
            copy.start()
        fourth = {"x": [], "y": []}
        for axis in ("x", "y"):
            for (src, ref, base, n), copies in zip(first[axis], third[axis]):
                for (p, s), copy in zip(HALVES, copies):
                    copy.arrived()
                    place = net.near(then[axis], -s)
                    here = line(axis, ref, base, n, place, pl.ds(48 * p, 48))
                    fourth[axis].append(go(here, here, then[axis], s))
                    here = line(axis, ref, base, n, place)
                    go(here, here, "c")
        arrive(o2)
        for copy in o3:
            copy.start()
        for axis in ("x", "y"):
            arrive(fourth[axis])
            for src, ref, base, n in first[axis]:
                here = line(axis, ref, base, n, net.near(then[axis], 2))
                go(here, here, "c")
        for copy in done:
            copy.arrived()
        for copy in done:
            copy.left()
        for n in range(4):
            leave(n).start()
        ext[...] = jnp.zeros_like(ext)
        extbc[...] = jnp.zeros_like(extbc)
        state[...] = jnp.zeros_like(state)
        stat[...] = jnp.zeros_like(stat)
        cross[...] = jnp.zeros_like(cross)

    @pl.when(i == 2)
    def _():
        for copy, start in zip(c1[:2], c2):
            copy.arrived()
            start.start()
        for copy, start in zip(o3, o4):
            copy.arrived()
            start.start()
        for copy in oc[:3]:
            copy.start()

    @pl.when(i < BLOCKS)
    def _():
        xb = normed[pl.ds(pl.multiple_of(i * BLOCK, BLOCK), BLOCK), :]
        turned = jnp.transpose(xb).reshape(2, 4, 2, 96, BLOCK)
        for core in range(2):
            normed_t[core] = turned[:, :, core]
        bc_in = dot(xb, wbc[...].reshape(D, 256))
        bcin_out[...] = bc_in.astype(BF16)
        before_bc = extbc[...]
        extbc[...] = bc_in[BLOCK - 8 :, :]
        zb = bias_bc[...].reshape(1, 256) + sum(conv_bc[j : j + 1, :] * earlier(bc_in, before_bc, 3 - j) for j in range(4))
        zbc_out[...] = zb.astype(BF16)
        bc = (zb * sigmoid(zb)).astype(BF16)
        bc_out[...] = bc
        b, c = bc[:, :STATE], bc[:, STATE:]
        scores = jnp.where(iota((BLOCK, BLOCK), 0) >= iota((BLOCK, BLOCK), 1), dot_nt(c, b), 0.0)
        tri, ones = lower(), expander()
        left = iota((BLOCK, 128), 1) < 64
        weight = lambda first, n: wx[:, :, :, :, first : first + n].reshape(D, n)
        steps = dot(xb, weight(STEPS, 256))
        total = jnp.zeros((BLOCK, 128), F32)
        for g in range(GROUPS):
            if g == 1:

                @pl.when(i == BLOCKS - 1)
                def _():
                    arrive(o4)
                    oc[3].start()

            cut = slice(g * COLS, (g + 1) * COLS)
            u = steps[:, 128 * g : 128 * (g + 1)] + prm[g, 6:7, 0:128]
            dt = jnp.maximum(u, 0.0) + jnp.log(1.0 + jnp.exp(-jnp.abs(u)))
            rate = -jnp.exp(prm[g, 7:8, 0:128]) * LOG2E
            r = dot_right(tri, dt * rate, 3)
            dt_out[g] = dt
            r_out[g] = r
            rt = jnp.transpose(r)
            gate = dot(xb, weight(g * COLS, COLS))
            inner = dot(xb, weight(WIDE + g * COLS, COLS))
            inner_out[:, cut] = inner.astype(BF16)
            before = ext[:, cut]
            ext[:, cut] = inner[BLOCK - 8 :, :]
            zv = prm[g, 4:5, :] + sum(prm[g, j : j + 1, :] * earlier(inner, before, 3 - j) for j in range(4))
            z_out[:, cut] = zv
            xv = zv * sigmoid(zv)
            last = r[BLOCK - 1 : BLOCK, :]
            w = xv * spread(dt, ones)
            grow = spread(jnp.exp2(r), ones)
            tail = spread(jnp.exp2(last - r), ones)
            skip = spread(prm[g, 8:16, 0:128], ones)[0:1, :]
            wl = w.astype(BF16)
            h = state[:, cut]
            h_out[0, g] = h.astype(BF16)
            parts = []
            for p in range(HEADS // 2):
                halves = []
                for n in (2 * p, 2 * p + 1):
                    gap = jnp.minimum(r[:, n : n + 1] - rt[n : n + 1, :], 0.0)
                    halves.append(dot((scores * jnp.exp2(gap)).astype(BF16), wl[:, 128 * p : 128 * (p + 1)]))
                parts.append(jnp.where(left, halves[0], halves[1]))
            yv = jnp.concatenate(parts, axis=1) + grow * dot(c, h.astype(BF16)) + skip * xv
            y_out[:, cut] = yv
            state[:, cut] = grow[BLOCK - 1 : BLOCK, :] * h + dot_tn(b, (tail * w).astype(BF16))
            sig = sigmoid(gate)
            act = gate * sig
            gp = yv * act
            here_now = pl.ds(pl.multiple_of(i * BLOCK, BLOCK), BLOCK)
            gps[here_now, cut] = gp
            acts[here_now, cut] = act
            slopes[here_now, cut] = yv * (sig + act * (1.0 - sig))
            sq = gp * gp
            total = total + (sq[:, 0:128] + sq[:, 128:256] + sq[:, 256:384])
        stat[pl.ds(i, 1), :] = token_row(total)

    @pl.when(i == BLOCKS)
    def _():
        for copy in q:
            copy.start()
        slots[z] = stat[...]
        own().wait()
        arrive(oc)
        leave(4).start()
        gain = jnp.concatenate([prm[0, 5:6, :], prm[1, 5:6, :]], axis=1)
        moved = []

        def away(src, dst, *cut):
            moved.append(pltpu.make_async_copy(src.at[cut], dst.at[cut], local.at[14 + len(moved)]))
            moved[-1].start()

        for n, step in enumerate((0, -1, 1, 2)):
            arrive(((), c1, (), c2)[n])
            block = net.near("z", step) if step else z
            at = pl.ds(pl.multiple_of(block * BLOCK, BLOCK), BLOCK)
            cb = cots[at, :]
            turned = jnp.transpose(cb).reshape(2, 4, 2, 96, BLOCK)
            for core in range(2):
                turned_c[core, :, :, :, at] = turned[:, :, core]
            full = slice(None)
            away(turned_c, cot_t, full, full, full, full, at)
            gm = dot(cb, wout[...].reshape(D, WIDE)) * gain
            gms[at, :] = gm
            cross[pl.ds(block, 1), :] = token_row(gm * gps[at, :])
        for copy in qc:
            copy.start()
        slots_c[z] = cross[...]
        arrive(q)
        for copy in q:
            copy.left()
        root = lax.rsqrt(((slots[0] + slots[1]) + (slots[2] + slots[3])) * (1.0 / INNER) + EPS)
        columns = jnp.transpose(root)
        gain_grad = jnp.zeros((1, WIDE), F32)
        for k in range(BLOCKS):
            at = slice(k * BLOCK, (k + 1) * BLOCK)
            normal, gm = gps[at, :] * columns[:, k : k + 1], gms[at, :]
            mixed[at, :] = (normal * gain).astype(BF16)
            away(mixed, mixed_out, pl.ds(k * BLOCK, BLOCK))
            gain_grad = gain_grad + jnp.sum(gm * normal, axis=0, keepdims=True)
            gms[at, :] = gm * columns[:, k : k + 1]
        gain_grad = gain_grad / gain
        arrive(qc)
        sums = (slots_c[0] + slots_c[1]) + (slots_c[2] + slots_c[3])
        columns = jnp.transpose(root * root * root * (sums * (1.0 / INNER)))
        for k in range(BLOCKS):
            at = slice(k * BLOCK, (k + 1) * BLOCK)
            gated = gms[at, :] - gps[at, :] * columns[:, k : k + 1]
            gms[at, :] = gated * acts[at, :]
            gg[at, :] = (gated * slopes[at, :]).astype(BF16)
            away(gms, gs_out, pl.ds(k * BLOCK, BLOCK))
            away(gg, gg_out, pl.ds(k * BLOCK, BLOCK))
        gains_out[...] = jnp.concatenate([gain_grad, jnp.zeros((7, WIDE), F32)], axis=0)
        for copy in c1 + c2 + qc + o1 + o2 + o3 + o4 + oc:
            copy.left()
        for copy in moved:
            copy.wait()
        for n in range(len(pairs)):
            leave(n).wait()


def run_front(*args):
    first = lambda k: jnp.minimum(k, BLOCKS - 1)
    keep = lambda *s: pl.BlockSpec(s, lambda k: (0,) * len(s))
    block = lambda n: pl.BlockSpec((BLOCK, n), lambda k: (first(k), 0))
    small = lambda: pl.BlockSpec((GROUPS, BLOCK, 128), lambda k: (0, first(k), 0))
    wide = SHAPE((LEN, WIDE), F32)
    narrow = SHAPE((GROUPS, LEN, 128), F32)
    bf = lambda *s: pltpu.VMEM(s, BF16)
    f32 = lambda *s: pltpu.VMEM(s, F32)
    return pl.pallas_call(
        front_kernel,
        grid=(BLOCKS + 1,),
        out_shape=[
            SHAPE((LEN, WIDE), BF16),
            wide,
            wide,
            SHAPE((BLOCKS, GROUPS, STATE, COLS), BF16),
            narrow,
            narrow,
            SHAPE((LEN, 256), BF16),
            SHAPE((LEN, 256), BF16),
            SHAPE((LEN, 256), BF16),
            SHAPE((2, 2, 4, 96, LEN), BF16),
            SHAPE((8, WIDE), F32),
            SHAPE((LEN, WIDE), BF16),
            wide,
            SHAPE((LEN, WIDE), BF16),
            SHAPE((2, 2, 4, 96, LEN), BF16),
            SHAPE((LEN, D), BF16),
            SHAPE((2, 4, 2, 96, PROJ), BF16),
            SHAPE((2, 4, 2, 96, WIDE), BF16),
            SHAPE((2, 4, 2, 96, 256), BF16),
            SHAPE((GROUPS, 16, COLS), F32),
        ],
        in_specs=[ANY, VMEM, ANY, ANY, ANY, ANY] + [VMEM] * 9 + [ANY],
        out_specs=[
            block(WIDE),
            block(WIDE),
            block(WIDE),
            pl.BlockSpec((1, GROUPS, STATE, COLS), lambda k: (first(k), 0, 0, 0)),
            small(),
            small(),
            block(256),
            block(256),
            block(256),
            pl.BlockSpec((2, 2, 4, 96, BLOCK), lambda k: (0, 0, 0, 0, first(k))),
            keep(8, WIDE),
        ]
        + [ANY] * 9,
        scratch_shapes=[
            bf(LEN, D),
            bf(2, 4, 2, 96, PROJ),
            bf(2, 4, 2, 96, WIDE),
            bf(2, 4, 2, 96, 256),
            f32(GROUPS, 16, COLS),
            bf(256, D),
            bf(96, 128),
            f32(128, 128),
            f32(16, COLS),
            bf(LEN, D),
            f32(LEN, WIDE),
            f32(LEN, WIDE),
            f32(LEN, WIDE),
            f32(LEN, WIDE),
            bf(LEN, WIDE),
            bf(LEN, WIDE),
            bf(2, 2, 4, 96, LEN),
            f32(8, WIDE),
            f32(8, 256),
            f32(STATE, WIDE),
            f32(8, BLOCK),
            f32(8, BLOCK),
            f32(4, 8, BLOCK),
            f32(4, 8, BLOCK),
        ]
        + sems(96)
        + [pltpu.SemaphoreType.DMA((30,))],
        compiler_params=pltpu.CompilerParams(collective_id=1, has_side_effects=True, vmem_limit_bytes=ROOM),
        name="front",
    )(*args)


def later(v, after, step):
    turned = pltpu.roll(v, BLOCK - step, 0)
    ends = jnp.where(iota(after.shape, 0) < 8 - step, turned[BLOCK - 8 :, :], pltpu.roll(after, 8 - step, 0))
    return jnp.concatenate([turned[: BLOCK - 8, :], ends], axis=0)


def backward_kernel(
    gs_in, inner, zin, y, hin, prm, bc, dt, r, gains, mixed, wout, cot_t, gg, normed_t, tokens, zbc, bc_in, conv_bc,
    cat_out, acc, acc_bc, branch_out, wout_out, wgate_out,
    ext, extbc, dstate, dst, dbc, held, got, away, mv, wv, cv, gv, nv, ownb, g0, g1, g2, g3, s1, s2, s3, t1, t2, t3, send, recv, local,
):
    k = pl.program_id(0)
    net = Net(send, recv)
    cc, z = net.at["c"], net.at["z"]
    cross = [net.plan(lambda n=n: away.at[n], lambda n=n: got.at[n], "c") for n in range(2)]
    token = TokenSum(net, (g0, g1, g2, g3))
    rings = (GridSum(net, "y", held.at[0], ((0, COLS),), (s1, s2, s3)), GridSum(net, "x", held.at[1], ((0, COLS),), (t1, t2, t3)))

    @pl.when(k == 0)
    def _():
        net.greet([("z", 1), ("z", -1)] + [(a, s) for a in ("x", "y") for s in (1, -1, 2)] + [("c", 1)])
        loads = [pltpu.make_async_copy(src, dst, local.at[n]) for n, (src, dst) in enumerate(((mixed, mv), (wout, wv), (cot_t, cv), (gg, gv), (normed_t, nv)))]
        for copy in loads:
            copy.start()
        loads[0].wait()
        loads[1].wait()
        branch = lambda place: dot_nt(mv[pl.ds(pl.multiple_of(place * 256, 256), 256), :], wv[...])
        grads = lambda left, right, core: dot(left[core].reshape(8 * 96, LEN), right[...]).astype(BF16).reshape(2, 4, 96, WIDE)
        g0[...] = branch(net.near("z", 2)).astype(BF16)
        net.met()
        token.step1()
        for p, step in HALVES:
            g2[p] = branch(net.near("z", step)).astype(BF16)
            token.folded(p)
        ownb[...] = branch(z)
        loads[2].wait()
        away[0] = grads(cv, mv, net.other)
        cross[0].start()
        loads[3].wait()
        loads[4].wait()
        away[1] = grads(nv, gv, net.other)
        cross[1].start()
        held[0] = grads(cv, mv, cc)
        held[1] = grads(nv, gv, cc)
        acc[...] = jnp.zeros_like(acc)
        acc_bc[...] = jnp.zeros_like(acc_bc)
        extbc[BLOCK : BLOCK + 8, :] = jnp.zeros((8, 256), F32)
        for g in range(GROUPS):
            acc[g, 5:6, :] = gains[0:1, g * COLS : (g + 1) * COLS]
        ext[BLOCK : BLOCK + 8, :] = jnp.zeros((8, WIDE), F32)
        dstate[...] = jnp.zeros_like(dstate)

    @pl.when(k > 0)
    def _():
        ext[BLOCK : BLOCK + 8, :] = ext[0:8, :]
        extbc[BLOCK : BLOCK + 8, :] = extbc[0:8, :]

    b, c = bc[:, :STATE], bc[:, STATE:]
    valid = iota((BLOCK, BLOCK), 1) >= iota((BLOCK, BLOCK), 0)
    scores = jnp.where(valid, dot_nt(b, c), 0.0)
    ones, fold = expander(), reducer()
    left = iota((BLOCK, 128), 1) < 64
    suffix, prefix = upper(), lower(strict=True)
    dst[...] = jnp.zeros_like(dst)
    dbc[...] = jnp.zeros_like(dbc)
    for g in range(GROUPS):
        if g == 0:

            @pl.when(k == 1)
            def _():
                token.step2()

            @pl.when(k == 3)
            def _():
                for ring in rings:
                    ring.step2()

        else:

            @pl.when(k == 0)
            def _():
                for n in range(2):
                    cross[n].arrived()
                    held[n] += got[n]
                    rings[n].step1()

        cut = slice(g * COLS, (g + 1) * COLS)
        yv = y[:, cut]
        gs = gs_in[:, cut]
        xi = inner[:, cut].astype(F32)
        zv = zin[:, cut]
        zs = sigmoid(zv)
        xv = zv * zs
        dtv = dt[g]
        rate = -jnp.exp(prm[g, 7:8, 0:128])
        rv = r[g]
        rt = jnp.transpose(rv)
        last = rv[BLOCK - 1 : BLOCK, :]
        dte = spread(dt[g], ones)
        grow = spread(jnp.exp2(rv), ones)
        tail = spread(jnp.exp2(last - rv), ones)
        skip = spread(prm[g, 8:16, 0:128], ones)[0:1, :]
        w = xv * dte
        wl = w.astype(BF16)
        gl = gs.astype(BF16)
        hl = hin[0, g]
        h = hl.astype(F32)
        dh = dstate[:, cut]
        dhl = dh.astype(BF16)
        parts = []
        for p in range(HEADS // 2):
            halves, shares = [], []
            pair = slice(128 * p, 128 * (p + 1))
            wp, gpair = wl[:, pair], gl[:, pair]
            zero = jnp.zeros_like(wp)
            w_low = pltpu.roll(w[:, pair] - wp.astype(F32), 64, 1).astype(BF16)
            g_low = (gs[:, pair] - gpair.astype(F32)).astype(BF16)
            g_turn = pltpu.roll(gpair.astype(F32), 64, 1).astype(BF16)
            for n in (2 * p, 2 * p + 1):
                decay = jnp.exp2(jnp.minimum(rt[n : n + 1, :] - rv[:, n : n + 1], 0.0))
                halves.append(dot((scores * decay).astype(BF16), gpair))
                pick = (lambda a, b: jnp.where(left, a, b)) if n % 2 == 0 else (lambda a, b: jnp.where(left, b, a))
                one = jnp.concatenate([pick(wp, w_low), pick(wp, zero)], axis=1)
                two = jnp.concatenate([pick(gpair, g_turn), g_low], axis=1)
                shares.append(dot_nt(one, two) * decay)
            parts.append(jnp.where(left, halves[0], halves[1]))
            dst[...] += shares[0] + shares[1]
        dwi = jnp.concatenate(parts, axis=1)
        dws = tail * dot(b, dhl)
        dw = dwi + dws
        skipgrad = gs * xv
        diff = folded(gl.astype(F32) * (yv - skip * xv) - wl.astype(F32) * dwi, fold)
        zsum = dot((w * dws).astype(BF16), fold)
        const = folded(jnp.sum(h * dh, axis=0, keepdims=True) * grow[BLOCK - 1 : BLOCK, :] + jnp.zeros((8, COLS), F32), fold)
        da = dot_right(suffix, diff, 3) + dot_right(prefix, zsum, 3) + const[0:1, :]
        dstep = (dot((xv * dw).astype(BF16), fold) + rate * da) * jnp.where(dtv < 0.02, dtv * (1.0 - dtv * (0.5 - dtv * (1.0 / 6.0))), 1.0 - jnp.exp(-dtv))
        cat_out[:, WIDE + 128 * g : WIDE + 128 * (g + 1)] = dstep.astype(BF16)
        gx = (grow * gs).astype(BF16)
        dbc[:, STATE:] += dot_nt(gx, hl)
        dbc[:, :STATE] += dot_nt((tail * w).astype(BF16), dhl)
        dstate[:, cut] = grow[BLOCK - 1 : BLOCK, :] * dh + dot_tn(c, gx)
        dx = dte * dw + skip * gs
        dz = dx * (zs * (1.0 + zv * (1.0 - zs)))
        after = ext[BLOCK : BLOCK + 8, cut]
        ext[0:8, cut] = dz[0:8, :]
        gi = jnp.zeros((BLOCK, COLS), F32)
        for j in range(4):
            moved = dz if j == 3 else later(dz, after, 3 - j)
            gi = gi + prm[g, j : j + 1, :] * moved
            acc[g, j : j + 1, :] += jnp.sum(xi * moved, axis=0, keepdims=True)
        cat_out[:, cut] = gi.astype(BF16)
        acc[g, 4:5, :] += jnp.sum(dz, axis=0, keepdims=True)
        acc[g, 6:7, 0:128] += jnp.sum(dstep, axis=0, keepdims=True)
        acc[g, 7:8, 0:128] += jnp.sum(da * dt[g], axis=0, keepdims=True) * rate
        acc[g, 8:9, 0:128] += folded(jnp.sum(skipgrad, axis=0, keepdims=True) + jnp.zeros((8, COLS), F32), fold)[0:1, :]
    ds = jnp.where(valid, dst[...], 0.0).astype(BF16)
    dbc[:, STATE:] += dot_tn(ds, b)
    dbc[:, :STATE] += dot(ds, c)
    zb = zbc[...].astype(F32)
    sig = sigmoid(zb)
    dz = dbc[...] * (sig + zb * sig * (1.0 - sig))
    extbc[0:BLOCK, :] = dz
    bi = bc_in[...].astype(F32)
    gi = jnp.zeros((BLOCK, 256), F32)
    for j in range(4):
        moved = extbc[3 - j : 3 - j + BLOCK, :]
        gi = gi + conv_bc[j : j + 1, :] * moved
        acc_bc[j : j + 1, :] += jnp.sum(bi * moved, axis=0, keepdims=True)
    acc_bc[4:5, :] += jnp.sum(dz, axis=0, keepdims=True)
    cat_out[:, MORE:] = gi.astype(BF16)

    @pl.when(k == BLOCKS - 1)
    def _():
        rings[0].step3(wout_out)
        rings[1].step3(wgate_out)
        branch_out[...] = (tokens[...].astype(F32) + (ownb[...] + token.step3())).astype(BF16)
        for copy in net.copies:
            copy.left()


def run_backward(*args):
    rev = lambda k: BLOCKS - 1 - k
    cols = lambda n: pl.BlockSpec((BLOCK, n), lambda k: (rev(k), 0))
    small = lambda: pl.BlockSpec((GROUPS, BLOCK, 128), lambda k: (0, rev(k), 0))
    keep = lambda *s: pl.BlockSpec(s, lambda k: (0,) * len(s))
    bf = lambda *s: pltpu.VMEM(s, BF16)
    f32 = lambda *s: pltpu.VMEM(s, F32)
    return pl.pallas_call(
        backward_kernel,
        grid=(BLOCKS,),
        out_shape=[
            SHAPE((LEN, MORE + 256), BF16),
            SHAPE((GROUPS, 16, COLS), F32),
            SHAPE((8, 256), F32),
            SHAPE((256, D), BF16),
            SHAPE((96, COLS), F32),
            SHAPE((96, COLS), F32),
        ],
        in_specs=[cols(WIDE)] * 4
        + [
            pl.BlockSpec((1, GROUPS, STATE, COLS), lambda k: (rev(k), 0, 0, 0)),
            keep(GROUPS, 16, COLS),
            cols(256),
            small(),
            small(),
            keep(8, WIDE),
        ]
        + [ANY] * 5
        + [keep(256, D), cols(256), cols(256), keep(4, 256)],
        out_specs=[cols(MORE + 256), keep(GROUPS, 16, COLS), keep(8, 256), keep(256, D), keep(96, COLS), keep(96, COLS)],
        scratch_shapes=[
            f32(BLOCK + 8, WIDE),
            f32(BLOCK + 8, 256),
            f32(STATE, WIDE),
            f32(BLOCK, BLOCK),
            f32(BLOCK, 256),
            bf(2, 2, 4, 96, WIDE),
            bf(2, 2, 4, 96, WIDE),
            bf(2, 2, 4, 96, WIDE),
            bf(LEN, WIDE),
            bf(D, WIDE),
            bf(2, 2, 4, 96, LEN),
            bf(LEN, WIDE),
            bf(2, 2, 4, 96, LEN),
            f32(256, D),
        ]
        + token_scratch()
        + grid_scratch("y", COLS)
        + grid_scratch("x", COLS)
        + sems(26)
        + [pltpu.SemaphoreType.DMA((5,))],
        compiler_params=pltpu.CompilerParams(collective_id=2, has_side_effects=True, vmem_limit_bytes=ROOM),
        name="backward",
    )(*args)


def tail_kernel(
    gg, cat, wx, normed_t, normed, acc, acc_bc, wbc, gain,
    tokens_out, inner_out, bc_out, small_out,
    far_gg, far_cat, ggv, catv, wxv, ntv, nv, wv, ownb, held, got, away, dbw, heldb, gotb, small, sp0, sp1, sp2, sp3, bz, by,
    g0, g1, g2, g3, a1, a2, a3, b1, b2, b3, c1, c2, c3, send, recv, local,
):
    net = Net(send, recv)
    at = net.at
    yh, cx, cc, z, y = at["yh"], at["x"], at["c"], at["z"], at["y"]
    net.greet([(a, s) for a in ("z", "x", "y") for s in (1, -1, 2)] + [("c", 1)])
    far_rows = lambda ref: rows(ref, net.near("z", 2) * 256, 256)
    pairs = ((far_rows(cat), far_cat), (far_rows(gg), far_gg), (wx, wxv), (wbc, wv), (cat, catv), (gg, ggv), (normed_t, ntv), (normed, nv))
    loads = [pltpu.make_async_copy(src, dst, local.at[i]) for i, (src, dst) in enumerate(pairs)]
    for copy in loads:
        copy.start()
    token = TokenSum(net, (g0, g1, g2, g3))
    spans = ((0, COLS), (WIDE, 128))
    rings = (GridSum(net, "x", held, spans, (a1, a2, a3), (0, 48)), GridSum(net, "y", held, spans, (b1, b2, b3), (48, 48)))
    ring_bc = GridSum(net, "x", heldb, ((0, 128),), (c1, c2, c3))

    def product(gates, others):
        return dot_nt(gates, wxv[:, 0:WIDE]) + dot_nt(others[:, 0:MORE], wxv[:, WIDE:]) + dot_nt(others[:, MORE:], wv[...])

    def block(place):
        cut = pl.ds(pl.multiple_of(place * 256, 256), 256)
        return product(ggv[cut, :], catv[cut, :])

    def of_norm(place, grad):
        cut = pl.ds(pl.multiple_of(place * 256, 256), 256)
        return jnp.sum(grad * nv[cut, :].astype(F32), axis=0, keepdims=True)

    for copy in loads[:4]:
        copy.wait()
    far = product(far_gg[...], far_cat[...])
    g0[...] = far.astype(BF16)
    net.met()
    token.step1()
    for copy in loads[4:7]:
        copy.wait()
    grads = lambda core, cut, n: dot(ntv[core].reshape(8 * 96, LEN), catv[:, cut]).astype(BF16).reshape(2, 4, 96, n)
    for core in range(2):
        dbw[core] = grads(core, slice(MORE, MORE + 256), 256)
    crossb = net.start(dbw.at[net.other], gotb, "c")
    loads[7].wait()
    norm_part = of_norm(net.near("z", 2), far)
    for p, step in HALVES:
        out = block(net.near("z", step))
        g2[p] = out.astype(BF16)
        norm_part = norm_part + of_norm(net.near("z", step), out)
        if p == 0:
            crossb.arrived()
            heldb[...] = dbw[cc] + gotb[...]
            ring_bc.step1()
    ownb[...] = block(z)
    norm_part = (norm_part + of_norm(z, ownb[...])) / gain[...].reshape(1, D)
    small[0:16, :] = acc[0]
    small[16:32, :] = acc[1]
    small[32:48, :] = jnp.zeros((16, COLS), F32)
    for k in range(4):
        small[32 + k : 33 + k, :] = norm_part[:, k * COLS : (k + 1) * COLS]
    small[36:41, 0:256] = acc_bc[0:5, :]
    sp0[z] = small[32:48, :]
    q = net.around(sp0.at[z], sp0.at[z], "z")
    for p, _ in HALVES:
        token.folded(p)
    ring_bc.step2()
    away[...] = grads(net.other, slice(0, MORE), MORE)
    cross = net.start(away, got, "c")
    held[...] = grads(cc, slice(0, MORE), MORE)
    cross.arrived()
    held[...] += got[...]
    ring_bc.step3(by.at[yh])
    qb = [net.start(by.at[yh], by.at[yh], "y", 2)]
    arrive(q)
    sp1[cx, 0:32, :] = small[0:32, :]
    sp1[cx, 32:48, :] = (sp0[0] + sp0[1]) + (sp0[2] + sp0[3])
    q = net.around(sp1.at[cx], sp1.at[cx], "x")
    for ring in rings:
        ring.step1()
    token.step2()
    arrive(qb)
    bz[z, :, 0:128] = by[0].astype(BF16)
    bz[z, :, 128:256] = by[1].astype(BF16)
    qb = net.around(bz.at[z], bz.at[z], "z")
    arrive(q)
    sp2[y] = (sp1[0] + sp1[1]) + (sp1[2] + sp1[3])
    q = net.around(sp2.at[y], sp2.at[y], "y")
    for ring in rings:
        ring.step2()
    arrive(q)
    sp3[cc] = (sp2[0] + sp2[1]) + (sp2[2] + sp2[3])
    q = [net.start(sp3.at[cc], sp3.at[cc], "c")]
    for ring in rings:
        ring.step3(inner_out)
    arrive(q)
    small_out[...] = sp3[0] + sp3[1]
    tokens_out[...] = token.step3() + ownb[...]
    arrive(qb)
    bc_out[...] = (bz[0].astype(F32) + bz[1].astype(F32)) + (bz[2].astype(F32) + bz[3].astype(F32))
    net.finish()


def run_tail(*args):
    bf = lambda *s: pltpu.VMEM(s, BF16)
    f32 = lambda *s: pltpu.VMEM(s, F32)
    return pl.pallas_call(
        tail_kernel,
        out_shape=[
            SHAPE((256, D), F32),
            SHAPE((96, COLS + 128), F32),
            SHAPE((96, 256), F32),
            SHAPE((48, COLS), F32),
        ],
        in_specs=[ANY] * 5 + [VMEM, VMEM, ANY, VMEM],
        out_specs=[VMEM] * 4,
        scratch_shapes=[
            bf(256, WIDE),
            bf(256, MORE + 256),
            bf(LEN, WIDE),
            bf(LEN, MORE + 256),
            bf(D, PROJ),
            bf(2, 2, 4, 96, LEN),
            bf(LEN, D),
            bf(D, 256),
            f32(256, D),
            bf(2, 4, 96, MORE),
            bf(2, 4, 96, MORE),
            bf(2, 4, 96, MORE),
            bf(2, 2, 4, 96, 256),
            bf(2, 4, 96, 256),
            bf(2, 4, 96, 256),
            f32(48, COLS),
            f32(4, 16, COLS),
            f32(4, 48, COLS),
            f32(4, 48, COLS),
            f32(2, 48, COLS),
            bf(4, 96, 256),
            f32(2, 96, 128),
        ]
        + token_scratch()
        + grid_scratch("x", COLS + 128, 48)
        + grid_scratch("y", COLS + 128, 48)
        + grid_scratch("x", 128)
        + sems(64)
        + [pltpu.SemaphoreType.DMA((8,))],
        compiler_params=pltpu.CompilerParams(collective_id=3, has_side_effects=True, vmem_limit_bytes=ROOM),
        name="tail",
    )(*args)


def finish_kernel(grad, tokens, cot, branch, norm_gain, inner, bc, small, gate, wout, tokens_out, branch_out, inner_out, bc_out, gate_out, wout_out, step_out, norm, conv, bias, conv_bc, bias_bc, step_bias, decay, skip, gain):
    v = tokens[...].astype(F32)
    root = lax.rsqrt(jnp.mean(v * v, axis=1, keepdims=True) + EPS)
    scaled = grad[...] * norm_gain[...].reshape(1, D)
    tokens_out[...] = cot[...].astype(F32) + root * scaled - v * (root * root * root) * jnp.mean(scaled * v, axis=1, keepdims=True)
    branch_out[...] = branch[...]

    @pl.when(pl.program_id(0) == 0)
    def _():
        inner_out[...] = inner[:, :COLS]
        bc_out[...] = bc[...]
        gate_out[...] = gate[...]
        wout_out[...] = wout[...]
        step_out[...] = jnp.transpose(jnp.concatenate([inner[:, COLS:], jnp.zeros((32, 128), F32)], axis=0))[0:HEADS, 0:96]
        norm[...] = jnp.concatenate([small[32 + k : 33 + k, :] for k in range(4)], axis=1).reshape(D)
        conv_bc[...] = small[36:40, 0:256]
        bias_bc[...] = small[40:41, 0:256].reshape(256)
        mine = small[pl.ds(pl.multiple_of(lax.axis_index("yh") * 16, 8), 16), :]
        conv[...] = mine[0:4, :]
        bias[...] = mine[4:5, :].reshape(COLS)
        gain[...] = mine[5:6, :].reshape(COLS)
        step_bias[...] = mine[6:7, 0:HEADS].reshape(HEADS)
        decay[...] = mine[7:8, 0:HEADS].reshape(HEADS)
        skip[...] = mine[8:9, 0:HEADS].reshape(HEADS)


def run_finish(*args):
    f32 = lambda *s: SHAPE(s, F32)
    strip = lambda: pl.BlockSpec((128, D), lambda k: (k, 0))
    whole = lambda *s: pl.BlockSpec(s, lambda k: (0,) * len(s))
    shapes = (
        (96, COLS), (96, 256), (96, COLS), (96, COLS), (HEADS, 96), (D,), (4, COLS), (COLS,), (4, 256), (256,), (HEADS,), (HEADS,), (HEADS,), (COLS,),
    )
    return pl.pallas_call(
        finish_kernel,
        grid=(2,),
        out_shape=[f32(256, D), SHAPE((256, D), BF16)] + [f32(*s) for s in shapes],
        in_specs=[strip(), strip(), strip(), strip()]
        + [whole(*s) for s in ((D,), (96, COLS + 128), (96, 256), (48, COLS), (96, COLS), (96, COLS))],
        out_specs=[strip(), strip()] + [whole(*s) for s in shapes],
        compiler_params=pltpu.CompilerParams(vmem_limit_bytes=ROOM),
        name="finish",
    )(*args)


def shards(tokens, norm_gain, w_gate, w_inner, w_bc, w_step, conv_inner, bias_inner, conv_bc, bias_bc, step_bias, decay_log, skip_gain, gate_gain, w_out, cotangent):
    (
        inner, zin, y, hin, dt, r, bc, bc_in, zbc, normed_t, gains, mixed, gs, gg, cot_t, normed, wx, wout, wbc, prm,
    ) = run_front(
        tokens, norm_gain, w_gate, w_inner, w_out, w_bc, w_step.T, conv_inner, bias_inner, gate_gain, step_bias, decay_log,
        skip_gain, conv_bc, bias_bc, cotangent,
    )
    wx, wout, wbc = wx.reshape(D, PROJ), wout.reshape(D, WIDE), wbc.reshape(D, 256)
    cat, acc, acc_bc, output, wout_grad, gate_grad = run_backward(
        gs, inner, zin, y, hin, prm, bc, dt, r, gains, mixed, wout, cot_t, gg, normed_t, tokens, zbc, bc_in, conv_bc
    )
    grad, inner_grad, bc_grad, small = run_tail(gg, cat, wx, normed_t, normed, acc, acc_bc, wbc, norm_gain)
    (
        tokens_grad, output, inner_grad, bc_grad, gate_grad, wout_grad, step_grad,
        norm, conv, bias, conv_bc_grad, bias_bc_grad, step_bias_grad, decay, skip, gate_gain_grad,
    ) = run_finish(grad, tokens, cotangent, output, norm_gain, inner_grad, bc_grad, small, gate_grad, wout_grad)
    return (
        output, tokens_grad, norm, gate_grad, inner_grad, bc_grad, step_grad.T, conv, bias, conv_bc_grad,
        bias_bc_grad, step_bias_grad, decay, skip, gate_gain_grad, wout_grad,
    )


def solution(mesh):
    fine = Mesh(mesh.devices.reshape(2, 4, 2, 2, 4), AXES)
    dp, tensor = ("yl", "x", "c"), ("yh", "z")
    tokens, weight = P(dp + tensor, None), P(dp, tensor)
    heads, shared = P(tensor), P()
    return jax.shard_map(
        shards,
        mesh=fine,
        in_specs=(
            tokens, shared, weight, weight, P(dp, None), weight, P(None, tensor), heads,
            shared, shared, heads, heads, heads, heads, weight, tokens,
        ),
        out_specs=(
            tokens, tokens, shared, weight, weight, P(dp, None), weight, P(None, tensor), heads,
            shared, shared, heads, heads, heads, heads, weight,
        ),
        check_vma=False,
    )
```

```python
import jax
import jax.numpy as jnp
from jax import lax
from jax.experimental import pallas as pl
from jax.experimental.pallas import tpu as pltpu
from jax.sharding import Mesh
from jax.sharding import PartitionSpec as P

D = 1536
LEN = 1024
INNER = 3072
STATE = 128
BLOCK = 256
BLOCKS = LEN // BLOCK
GROUPS = 2
HEADS = 6
COLS = HEADS * 64
WIDE = GROUPS * COLS
STEPS = 2 * WIDE
PROJ = STEPS + GROUPS * 128
MORE = PROJ - WIDE
LOG2E = 1.4426950408889634
EPS = 1e-05
F32 = jnp.float32
BF16 = jnp.bfloat16
MESH = pl.DeviceIdType.MESH
AXES = ("yl", "x", "c", "yh", "z")
ANY = pl.BlockSpec(memory_space=pl.ANY)
VMEM = pl.BlockSpec(memory_space=pltpu.VMEM)
SHAPE = jax.ShapeDtypeStruct
ROOM = 60 * 2**20


def dot(a, b):
    return jnp.dot(a, b, preferred_element_type=F32)


def dot_nt(a, b):
    return lax.dot_general(a, b, (((1,), (1,)), ((), ())), preferred_element_type=F32)


def dot_tn(a, b):
    return lax.dot_general(a, b, (((0,), (0,)), ((), ())), preferred_element_type=F32)


def pieces(v, n):
    out = []
    for _ in range(n):
        hi = v.astype(BF16)
        out.append(hi)
        v = v - hi.astype(F32)
    return out


def dot_left(v, ones, n):
    return sum(dot(p, ones) for p in pieces(v, n))


def spread(v, ones):
    hi = v.astype(BF16).astype(F32)
    low = pltpu.roll(v - hi, 64, 1)
    return dot(jnp.where(iota(v.shape, 1) < 64, hi, low).astype(BF16), ones)


def folded(v, ones):
    hi = v.astype(BF16)
    low = (v - hi.astype(F32)).astype(BF16)
    return dot(hi, ones) + dot(low, ones)


def dot_right(ones, v, n):
    return sum(dot(ones, p) for p in pieces(v, n))


def iota(shape, axis):
    return lax.broadcasted_iota(jnp.int32, shape, axis)


def expander():
    row, col = iota((128, COLS), 0), iota((128, COLS), 1)
    return ((row & 63) == lax.shift_right_logical(col, 6)).astype(BF16)


def reducer():
    row, col = iota((COLS, 128), 0), iota((COLS, 128), 1)
    return (col == lax.shift_right_logical(row, 6)).astype(BF16)


def sigmoid(v):
    return 0.5 * jnp.tanh(0.5 * v) + 0.5


def lower(strict=False):
    row, col = iota((BLOCK, BLOCK), 0), iota((BLOCK, BLOCK), 1)
    return ((row > col) if strict else (row >= col)).astype(BF16)


def upper():
    return (iota((BLOCK, BLOCK), 0) <= iota((BLOCK, BLOCK), 1)).astype(BF16)


def token_row(v):
    v = sum(v[:, 128 * i : 128 * (i + 1)] for i in range(v.shape[1] // 128))
    ones = jnp.ones((8, 128), BF16)
    return sum(dot_nt(ones, p) for p in pieces(v, 3))[0:1, :]


class Net:
    def __init__(self, send, recv):
        self.send, self.recv, self.copies = send, recv, []
        self.at = {name: lax.axis_index(name) for name in AXES}
        self.at["y"] = self.at["yh"] * 2 + self.at["yl"]
        self.places = {(a, s): lax.rem(self.at[a] + s + 4, 4) for a in ("x", "y", "z") for s in (1, -1, 2)}
        self.other = 1 - self.at["c"]
        self.targets = {("c", 1): {"c": self.other}}
        for (a, s), place in self.places.items():
            self.targets[a, s] = {"yh": place // 2, "yl": lax.rem(place, 2)} if a == "y" else {a: place}

    def near(self, axis, step):
        return self.places[axis, step]

    def plan(self, src, dst, axis, step=1):
        copy = Copy(self, len(self.copies), src, dst, self.targets[axis, step])
        self.copies.append(copy)
        return copy

    def start(self, src, dst, axis, step=1):
        return self.plan(lambda: src, lambda: dst, axis, step).start()

    def around(self, src, dst, axis):
        return [self.start(src, dst, axis, step) for step in (1, -1, 2)]

    def greet(self, peers):
        here, self.peers = pltpu.get_barrier_semaphore(), len(peers)
        for peer in peers:
            pl.semaphore_signal(here, inc=1, device_id=self.targets[peer], device_id_type=MESH)

    def met(self):
        pl.semaphore_wait(pltpu.get_barrier_semaphore(), self.peers)

    def finish(self):
        for copy in self.copies:
            copy.arrived()
        for copy in self.copies:
            copy.left()


class Copy:
    def __init__(self, net, index, src, dst, target):
        self.net, self.index, self.src, self.dst, self.target = net, index, src, dst, target
        self.here, self.gone = False, False

    def made(self):
        return pltpu.make_async_remote_copy(
            src_ref=self.src(),
            dst_ref=self.dst(),
            send_sem=self.net.send.at[self.index],
            recv_sem=self.net.recv.at[self.index],
            device_id=self.target,
            device_id_type=MESH,
        )

    def start(self):
        self.made().start()
        return self

    def arrived(self):
        if not self.here:
            self.here = True
            self.made().wait_recv()

    def left(self):
        if not self.gone:
            self.gone = True
            self.made().wait_send()


def sems(n):
    return [pltpu.SemaphoreType.DMA((n,)), pltpu.SemaphoreType.DMA((n,))]


def rows(ref, first, count):
    return ref.at[pl.ds(pl.multiple_of(first, 16), count)]


def lanes(first, count):
    return pl.ds(pl.multiple_of(first, 128), count)


def arrive(copies):
    for copy in copies:
        copy.arrived()


HALVES = ((0, 1), (1, -1))


class GridSum:
    def __init__(self, net, first, held, spans, scratch, cut=(0, 96)):
        self.net, self.first, self.held, self.spans = net, first, held, spans
        self.land, self.mid, self.last = scratch
        self.rows = pl.ds(*cut)
        self.one, self.two = [], []
        for slot, step in enumerate((2, 1, -1)):
            if first == "x":
                self.plan(self.one, lambda step=step: held.at[:, net.near("x", step), self.rows], lambda slot=slot: self.land.at[slot], "x", step)
            else:
                self.plan(self.two, lambda step=step: self.mid.at[net.near("x", step)], lambda slot=slot: self.last.at[slot], "x", step)
            lane = 0
            for base, n in spans:
                there = lambda step=step, base=base, n=n: lanes(base + (net.near("y", step) // 2) * n, n)
                if first == "x":
                    src = lambda step=step, there=there: self.mid.at[lax.rem(net.near("y", step), 2), :, there()]
                    self.plan(self.two, src, lambda slot=slot, lane=lane, n=n: self.last.at[slot, :, pl.ds(lane, n)], "y", step)
                else:
                    src = lambda step=step, there=there: held.at[lax.rem(net.near("y", step), 2), :, self.rows, there()]
                    self.plan(self.one, src, lambda slot=slot, lane=lane, n=n: self.land.at[slot, :, :, pl.ds(lane, n)], "y", step)
                lane += n

    def plan(self, to, src, dst, axis, step):
        to.append(self.net.plan(src, dst, axis, step))

    def step1(self):
        for copy in self.one:
            copy.start()

    def step2(self):
        arrive(self.one)
        at = self.net.at
        if self.first == "x":
            self.mid[...] = self.total(self.held[:, at["x"], self.rows], self.land, slice(None)).astype(BF16)
        else:
            lane = 0
            for base, n in self.spans:
                cut = slice(lane, lane + n)
                own = self.held[at["yl"], :, self.rows, lanes(base + at["yh"] * n, n)]
                self.mid[:, :, cut] = self.total(own, self.land, cut).astype(BF16)
                lane += n
        for copy in self.two:
            copy.start()

    def total(self, own, others, cut):
        return (own.astype(F32) + others[0, ..., cut].astype(F32)) + (others[1, ..., cut].astype(F32) + others[2, ..., cut].astype(F32))

    def step3(self, out):
        arrive(self.two)
        at = self.net.at
        if self.first == "y":
            out[self.rows, :] = self.total(self.mid[at["x"]], self.last, slice(None))
            return
        lane = 0
        for base, n in self.spans:
            cut = slice(lane, lane + n)
            out[self.rows, cut] = self.total(self.mid[at["yl"], :, lanes(base + at["yh"] * n, n)], self.last, cut)
            lane += n


def grid_scratch(first, width, count=96):
    blocks, wide = (2, 2 * width) if first == "x" else (4, width)
    return [pltpu.VMEM(s, BF16) for s in ((3, blocks, count, wide), (blocks, count, wide), (3, count, width))]


class TokenSum:
    def __init__(self, net, scratch):
        self.net, self.far, self.half, self.fold, self.whole = net, *scratch
        self.one = [
            net.plan(lambda p=p: self.far.at[pl.ds(128 * p, 128)], lambda p=p: self.half.at[p], "z", step) for p, step in HALVES
        ]
        half = lambda ref, p, n: ref.at[p, pl.ds(128 * n, 128)]
        self.ready = [net.plan(lambda p=p: half(self.fold, p, 1 - p), lambda p=p: half(self.whole, p, 1 - p), "z", step) for p, step in HALVES]
        self.added = [net.plan(lambda p=p: half(self.fold, p, p), lambda p=p: half(self.whole, p, p), "z", step) for p, step in HALVES]

    def step1(self):
        for copy in self.one:
            copy.start()

    def folded(self, p):
        self.ready[p].start()

    def step2(self):
        arrive(self.one)
        for p, _ in HALVES:
            self.fold[p, 128 * p : 128 * p + 128, :] += self.half[p]
            self.added[p].start()

    def step3(self):
        arrive(self.ready + self.added)
        return self.whole[0].astype(F32) + self.whole[1].astype(F32)


def token_scratch():
    return [pltpu.VMEM((256, D), BF16), pltpu.VMEM((2, 128, D), BF16), pltpu.VMEM((2, 256, D), BF16), pltpu.VMEM((2, 256, D), BF16)]


def earlier(v, before, step):
    if step == 0:
        return v
    turned = pltpu.roll(v, step, 0)
    starts = jnp.where(iota(before.shape, 0) < step, pltpu.roll(before, step, 0), turned[0:8, :])
    return jnp.concatenate([starts, turned[8:, :]], axis=0)


def front_kernel(
    x, gain, w_gate, w_inner, w_out, w_bc, w_step, conv, bias, gate_gain, step_bias, decay_log, skip_gain, conv_bc, bias_bc, cot,
    inner_out, z_out, y_out, h_out, dt_out, r_out, bc_out, bcin_out, zbc_out, normed_t, gains_out,
    mixed_out, gs_out, gg_out, cot_t, normed_out, wx_out, wout_out, wbc_out, prm_out,
    normed, wx, wout, wbc, prm, xv, stepv, stept, pk,
    cots, gps, acts, slopes, gms, mixed, gg, turned_c, ext, extbc, state, stat, cross, slots, slots_c, send, recv, local,
):
    i = pl.program_id(0)
    net = Net(send, recv)
    at = net.at
    yh, cx, cc, z, y = at["yh"], at["x"], at["c"], at["z"], at["y"]
    own_rows = lambda ref: rows(ref, z * 256, 256)
    order = ((0, 1), (1, -1), (1, 1), (0, -1))
    part = lambda ref, p, s: rows(ref, net.near("z", -s) * 256 + 128 * p, 128)
    c1 = [
        net.plan(lambda p=p: cot.at[pl.ds(128 * p, 128)], lambda p=p: rows(cots, z * 256 + 128 * p, 128), "z", s) for p, s in order
    ]
    c2 = [net.plan(lambda p=p, s=s: part(cots, p, s), lambda p=p, s=s: part(cots, p, s), "z", s) for p, s in HALVES]
    q = [net.plan(lambda: stat, lambda: slots.at[z], "z", step) for step in (1, -1, 2)]
    qc = [net.plan(lambda: cross, lambda: slots_c.at[z], "z", step) for step in (1, -1, 2)]
    spot_o = lambda xx, cut=pl.ds(0, 96): wout.at[at["yl"], xx, cc, cut, lanes(yh * COLS, COLS)]
    line_o = lambda yy, cut=pl.ds(0, 96): wout.at[lax.rem(yy, 2), :, cc, cut, lanes((yy // 2) * COLS, COLS)]
    same = lambda ref, axis, step=1: net.plan(ref, ref, axis, step)
    o1 = [net.plan(lambda: w_out, lambda: spot_o(cx), "x", step) for _, step in HALVES]
    o2 = [same(lambda p=p, s=s: spot_o(net.near("x", -s), pl.ds(48 * p, 48)), "x", s) for p, s in HALVES]
    o3 = [same(lambda: line_o(y), "y", step) for _, step in HALVES]
    o4 = [same(lambda p=p, s=s: line_o(net.near("y", -s), pl.ds(48 * p, 48)), "y", s) for p, s in HALVES]
    oc = [same(lambda: line_o(y), "c")] + [same(lambda s=s: line_o(net.near("y", s)), "c") for s in (1, -1, 2)]
    own = lambda: pltpu.make_async_copy(cot, own_rows(cots), local.at[0])
    pairs = ((normed, normed_out), (wx, wx_out), (wbc, wbc_out), (prm, prm_out), (wout, wout_out))
    leave = lambda n: pltpu.make_async_copy(*pairs[n], local.at[1 + n])

    @pl.when(i == 0)
    def _():
        load = pltpu.make_async_copy(x, xv, local.at[7])
        load.start()
        net.greet([("z", 1), ("z", -1), ("z", 2), ("x", 1), ("x", -1), ("y", 1), ("y", -1), ("y", 2), ("c", 1)])
        own().start()
        stept[...] = jnp.zeros_like(stept)
        stept[0:HEADS, 0:96] = w_step[...].astype(F32)
        stepv[...] = jnp.transpose(stept[...])[0:96, :].astype(BF16)
        pk[...] = jnp.zeros_like(pk)
        pk[0:4, :] = conv[...]
        pk[4:5, :] = bias[...].reshape(1, COLS)
        pk[5:6, :] = gate_gain[...].reshape(1, COLS)
        pk[6:7, 0:HEADS] = step_bias[...].reshape(1, HEADS)
        pk[7:8, 0:HEADS] = decay_log[...].reshape(1, HEADS)
        pk[8:9, 0:HEADS] = skip_gain[...].reshape(1, HEADS)
        first = {
            "x": ((w_gate, wx, 0, COLS), (w_bc.at[:, lanes(yh * 128, 128)], wbc, 0, 128)),
            "y": ((w_inner, wx, WIDE, COLS), (stepv, wx, STEPS, 128)),
        }
        then = {"x": "y", "y": "x"}
        done = []

        def go(src, dst, axis, step=1):
            done.append(net.start(src, dst, axis, step))
            return done[-1]

        def spot(ref, base, n, yy, xx, cut=pl.ds(0, 96)):
            return ref.at[lax.rem(yy, 2), xx, cc, cut, lanes(base + (yy // 2) * n, n)]

        def line(axis, ref, base, n, place, cut=pl.ds(0, 96)):
            if axis == "x":
                return ref.at[lax.rem(place, 2), :, cc, cut, lanes(base + (place // 2) * n, n)]
            return ref.at[:, place, cc, cut, lanes(base, 2 * n)]

        load.wait()
        v = xv[...].astype(F32)
        root = lax.rsqrt(jnp.mean(v * v, axis=1, keepdims=True) + EPS)
        normed[pl.ds(pl.multiple_of(z * 256, 256), 256), :] = (v * root * gain[...].reshape(1, D)).astype(BF16)
        net.met()
        zs = {}
        for p, s in order:
            here = rows(normed, z * 256 + 128 * p, 128)
            zs[p, s] = go(here, here, "z", s)
        sent = {"x": [], "y": []}
        for axis in ("x", "y"):
            for src, ref, base, n in first[axis]:
                sent[axis].append([go(src, spot(ref, base, n, y, cx), axis, step) for _, step in HALVES])
        mine = [
            pltpu.make_async_copy(src, spot(ref, base, n, y, cx), local.at[8 + k])
            for k, (src, ref, base, n) in enumerate(first["x"] + first["y"])
        ]
        mine.append(pltpu.make_async_copy(pk, prm.at[yh], local.at[12]))
        mine.append(pltpu.make_async_copy(w_out, spot_o(cx), local.at[13]))
        for copy in mine:
            copy.start()
        for copy in o1:
            copy.start()
        for axis in ("x", "y"):
            for src, ref, base, n in first[axis]:
                go(src, spot(ref, base, n, y, cx), "c")
        go(pk, prm.at[yh], "y", 2)
        second = {"x": [], "y": []}
        for axis in ("x", "y"):
            for (src, ref, base, n), copies in zip(first[axis], sent[axis]):
                for (p, s), copy in zip(HALVES, copies):
                    copy.arrived()
                    cut = pl.ds(48 * p, 48)
                    here = spot(ref, base, n, y, net.near("x", -s), cut) if axis == "x" else spot(ref, base, n, net.near("y", -s), cx, cut)
                    second[axis].append(go(here, here, axis, s))
        for copy in mine:
            copy.wait()
        third = {"x": [], "y": []}
        for axis in ("x", "y"):
            arrive(second[axis])
            for src, ref, base, n in first[axis]:
                here = line(axis, ref, base, n, at[then[axis]])
                third[axis].append([go(here, here, then[axis], s) for _, s in HALVES])
        for copy, start in zip(o1, o2):
            copy.arrived()
            start.start()
        for axis in ("x", "y"):
            for src, ref, base, n in first[axis]:
                for s in (1, -1, 2):
                    here = spot(ref, base, n, y, net.near("x", s)) if axis == "x" else spot(ref, base, n, net.near("y", s), cx)
                    go(here, here, "c")
        for p, s in HALVES:
            zs[p, s].arrived()
            here = part(normed, p, s)
            go(here, here, "z", s)
        for copy in c1:
            copy.start()
        fourth = {"x": [], "y": []}
        for axis in ("x", "y"):
            for (src, ref, base, n), copies in zip(first[axis], third[axis]):
                for (p, s), copy in zip(HALVES, copies):
                    copy.arrived()
                    place = net.near(then[axis], -s)
                    here = line(axis, ref, base, n, place, pl.ds(48 * p, 48))
                    fourth[axis].append(go(here, here, then[axis], s))
                    here = line(axis, ref, base, n, place)
                    go(here, here, "c")
        arrive(o2)
        for copy in o3:
            copy.start()
        for axis in ("x", "y"):
            arrive(fourth[axis])
            for src, ref, base, n in first[axis]:
                here = line(axis, ref, base, n, net.near(then[axis], 2))
                go(here, here, "c")
        for copy in done:
            copy.arrived()
        for copy in done:
            copy.left()
        for n in range(4):
            leave(n).start()
        ext[...] = jnp.zeros_like(ext)
        extbc[...] = jnp.zeros_like(extbc)
        state[...] = jnp.zeros_like(state)
        stat[...] = jnp.zeros_like(stat)
        cross[...] = jnp.zeros_like(cross)

    @pl.when(i == 2)
    def _():
        for copy, start in zip(c1[:2], c2):
            copy.arrived()
            start.start()
        for copy, start in zip(o3, o4):
            copy.arrived()
            start.start()
        for copy in oc[:3]:
            copy.start()

    @pl.when(i < BLOCKS)
    def _():
        xb = normed[pl.ds(pl.multiple_of(i * BLOCK, BLOCK), BLOCK), :]
        turned = jnp.transpose(xb).reshape(2, 4, 2, 96, BLOCK)
        for core in range(2):
            normed_t[core] = turned[:, :, core]
        bc_in = dot(xb, wbc[...].reshape(D, 256))
        bcin_out[...] = bc_in.astype(BF16)
        before_bc = extbc[...]
        extbc[...] = bc_in[BLOCK - 8 :, :]
        zb = bias_bc[...].reshape(1, 256) + sum(conv_bc[j : j + 1, :] * earlier(bc_in, before_bc, 3 - j) for j in range(4))
        zbc_out[...] = zb.astype(BF16)
        bc = (zb * sigmoid(zb)).astype(BF16)
        bc_out[...] = bc
        b, c = bc[:, :STATE], bc[:, STATE:]
        scores = jnp.where(iota((BLOCK, BLOCK), 0) >= iota((BLOCK, BLOCK), 1), dot_nt(c, b), 0.0)
        tri, ones = lower(), expander()
        left = iota((BLOCK, 128), 1) < 64
        weight = lambda first, n: wx[:, :, :, :, first : first + n].reshape(D, n)
        steps = dot(xb, weight(STEPS, 256))
        total = jnp.zeros((BLOCK, 128), F32)
        for g in range(GROUPS):
            if g == 1:

                @pl.when(i == BLOCKS - 1)
                def _():
                    arrive(o4)
                    oc[3].start()

            cut = slice(g * COLS, (g + 1) * COLS)
            u = steps[:, 128 * g : 128 * (g + 1)] + prm[g, 6:7, 0:128]
            dt = jnp.maximum(u, 0.0) + jnp.log(1.0 + jnp.exp(-jnp.abs(u)))
            rate = -jnp.exp(prm[g, 7:8, 0:128]) * LOG2E
            r = dot_right(tri, dt * rate, 3)
            dt_out[g] = dt
            r_out[g] = r
            rt = jnp.transpose(r)
            gate = dot(xb, weight(g * COLS, COLS))
            inner = dot(xb, weight(WIDE + g * COLS, COLS))
            inner_out[:, cut] = inner.astype(BF16)
            before = ext[:, cut]
            ext[:, cut] = inner[BLOCK - 8 :, :]
            zv = prm[g, 4:5, :] + sum(prm[g, j : j + 1, :] * earlier(inner, before, 3 - j) for j in range(4))
            z_out[:, cut] = zv
            xv = zv * sigmoid(zv)
            last = r[BLOCK - 1 : BLOCK, :]
            w = xv * spread(dt, ones)
            grow = spread(jnp.exp2(r), ones)
            tail = spread(jnp.exp2(last - r), ones)
            skip = spread(prm[g, 8:16, 0:128], ones)[0:1, :]
            wl = w.astype(BF16)
            h = state[:, cut]
            h_out[0, g] = h.astype(BF16)
            parts = []
            for p in range(HEADS // 2):
                halves = []
                for n in (2 * p, 2 * p + 1):
                    gap = jnp.minimum(r[:, n : n + 1] - rt[n : n + 1, :], 0.0)
                    halves.append(dot((scores * jnp.exp2(gap)).astype(BF16), wl[:, 128 * p : 128 * (p + 1)]))
                parts.append(jnp.where(left, halves[0], halves[1]))
            yv = jnp.concatenate(parts, axis=1) + grow * dot(c, h.astype(BF16)) + skip * xv
            y_out[:, cut] = yv
            state[:, cut] = grow[BLOCK - 1 : BLOCK, :] * h + dot_tn(b, (tail * w).astype(BF16))
            sig = sigmoid(gate)
            act = gate * sig
            gp = yv * act
            here_now = pl.ds(pl.multiple_of(i * BLOCK, BLOCK), BLOCK)
            gps[here_now, cut] = gp
            acts[here_now, cut] = act
            slopes[here_now, cut] = yv * (sig + act * (1.0 - sig))
            sq = gp * gp
            total = total + (sq[:, 0:128] + sq[:, 128:256] + sq[:, 256:384])
        stat[pl.ds(i, 1), :] = token_row(total)

    @pl.when(i == BLOCKS)
    def _():
        for copy in q:
            copy.start()
        slots[z] = stat[...]
        own().wait()
        arrive(oc)
        leave(4).start()
        gain = jnp.concatenate([prm[0, 5:6, :], prm[1, 5:6, :]], axis=1)
        moved = []

        def away(src, dst, *cut):
            moved.append(pltpu.make_async_copy(src.at[cut], dst.at[cut], local.at[14 + len(moved)]))
            moved[-1].start()

        def place(n):
            block = lax.rem(z + n + lax.div(n, 2) - 2 * lax.div(n, 3), 4)
            return block, pl.ds(pl.multiple_of(block * BLOCK, BLOCK), BLOCK)

        def turn_out(n):
            full, (block, at) = slice(None), place(n)
            cut = (full, full, full, full, at)
            return pltpu.make_async_copy(turned_c.at[cut], cot_t.at[cut], local.at[26 + n])

        def products(n, nothing):
            @pl.when(n == 1)
            def _():
                arrive(c1)

            @pl.when(n == 3)
            def _():
                arrive(c2)

            block, at = place(n)
            cb = cots[at, :]
            turned = jnp.transpose(cb).reshape(2, 4, 2, 96, BLOCK)
            for core in range(2):
                turned_c[core, :, :, :, at] = turned[:, :, core]
            turn_out(n).start()
            gm = dot(cb, wout[...].reshape(D, WIDE)) * gain
            gms[at, :] = gm
            cross[pl.ds(block, 1), :] = token_row(gm * gps[at, :])
            return nothing

        lax.fori_loop(0, BLOCKS, products, 0)
        for copy in qc:
            copy.start()
        slots_c[z] = cross[...]
        arrive(q)
        for copy in q:
            copy.left()
        root = lax.rsqrt(((slots[0] + slots[1]) + (slots[2] + slots[3])) * (1.0 / INNER) + EPS)
        columns = jnp.transpose(root)
        gain_grad = jnp.zeros((1, WIDE), F32)
        for k in range(BLOCKS):
            at = slice(k * BLOCK, (k + 1) * BLOCK)
            normal, gm = gps[at, :] * columns[:, k : k + 1], gms[at, :]
            mixed[at, :] = (normal * gain).astype(BF16)
            away(mixed, mixed_out, pl.ds(k * BLOCK, BLOCK))
            gain_grad = gain_grad + jnp.sum(gm * normal, axis=0, keepdims=True)
            gms[at, :] = gm * columns[:, k : k + 1]
        gain_grad = gain_grad / gain
        arrive(qc)
        sums = (slots_c[0] + slots_c[1]) + (slots_c[2] + slots_c[3])
        columns = jnp.transpose(root * root * root * (sums * (1.0 / INNER)))
        for k in range(BLOCKS):
            at = slice(k * BLOCK, (k + 1) * BLOCK)
            gated = gms[at, :] - gps[at, :] * columns[:, k : k + 1]
            gms[at, :] = gated * acts[at, :]
            gg[at, :] = (gated * slopes[at, :]).astype(BF16)
            away(gms, gs_out, pl.ds(k * BLOCK, BLOCK))
            away(gg, gg_out, pl.ds(k * BLOCK, BLOCK))
        gains_out[...] = jnp.concatenate([gain_grad, jnp.zeros((7, WIDE), F32)], axis=0)
        for copy in c1 + c2 + qc + o1 + o2 + o3 + o4 + oc:
            copy.left()
        for copy in moved:
            copy.wait()
        for n in range(len(pairs)):
            leave(n).wait()
        for n in range(BLOCKS):
            turn_out(jnp.int32(n)).wait()


def run_front(*args):
    first = lambda k: jnp.minimum(k, BLOCKS - 1)
    keep = lambda *s: pl.BlockSpec(s, lambda k: (0,) * len(s))
    block = lambda n: pl.BlockSpec((BLOCK, n), lambda k: (first(k), 0))
    small = lambda: pl.BlockSpec((GROUPS, BLOCK, 128), lambda k: (0, first(k), 0))
    wide = SHAPE((LEN, WIDE), F32)
    narrow = SHAPE((GROUPS, LEN, 128), F32)
    bf = lambda *s: pltpu.VMEM(s, BF16)
    f32 = lambda *s: pltpu.VMEM(s, F32)
    return pl.pallas_call(
        front_kernel,
        grid=(BLOCKS + 1,),
        out_shape=[
            SHAPE((LEN, WIDE), BF16),
            wide,
            wide,
            SHAPE((BLOCKS, GROUPS, STATE, COLS), BF16),
            narrow,
            narrow,
            SHAPE((LEN, 256), BF16),
            SHAPE((LEN, 256), BF16),
            SHAPE((LEN, 256), BF16),
            SHAPE((2, 2, 4, 96, LEN), BF16),
            SHAPE((8, WIDE), F32),
            SHAPE((LEN, WIDE), BF16),
            wide,
            SHAPE((LEN, WIDE), BF16),
            SHAPE((2, 2, 4, 96, LEN), BF16),
            SHAPE((LEN, D), BF16),
            SHAPE((2, 4, 2, 96, PROJ), BF16),
            SHAPE((2, 4, 2, 96, WIDE), BF16),
            SHAPE((2, 4, 2, 96, 256), BF16),
            SHAPE((GROUPS, 16, COLS), F32),
        ],
        in_specs=[ANY, VMEM, ANY, ANY, ANY, ANY] + [VMEM] * 9 + [ANY],
        out_specs=[
            block(WIDE),
            block(WIDE),
            block(WIDE),
            pl.BlockSpec((1, GROUPS, STATE, COLS), lambda k: (first(k), 0, 0, 0)),
            small(),
            small(),
            block(256),
            block(256),
            block(256),
            pl.BlockSpec((2, 2, 4, 96, BLOCK), lambda k: (0, 0, 0, 0, first(k))),
            keep(8, WIDE),
        ]
        + [ANY] * 9,
        scratch_shapes=[
            bf(LEN, D),
            bf(2, 4, 2, 96, PROJ),
            bf(2, 4, 2, 96, WIDE),
            bf(2, 4, 2, 96, 256),
            f32(GROUPS, 16, COLS),
            bf(256, D),
            bf(96, 128),
            f32(128, 128),
            f32(16, COLS),
            bf(LEN, D),
            f32(LEN, WIDE),
            f32(LEN, WIDE),
            f32(LEN, WIDE),
            f32(LEN, WIDE),
            bf(LEN, WIDE),
            bf(LEN, WIDE),
            bf(2, 2, 4, 96, LEN),
            f32(8, WIDE),
            f32(8, 256),
            f32(STATE, WIDE),
            f32(8, BLOCK),
            f32(8, BLOCK),
            f32(4, 8, BLOCK),
            f32(4, 8, BLOCK),
        ]
        + sems(96)
        + [pltpu.SemaphoreType.DMA((30,))],
        compiler_params=pltpu.CompilerParams(collective_id=1, has_side_effects=True, vmem_limit_bytes=ROOM),
        name="front",
    )(*args)


def later(v, after, step):
    turned = pltpu.roll(v, BLOCK - step, 0)
    ends = jnp.where(iota(after.shape, 0) < 8 - step, turned[BLOCK - 8 :, :], pltpu.roll(after, 8 - step, 0))
    return jnp.concatenate([turned[: BLOCK - 8, :], ends], axis=0)


def backward_kernel(
    gs_in, inner, zin, y, hin, prm, bc, dt, r, gains, mixed, wout, cot_t, gg, normed_t, tokens, zbc, bc_in, conv_bc,
    cat_out, acc, acc_bc, branch_out, wout_out, wgate_out,
    ext, extbc, dstate, dst, dbc, held, got, away, mv, wv, cv, gv, nv, ownb, g0, g1, g2, g3, s1, s2, s3, t1, t2, t3, send, recv, local,
):
    k = pl.program_id(0)
    net = Net(send, recv)
    cc, z = net.at["c"], net.at["z"]
    cross = [net.plan(lambda n=n: away.at[n], lambda n=n: got.at[n], "c") for n in range(2)]
    token = TokenSum(net, (g0, g1, g2, g3))
    rings = (GridSum(net, "y", held.at[0], ((0, COLS),), (s1, s2, s3)), GridSum(net, "x", held.at[1], ((0, COLS),), (t1, t2, t3)))

    @pl.when(k == 0)
    def _():
        net.greet([("z", 1), ("z", -1)] + [(a, s) for a in ("x", "y") for s in (1, -1, 2)] + [("c", 1)])
        loads = [pltpu.make_async_copy(src, dst, local.at[n]) for n, (src, dst) in enumerate(((mixed, mv), (wout, wv), (cot_t, cv), (gg, gv), (normed_t, nv)))]
        for copy in loads:
            copy.start()
        loads[0].wait()
        loads[1].wait()
        branch = lambda place: dot_nt(mv[pl.ds(pl.multiple_of(place * 256, 256), 256), :], wv[...])
        grads = lambda left, right, core: dot(left[core].reshape(8 * 96, LEN), right[...]).astype(BF16).reshape(2, 4, 96, WIDE)
        g0[...] = branch(net.near("z", 2)).astype(BF16)
        net.met()
        token.step1()
        for p, step in HALVES:
            g2[p] = branch(net.near("z", step)).astype(BF16)
            token.folded(p)
        ownb[...] = branch(z)
        loads[2].wait()
        away[0] = grads(cv, mv, net.other)
        cross[0].start()
        loads[3].wait()
        loads[4].wait()
        away[1] = grads(nv, gv, net.other)
        cross[1].start()
        held[0] = grads(cv, mv, cc)
        held[1] = grads(nv, gv, cc)
        acc[...] = jnp.zeros_like(acc)
        acc_bc[...] = jnp.zeros_like(acc_bc)
        extbc[BLOCK : BLOCK + 8, :] = jnp.zeros((8, 256), F32)
        for g in range(GROUPS):
            acc[g, 5:6, :] = gains[0:1, g * COLS : (g + 1) * COLS]
        ext[BLOCK : BLOCK + 8, :] = jnp.zeros((8, WIDE), F32)
        dstate[...] = jnp.zeros_like(dstate)

    @pl.when(k > 0)
    def _():
        ext[BLOCK : BLOCK + 8, :] = ext[0:8, :]
        extbc[BLOCK : BLOCK + 8, :] = extbc[0:8, :]

    b, c = bc[:, :STATE], bc[:, STATE:]
    valid = iota((BLOCK, BLOCK), 1) >= iota((BLOCK, BLOCK), 0)
    scores = jnp.where(valid, dot_nt(b, c), 0.0)
    ones, fold = expander(), reducer()
    left = iota((BLOCK, 128), 1) < 64
    suffix, prefix = upper(), lower(strict=True)
    dst[...] = jnp.zeros_like(dst)
    dbc[...] = jnp.zeros_like(dbc)
    for g in range(GROUPS):
        if g == 0:

            @pl.when(k == 1)
            def _():
                token.step2()

            @pl.when(k == 3)
            def _():
                for ring in rings:
                    ring.step2()

        else:

            @pl.when(k == 0)
            def _():
                for n in range(2):
                    cross[n].arrived()
                    held[n] += got[n]
                    rings[n].step1()

        cut = slice(g * COLS, (g + 1) * COLS)
        yv = y[:, cut]
        gs = gs_in[:, cut]
        xi = inner[:, cut].astype(F32)
        zv = zin[:, cut]
        zs = sigmoid(zv)
        xv = zv * zs
        dtv = dt[g]
        rate = -jnp.exp(prm[g, 7:8, 0:128])
        rv = r[g]
        rt = jnp.transpose(rv)
        last = rv[BLOCK - 1 : BLOCK, :]
        dte = spread(dt[g], ones)
        grow = spread(jnp.exp2(rv), ones)
        tail = spread(jnp.exp2(last - rv), ones)
        skip = spread(prm[g, 8:16, 0:128], ones)[0:1, :]
        w = xv * dte
        wl = w.astype(BF16)
        gl = gs.astype(BF16)
        hl = hin[0, g]
        h = hl.astype(F32)
        dh = dstate[:, cut]
        dhl = dh.astype(BF16)
        parts = []
        for p in range(HEADS // 2):
            halves, shares = [], []
            pair = slice(128 * p, 128 * (p + 1))
            wp, gpair = wl[:, pair], gl[:, pair]
            zero = jnp.zeros_like(wp)
            w_low = pltpu.roll(w[:, pair] - wp.astype(F32), 64, 1).astype(BF16)
            g_low = (gs[:, pair] - gpair.astype(F32)).astype(BF16)
            g_turn = pltpu.roll(gpair.astype(F32), 64, 1).astype(BF16)
            for n in (2 * p, 2 * p + 1):
                decay = jnp.exp2(jnp.minimum(rt[n : n + 1, :] - rv[:, n : n + 1], 0.0))
                halves.append(dot((scores * decay).astype(BF16), gpair))
                pick = (lambda a, b: jnp.where(left, a, b)) if n % 2 == 0 else (lambda a, b: jnp.where(left, b, a))
                one = jnp.concatenate([pick(wp, w_low), pick(wp, zero)], axis=1)
                two = jnp.concatenate([pick(gpair, g_turn), g_low], axis=1)
                shares.append(dot_nt(one, two) * decay)
            parts.append(jnp.where(left, halves[0], halves[1]))
            dst[...] += shares[0] + shares[1]
        dwi = jnp.concatenate(parts, axis=1)
        dws = tail * dot(b, dhl)
        dw = dwi + dws
        skipgrad = gs * xv
        diff = folded(gl.astype(F32) * (yv - skip * xv) - wl.astype(F32) * dwi, fold)
        zsum = dot((w * dws).astype(BF16), fold)
        const = folded(jnp.sum(h * dh, axis=0, keepdims=True) * grow[BLOCK - 1 : BLOCK, :] + jnp.zeros((8, COLS), F32), fold)
        da = dot_right(suffix, diff, 3) + dot_right(prefix, zsum, 3) + const[0:1, :]
        dstep = (dot((xv * dw).astype(BF16), fold) + rate * da) * jnp.where(dtv < 0.02, dtv * (1.0 - dtv * (0.5 - dtv * (1.0 / 6.0))), 1.0 - jnp.exp(-dtv))
        cat_out[:, WIDE + 128 * g : WIDE + 128 * (g + 1)] = dstep.astype(BF16)
        gx = (grow * gs).astype(BF16)
        dbc[:, STATE:] += dot_nt(gx, hl)
        dbc[:, :STATE] += dot_nt((tail * w).astype(BF16), dhl)
        dstate[:, cut] = grow[BLOCK - 1 : BLOCK, :] * dh + dot_tn(c, gx)
        dx = dte * dw + skip * gs
        dz = dx * (zs * (1.0 + zv * (1.0 - zs)))
        after = ext[BLOCK : BLOCK + 8, cut]
        ext[0:8, cut] = dz[0:8, :]
        gi = jnp.zeros((BLOCK, COLS), F32)
        for j in range(4):
            moved = dz if j == 3 else later(dz, after, 3 - j)
            gi = gi + prm[g, j : j + 1, :] * moved
            acc[g, j : j + 1, :] += jnp.sum(xi * moved, axis=0, keepdims=True)
        cat_out[:, cut] = gi.astype(BF16)
        acc[g, 4:5, :] += jnp.sum(dz, axis=0, keepdims=True)
        acc[g, 6:7, 0:128] += jnp.sum(dstep, axis=0, keepdims=True)
        acc[g, 7:8, 0:128] += jnp.sum(da * dt[g], axis=0, keepdims=True) * rate
        acc[g, 8:9, 0:128] += folded(jnp.sum(skipgrad, axis=0, keepdims=True) + jnp.zeros((8, COLS), F32), fold)[0:1, :]
    ds = jnp.where(valid, dst[...], 0.0).astype(BF16)
    dbc[:, STATE:] += dot_tn(ds, b)
    dbc[:, :STATE] += dot(ds, c)
    zb = zbc[...].astype(F32)
    sig = sigmoid(zb)
    dz = dbc[...] * (sig + zb * sig * (1.0 - sig))
    extbc[0:BLOCK, :] = dz
    bi = bc_in[...].astype(F32)
    gi = jnp.zeros((BLOCK, 256), F32)
    for j in range(4):
        moved = extbc[3 - j : 3 - j + BLOCK, :]
        gi = gi + conv_bc[j : j + 1, :] * moved
        acc_bc[j : j + 1, :] += jnp.sum(bi * moved, axis=0, keepdims=True)
    acc_bc[4:5, :] += jnp.sum(dz, axis=0, keepdims=True)
    cat_out[:, MORE:] = gi.astype(BF16)

    @pl.when(k == BLOCKS - 1)
    def _():
        rings[0].step3(wout_out)
        rings[1].step3(wgate_out)
        branch_out[...] = (tokens[...].astype(F32) + (ownb[...] + token.step3())).astype(BF16)
        for copy in net.copies:
            copy.left()


def run_backward(*args):
    rev = lambda k: BLOCKS - 1 - k
    cols = lambda n: pl.BlockSpec((BLOCK, n), lambda k: (rev(k), 0))
    small = lambda: pl.BlockSpec((GROUPS, BLOCK, 128), lambda k: (0, rev(k), 0))
    keep = lambda *s: pl.BlockSpec(s, lambda k: (0,) * len(s))
    bf = lambda *s: pltpu.VMEM(s, BF16)
    f32 = lambda *s: pltpu.VMEM(s, F32)
    return pl.pallas_call(
        backward_kernel,
        grid=(BLOCKS,),
        out_shape=[
            SHAPE((LEN, MORE + 256), BF16),
            SHAPE((GROUPS, 16, COLS), F32),
            SHAPE((8, 256), F32),
            SHAPE((256, D), BF16),
            SHAPE((96, COLS), F32),
            SHAPE((96, COLS), F32),
        ],
        in_specs=[cols(WIDE)] * 4
        + [
            pl.BlockSpec((1, GROUPS, STATE, COLS), lambda k: (rev(k), 0, 0, 0)),
            keep(GROUPS, 16, COLS),
            cols(256),
            small(),
            small(),
            keep(8, WIDE),
        ]
        + [ANY] * 5
        + [keep(256, D), cols(256), cols(256), keep(4, 256)],
        out_specs=[cols(MORE + 256), keep(GROUPS, 16, COLS), keep(8, 256), keep(256, D), keep(96, COLS), keep(96, COLS)],
        scratch_shapes=[
            f32(BLOCK + 8, WIDE),
            f32(BLOCK + 8, 256),
            f32(STATE, WIDE),
            f32(BLOCK, BLOCK),
            f32(BLOCK, 256),
            bf(2, 2, 4, 96, WIDE),
            bf(2, 2, 4, 96, WIDE),
            bf(2, 2, 4, 96, WIDE),
            bf(LEN, WIDE),
            bf(D, WIDE),
            bf(2, 2, 4, 96, LEN),
            bf(LEN, WIDE),
            bf(2, 2, 4, 96, LEN),
            f32(256, D),
        ]
        + token_scratch()
        + grid_scratch("y", COLS)
        + grid_scratch("x", COLS)
        + sems(26)
        + [pltpu.SemaphoreType.DMA((5,))],
        compiler_params=pltpu.CompilerParams(collective_id=2, has_side_effects=True, vmem_limit_bytes=ROOM),
        name="backward",
    )(*args)


def tail_kernel(
    gg, cat, wx, normed_t, normed, acc, acc_bc, wbc, gain,
    tokens_out, inner_out, bc_out, small_out,
    far_gg, far_cat, ggv, catv, wxv, ntv, nv, wv, ownb, held, got, away, dbw, heldb, gotb, small, sp0, sp1, sp2, sp3, bz, by,
    g0, g1, g2, g3, a1, a2, a3, b1, b2, b3, c1, c2, c3, send, recv, local,
):
    net = Net(send, recv)
    at = net.at
    yh, cx, cc, z, y = at["yh"], at["x"], at["c"], at["z"], at["y"]
    net.greet([(a, s) for a in ("z", "x", "y") for s in (1, -1, 2)] + [("c", 1)])
    far_rows = lambda ref: rows(ref, net.near("z", 2) * 256, 256)
    pairs = ((far_rows(cat), far_cat), (far_rows(gg), far_gg), (wx, wxv), (wbc, wv), (cat, catv), (gg, ggv), (normed_t, ntv), (normed, nv))
    loads = [pltpu.make_async_copy(src, dst, local.at[i]) for i, (src, dst) in enumerate(pairs)]
    for copy in loads:
        copy.start()
    token = TokenSum(net, (g0, g1, g2, g3))
    spans = ((0, COLS), (WIDE, 128))
    rings = (GridSum(net, "x", held, spans, (a1, a2, a3), (0, 48)), GridSum(net, "y", held, spans, (b1, b2, b3), (48, 48)))
    ring_bc = GridSum(net, "x", heldb, ((0, 128),), (c1, c2, c3))

    def product(gates, others):
        return dot_nt(gates, wxv[:, 0:WIDE]) + dot_nt(others[:, 0:MORE], wxv[:, WIDE:]) + dot_nt(others[:, MORE:], wv[...])

    def block(place):
        cut = pl.ds(pl.multiple_of(place * 256, 256), 256)
        return product(ggv[cut, :], catv[cut, :])

    def of_norm(place, grad):
        cut = pl.ds(pl.multiple_of(place * 256, 256), 256)
        return jnp.sum(grad * nv[cut, :].astype(F32), axis=0, keepdims=True)

    for copy in loads[:4]:
        copy.wait()
    far = product(far_gg[...], far_cat[...])
    g0[...] = far.astype(BF16)
    net.met()
    token.step1()
    for copy in loads[4:7]:
        copy.wait()
    grads = lambda core, cut, n: dot(ntv[core].reshape(8 * 96, LEN), catv[:, cut]).astype(BF16).reshape(2, 4, 96, n)
    for core in range(2):
        dbw[core] = grads(core, slice(MORE, MORE + 256), 256)
    crossb = net.start(dbw.at[net.other], gotb, "c")
    loads[7].wait()
    norm_part = of_norm(net.near("z", 2), far)
    for p, step in HALVES:
        out = block(net.near("z", step))
        g2[p] = out.astype(BF16)
        norm_part = norm_part + of_norm(net.near("z", step), out)
        if p == 0:
            crossb.arrived()
            heldb[...] = dbw[cc] + gotb[...]
            ring_bc.step1()
    ownb[...] = block(z)
    norm_part = (norm_part + of_norm(z, ownb[...])) / gain[...].reshape(1, D)
    small[0:16, :] = acc[0]
    small[16:32, :] = acc[1]
    small[32:48, :] = jnp.zeros((16, COLS), F32)
    for k in range(4):
        small[32 + k : 33 + k, :] = norm_part[:, k * COLS : (k + 1) * COLS]
    small[36:41, 0:256] = acc_bc[0:5, :]
    sp0[z] = small[32:48, :]
    q = net.around(sp0.at[z], sp0.at[z], "z")
    for p, _ in HALVES:
        token.folded(p)
    ring_bc.step2()
    away[...] = grads(net.other, slice(0, MORE), MORE)
    cross = net.start(away, got, "c")
    held[...] = grads(cc, slice(0, MORE), MORE)
    cross.arrived()
    held[...] += got[...]
    ring_bc.step3(by.at[yh])
    qb = [net.start(by.at[yh], by.at[yh], "y", 2)]
    arrive(q)
    sp1[cx, 0:32, :] = small[0:32, :]
    sp1[cx, 32:48, :] = (sp0[0] + sp0[1]) + (sp0[2] + sp0[3])
    q = net.around(sp1.at[cx], sp1.at[cx], "x")
    for ring in rings:
        ring.step1()
    token.step2()
    arrive(qb)
    bz[z, :, 0:128] = by[0].astype(BF16)
    bz[z, :, 128:256] = by[1].astype(BF16)
    qb = net.around(bz.at[z], bz.at[z], "z")
    arrive(q)
    sp2[y] = (sp1[0] + sp1[1]) + (sp1[2] + sp1[3])
    q = net.around(sp2.at[y], sp2.at[y], "y")
    for ring in rings:
        ring.step2()
    arrive(q)
    sp3[cc] = (sp2[0] + sp2[1]) + (sp2[2] + sp2[3])
    q = [net.start(sp3.at[cc], sp3.at[cc], "c")]
    for ring in rings:
        ring.step3(inner_out)
    arrive(q)
    small_out[...] = sp3[0] + sp3[1]
    tokens_out[...] = token.step3() + ownb[...]
    arrive(qb)
    bc_out[...] = (bz[0].astype(F32) + bz[1].astype(F32)) + (bz[2].astype(F32) + bz[3].astype(F32))
    net.finish()


def run_tail(*args):
    bf = lambda *s: pltpu.VMEM(s, BF16)
    f32 = lambda *s: pltpu.VMEM(s, F32)
    return pl.pallas_call(
        tail_kernel,
        out_shape=[
            SHAPE((256, D), F32),
            SHAPE((96, COLS + 128), F32),
            SHAPE((96, 256), F32),
            SHAPE((48, COLS), F32),
        ],
        in_specs=[ANY] * 5 + [VMEM, VMEM, ANY, VMEM],
        out_specs=[VMEM] * 4,
        scratch_shapes=[
            bf(256, WIDE),
            bf(256, MORE + 256),
            bf(LEN, WIDE),
            bf(LEN, MORE + 256),
            bf(D, PROJ),
            bf(2, 2, 4, 96, LEN),
            bf(LEN, D),
            bf(D, 256),
            f32(256, D),
            bf(2, 4, 96, MORE),
            bf(2, 4, 96, MORE),
            bf(2, 4, 96, MORE),
            bf(2, 2, 4, 96, 256),
            bf(2, 4, 96, 256),
            bf(2, 4, 96, 256),
            f32(48, COLS),
            f32(4, 16, COLS),
            f32(4, 48, COLS),
            f32(4, 48, COLS),
            f32(2, 48, COLS),
            bf(4, 96, 256),
            f32(2, 96, 128),
        ]
        + token_scratch()
        + grid_scratch("x", COLS + 128, 48)
        + grid_scratch("y", COLS + 128, 48)
        + grid_scratch("x", 128)
        + sems(64)
        + [pltpu.SemaphoreType.DMA((8,))],
        compiler_params=pltpu.CompilerParams(collective_id=3, has_side_effects=True, vmem_limit_bytes=ROOM),
        name="tail",
    )(*args)


def finish_kernel(grad, tokens, cot, branch, norm_gain, inner, bc, small, gate, wout, tokens_out, branch_out, inner_out, bc_out, gate_out, wout_out, step_out, norm, conv, bias, conv_bc, bias_bc, step_bias, decay, skip, gain):
    v = tokens[...].astype(F32)
    root = lax.rsqrt(jnp.mean(v * v, axis=1, keepdims=True) + EPS)
    scaled = grad[...] * norm_gain[...].reshape(1, D)
    tokens_out[...] = cot[...].astype(F32) + root * scaled - v * (root * root * root) * jnp.mean(scaled * v, axis=1, keepdims=True)
    branch_out[...] = branch[...]

    @pl.when(pl.program_id(0) == 0)
    def _():
        inner_out[...] = inner[:, :COLS]
        bc_out[...] = bc[...]
        gate_out[...] = gate[...]
        wout_out[...] = wout[...]
        step_out[...] = jnp.transpose(jnp.concatenate([inner[:, COLS:], jnp.zeros((32, 128), F32)], axis=0))[0:HEADS, 0:96]
        norm[...] = jnp.concatenate([small[32 + k : 33 + k, :] for k in range(4)], axis=1).reshape(D)
        conv_bc[...] = small[36:40, 0:256]
        bias_bc[...] = small[40:41, 0:256].reshape(256)
        mine = small[pl.ds(pl.multiple_of(lax.axis_index("yh") * 16, 8), 16), :]
        conv[...] = mine[0:4, :]
        bias[...] = mine[4:5, :].reshape(COLS)
        gain[...] = mine[5:6, :].reshape(COLS)
        step_bias[...] = mine[6:7, 0:HEADS].reshape(HEADS)
        decay[...] = mine[7:8, 0:HEADS].reshape(HEADS)
        skip[...] = mine[8:9, 0:HEADS].reshape(HEADS)


def run_finish(*args):
    f32 = lambda *s: SHAPE(s, F32)
    strip = lambda: pl.BlockSpec((128, D), lambda k: (k, 0))
    whole = lambda *s: pl.BlockSpec(s, lambda k: (0,) * len(s))
    shapes = (
        (96, COLS), (96, 256), (96, COLS), (96, COLS), (HEADS, 96), (D,), (4, COLS), (COLS,), (4, 256), (256,), (HEADS,), (HEADS,), (HEADS,), (COLS,),
    )
    return pl.pallas_call(
        finish_kernel,
        grid=(2,),
        out_shape=[f32(256, D), SHAPE((256, D), BF16)] + [f32(*s) for s in shapes],
        in_specs=[strip(), strip(), strip(), strip()]
        + [whole(*s) for s in ((D,), (96, COLS + 128), (96, 256), (48, COLS), (96, COLS), (96, COLS))],
        out_specs=[strip(), strip()] + [whole(*s) for s in shapes],
        compiler_params=pltpu.CompilerParams(vmem_limit_bytes=ROOM),
        name="finish",
    )(*args)


def shards(tokens, norm_gain, w_gate, w_inner, w_bc, w_step, conv_inner, bias_inner, conv_bc, bias_bc, step_bias, decay_log, skip_gain, gate_gain, w_out, cotangent):
    (
        inner, zin, y, hin, dt, r, bc, bc_in, zbc, normed_t, gains, mixed, gs, gg, cot_t, normed, wx, wout, wbc, prm,
    ) = run_front(
        tokens, norm_gain, w_gate, w_inner, w_out, w_bc, w_step.T, conv_inner, bias_inner, gate_gain, step_bias, decay_log,
        skip_gain, conv_bc, bias_bc, cotangent,
    )
    wx, wout, wbc = wx.reshape(D, PROJ), wout.reshape(D, WIDE), wbc.reshape(D, 256)
    cat, acc, acc_bc, output, wout_grad, gate_grad = run_backward(
        gs, inner, zin, y, hin, prm, bc, dt, r, gains, mixed, wout, cot_t, gg, normed_t, tokens, zbc, bc_in, conv_bc
    )
    grad, inner_grad, bc_grad, small = run_tail(gg, cat, wx, normed_t, normed, acc, acc_bc, wbc, norm_gain)
    (
        tokens_grad, output, inner_grad, bc_grad, gate_grad, wout_grad, step_grad,
        norm, conv, bias, conv_bc_grad, bias_bc_grad, step_bias_grad, decay, skip, gate_gain_grad,
    ) = run_finish(grad, tokens, cotangent, output, norm_gain, inner_grad, bc_grad, small, gate_grad, wout_grad)
    return (
        output, tokens_grad, norm, gate_grad, inner_grad, bc_grad, step_grad.T, conv, bias, conv_bc_grad,
        bias_bc_grad, step_bias_grad, decay, skip, gate_gain_grad, wout_grad,
    )


def solution(mesh):
    fine = Mesh(mesh.devices.reshape(2, 4, 2, 2, 4), AXES)
    dp, tensor = ("yl", "x", "c"), ("yh", "z")
    tokens, weight = P(dp + tensor, None), P(dp, tensor)
    heads, shared = P(tensor), P()
    return jax.shard_map(
        shards,
        mesh=fine,
        in_specs=(
            tokens, shared, weight, weight, P(dp, None), weight, P(None, tensor), heads,
            shared, shared, heads, heads, heads, heads, weight, tokens,
        ),
        out_specs=(
            tokens, tokens, shared, weight, weight, P(dp, None), weight, P(None, tensor), heads,
            shared, shared, heads, heads, heads, heads, weight,
        ),
        check_vma=False,
    )
```

```python
import jax
import jax.numpy as jnp
from jax import lax
from jax.experimental import pallas as pl
from jax.experimental.pallas import tpu as pltpu
from jax.sharding import Mesh
from jax.sharding import PartitionSpec as P

D = 1536
LEN = 1024
INNER = 3072
STATE = 128
BLOCK = 256
BLOCKS = LEN // BLOCK
GROUPS = 2
HEADS = 6
COLS = HEADS * 64
WIDE = GROUPS * COLS
STEPS = 2 * WIDE
PROJ = STEPS + GROUPS * 128
MORE = PROJ - WIDE
LOG2E = 1.4426950408889634
EPS = 1e-05
F32 = jnp.float32
BF16 = jnp.bfloat16
MESH = pl.DeviceIdType.MESH
AXES = ("yl", "x", "c", "yh", "z")
ANY = pl.BlockSpec(memory_space=pl.ANY)
VMEM = pl.BlockSpec(memory_space=pltpu.VMEM)
SHAPE = jax.ShapeDtypeStruct
ROOM = 60 * 2**20


def dot(a, b):
    return jnp.dot(a, b, preferred_element_type=F32)


def dot_nt(a, b):
    return lax.dot_general(a, b, (((1,), (1,)), ((), ())), preferred_element_type=F32)


def dot_tn(a, b):
    return lax.dot_general(a, b, (((0,), (0,)), ((), ())), preferred_element_type=F32)


def pieces(v, n):
    out = []
    for _ in range(n):
        hi = v.astype(BF16)
        out.append(hi)
        v = v - hi.astype(F32)
    return out


def dot_left(v, ones, n):
    return sum(dot(p, ones) for p in pieces(v, n))


def spread(v, ones):
    hi = v.astype(BF16).astype(F32)
    low = pltpu.roll(v - hi, 64, 1)
    return dot(jnp.where(iota(v.shape, 1) < 64, hi, low).astype(BF16), ones)


def folded(v, ones):
    hi = v.astype(BF16)
    low = (v - hi.astype(F32)).astype(BF16)
    return dot(hi, ones) + dot(low, ones)


def dot_right(ones, v, n):
    return sum(dot(ones, p) for p in pieces(v, n))


def iota(shape, axis):
    return lax.broadcasted_iota(jnp.int32, shape, axis)


def expander():
    row, col = iota((128, COLS), 0), iota((128, COLS), 1)
    return ((row & 63) == lax.shift_right_logical(col, 6)).astype(BF16)


def reducer():
    row, col = iota((COLS, 128), 0), iota((COLS, 128), 1)
    return (col == lax.shift_right_logical(row, 6)).astype(BF16)


def sigmoid(v):
    return 0.5 * jnp.tanh(0.5 * v) + 0.5


def lower(strict=False):
    row, col = iota((BLOCK, BLOCK), 0), iota((BLOCK, BLOCK), 1)
    return ((row > col) if strict else (row >= col)).astype(BF16)


def upper():
    return (iota((BLOCK, BLOCK), 0) <= iota((BLOCK, BLOCK), 1)).astype(BF16)


def token_row(v):
    v = sum(v[:, 128 * i : 128 * (i + 1)] for i in range(v.shape[1] // 128))
    ones = jnp.ones((8, 128), BF16)
    return sum(dot_nt(ones, p) for p in pieces(v, 3))[0:1, :]


class Net:
    def __init__(self, send, recv):
        self.send, self.recv, self.copies = send, recv, []
        self.at = {name: lax.axis_index(name) for name in AXES}
        self.at["y"] = self.at["yh"] * 2 + self.at["yl"]
        self.places = {(a, s): lax.rem(self.at[a] + s + 4, 4) for a in ("x", "y", "z") for s in (1, -1, 2)}
        self.other = 1 - self.at["c"]
        self.targets = {("c", 1): {"c": self.other}}
        for (a, s), place in self.places.items():
            self.targets[a, s] = {"yh": place // 2, "yl": lax.rem(place, 2)} if a == "y" else {a: place}

    def near(self, axis, step):
        return self.places[axis, step]

    def plan(self, src, dst, axis, step=1):
        copy = Copy(self, len(self.copies), src, dst, self.targets[axis, step])
        self.copies.append(copy)
        return copy

    def start(self, src, dst, axis, step=1):
        return self.plan(lambda: src, lambda: dst, axis, step).start()

    def around(self, src, dst, axis):
        return [self.start(src, dst, axis, step) for step in (1, -1, 2)]

    def greet(self, peers):
        here, self.peers = pltpu.get_barrier_semaphore(), len(peers)
        for peer in peers:
            pl.semaphore_signal(here, inc=1, device_id=self.targets[peer], device_id_type=MESH)

    def met(self):
        pl.semaphore_wait(pltpu.get_barrier_semaphore(), self.peers)

    def finish(self):
        for copy in self.copies:
            copy.arrived()
        for copy in self.copies:
            copy.left()


class Copy:
    def __init__(self, net, index, src, dst, target):
        self.net, self.index, self.src, self.dst, self.target = net, index, src, dst, target
        self.here, self.gone = False, False

    def made(self):
        return pltpu.make_async_remote_copy(
            src_ref=self.src(),
            dst_ref=self.dst(),
            send_sem=self.net.send.at[self.index],
            recv_sem=self.net.recv.at[self.index],
            device_id=self.target,
            device_id_type=MESH,
        )

    def start(self):
        self.made().start()
        return self

    def arrived(self):
        if not self.here:
            self.here = True
            self.made().wait_recv()

    def left(self):
        if not self.gone:
            self.gone = True
            self.made().wait_send()


def sems(n):
    return [pltpu.SemaphoreType.DMA((n,)), pltpu.SemaphoreType.DMA((n,))]


def rows(ref, first, count):
    return ref.at[pl.ds(pl.multiple_of(first, 16), count)]


def lanes(first, count):
    return pl.ds(pl.multiple_of(first, 128), count)


def arrive(copies):
    for copy in copies:
        copy.arrived()


HALVES = ((0, 1), (1, -1))


class GridSum:
    def __init__(self, net, first, held, spans, scratch, cut=(0, 96)):
        self.net, self.first, self.held, self.spans = net, first, held, spans
        self.land, self.mid, self.last = scratch
        self.rows = pl.ds(*cut)
        self.one, self.two = [], []
        for slot, step in enumerate((2, 1, -1)):
            if first == "x":
                self.plan(self.one, lambda step=step: held.at[:, net.near("x", step), self.rows], lambda slot=slot: self.land.at[slot], "x", step)
            else:
                self.plan(self.two, lambda step=step: self.mid.at[net.near("x", step)], lambda slot=slot: self.last.at[slot], "x", step)
            lane = 0
            for base, n in spans:
                there = lambda step=step, base=base, n=n: lanes(base + (net.near("y", step) // 2) * n, n)
                if first == "x":
                    src = lambda step=step, there=there: self.mid.at[lax.rem(net.near("y", step), 2), :, there()]
                    self.plan(self.two, src, lambda slot=slot, lane=lane, n=n: self.last.at[slot, :, pl.ds(lane, n)], "y", step)
                else:
                    src = lambda step=step, there=there: held.at[lax.rem(net.near("y", step), 2), :, self.rows, there()]
                    self.plan(self.one, src, lambda slot=slot, lane=lane, n=n: self.land.at[slot, :, :, pl.ds(lane, n)], "y", step)
                lane += n

    def plan(self, to, src, dst, axis, step):
        to.append(self.net.plan(src, dst, axis, step))

    def step1(self):
        for copy in self.one:
            copy.start()

    def step2(self):
        arrive(self.one)
        at = self.net.at
        if self.first == "x":
            self.mid[...] = self.total(self.held[:, at["x"], self.rows], self.land, slice(None)).astype(BF16)
        else:
            lane = 0
            for base, n in self.spans:
                cut = slice(lane, lane + n)
                own = self.held[at["yl"], :, self.rows, lanes(base + at["yh"] * n, n)]
                self.mid[:, :, cut] = self.total(own, self.land, cut).astype(BF16)
                lane += n
        for copy in self.two:
            copy.start()

    def total(self, own, others, cut):
        return (own.astype(F32) + others[0, ..., cut].astype(F32)) + (others[1, ..., cut].astype(F32) + others[2, ..., cut].astype(F32))

    def step3(self, out):
        arrive(self.two)
        at = self.net.at
        if self.first == "y":
            out[self.rows, :] = self.total(self.mid[at["x"]], self.last, slice(None))
            return
        lane = 0
        for base, n in self.spans:
            cut = slice(lane, lane + n)
            out[self.rows, cut] = self.total(self.mid[at["yl"], :, lanes(base + at["yh"] * n, n)], self.last, cut)
            lane += n


def grid_scratch(first, width, count=96):
    blocks, wide = (2, 2 * width) if first == "x" else (4, width)
    return [pltpu.VMEM(s, BF16) for s in ((3, blocks, count, wide), (blocks, count, wide), (3, count, width))]


class TokenSum:
    def __init__(self, net, scratch):
        self.net, self.far, self.half, self.fold, self.whole = net, *scratch
        self.one = [
            net.plan(lambda p=p: self.far.at[pl.ds(128 * p, 128)], lambda p=p: self.half.at[p], "z", step) for p, step in HALVES
        ]
        half = lambda ref, p, n: ref.at[p, pl.ds(128 * n, 128)]
        self.ready = [net.plan(lambda p=p: half(self.fold, p, 1 - p), lambda p=p: half(self.whole, p, 1 - p), "z", step) for p, step in HALVES]
        self.added = [net.plan(lambda p=p: half(self.fold, p, p), lambda p=p: half(self.whole, p, p), "z", step) for p, step in HALVES]

    def step1(self):
        for copy in self.one:
            copy.start()

    def folded(self, p):
        self.ready[p].start()

    def step2(self):
        arrive(self.one)
        for p, _ in HALVES:
            self.fold[p, 128 * p : 128 * p + 128, :] += self.half[p]
            self.added[p].start()

    def step3(self):
        arrive(self.ready + self.added)
        return self.whole[0].astype(F32) + self.whole[1].astype(F32)


def token_scratch():
    return [pltpu.VMEM((256, D), BF16), pltpu.VMEM((2, 128, D), BF16), pltpu.VMEM((2, 256, D), BF16), pltpu.VMEM((2, 256, D), BF16)]


def earlier(v, before, step):
    if step == 0:
        return v
    turned = pltpu.roll(v, step, 0)
    starts = jnp.where(iota(before.shape, 0) < step, pltpu.roll(before, step, 0), turned[0:8, :])
    return jnp.concatenate([starts, turned[8:, :]], axis=0)


def front_kernel(
    x, gain, w_gate, w_inner, w_out, w_bc, w_step, conv, bias, gate_gain, step_bias, decay_log, skip_gain, conv_bc, bias_bc, cot,
    inner_out, z_out, y_out, h_out, dt_out, r_out, bc_out, bcin_out, zbc_out, normed_t, gains_out,
    mixed_out, gs_out, gg_out, cot_t, normed_out, wx_out, wout_out, wbc_out, prm_out,
    normed, wx, wout, wbc, prm, xv, stepv, stept, pk,
    cots, gps, acts, slopes, gms, mixed, gg, turned_c, ext, extbc, state, stat, cross, slots, slots_c, send, recv, local,
):
    i = pl.program_id(0)
    net = Net(send, recv)
    at = net.at
    yh, cx, cc, z, y = at["yh"], at["x"], at["c"], at["z"], at["y"]
    own_rows = lambda ref: rows(ref, z * 256, 256)
    order = ((0, 1), (1, -1), (1, 1), (0, -1))
    part = lambda ref, p, s: rows(ref, net.near("z", -s) * 256 + 128 * p, 128)
    c1 = [
        net.plan(lambda p=p: cot.at[pl.ds(128 * p, 128)], lambda p=p: rows(cots, z * 256 + 128 * p, 128), "z", s) for p, s in order
    ]
    c2 = [net.plan(lambda p=p, s=s: part(cots, p, s), lambda p=p, s=s: part(cots, p, s), "z", s) for p, s in HALVES]
    q = [net.plan(lambda: stat, lambda: slots.at[z], "z", step) for step in (1, -1, 2)]
    qc = [net.plan(lambda: cross, lambda: slots_c.at[z], "z", step) for step in (1, -1, 2)]
    spot_o = lambda xx, cut=pl.ds(0, 96): wout.at[at["yl"], xx, cc, cut, lanes(yh * COLS, COLS)]
    line_o = lambda yy, cut=pl.ds(0, 96): wout.at[lax.rem(yy, 2), :, cc, cut, lanes((yy // 2) * COLS, COLS)]
    same = lambda ref, axis, step=1: net.plan(ref, ref, axis, step)
    o1 = [net.plan(lambda: w_out, lambda: spot_o(cx), "x", step) for _, step in HALVES]
    o2 = [same(lambda p=p, s=s: spot_o(net.near("x", -s), pl.ds(48 * p, 48)), "x", s) for p, s in HALVES]
    o3 = [same(lambda: line_o(y), "y", step) for _, step in HALVES]
    o4 = [same(lambda p=p, s=s: line_o(net.near("y", -s), pl.ds(48 * p, 48)), "y", s) for p, s in HALVES]
    oc = [same(lambda: line_o(y), "c")] + [same(lambda s=s: line_o(net.near("y", s)), "c") for s in (1, -1, 2)]
    own = lambda: pltpu.make_async_copy(cot, own_rows(cots), local.at[0])
    pairs = ((normed, normed_out), (wx, wx_out), (wbc, wbc_out), (prm, prm_out), (wout, wout_out))
    leave = lambda n: pltpu.make_async_copy(*pairs[n], local.at[1 + n])

    @pl.when(i == 0)
    def _():
        load = pltpu.make_async_copy(x, xv, local.at[7])
        load.start()
        net.greet([("z", 1), ("z", -1), ("z", 2), ("x", 1), ("x", -1), ("y", 1), ("y", -1), ("y", 2), ("c", 1)])
        own().start()
        stept[...] = jnp.zeros_like(stept)
        stept[0:HEADS, 0:96] = w_step[...].astype(F32)
        stepv[...] = jnp.transpose(stept[...])[0:96, :].astype(BF16)
        pk[...] = jnp.zeros_like(pk)
        pk[0:4, :] = conv[...]
        pk[4:5, :] = bias[...].reshape(1, COLS)
        pk[5:6, :] = gate_gain[...].reshape(1, COLS)
        pk[6:7, 0:HEADS] = step_bias[...].reshape(1, HEADS)
        pk[7:8, 0:HEADS] = decay_log[...].reshape(1, HEADS)
        pk[8:9, 0:HEADS] = skip_gain[...].reshape(1, HEADS)
        first = {
            "x": ((w_gate, wx, 0, COLS), (w_bc.at[:, lanes(yh * 128, 128)], wbc, 0, 128)),
            "y": ((w_inner, wx, WIDE, COLS), (stepv, wx, STEPS, 128)),
        }
        then = {"x": "y", "y": "x"}
        done = []

        def go(src, dst, axis, step=1):
            done.append(net.start(src, dst, axis, step))
            return done[-1]

        def spot(ref, base, n, yy, xx, cut=pl.ds(0, 96)):
            return ref.at[lax.rem(yy, 2), xx, cc, cut, lanes(base + (yy // 2) * n, n)]

        def line(axis, ref, base, n, place, cut=pl.ds(0, 96)):
            if axis == "x":
                return ref.at[lax.rem(place, 2), :, cc, cut, lanes(base + (place // 2) * n, n)]
            return ref.at[:, place, cc, cut, lanes(base, 2 * n)]

        load.wait()
        v = xv[...].astype(F32)
        root = lax.rsqrt(jnp.mean(v * v, axis=1, keepdims=True) + EPS)
        normed[pl.ds(pl.multiple_of(z * 256, 256), 256), :] = (v * root * gain[...].reshape(1, D)).astype(BF16)
        net.met()
        zs = {}
        for p, s in order:
            here = rows(normed, z * 256 + 128 * p, 128)
            zs[p, s] = go(here, here, "z", s)
        sent = {"x": [], "y": []}
        for axis in ("x", "y"):
            for src, ref, base, n in first[axis]:
                sent[axis].append([go(src, spot(ref, base, n, y, cx), axis, step) for _, step in HALVES])
        mine = [
            pltpu.make_async_copy(src, spot(ref, base, n, y, cx), local.at[8 + k])
            for k, (src, ref, base, n) in enumerate(first["x"] + first["y"])
        ]
        mine.append(pltpu.make_async_copy(pk, prm.at[yh], local.at[12]))
        mine.append(pltpu.make_async_copy(w_out, spot_o(cx), local.at[13]))
        for copy in mine:
            copy.start()
        for copy in o1:
            copy.start()
        for axis in ("x", "y"):
            for src, ref, base, n in first[axis]:
                go(src, spot(ref, base, n, y, cx), "c")
        go(pk, prm.at[yh], "y", 2)
        second = {"x": [], "y": []}
        for axis in ("x", "y"):
            for (src, ref, base, n), copies in zip(first[axis], sent[axis]):
                for (p, s), copy in zip(HALVES, copies):
                    copy.arrived()
                    cut = pl.ds(48 * p, 48)
                    here = spot(ref, base, n, y, net.near("x", -s), cut) if axis == "x" else spot(ref, base, n, net.near("y", -s), cx, cut)
                    second[axis].append(go(here, here, axis, s))
        for copy in mine:
            copy.wait()
        third = {"x": [], "y": []}
        for axis in ("x", "y"):
            arrive(second[axis])
            for src, ref, base, n in first[axis]:
                here = line(axis, ref, base, n, at[then[axis]])
                third[axis].append([go(here, here, then[axis], s) for _, s in HALVES])
        for copy, start in zip(o1, o2):
            copy.arrived()
            start.start()
        for axis in ("x", "y"):
            for src, ref, base, n in first[axis]:
                for s in (1, -1, 2):
                    here = spot(ref, base, n, y, net.near("x", s)) if axis == "x" else spot(ref, base, n, net.near("y", s), cx)
                    go(here, here, "c")
        for p, s in HALVES:
            zs[p, s].arrived()
            here = part(normed, p, s)
            go(here, here, "z", s)
        for copy in c1:
            copy.start()
        fourth = {"x": [], "y": []}
        for axis in ("x", "y"):
            for (src, ref, base, n), copies in zip(first[axis], third[axis]):
                for (p, s), copy in zip(HALVES, copies):
                    copy.arrived()
                    place = net.near(then[axis], -s)
                    here = line(axis, ref, base, n, place, pl.ds(48 * p, 48))
                    fourth[axis].append(go(here, here, then[axis], s))
                    here = line(axis, ref, base, n, place)
                    go(here, here, "c")
        arrive(o2)
        for copy in o3:
            copy.start()
        for axis in ("x", "y"):
            arrive(fourth[axis])
            for src, ref, base, n in first[axis]:
                here = line(axis, ref, base, n, net.near(then[axis], 2))
                go(here, here, "c")
        for copy in done:
            copy.arrived()
        for copy in done:
            copy.left()
        for n in range(4):
            leave(n).start()
        ext[...] = jnp.zeros_like(ext)
        extbc[...] = jnp.zeros_like(extbc)
        state[...] = jnp.zeros_like(state)
        stat[...] = jnp.zeros_like(stat)
        cross[...] = jnp.zeros_like(cross)

    @pl.when(i == 2)
    def _():
        for copy, start in zip(c1[:2], c2):
            copy.arrived()
            start.start()
        for copy, start in zip(o3, o4):
            copy.arrived()
            start.start()
        for copy in oc[:3]:
            copy.start()

    @pl.when(i < BLOCKS)
    def _():
        xb = normed[pl.ds(pl.multiple_of(i * BLOCK, BLOCK), BLOCK), :]
        turned = jnp.transpose(xb).reshape(2, 4, 2, 96, BLOCK)
        for core in range(2):
            normed_t[core] = turned[:, :, core]
        bc_in = dot(xb, wbc[...].reshape(D, 256))
        bcin_out[...] = bc_in.astype(BF16)
        before_bc = extbc[...]
        extbc[...] = bc_in[BLOCK - 8 :, :]
        zb = bias_bc[...].reshape(1, 256) + sum(conv_bc[j : j + 1, :] * earlier(bc_in, before_bc, 3 - j) for j in range(4))
        zbc_out[...] = zb.astype(BF16)
        bc = (zb * sigmoid(zb)).astype(BF16)
        bc_out[...] = bc
        b, c = bc[:, :STATE], bc[:, STATE:]
        scores = jnp.where(iota((BLOCK, BLOCK), 0) >= iota((BLOCK, BLOCK), 1), dot_nt(c, b), 0.0)
        tri, ones = lower(), expander()
        left = iota((BLOCK, 128), 1) < 64
        weight = lambda first, n: wx[:, :, :, :, first : first + n].reshape(D, n)
        steps = dot(xb, weight(STEPS, 256))
        total = jnp.zeros((BLOCK, 128), F32)
        for g in range(GROUPS):
            if g == 1:

                @pl.when(i == BLOCKS - 1)
                def _():
                    arrive(o4)
                    oc[3].start()

            cut = slice(g * COLS, (g + 1) * COLS)
            u = steps[:, 128 * g : 128 * (g + 1)] + prm[g, 6:7, 0:128]
            low = jnp.exp(-jnp.abs(u))
            series = low * (1.0 - low * (0.5 - low * (1.0 / 3.0 - low * 0.25)))
            dt = jnp.maximum(u, 0.0) + jnp.where(low < 0.01, series, jnp.log(1.0 + low))
            rate = -jnp.exp(prm[g, 7:8, 0:128]) * LOG2E
            r = dot_right(tri, dt * rate, 3)
            dt_out[g] = dt
            r_out[g] = r
            rt = jnp.transpose(r)
            gate = dot(xb, weight(g * COLS, COLS))
            inner = dot(xb, weight(WIDE + g * COLS, COLS))
            inner_out[:, cut] = inner.astype(BF16)
            before = ext[:, cut]
            ext[:, cut] = inner[BLOCK - 8 :, :]
            zv = prm[g, 4:5, :] + sum(prm[g, j : j + 1, :] * earlier(inner, before, 3 - j) for j in range(4))
            z_out[:, cut] = zv
            xv = zv * sigmoid(zv)
            last = r[BLOCK - 1 : BLOCK, :]
            w = xv * spread(dt, ones)
            grow = spread(jnp.exp2(r), ones)
            tail = spread(jnp.exp2(last - r), ones)
            skip = spread(prm[g, 8:16, 0:128], ones)[0:1, :]
            wl = w.astype(BF16)
            h = state[:, cut]
            h_out[0, g] = h.astype(BF16)
            parts = []
            for p in range(HEADS // 2):
                halves = []
                for n in (2 * p, 2 * p + 1):
                    gap = jnp.minimum(r[:, n : n + 1] - rt[n : n + 1, :], 0.0)
                    halves.append(dot((scores * jnp.exp2(gap)).astype(BF16), wl[:, 128 * p : 128 * (p + 1)]))
                parts.append(jnp.where(left, halves[0], halves[1]))
            yv = jnp.concatenate(parts, axis=1) + grow * dot(c, h.astype(BF16)) + skip * xv
            y_out[:, cut] = yv
            state[:, cut] = grow[BLOCK - 1 : BLOCK, :] * h + dot_tn(b, (tail * w).astype(BF16))
            sig = sigmoid(gate)
            act = gate * sig
            gp = yv * act
            here_now = pl.ds(pl.multiple_of(i * BLOCK, BLOCK), BLOCK)
            gps[here_now, cut] = gp
            acts[here_now, cut] = act
            slopes[here_now, cut] = yv * (sig + act * (1.0 - sig))
            sq = gp * gp
            total = total + (sq[:, 0:128] + sq[:, 128:256] + sq[:, 256:384])
        stat[pl.ds(i, 1), :] = token_row(total)

    @pl.when(i == BLOCKS)
    def _():
        for copy in q:
            copy.start()
        slots[z] = stat[...]
        own().wait()
        arrive(oc)
        leave(4).start()
        gain = jnp.concatenate([prm[0, 5:6, :], prm[1, 5:6, :]], axis=1)
        moved = []

        def away(src, dst, *cut):
            moved.append(pltpu.make_async_copy(src.at[cut], dst.at[cut], local.at[14 + len(moved)]))
            moved[-1].start()

        def place(n):
            block = lax.rem(z + n + lax.div(n, 2) - 2 * lax.div(n, 3), 4)
            return block, pl.ds(pl.multiple_of(block * BLOCK, BLOCK), BLOCK)

        def turn_out(n):
            full, (block, at) = slice(None), place(n)
            cut = (full, full, full, full, at)
            return pltpu.make_async_copy(turned_c.at[cut], cot_t.at[cut], local.at[26 + n])

        def products(n, nothing):
            @pl.when(n == 1)
            def _():
                arrive(c1)

            @pl.when(n == 3)
            def _():
                arrive(c2)

            block, at = place(n)
            cb = cots[at, :]
            turned = jnp.transpose(cb).reshape(2, 4, 2, 96, BLOCK)
            for core in range(2):
                turned_c[core, :, :, :, at] = turned[:, :, core]
            turn_out(n).start()
            gm = dot(cb, wout[...].reshape(D, WIDE)) * gain
            gms[at, :] = gm
            cross[pl.ds(block, 1), :] = token_row(gm * gps[at, :])
            return nothing

        lax.fori_loop(0, BLOCKS, products, 0)
        for copy in qc:
            copy.start()
        slots_c[z] = cross[...]
        arrive(q)
        for copy in q:
            copy.left()
        root = lax.rsqrt(((slots[0] + slots[1]) + (slots[2] + slots[3])) * (1.0 / INNER) + EPS)
        columns = jnp.transpose(root)
        gain_grad = jnp.zeros((1, WIDE), F32)
        for k in range(BLOCKS):
            at = slice(k * BLOCK, (k + 1) * BLOCK)
            normal, gm = gps[at, :] * columns[:, k : k + 1], gms[at, :]
            mixed[at, :] = (normal * gain).astype(BF16)
            away(mixed, mixed_out, pl.ds(k * BLOCK, BLOCK))
            gain_grad = gain_grad + jnp.sum(gm * normal, axis=0, keepdims=True)
            gms[at, :] = gm * columns[:, k : k + 1]
        gain_grad = gain_grad / gain
        arrive(qc)
        sums = (slots_c[0] + slots_c[1]) + (slots_c[2] + slots_c[3])
        columns = jnp.transpose(root * root * root * (sums * (1.0 / INNER)))
        for k in range(BLOCKS):
            at = slice(k * BLOCK, (k + 1) * BLOCK)
            gated = gms[at, :] - gps[at, :] * columns[:, k : k + 1]
            gms[at, :] = gated * acts[at, :]
            gg[at, :] = (gated * slopes[at, :]).astype(BF16)
            away(gms, gs_out, pl.ds(k * BLOCK, BLOCK))
            away(gg, gg_out, pl.ds(k * BLOCK, BLOCK))
        gains_out[...] = jnp.concatenate([gain_grad, jnp.zeros((7, WIDE), F32)], axis=0)
        for copy in c1 + c2 + qc + o1 + o2 + o3 + o4 + oc:
            copy.left()
        for copy in moved:
            copy.wait()
        for n in range(len(pairs)):
            leave(n).wait()
        for n in range(BLOCKS):
            turn_out(jnp.int32(n)).wait()


def run_front(*args):
    first = lambda k: jnp.minimum(k, BLOCKS - 1)
    keep = lambda *s: pl.BlockSpec(s, lambda k: (0,) * len(s))
    block = lambda n: pl.BlockSpec((BLOCK, n), lambda k: (first(k), 0))
    small = lambda: pl.BlockSpec((GROUPS, BLOCK, 128), lambda k: (0, first(k), 0))
    wide = SHAPE((LEN, WIDE), F32)
    narrow = SHAPE((GROUPS, LEN, 128), F32)
    bf = lambda *s: pltpu.VMEM(s, BF16)
    f32 = lambda *s: pltpu.VMEM(s, F32)
    return pl.pallas_call(
        front_kernel,
        grid=(BLOCKS + 1,),
        out_shape=[
            SHAPE((LEN, WIDE), BF16),
            wide,
            wide,
            SHAPE((BLOCKS, GROUPS, STATE, COLS), BF16),
            narrow,
            narrow,
            SHAPE((LEN, 256), BF16),
            SHAPE((LEN, 256), BF16),
            SHAPE((LEN, 256), BF16),
            SHAPE((2, 2, 4, 96, LEN), BF16),
            SHAPE((8, WIDE), F32),
            SHAPE((LEN, WIDE), BF16),
            wide,
            SHAPE((LEN, WIDE), BF16),
            SHAPE((2, 2, 4, 96, LEN), BF16),
            SHAPE((LEN, D), BF16),
            SHAPE((2, 4, 2, 96, PROJ), BF16),
            SHAPE((2, 4, 2, 96, WIDE), BF16),
            SHAPE((2, 4, 2, 96, 256), BF16),
            SHAPE((GROUPS, 16, COLS), F32),
        ],
        in_specs=[ANY, VMEM, ANY, ANY, ANY, ANY] + [VMEM] * 9 + [ANY],
        out_specs=[
            block(WIDE),
            block(WIDE),
            block(WIDE),
            pl.BlockSpec((1, GROUPS, STATE, COLS), lambda k: (first(k), 0, 0, 0)),
            small(),
            small(),
            block(256),
            block(256),
            block(256),
            pl.BlockSpec((2, 2, 4, 96, BLOCK), lambda k: (0, 0, 0, 0, first(k))),
            keep(8, WIDE),
        ]
        + [ANY] * 9,
        scratch_shapes=[
            bf(LEN, D),
            bf(2, 4, 2, 96, PROJ),
            bf(2, 4, 2, 96, WIDE),
            bf(2, 4, 2, 96, 256),
            f32(GROUPS, 16, COLS),
            bf(256, D),
            bf(96, 128),
            f32(128, 128),
            f32(16, COLS),
            bf(LEN, D),
            f32(LEN, WIDE),
            f32(LEN, WIDE),
            f32(LEN, WIDE),
            f32(LEN, WIDE),
            bf(LEN, WIDE),
            bf(LEN, WIDE),
            bf(2, 2, 4, 96, LEN),
            f32(8, WIDE),
            f32(8, 256),
            f32(STATE, WIDE),
            f32(8, BLOCK),
            f32(8, BLOCK),
            f32(4, 8, BLOCK),
            f32(4, 8, BLOCK),
        ]
        + sems(96)
        + [pltpu.SemaphoreType.DMA((30,))],
        compiler_params=pltpu.CompilerParams(collective_id=1, has_side_effects=True, vmem_limit_bytes=ROOM),
        name="front",
    )(*args)


def later(v, after, step):
    turned = pltpu.roll(v, BLOCK - step, 0)
    ends = jnp.where(iota(after.shape, 0) < 8 - step, turned[BLOCK - 8 :, :], pltpu.roll(after, 8 - step, 0))
    return jnp.concatenate([turned[: BLOCK - 8, :], ends], axis=0)


def backward_kernel(
    gs_in, inner, zin, y, hin, prm, bc, dt, r, gains, mixed, wout, cot_t, gg, normed_t, tokens, zbc, bc_in, conv_bc,
    cat_out, acc, acc_bc, branch_out, wout_out, wgate_out,
    ext, extbc, dstate, dst, dbc, held, got, away, mv, wv, cv, gv, nv, ownb, g0, g1, g2, g3, s1, s2, s3, t1, t2, t3, send, recv, local,
):
    k = pl.program_id(0)
    net = Net(send, recv)
    cc, z = net.at["c"], net.at["z"]
    cross = [net.plan(lambda n=n: away.at[n], lambda n=n: got.at[n], "c") for n in range(2)]
    token = TokenSum(net, (g0, g1, g2, g3))
    rings = (GridSum(net, "y", held.at[0], ((0, COLS),), (s1, s2, s3)), GridSum(net, "x", held.at[1], ((0, COLS),), (t1, t2, t3)))

    @pl.when(k == 0)
    def _():
        net.greet([("z", 1), ("z", -1)] + [(a, s) for a in ("x", "y") for s in (1, -1, 2)] + [("c", 1)])
        loads = [pltpu.make_async_copy(src, dst, local.at[n]) for n, (src, dst) in enumerate(((mixed, mv), (wout, wv), (cot_t, cv), (gg, gv), (normed_t, nv)))]
        for copy in loads:
            copy.start()
        loads[0].wait()
        loads[1].wait()
        branch = lambda place: dot_nt(mv[pl.ds(pl.multiple_of(place * 256, 256), 256), :], wv[...])
        grads = lambda left, right, core: dot(left[core].reshape(8 * 96, LEN), right[...]).astype(BF16).reshape(2, 4, 96, WIDE)
        g0[...] = branch(net.near("z", 2)).astype(BF16)
        net.met()
        token.step1()
        for p, step in HALVES:
            g2[p] = branch(net.near("z", step)).astype(BF16)
            token.folded(p)
        ownb[...] = branch(z)
        loads[2].wait()
        away[0] = grads(cv, mv, net.other)
        cross[0].start()
        loads[3].wait()
        loads[4].wait()
        away[1] = grads(nv, gv, net.other)
        cross[1].start()
        held[0] = grads(cv, mv, cc)
        held[1] = grads(nv, gv, cc)
        acc[...] = jnp.zeros_like(acc)
        acc_bc[...] = jnp.zeros_like(acc_bc)
        extbc[BLOCK : BLOCK + 8, :] = jnp.zeros((8, 256), F32)
        for g in range(GROUPS):
            acc[g, 5:6, :] = gains[0:1, g * COLS : (g + 1) * COLS]
        ext[BLOCK : BLOCK + 8, :] = jnp.zeros((8, WIDE), F32)
        dstate[...] = jnp.zeros_like(dstate)

    @pl.when(k > 0)
    def _():
        ext[BLOCK : BLOCK + 8, :] = ext[0:8, :]
        extbc[BLOCK : BLOCK + 8, :] = extbc[0:8, :]

    b, c = bc[:, :STATE], bc[:, STATE:]
    valid = iota((BLOCK, BLOCK), 1) >= iota((BLOCK, BLOCK), 0)
    scores = jnp.where(valid, dot_nt(b, c), 0.0)
    ones, fold = expander(), reducer()
    left = iota((BLOCK, 128), 1) < 64
    suffix, prefix = upper(), lower(strict=True)
    dst[...] = jnp.zeros_like(dst)
    dbc[...] = jnp.zeros_like(dbc)
    for g in range(GROUPS):
        if g == 0:

            @pl.when(k == 1)
            def _():
                token.step2()

            @pl.when(k == 3)
            def _():
                for ring in rings:
                    ring.step2()

        else:

            @pl.when(k == 0)
            def _():
                for n in range(2):
                    cross[n].arrived()
                    held[n] += got[n]
                    rings[n].step1()

        cut = slice(g * COLS, (g + 1) * COLS)
        yv = y[:, cut]
        gs = gs_in[:, cut]
        xi = inner[:, cut].astype(F32)
        zv = zin[:, cut]
        zs = sigmoid(zv)
        xv = zv * zs
        dtv = dt[g]
        rate = -jnp.exp(prm[g, 7:8, 0:128])
        rv = r[g]
        rt = jnp.transpose(rv)
        last = rv[BLOCK - 1 : BLOCK, :]
        dte = spread(dt[g], ones)
        grow = spread(jnp.exp2(rv), ones)
        tail = spread(jnp.exp2(last - rv), ones)
        skip = spread(prm[g, 8:16, 0:128], ones)[0:1, :]
        w = xv * dte
        wl = w.astype(BF16)
        gl = gs.astype(BF16)
        hl = hin[0, g]
        h = hl.astype(F32)
        dh = dstate[:, cut]
        dhl = dh.astype(BF16)
        parts = []
        for p in range(HEADS // 2):
            halves, shares = [], []
            pair = slice(128 * p, 128 * (p + 1))
            wp, gpair = wl[:, pair], gl[:, pair]
            zero = jnp.zeros_like(wp)
            w_low = pltpu.roll(w[:, pair] - wp.astype(F32), 64, 1).astype(BF16)
            g_low = (gs[:, pair] - gpair.astype(F32)).astype(BF16)
            g_turn = pltpu.roll(gpair.astype(F32), 64, 1).astype(BF16)
            for n in (2 * p, 2 * p + 1):
                decay = jnp.exp2(jnp.minimum(rt[n : n + 1, :] - rv[:, n : n + 1], 0.0))
                halves.append(dot((scores * decay).astype(BF16), gpair))
                pick = (lambda a, b: jnp.where(left, a, b)) if n % 2 == 0 else (lambda a, b: jnp.where(left, b, a))
                one = jnp.concatenate([pick(wp, w_low), pick(wp, zero)], axis=1)
                two = jnp.concatenate([pick(gpair, g_turn), g_low], axis=1)
                shares.append(dot_nt(one, two) * decay)
            parts.append(jnp.where(left, halves[0], halves[1]))
            dst[...] += shares[0] + shares[1]
        dwi = jnp.concatenate(parts, axis=1)
        dws = tail * dot(b, dhl)
        dw = dwi + dws
        skipgrad = gs * xv
        diff = folded(gl.astype(F32) * (yv - skip * xv) - wl.astype(F32) * dwi, fold)
        zsum = dot((w * dws).astype(BF16), fold)
        const = folded(jnp.sum(h * dh, axis=0, keepdims=True) * grow[BLOCK - 1 : BLOCK, :] + jnp.zeros((8, COLS), F32), fold)
        da = dot_right(suffix, diff, 3) + dot_right(prefix, zsum, 3) + const[0:1, :]
        dstep = (dot((xv * dw).astype(BF16), fold) + rate * da) * jnp.where(dtv < 0.02, dtv * (1.0 - dtv * (0.5 - dtv * (1.0 / 6.0))), 1.0 - jnp.exp(-dtv))
        cat_out[:, WIDE + 128 * g : WIDE + 128 * (g + 1)] = dstep.astype(BF16)
        gx = (grow * gs).astype(BF16)
        dbc[:, STATE:] += dot_nt(gx, hl)
        dbc[:, :STATE] += dot_nt((tail * w).astype(BF16), dhl)
        dstate[:, cut] = grow[BLOCK - 1 : BLOCK, :] * dh + dot_tn(c, gx)
        dx = dte * dw + skip * gs
        dz = dx * (zs * (1.0 + zv * (1.0 - zs)))
        after = ext[BLOCK : BLOCK + 8, cut]
        ext[0:8, cut] = dz[0:8, :]
        gi = jnp.zeros((BLOCK, COLS), F32)
        for j in range(4):
            moved = dz if j == 3 else later(dz, after, 3 - j)
            gi = gi + prm[g, j : j + 1, :] * moved
            acc[g, j : j + 1, :] += jnp.sum(xi * moved, axis=0, keepdims=True)
        cat_out[:, cut] = gi.astype(BF16)
        acc[g, 4:5, :] += jnp.sum(dz, axis=0, keepdims=True)
        acc[g, 6:7, 0:128] += jnp.sum(dstep, axis=0, keepdims=True)
        acc[g, 7:8, 0:128] += jnp.sum(da * dt[g], axis=0, keepdims=True) * rate
        acc[g, 8:9, 0:128] += folded(jnp.sum(skipgrad, axis=0, keepdims=True) + jnp.zeros((8, COLS), F32), fold)[0:1, :]
    ds = jnp.where(valid, dst[...], 0.0).astype(BF16)
    dbc[:, STATE:] += dot_tn(ds, b)
    dbc[:, :STATE] += dot(ds, c)
    zb = zbc[...].astype(F32)
    sig = sigmoid(zb)
    dz = dbc[...] * (sig + zb * sig * (1.0 - sig))
    extbc[0:BLOCK, :] = dz
    bi = bc_in[...].astype(F32)
    gi = jnp.zeros((BLOCK, 256), F32)
    for j in range(4):
        moved = extbc[3 - j : 3 - j + BLOCK, :]
        gi = gi + conv_bc[j : j + 1, :] * moved
        acc_bc[j : j + 1, :] += jnp.sum(bi * moved, axis=0, keepdims=True)
    acc_bc[4:5, :] += jnp.sum(dz, axis=0, keepdims=True)
    cat_out[:, MORE:] = gi.astype(BF16)

    @pl.when(k == BLOCKS - 1)
    def _():
        rings[0].step3(wout_out)
        rings[1].step3(wgate_out)
        branch_out[...] = (tokens[...].astype(F32) + (ownb[...] + token.step3())).astype(BF16)
        for copy in net.copies:
            copy.left()


def run_backward(*args):
    rev = lambda k: BLOCKS - 1 - k
    cols = lambda n: pl.BlockSpec((BLOCK, n), lambda k: (rev(k), 0))
    small = lambda: pl.BlockSpec((GROUPS, BLOCK, 128), lambda k: (0, rev(k), 0))
    keep = lambda *s: pl.BlockSpec(s, lambda k: (0,) * len(s))
    bf = lambda *s: pltpu.VMEM(s, BF16)
    f32 = lambda *s: pltpu.VMEM(s, F32)
    return pl.pallas_call(
        backward_kernel,
        grid=(BLOCKS,),
        out_shape=[
            SHAPE((LEN, MORE + 256), BF16),
            SHAPE((GROUPS, 16, COLS), F32),
            SHAPE((8, 256), F32),
            SHAPE((256, D), BF16),
            SHAPE((96, COLS), F32),
            SHAPE((96, COLS), F32),
        ],
        in_specs=[cols(WIDE)] * 4
        + [
            pl.BlockSpec((1, GROUPS, STATE, COLS), lambda k: (rev(k), 0, 0, 0)),
            keep(GROUPS, 16, COLS),
            cols(256),
            small(),
            small(),
            keep(8, WIDE),
        ]
        + [ANY] * 5
        + [keep(256, D), cols(256), cols(256), keep(4, 256)],
        out_specs=[cols(MORE + 256), keep(GROUPS, 16, COLS), keep(8, 256), keep(256, D), keep(96, COLS), keep(96, COLS)],
        scratch_shapes=[
            f32(BLOCK + 8, WIDE),
            f32(BLOCK + 8, 256),
            f32(STATE, WIDE),
            f32(BLOCK, BLOCK),
            f32(BLOCK, 256),
            bf(2, 2, 4, 96, WIDE),
            bf(2, 2, 4, 96, WIDE),
            bf(2, 2, 4, 96, WIDE),
            bf(LEN, WIDE),
            bf(D, WIDE),
            bf(2, 2, 4, 96, LEN),
            bf(LEN, WIDE),
            bf(2, 2, 4, 96, LEN),
            f32(256, D),
        ]
        + token_scratch()
        + grid_scratch("y", COLS)
        + grid_scratch("x", COLS)
        + sems(26)
        + [pltpu.SemaphoreType.DMA((5,))],
        compiler_params=pltpu.CompilerParams(collective_id=2, has_side_effects=True, vmem_limit_bytes=ROOM),
        name="backward",
    )(*args)


def tail_kernel(
    gg, cat, wx, normed_t, normed, acc, acc_bc, wbc, gain,
    tokens_out, inner_out, bc_out, small_out,
    far_gg, far_cat, ggv, catv, wxv, ntv, nv, wv, ownb, held, got, away, dbw, heldb, gotb, small, sp0, sp1, sp2, sp3, bz, by,
    g0, g1, g2, g3, a1, a2, a3, b1, b2, b3, c1, c2, c3, send, recv, local,
):
    net = Net(send, recv)
    at = net.at
    yh, cx, cc, z, y = at["yh"], at["x"], at["c"], at["z"], at["y"]
    net.greet([(a, s) for a in ("z", "x", "y") for s in (1, -1, 2)] + [("c", 1)])
    far_rows = lambda ref: rows(ref, net.near("z", 2) * 256, 256)
    pairs = ((far_rows(cat), far_cat), (far_rows(gg), far_gg), (wx, wxv), (wbc, wv), (cat, catv), (gg, ggv), (normed_t, ntv), (normed, nv))
    loads = [pltpu.make_async_copy(src, dst, local.at[i]) for i, (src, dst) in enumerate(pairs)]
    for copy in loads:
        copy.start()
    token = TokenSum(net, (g0, g1, g2, g3))
    spans = ((0, COLS), (WIDE, 128))
    rings = (GridSum(net, "x", held, spans, (a1, a2, a3), (0, 48)), GridSum(net, "y", held, spans, (b1, b2, b3), (48, 48)))
    ring_bc = GridSum(net, "x", heldb, ((0, 128),), (c1, c2, c3))

    def product(gates, others):
        return dot_nt(gates, wxv[:, 0:WIDE]) + dot_nt(others[:, 0:MORE], wxv[:, WIDE:]) + dot_nt(others[:, MORE:], wv[...])

    def block(place):
        cut = pl.ds(pl.multiple_of(place * 256, 256), 256)
        return product(ggv[cut, :], catv[cut, :])

    def of_norm(place, grad):
        cut = pl.ds(pl.multiple_of(place * 256, 256), 256)
        return jnp.sum(grad * nv[cut, :].astype(F32), axis=0, keepdims=True)

    for copy in loads[:4]:
        copy.wait()
    far = product(far_gg[...], far_cat[...])
    g0[...] = far.astype(BF16)
    net.met()
    token.step1()
    for copy in loads[4:7]:
        copy.wait()
    grads = lambda core, cut, n: dot(ntv[core].reshape(8 * 96, LEN), catv[:, cut]).astype(BF16).reshape(2, 4, 96, n)
    for core in range(2):
        dbw[core] = grads(core, slice(MORE, MORE + 256), 256)
    crossb = net.start(dbw.at[net.other], gotb, "c")
    loads[7].wait()
    norm_part = of_norm(net.near("z", 2), far)
    for p, step in HALVES:
        out = block(net.near("z", step))
        g2[p] = out.astype(BF16)
        norm_part = norm_part + of_norm(net.near("z", step), out)
        if p == 0:
            crossb.arrived()
            heldb[...] = dbw[cc] + gotb[...]
            ring_bc.step1()
    ownb[...] = block(z)
    norm_part = (norm_part + of_norm(z, ownb[...])) / gain[...].reshape(1, D)
    small[0:16, :] = acc[0]
    small[16:32, :] = acc[1]
    small[32:48, :] = jnp.zeros((16, COLS), F32)
    for k in range(4):
        small[32 + k : 33 + k, :] = norm_part[:, k * COLS : (k + 1) * COLS]
    small[36:41, 0:256] = acc_bc[0:5, :]
    sp0[z] = small[32:48, :]
    q = net.around(sp0.at[z], sp0.at[z], "z")
    for p, _ in HALVES:
        token.folded(p)
    ring_bc.step2()
    away[...] = grads(net.other, slice(0, MORE), MORE)
    cross = net.start(away, got, "c")
    held[...] = grads(cc, slice(0, MORE), MORE)
    cross.arrived()
    held[...] += got[...]
    ring_bc.step3(by.at[yh])
    qb = [net.start(by.at[yh], by.at[yh], "y", 2)]
    arrive(q)
    sp1[cx, 0:32, :] = small[0:32, :]
    sp1[cx, 32:48, :] = (sp0[0] + sp0[1]) + (sp0[2] + sp0[3])
    q = net.around(sp1.at[cx], sp1.at[cx], "x")
    for ring in rings:
        ring.step1()
    token.step2()
    arrive(qb)
    bz[z, :, 0:128] = by[0].astype(BF16)
    bz[z, :, 128:256] = by[1].astype(BF16)
    qb = net.around(bz.at[z], bz.at[z], "z")
    arrive(q)
    sp2[y] = (sp1[0] + sp1[1]) + (sp1[2] + sp1[3])
    q = net.around(sp2.at[y], sp2.at[y], "y")
    for ring in rings:
        ring.step2()
    arrive(q)
    sp3[cc] = (sp2[0] + sp2[1]) + (sp2[2] + sp2[3])
    q = [net.start(sp3.at[cc], sp3.at[cc], "c")]
    for ring in rings:
        ring.step3(inner_out)
    arrive(q)
    small_out[...] = sp3[0] + sp3[1]
    tokens_out[...] = token.step3() + ownb[...]
    arrive(qb)
    bc_out[...] = (bz[0].astype(F32) + bz[1].astype(F32)) + (bz[2].astype(F32) + bz[3].astype(F32))
    net.finish()


def run_tail(*args):
    bf = lambda *s: pltpu.VMEM(s, BF16)
    f32 = lambda *s: pltpu.VMEM(s, F32)
    return pl.pallas_call(
        tail_kernel,
        out_shape=[
            SHAPE((256, D), F32),
            SHAPE((96, COLS + 128), F32),
            SHAPE((96, 256), F32),
            SHAPE((48, COLS), F32),
        ],
        in_specs=[ANY] * 5 + [VMEM, VMEM, ANY, VMEM],
        out_specs=[VMEM] * 4,
        scratch_shapes=[
            bf(256, WIDE),
            bf(256, MORE + 256),
            bf(LEN, WIDE),
            bf(LEN, MORE + 256),
            bf(D, PROJ),
            bf(2, 2, 4, 96, LEN),
            bf(LEN, D),
            bf(D, 256),
            f32(256, D),
            bf(2, 4, 96, MORE),
            bf(2, 4, 96, MORE),
            bf(2, 4, 96, MORE),
            bf(2, 2, 4, 96, 256),
            bf(2, 4, 96, 256),
            bf(2, 4, 96, 256),
            f32(48, COLS),
            f32(4, 16, COLS),
            f32(4, 48, COLS),
            f32(4, 48, COLS),
            f32(2, 48, COLS),
            bf(4, 96, 256),
            f32(2, 96, 128),
        ]
        + token_scratch()
        + grid_scratch("x", COLS + 128, 48)
        + grid_scratch("y", COLS + 128, 48)
        + grid_scratch("x", 128)
        + sems(64)
        + [pltpu.SemaphoreType.DMA((8,))],
        compiler_params=pltpu.CompilerParams(collective_id=3, has_side_effects=True, vmem_limit_bytes=ROOM),
        name="tail",
    )(*args)


def finish_kernel(grad, tokens, cot, branch, norm_gain, inner, bc, small, gate, wout, tokens_out, branch_out, inner_out, bc_out, gate_out, wout_out, step_out, norm, conv, bias, conv_bc, bias_bc, step_bias, decay, skip, gain):
    v = tokens[...].astype(F32)
    root = lax.rsqrt(jnp.mean(v * v, axis=1, keepdims=True) + EPS)
    scaled = grad[...] * norm_gain[...].reshape(1, D)
    tokens_out[...] = cot[...].astype(F32) + root * scaled - v * (root * root * root) * jnp.mean(scaled * v, axis=1, keepdims=True)
    branch_out[...] = branch[...]

    @pl.when(pl.program_id(0) == 0)
    def _():
        inner_out[...] = inner[:, :COLS]
        bc_out[...] = bc[...]
        gate_out[...] = gate[...]
        wout_out[...] = wout[...]
        step_out[...] = jnp.transpose(jnp.concatenate([inner[:, COLS:], jnp.zeros((32, 128), F32)], axis=0))[0:HEADS, 0:96]
        norm[...] = jnp.concatenate([small[32 + k : 33 + k, :] for k in range(4)], axis=1).reshape(D)
        conv_bc[...] = small[36:40, 0:256]
        bias_bc[...] = small[40:41, 0:256].reshape(256)
        mine = small[pl.ds(pl.multiple_of(lax.axis_index("yh") * 16, 8), 16), :]
        conv[...] = mine[0:4, :]
        bias[...] = mine[4:5, :].reshape(COLS)
        gain[...] = mine[5:6, :].reshape(COLS)
        step_bias[...] = mine[6:7, 0:HEADS].reshape(HEADS)
        decay[...] = mine[7:8, 0:HEADS].reshape(HEADS)
        skip[...] = mine[8:9, 0:HEADS].reshape(HEADS)


def run_finish(*args):
    f32 = lambda *s: SHAPE(s, F32)
    strip = lambda: pl.BlockSpec((128, D), lambda k: (k, 0))
    whole = lambda *s: pl.BlockSpec(s, lambda k: (0,) * len(s))
    shapes = (
        (96, COLS), (96, 256), (96, COLS), (96, COLS), (HEADS, 96), (D,), (4, COLS), (COLS,), (4, 256), (256,), (HEADS,), (HEADS,), (HEADS,), (COLS,),
    )
    return pl.pallas_call(
        finish_kernel,
        grid=(2,),
        out_shape=[f32(256, D), SHAPE((256, D), BF16)] + [f32(*s) for s in shapes],
        in_specs=[strip(), strip(), strip(), strip()]
        + [whole(*s) for s in ((D,), (96, COLS + 128), (96, 256), (48, COLS), (96, COLS), (96, COLS))],
        out_specs=[strip(), strip()] + [whole(*s) for s in shapes],
        compiler_params=pltpu.CompilerParams(vmem_limit_bytes=ROOM),
        name="finish",
    )(*args)


def shards(tokens, norm_gain, w_gate, w_inner, w_bc, w_step, conv_inner, bias_inner, conv_bc, bias_bc, step_bias, decay_log, skip_gain, gate_gain, w_out, cotangent):
    (
        inner, zin, y, hin, dt, r, bc, bc_in, zbc, normed_t, gains, mixed, gs, gg, cot_t, normed, wx, wout, wbc, prm,
    ) = run_front(
        tokens, norm_gain, w_gate, w_inner, w_out, w_bc, w_step.T, conv_inner, bias_inner, gate_gain, step_bias, decay_log,
        skip_gain, conv_bc, bias_bc, cotangent,
    )
    wx, wout, wbc = wx.reshape(D, PROJ), wout.reshape(D, WIDE), wbc.reshape(D, 256)
    cat, acc, acc_bc, output, wout_grad, gate_grad = run_backward(
        gs, inner, zin, y, hin, prm, bc, dt, r, gains, mixed, wout, cot_t, gg, normed_t, tokens, zbc, bc_in, conv_bc
    )
    grad, inner_grad, bc_grad, small = run_tail(gg, cat, wx, normed_t, normed, acc, acc_bc, wbc, norm_gain)
    (
        tokens_grad, output, inner_grad, bc_grad, gate_grad, wout_grad, step_grad,
        norm, conv, bias, conv_bc_grad, bias_bc_grad, step_bias_grad, decay, skip, gate_gain_grad,
    ) = run_finish(grad, tokens, cotangent, output, norm_gain, inner_grad, bc_grad, small, gate_grad, wout_grad)
    return (
        output, tokens_grad, norm, gate_grad, inner_grad, bc_grad, step_grad.T, conv, bias, conv_bc_grad,
        bias_bc_grad, step_bias_grad, decay, skip, gate_gain_grad, wout_grad,
    )


def solution(mesh):
    fine = Mesh(mesh.devices.reshape(2, 4, 2, 2, 4), AXES)
    dp, tensor = ("yl", "x", "c"), ("yh", "z")
    tokens, weight = P(dp + tensor, None), P(dp, tensor)
    heads, shared = P(tensor), P()
    return jax.shard_map(
        shards,
        mesh=fine,
        in_specs=(
            tokens, shared, weight, weight, P(dp, None), weight, P(None, tensor), heads,
            shared, shared, heads, heads, heads, heads, weight, tokens,
        ),
        out_specs=(
            tokens, tokens, shared, weight, weight, P(dp, None), weight, P(None, tensor), heads,
            shared, shared, heads, heads, heads, heads, weight,
        ),
        check_vma=False,
    )
```

```python
import jax
import jax.numpy as jnp
from jax import lax
from jax.experimental import pallas as pl
from jax.experimental.pallas import tpu as pltpu
from jax.sharding import Mesh
from jax.sharding import PartitionSpec as P

D = 1536
LEN = 1024
INNER = 3072
STATE = 128
BLOCK = 256
BLOCKS = LEN // BLOCK
GROUPS = 2
HEADS = 6
COLS = HEADS * 64
WIDE = GROUPS * COLS
STEPS = 2 * WIDE
PROJ = STEPS + GROUPS * 128
MORE = PROJ - WIDE
LOG2E = 1.4426950408889634
EPS = 1e-05
F32 = jnp.float32
BF16 = jnp.bfloat16
MESH = pl.DeviceIdType.MESH
AXES = ("yl", "x", "c", "yh", "z")
ANY = pl.BlockSpec(memory_space=pl.ANY)
VMEM = pl.BlockSpec(memory_space=pltpu.VMEM)
SHAPE = jax.ShapeDtypeStruct
ROOM = 60 * 2**20


def dot(a, b):
    return jnp.dot(a, b, preferred_element_type=F32)


def dot_nt(a, b):
    return lax.dot_general(a, b, (((1,), (1,)), ((), ())), preferred_element_type=F32)


def dot_tn(a, b):
    return lax.dot_general(a, b, (((0,), (0,)), ((), ())), preferred_element_type=F32)


def pieces(v, n):
    out = []
    for _ in range(n):
        hi = v.astype(BF16)
        out.append(hi)
        v = v - hi.astype(F32)
    return out


def dot_left(v, ones, n):
    return sum(dot(p, ones) for p in pieces(v, n))


def spread(v, ones):
    hi = v.astype(BF16).astype(F32)
    low = pltpu.roll(v - hi, 64, 1)
    return dot(jnp.where(iota(v.shape, 1) < 64, hi, low).astype(BF16), ones)


def folded(v, ones):
    hi = v.astype(BF16)
    low = (v - hi.astype(F32)).astype(BF16)
    return dot(hi, ones) + dot(low, ones)


def dot_right(ones, v, n):
    return sum(dot(ones, p) for p in pieces(v, n))


def iota(shape, axis):
    return lax.broadcasted_iota(jnp.int32, shape, axis)


def expander():
    row, col = iota((128, COLS), 0), iota((128, COLS), 1)
    return ((row & 63) == lax.shift_right_logical(col, 6)).astype(BF16)


def reducer():
    row, col = iota((COLS, 128), 0), iota((COLS, 128), 1)
    return (col == lax.shift_right_logical(row, 6)).astype(BF16)


def sigmoid(v):
    return 0.5 * jnp.tanh(0.5 * v) + 0.5


def lower(strict=False):
    row, col = iota((BLOCK, BLOCK), 0), iota((BLOCK, BLOCK), 1)
    return ((row > col) if strict else (row >= col)).astype(BF16)


def upper():
    return (iota((BLOCK, BLOCK), 0) <= iota((BLOCK, BLOCK), 1)).astype(BF16)


def token_row(v):
    v = sum(v[:, 128 * i : 128 * (i + 1)] for i in range(v.shape[1] // 128))
    ones = jnp.ones((8, 128), BF16)
    return sum(dot_nt(ones, p) for p in pieces(v, 3))[0:1, :]


class Net:
    def __init__(self, send, recv):
        self.send, self.recv, self.copies = send, recv, []
        self.at = {name: lax.axis_index(name) for name in AXES}
        self.at["y"] = self.at["yh"] * 2 + self.at["yl"]
        self.places = {(a, s): lax.rem(self.at[a] + s + 4, 4) for a in ("x", "y", "z") for s in (1, -1, 2)}
        self.other = 1 - self.at["c"]
        self.targets = {("c", 1): {"c": self.other}}
        for (a, s), place in self.places.items():
            self.targets[a, s] = {"yh": place // 2, "yl": lax.rem(place, 2)} if a == "y" else {a: place}

    def near(self, axis, step):
        return self.places[axis, step]

    def plan(self, src, dst, axis, step=1):
        copy = Copy(self, len(self.copies), src, dst, self.targets[axis, step])
        self.copies.append(copy)
        return copy

    def start(self, src, dst, axis, step=1):
        return self.plan(lambda: src, lambda: dst, axis, step).start()

    def around(self, src, dst, axis):
        return [self.start(src, dst, axis, step) for step in (1, -1, 2)]

    def greet(self, peers):
        here, self.peers = pltpu.get_barrier_semaphore(), len(peers)
        for peer in peers:
            pl.semaphore_signal(here, inc=1, device_id=self.targets[peer], device_id_type=MESH)

    def met(self):
        pl.semaphore_wait(pltpu.get_barrier_semaphore(), self.peers)

    def finish(self):
        for copy in self.copies:
            copy.arrived()
        for copy in self.copies:
            copy.left()


class Copy:
    def __init__(self, net, index, src, dst, target):
        self.net, self.index, self.src, self.dst, self.target = net, index, src, dst, target
        self.here, self.gone = False, False

    def made(self):
        return pltpu.make_async_remote_copy(
            src_ref=self.src(),
            dst_ref=self.dst(),
            send_sem=self.net.send.at[self.index],
            recv_sem=self.net.recv.at[self.index],
            device_id=self.target,
            device_id_type=MESH,
        )

    def start(self):
        self.made().start()
        return self

    def arrived(self):
        if not self.here:
            self.here = True
            self.made().wait_recv()

    def left(self):
        if not self.gone:
            self.gone = True
            self.made().wait_send()


def sems(n):
    return [pltpu.SemaphoreType.DMA((n,)), pltpu.SemaphoreType.DMA((n,))]


def rows(ref, first, count):
    return ref.at[pl.ds(pl.multiple_of(first, 16), count)]


def lanes(first, count):
    return pl.ds(pl.multiple_of(first, 128), count)


def arrive(copies):
    for copy in copies:
        copy.arrived()


HALVES = ((0, 1), (1, -1))


class GridSum:
    def __init__(self, net, first, held, spans, scratch, cut=(0, 96)):
        self.net, self.first, self.held, self.spans = net, first, held, spans
        self.land, self.mid, self.last = scratch
        self.rows = pl.ds(*cut)
        self.one, self.two = [], []
        for slot, step in enumerate((2, 1, -1)):
            if first == "x":
                self.plan(self.one, lambda step=step: held.at[:, net.near("x", step), self.rows], lambda slot=slot: self.land.at[slot], "x", step)
            else:
                self.plan(self.two, lambda step=step: self.mid.at[net.near("x", step)], lambda slot=slot: self.last.at[slot], "x", step)
            lane = 0
            for base, n in spans:
                there = lambda step=step, base=base, n=n: lanes(base + (net.near("y", step) // 2) * n, n)
                if first == "x":
                    src = lambda step=step, there=there: self.mid.at[lax.rem(net.near("y", step), 2), :, there()]
                    self.plan(self.two, src, lambda slot=slot, lane=lane, n=n: self.last.at[slot, :, pl.ds(lane, n)], "y", step)
                else:
                    src = lambda step=step, there=there: held.at[lax.rem(net.near("y", step), 2), :, self.rows, there()]
                    self.plan(self.one, src, lambda slot=slot, lane=lane, n=n: self.land.at[slot, :, :, pl.ds(lane, n)], "y", step)
                lane += n

    def plan(self, to, src, dst, axis, step):
        to.append(self.net.plan(src, dst, axis, step))

    def step1(self):
        for copy in self.one:
            copy.start()

    def step2(self):
        arrive(self.one)
        at = self.net.at
        if self.first == "x":
            self.mid[...] = self.total(self.held[:, at["x"], self.rows], self.land, slice(None)).astype(BF16)
        else:
            lane = 0
            for base, n in self.spans:
                cut = slice(lane, lane + n)
                own = self.held[at["yl"], :, self.rows, lanes(base + at["yh"] * n, n)]
                self.mid[:, :, cut] = self.total(own, self.land, cut).astype(BF16)
                lane += n
        for copy in self.two:
            copy.start()

    def total(self, own, others, cut):
        return (own.astype(F32) + others[0, ..., cut].astype(F32)) + (others[1, ..., cut].astype(F32) + others[2, ..., cut].astype(F32))

    def step3(self, out):
        arrive(self.two)
        at = self.net.at
        if self.first == "y":
            out[self.rows, :] = self.total(self.mid[at["x"]], self.last, slice(None))
            return
        lane = 0
        for base, n in self.spans:
            cut = slice(lane, lane + n)
            out[self.rows, cut] = self.total(self.mid[at["yl"], :, lanes(base + at["yh"] * n, n)], self.last, cut)
            lane += n


def grid_scratch(first, width, count=96):
    blocks, wide = (2, 2 * width) if first == "x" else (4, width)
    return [pltpu.VMEM(s, BF16) for s in ((3, blocks, count, wide), (blocks, count, wide), (3, count, width))]


class TokenSum:
    def __init__(self, net, scratch):
        self.net, self.far, self.half, self.fold, self.whole = net, *scratch
        self.one = [
            net.plan(lambda p=p: self.far.at[pl.ds(128 * p, 128)], lambda p=p: self.half.at[p], "z", step) for p, step in HALVES
        ]
        half = lambda ref, p, n: ref.at[p, pl.ds(128 * n, 128)]
        self.ready = [net.plan(lambda p=p: half(self.fold, p, 1 - p), lambda p=p: half(self.whole, p, 1 - p), "z", step) for p, step in HALVES]
        self.added = [net.plan(lambda p=p: half(self.fold, p, p), lambda p=p: half(self.whole, p, p), "z", step) for p, step in HALVES]

    def step1(self):
        for copy in self.one:
            copy.start()

    def folded(self, p):
        self.ready[p].start()

    def step2(self):
        arrive(self.one)
        for p, _ in HALVES:
            self.fold[p, 128 * p : 128 * p + 128, :] += self.half[p]
            self.added[p].start()

    def step3(self):
        arrive(self.ready + self.added)
        return self.whole[0].astype(F32) + self.whole[1].astype(F32)


def token_scratch():
    return [pltpu.VMEM((256, D), BF16), pltpu.VMEM((2, 128, D), BF16), pltpu.VMEM((2, 256, D), BF16), pltpu.VMEM((2, 256, D), BF16)]


def earlier(v, before, step):
    if step == 0:
        return v
    turned = pltpu.roll(v, step, 0)
    starts = jnp.where(iota(before.shape, 0) < step, pltpu.roll(before, step, 0), turned[0:8, :])
    return jnp.concatenate([starts, turned[8:, :]], axis=0)


def front_kernel(
    x, gain, w_gate, w_inner, w_out, w_bc, w_step, conv, bias, gate_gain, step_bias, decay_log, skip_gain, conv_bc, bias_bc, cot,
    inner_out, z_out, y_out, h_out, dt_out, r_out, bc_out, bcin_out, zbc_out, normed_t, gains_out,
    mixed_out, gs_out, gg_out, cot_t, normed_out, wx_out, wout_out, wbc_out, prm_out,
    normed, wx, wout, wbc, prm, xv, stepv, stept, pk,
    cots, gps, acts, slopes, gms, mixed, gg, turned_c, ext, extbc, state, stat, cross, slots, slots_c, send, recv, local,
):
    i = pl.program_id(0)
    net = Net(send, recv)
    at = net.at
    yh, cx, cc, z, y = at["yh"], at["x"], at["c"], at["z"], at["y"]
    own_rows = lambda ref: rows(ref, z * 256, 256)
    order = ((0, 1), (1, -1), (1, 1), (0, -1))
    part = lambda ref, p, s: rows(ref, net.near("z", -s) * 256 + 128 * p, 128)
    c1 = [
        net.plan(lambda p=p: cot.at[pl.ds(128 * p, 128)], lambda p=p: rows(cots, z * 256 + 128 * p, 128), "z", s) for p, s in order
    ]
    c2 = [net.plan(lambda p=p, s=s: part(cots, p, s), lambda p=p, s=s: part(cots, p, s), "z", s) for p, s in HALVES]
    q = [net.plan(lambda: stat, lambda: slots.at[z], "z", step) for step in (1, -1, 2)]
    qc = [net.plan(lambda: cross, lambda: slots_c.at[z], "z", step) for step in (1, -1, 2)]
    spot_o = lambda xx, cut=pl.ds(0, 96): wout.at[at["yl"], xx, cc, cut, lanes(yh * COLS, COLS)]
    line_o = lambda yy, cut=pl.ds(0, 96): wout.at[lax.rem(yy, 2), :, cc, cut, lanes((yy // 2) * COLS, COLS)]
    same = lambda ref, axis, step=1: net.plan(ref, ref, axis, step)
    o1 = [net.plan(lambda: w_out, lambda: spot_o(cx), "x", step) for _, step in HALVES]
    o2 = [same(lambda p=p, s=s: spot_o(net.near("x", -s), pl.ds(48 * p, 48)), "x", s) for p, s in HALVES]
    o3 = [same(lambda: line_o(y), "y", step) for _, step in HALVES]
    o4 = [same(lambda p=p, s=s: line_o(net.near("y", -s), pl.ds(48 * p, 48)), "y", s) for p, s in HALVES]
    oc = [same(lambda: line_o(y), "c")] + [same(lambda s=s: line_o(net.near("y", s)), "c") for s in (1, -1, 2)]
    own = lambda: pltpu.make_async_copy(cot, own_rows(cots), local.at[0])
    pairs = ((normed, normed_out), (wx, wx_out), (wbc, wbc_out), (prm, prm_out), (wout, wout_out))
    leave = lambda n: pltpu.make_async_copy(*pairs[n], local.at[1 + n])

    @pl.when(i == 0)
    def _():
        load = pltpu.make_async_copy(x, xv, local.at[7])
        load.start()
        net.greet([("z", 1), ("z", -1), ("z", 2), ("x", 1), ("x", -1), ("y", 1), ("y", -1), ("y", 2), ("c", 1)])
        own().start()
        stept[...] = jnp.zeros_like(stept)
        stept[0:HEADS, 0:96] = w_step[...].astype(F32)
        stepv[...] = jnp.transpose(stept[...])[0:96, :].astype(BF16)
        pk[...] = jnp.zeros_like(pk)
        pk[0:4, :] = conv[...]
        pk[4:5, :] = bias[...].reshape(1, COLS)
        pk[5:6, :] = gate_gain[...].reshape(1, COLS)
        pk[6:7, 0:HEADS] = step_bias[...].reshape(1, HEADS)
        pk[7:8, 0:HEADS] = decay_log[...].reshape(1, HEADS)
        pk[8:9, 0:HEADS] = skip_gain[...].reshape(1, HEADS)
        first = {
            "x": ((w_gate, wx, 0, COLS), (w_bc.at[:, lanes(yh * 128, 128)], wbc, 0, 128)),
            "y": ((w_inner, wx, WIDE, COLS), (stepv, wx, STEPS, 128)),
        }
        then = {"x": "y", "y": "x"}
        done = []

        def go(src, dst, axis, step=1):
            done.append(net.start(src, dst, axis, step))
            return done[-1]

        def spot(ref, base, n, yy, xx, cut=pl.ds(0, 96)):
            return ref.at[lax.rem(yy, 2), xx, cc, cut, lanes(base + (yy // 2) * n, n)]

        def line(axis, ref, base, n, place, cut=pl.ds(0, 96)):
            if axis == "x":
                return ref.at[lax.rem(place, 2), :, cc, cut, lanes(base + (place // 2) * n, n)]
            return ref.at[:, place, cc, cut, lanes(base, 2 * n)]

        load.wait()
        v = xv[...].astype(F32)
        root = lax.rsqrt(jnp.mean(v * v, axis=1, keepdims=True) + EPS)
        normed[pl.ds(pl.multiple_of(z * 256, 256), 256), :] = (v * root * gain[...].reshape(1, D)).astype(BF16)
        net.met()
        zs = {}
        for p, s in order:
            here = rows(normed, z * 256 + 128 * p, 128)
            zs[p, s] = go(here, here, "z", s)
        sent = {"x": [], "y": []}
        for axis in ("x", "y"):
            for src, ref, base, n in first[axis]:
                sent[axis].append([go(src, spot(ref, base, n, y, cx), axis, step) for _, step in HALVES])
        mine = [
            pltpu.make_async_copy(src, spot(ref, base, n, y, cx), local.at[8 + k])
            for k, (src, ref, base, n) in enumerate(first["x"] + first["y"])
        ]
        mine.append(pltpu.make_async_copy(pk, prm.at[yh], local.at[12]))
        mine.append(pltpu.make_async_copy(w_out, spot_o(cx), local.at[13]))
        for copy in mine:
            copy.start()
        for copy in o1:
            copy.start()
        for axis in ("x", "y"):
            for src, ref, base, n in first[axis]:
                go(src, spot(ref, base, n, y, cx), "c")
        go(pk, prm.at[yh], "y", 2)
        second = {"x": [], "y": []}
        for axis in ("x", "y"):
            for (src, ref, base, n), copies in zip(first[axis], sent[axis]):
                for (p, s), copy in zip(HALVES, copies):
                    copy.arrived()
                    cut = pl.ds(48 * p, 48)
                    here = spot(ref, base, n, y, net.near("x", -s), cut) if axis == "x" else spot(ref, base, n, net.near("y", -s), cx, cut)
                    second[axis].append(go(here, here, axis, s))
        for copy in mine:
            copy.wait()
        third = {"x": [], "y": []}
        for axis in ("x", "y"):
            arrive(second[axis])
            for src, ref, base, n in first[axis]:
                here = line(axis, ref, base, n, at[then[axis]])
                third[axis].append([go(here, here, then[axis], s) for _, s in HALVES])
        for copy, start in zip(o1, o2):
            copy.arrived()
            start.start()
        for axis in ("x", "y"):
            for src, ref, base, n in first[axis]:
                for s in (1, -1, 2):
                    here = spot(ref, base, n, y, net.near("x", s)) if axis == "x" else spot(ref, base, n, net.near("y", s), cx)
                    go(here, here, "c")
        for p, s in HALVES:
            zs[p, s].arrived()
            here = part(normed, p, s)
            go(here, here, "z", s)
        for copy in c1:
            copy.start()
        fourth = {"x": [], "y": []}
        for axis in ("x", "y"):
            for (src, ref, base, n), copies in zip(first[axis], third[axis]):
                for (p, s), copy in zip(HALVES, copies):
                    copy.arrived()
                    place = net.near(then[axis], -s)
                    here = line(axis, ref, base, n, place, pl.ds(48 * p, 48))
                    fourth[axis].append(go(here, here, then[axis], s))
                    here = line(axis, ref, base, n, place)
                    go(here, here, "c")
        arrive(o2)
        for copy in o3:
            copy.start()
        for axis in ("x", "y"):
            arrive(fourth[axis])
            for src, ref, base, n in first[axis]:
                here = line(axis, ref, base, n, net.near(then[axis], 2))
                go(here, here, "c")
        for copy in done:
            copy.arrived()
        for copy in done:
            copy.left()
        for n in range(4):
            leave(n).start()
        ext[...] = jnp.zeros_like(ext)
        extbc[...] = jnp.zeros_like(extbc)
        state[...] = jnp.zeros_like(state)
        stat[...] = jnp.zeros_like(stat)
        cross[...] = jnp.zeros_like(cross)

    @pl.when(i == 2)
    def _():
        for copy, start in zip(c1[:2], c2):
            copy.arrived()
            start.start()
        for copy, start in zip(o3, o4):
            copy.arrived()
            start.start()
        for copy in oc[:3]:
            copy.start()

    @pl.when(i < BLOCKS)
    def _():
        xb = normed[pl.ds(pl.multiple_of(i * BLOCK, BLOCK), BLOCK), :]
        turned = jnp.transpose(xb).reshape(2, 4, 2, 96, BLOCK)
        for core in range(2):
            normed_t[core] = turned[:, :, core]
        bc_in = dot(xb, wbc[...].reshape(D, 256))
        bcin_out[...] = bc_in.astype(BF16)
        before_bc = extbc[...]
        extbc[...] = bc_in[BLOCK - 8 :, :]
        zb = bias_bc[...].reshape(1, 256) + sum(conv_bc[j : j + 1, :] * earlier(bc_in, before_bc, 3 - j) for j in range(4))
        zbc_out[...] = zb.astype(BF16)
        bc = (zb * sigmoid(zb)).astype(BF16)
        bc_out[...] = bc
        b, c = bc[:, :STATE], bc[:, STATE:]
        scores = jnp.where(iota((BLOCK, BLOCK), 0) >= iota((BLOCK, BLOCK), 1), dot_nt(c, b), 0.0)
        tri, ones = lower(), expander()
        left = iota((BLOCK, 128), 1) < 64
        weight = lambda first, n: wx[:, :, :, :, first : first + n].reshape(D, n)
        steps = dot(xb, weight(STEPS, 256))
        total = jnp.zeros((BLOCK, 128), F32)
        for g in range(GROUPS):
            if g == 1:

                @pl.when(i == BLOCKS - 1)
                def _():
                    arrive(o4)
                    oc[3].start()

            cut = slice(g * COLS, (g + 1) * COLS)
            u = steps[:, 128 * g : 128 * (g + 1)] + prm[g, 6:7, 0:128]
            low = jnp.exp(-jnp.abs(u))
            series = low * (1.0 - low * (0.5 - low * (1.0 / 3.0 - low * 0.25)))
            dt = jnp.maximum(u, 0.0) + jnp.where(low < 0.01, series, jnp.log(1.0 + low))
            rate = -jnp.exp(prm[g, 7:8, 0:128]) * LOG2E
            r = dot_right(tri, dt * rate, 3)
            dt_out[g] = dt
            r_out[g] = r
            rt = jnp.transpose(r)
            gate = dot(xb, weight(g * COLS, COLS))
            inner = dot(xb, weight(WIDE + g * COLS, COLS))
            inner_out[:, cut] = inner.astype(BF16)
            before = ext[:, cut]
            ext[:, cut] = inner[BLOCK - 8 :, :]
            zv = prm[g, 4:5, :] + sum(prm[g, j : j + 1, :] * earlier(inner, before, 3 - j) for j in range(4))
            z_out[:, cut] = zv
            xv = zv * sigmoid(zv)
            last = r[BLOCK - 1 : BLOCK, :]
            w = xv * spread(dt, ones)
            grow = spread(jnp.exp2(r), ones)
            tail = spread(jnp.exp2(last - r), ones)
            skip = spread(prm[g, 8:16, 0:128], ones)[0:1, :]
            wl = w.astype(BF16)
            h = state[:, cut]
            h_out[0, g] = h.astype(BF16)
            parts = []
            for p in range(HEADS // 2):
                halves = []
                for n in (2 * p, 2 * p + 1):
                    gap = jnp.minimum(r[:, n : n + 1] - rt[n : n + 1, :], 0.0)
                    halves.append(dot((scores * jnp.exp2(gap)).astype(BF16), wl[:, 128 * p : 128 * (p + 1)]))
                parts.append(jnp.where(left, halves[0], halves[1]))
            yv = jnp.concatenate(parts, axis=1) + grow * dot(c, h.astype(BF16)) + skip * xv
            y_out[:, cut] = yv
            state[:, cut] = grow[BLOCK - 1 : BLOCK, :] * h + dot_tn(b, (tail * w).astype(BF16))
            sig = sigmoid(gate)
            act = gate * sig
            gp = yv * act
            here_now = pl.ds(pl.multiple_of(i * BLOCK, BLOCK), BLOCK)
            gps[here_now, cut] = gp
            acts[here_now, cut] = act
            slopes[here_now, cut] = yv * (sig + act * (1.0 - sig))
            sq = gp * gp
            total = total + (sq[:, 0:128] + sq[:, 128:256] + sq[:, 256:384])
        stat[pl.ds(i, 1), :] = token_row(total)

    @pl.when(i == BLOCKS)
    def _():
        for copy in q:
            copy.start()
        slots[z] = stat[...]
        own().wait()
        arrive(oc)
        leave(4).start()
        gain = jnp.concatenate([prm[0, 5:6, :], prm[1, 5:6, :]], axis=1)
        moved = []

        def away(src, dst, *cut):
            moved.append(pltpu.make_async_copy(src.at[cut], dst.at[cut], local.at[14 + len(moved)]))
            moved[-1].start()

        def place(n):
            block = lax.rem(z + n + lax.div(n, 2) - 2 * lax.div(n, 3), 4)
            return block, pl.ds(pl.multiple_of(block * BLOCK, BLOCK), BLOCK)

        def turn_out(n):
            full, (block, at) = slice(None), place(n)
            cut = (full, full, full, full, at)
            return pltpu.make_async_copy(turned_c.at[cut], cot_t.at[cut], local.at[26 + n])

        def products(n, nothing):
            @pl.when(n == 1)
            def _():
                arrive(c1)

            @pl.when(n == 3)
            def _():
                arrive(c2)

            block, at = place(n)
            cb = cots[at, :]
            turned = jnp.transpose(cb).reshape(2, 4, 2, 96, BLOCK)
            for core in range(2):
                turned_c[core, :, :, :, at] = turned[:, :, core]
            turn_out(n).start()
            gm = dot(cb, wout[...].reshape(D, WIDE)) * gain
            gms[at, :] = gm
            cross[pl.ds(block, 1), :] = token_row(gm * gps[at, :])
            return nothing

        lax.fori_loop(0, BLOCKS, products, 0)
        for copy in qc:
            copy.start()
        slots_c[z] = cross[...]
        arrive(q)
        for copy in q:
            copy.left()
        root = lax.rsqrt(((slots[0] + slots[1]) + (slots[2] + slots[3])) * (1.0 / INNER) + EPS)
        columns = jnp.transpose(root)
        gain_grad = jnp.zeros((1, WIDE), F32)
        for k in range(BLOCKS):
            at = slice(k * BLOCK, (k + 1) * BLOCK)
            normal, gm = gps[at, :] * columns[:, k : k + 1], gms[at, :]
            mixed[at, :] = (normal * gain).astype(BF16)
            away(mixed, mixed_out, pl.ds(k * BLOCK, BLOCK))
            gain_grad = gain_grad + jnp.sum(gm * normal, axis=0, keepdims=True)
            gms[at, :] = gm * columns[:, k : k + 1]
        gain_grad = gain_grad / gain
        arrive(qc)
        sums = (slots_c[0] + slots_c[1]) + (slots_c[2] + slots_c[3])
        columns = jnp.transpose(root * root * root * (sums * (1.0 / INNER)))
        for k in range(BLOCKS):
            at = slice(k * BLOCK, (k + 1) * BLOCK)
            gated = gms[at, :] - gps[at, :] * columns[:, k : k + 1]
            gms[at, :] = gated * acts[at, :]
            gg[at, :] = (gated * slopes[at, :]).astype(BF16)
            away(gms, gs_out, pl.ds(k * BLOCK, BLOCK))
            away(gg, gg_out, pl.ds(k * BLOCK, BLOCK))
        gains_out[...] = jnp.concatenate([gain_grad, jnp.zeros((7, WIDE), F32)], axis=0)
        for copy in c1 + c2 + qc + o1 + o2 + o3 + o4 + oc:
            copy.left()
        for copy in moved:
            copy.wait()
        for n in range(len(pairs)):
            leave(n).wait()
        for n in range(BLOCKS):
            turn_out(jnp.int32(n)).wait()


def run_front(*args):
    first = lambda k: jnp.minimum(k, BLOCKS - 1)
    keep = lambda *s: pl.BlockSpec(s, lambda k: (0,) * len(s))
    block = lambda n: pl.BlockSpec((BLOCK, n), lambda k: (first(k), 0))
    small = lambda: pl.BlockSpec((GROUPS, BLOCK, 128), lambda k: (0, first(k), 0))
    wide = SHAPE((LEN, WIDE), F32)
    narrow = SHAPE((GROUPS, LEN, 128), F32)
    bf = lambda *s: pltpu.VMEM(s, BF16)
    f32 = lambda *s: pltpu.VMEM(s, F32)
    return pl.pallas_call(
        front_kernel,
        grid=(BLOCKS + 1,),
        out_shape=[
            SHAPE((LEN, WIDE), BF16),
            wide,
            wide,
            SHAPE((BLOCKS, GROUPS, STATE, COLS), BF16),
            narrow,
            narrow,
            SHAPE((LEN, 256), BF16),
            SHAPE((LEN, 256), BF16),
            SHAPE((LEN, 256), BF16),
            SHAPE((2, 2, 4, 96, LEN), BF16),
            SHAPE((8, WIDE), F32),
            SHAPE((LEN, WIDE), BF16),
            wide,
            SHAPE((LEN, WIDE), BF16),
            SHAPE((2, 2, 4, 96, LEN), BF16),
            SHAPE((LEN, D), BF16),
            SHAPE((2, 4, 2, 96, PROJ), BF16),
            SHAPE((2, 4, 2, 96, WIDE), BF16),
            SHAPE((2, 4, 2, 96, 256), BF16),
            SHAPE((GROUPS, 16, COLS), F32),
        ],
        in_specs=[ANY, VMEM, ANY, ANY, ANY, ANY] + [VMEM] * 9 + [ANY],
        out_specs=[
            block(WIDE),
            block(WIDE),
            block(WIDE),
            pl.BlockSpec((1, GROUPS, STATE, COLS), lambda k: (first(k), 0, 0, 0)),
            small(),
            small(),
            block(256),
            block(256),
            block(256),
            pl.BlockSpec((2, 2, 4, 96, BLOCK), lambda k: (0, 0, 0, 0, first(k))),
            keep(8, WIDE),
        ]
        + [ANY] * 9,
        scratch_shapes=[
            bf(LEN, D),
            bf(2, 4, 2, 96, PROJ),
            bf(2, 4, 2, 96, WIDE),
            bf(2, 4, 2, 96, 256),
            f32(GROUPS, 16, COLS),
            bf(256, D),
            bf(96, 128),
            f32(128, 128),
            f32(16, COLS),
            bf(LEN, D),
            f32(LEN, WIDE),
            f32(LEN, WIDE),
            f32(LEN, WIDE),
            f32(LEN, WIDE),
            bf(LEN, WIDE),
            bf(LEN, WIDE),
            bf(2, 2, 4, 96, LEN),
            f32(8, WIDE),
            f32(8, 256),
            f32(STATE, WIDE),
            f32(8, BLOCK),
            f32(8, BLOCK),
            f32(4, 8, BLOCK),
            f32(4, 8, BLOCK),
        ]
        + sems(96)
        + [pltpu.SemaphoreType.DMA((30,))],
        compiler_params=pltpu.CompilerParams(collective_id=1, has_side_effects=True, vmem_limit_bytes=ROOM),
        name="front",
    )(*args)


def later(v, after, step):
    turned = pltpu.roll(v, BLOCK - step, 0)
    ends = jnp.where(iota(after.shape, 0) < 8 - step, turned[BLOCK - 8 :, :], pltpu.roll(after, 8 - step, 0))
    return jnp.concatenate([turned[: BLOCK - 8, :], ends], axis=0)


def backward_kernel(
    gs_in, inner, zin, y, hin, prm, bc, dt, r, gains, mixed, wout, cot_t, gg, normed_t, tokens, zbc, bc_in, conv_bc,
    cat_out, acc, acc_bc, branch_out, wout_out, wgate_out,
    ext, extbc, dstate, dst, dbc, held, got, away, mv, wv, cv, gv, nv, ownb, g0, g1, g2, g3, s1, s2, s3, t1, t2, t3, send, recv, local,
):
    k = pl.program_id(0)
    net = Net(send, recv)
    cc, z = net.at["c"], net.at["z"]
    cross = [net.plan(lambda n=n: away.at[n], lambda n=n: got.at[n], "c") for n in range(2)]
    token = TokenSum(net, (g0, g1, g2, g3))
    rings = (GridSum(net, "y", held.at[0], ((0, COLS),), (s1, s2, s3)), GridSum(net, "x", held.at[1], ((0, COLS),), (t1, t2, t3)))

    @pl.when(k == 0)
    def _():
        net.greet([("z", 1), ("z", -1)] + [(a, s) for a in ("x", "y") for s in (1, -1, 2)] + [("c", 1)])
        loads = [pltpu.make_async_copy(src, dst, local.at[n]) for n, (src, dst) in enumerate(((mixed, mv), (wout, wv), (cot_t, cv), (gg, gv), (normed_t, nv)))]
        for copy in loads:
            copy.start()
        loads[0].wait()
        loads[1].wait()
        branch = lambda place: dot_nt(mv[pl.ds(pl.multiple_of(place * 256, 256), 256), :], wv[...])
        grads = lambda left, right, core: dot(left[core].reshape(8 * 96, LEN), right[...]).astype(BF16).reshape(2, 4, 96, WIDE)
        g0[...] = branch(net.near("z", 2)).astype(BF16)
        net.met()
        token.step1()
        for p, step in HALVES:
            g2[p] = branch(net.near("z", step)).astype(BF16)
            token.folded(p)
        ownb[...] = branch(z)
        loads[2].wait()
        away[0] = grads(cv, mv, net.other)
        cross[0].start()
        loads[3].wait()
        loads[4].wait()
        away[1] = grads(nv, gv, net.other)
        cross[1].start()
        held[0] = grads(cv, mv, cc)
        held[1] = grads(nv, gv, cc)
        acc[...] = jnp.zeros_like(acc)
        acc_bc[...] = jnp.zeros_like(acc_bc)
        extbc[BLOCK : BLOCK + 8, :] = jnp.zeros((8, 256), F32)
        for g in range(GROUPS):
            acc[g, 5:6, :] = gains[0:1, g * COLS : (g + 1) * COLS]
        ext[BLOCK : BLOCK + 8, :] = jnp.zeros((8, WIDE), F32)
        dstate[...] = jnp.zeros_like(dstate)

    @pl.when(k > 0)
    def _():
        ext[BLOCK : BLOCK + 8, :] = ext[0:8, :]
        extbc[BLOCK : BLOCK + 8, :] = extbc[0:8, :]

    b, c = bc[:, :STATE], bc[:, STATE:]
    valid = iota((BLOCK, BLOCK), 1) >= iota((BLOCK, BLOCK), 0)
    scores = jnp.where(valid, dot_nt(b, c), 0.0)
    ones, fold = expander(), reducer()
    left = iota((BLOCK, 128), 1) < 64
    suffix, prefix = upper(), lower(strict=True)
    dst[...] = jnp.zeros_like(dst)
    dbc[...] = jnp.zeros_like(dbc)
    for g in range(GROUPS):
        if g == 0:

            @pl.when(k == 1)
            def _():
                token.step2()

            @pl.when(k == 3)
            def _():
                for ring in rings:
                    ring.step2()

        else:

            @pl.when(k == 0)
            def _():
                for n in range(2):
                    cross[n].arrived()
                    held[n] += got[n]
                    rings[n].step1()

        cut = slice(g * COLS, (g + 1) * COLS)
        yv = y[:, cut]
        gs = gs_in[:, cut]
        xi = inner[:, cut].astype(F32)
        zv = zin[:, cut]
        zs = sigmoid(zv)
        xv = zv * zs
        dtv = dt[g]
        rate = -jnp.exp(prm[g, 7:8, 0:128])
        rv = r[g]
        rt = jnp.transpose(rv)
        last = rv[BLOCK - 1 : BLOCK, :]
        dte = spread(dt[g], ones)
        grow = spread(jnp.exp2(rv), ones)
        tail = spread(jnp.exp2(last - rv), ones)
        skip = spread(prm[g, 8:16, 0:128], ones)[0:1, :]
        w = xv * dte
        wl = w.astype(BF16)
        gl = gs.astype(BF16)
        hl = hin[0, g]
        h = hl.astype(F32)
        dh = dstate[:, cut]
        dhl = dh.astype(BF16)
        parts = []
        for p in range(HEADS // 2):
            halves, shares = [], []
            pair = slice(128 * p, 128 * (p + 1))
            wp, gpair = wl[:, pair], gl[:, pair]
            zero = jnp.zeros_like(wp)
            w_low = pltpu.roll(w[:, pair] - wp.astype(F32), 64, 1).astype(BF16)
            g_low = (gs[:, pair] - gpair.astype(F32)).astype(BF16)
            g_turn = pltpu.roll(gpair.astype(F32), 64, 1).astype(BF16)
            for n in (2 * p, 2 * p + 1):
                decay = jnp.exp2(jnp.minimum(rt[n : n + 1, :] - rv[:, n : n + 1], 0.0))
                halves.append(dot((scores * decay).astype(BF16), gpair))
                pick = (lambda a, b: jnp.where(left, a, b)) if n % 2 == 0 else (lambda a, b: jnp.where(left, b, a))
                one = jnp.concatenate([pick(wp, w_low), pick(wp, zero)], axis=1)
                two = jnp.concatenate([pick(gpair, g_turn), g_low], axis=1)
                shares.append(dot_nt(one, two) * decay)
            parts.append(jnp.where(left, halves[0], halves[1]))
            dst[...] += shares[0] + shares[1]
        dwi = jnp.concatenate(parts, axis=1)
        dws = tail * dot(b, dhl)
        dw = dwi + dws
        skipgrad = gs * xv
        diff = folded(gl.astype(F32) * (yv - skip * xv) - wl.astype(F32) * dwi, fold)
        zsum = dot((w * dws).astype(BF16), fold)
        const = folded(jnp.sum(h * dh, axis=0, keepdims=True) * grow[BLOCK - 1 : BLOCK, :] + jnp.zeros((8, COLS), F32), fold)
        da = dot_right(suffix, diff, 3) + dot_right(prefix, zsum, 3) + const[0:1, :]
        dstep = (dot((xv * dw).astype(BF16), fold) + rate * da) * jnp.where(dtv < 0.02, dtv * (1.0 - dtv * (0.5 - dtv * (1.0 / 6.0))), 1.0 - jnp.exp(-dtv))
        cat_out[:, WIDE + 128 * g : WIDE + 128 * (g + 1)] = dstep.astype(BF16)
        gx = (grow * gs).astype(BF16)
        dbc[:, STATE:] += dot_nt(gx, hl)
        dbc[:, :STATE] += dot_nt((tail * w).astype(BF16), dhl)
        dstate[:, cut] = grow[BLOCK - 1 : BLOCK, :] * dh + dot_tn(c, gx)
        dx = dte * dw + skip * gs
        dz = dx * (zs * (1.0 + zv * (1.0 - zs)))
        after = ext[BLOCK : BLOCK + 8, cut]
        ext[0:8, cut] = dz[0:8, :]
        gi = jnp.zeros((BLOCK, COLS), F32)
        for j in range(4):
            moved = dz if j == 3 else later(dz, after, 3 - j)
            gi = gi + prm[g, j : j + 1, :] * moved
            acc[g, j : j + 1, :] += jnp.sum(xi * moved, axis=0, keepdims=True)
        cat_out[:, cut] = gi.astype(BF16)
        acc[g, 4:5, :] += jnp.sum(dz, axis=0, keepdims=True)
        acc[g, 6:7, 0:128] += jnp.sum(dstep, axis=0, keepdims=True)
        acc[g, 7:8, 0:128] += jnp.sum(da * dt[g], axis=0, keepdims=True) * rate
        acc[g, 8:9, 0:128] += folded(jnp.sum(skipgrad, axis=0, keepdims=True) + jnp.zeros((8, COLS), F32), fold)[0:1, :]
    ds = jnp.where(valid, dst[...], 0.0).astype(BF16)
    dbc[:, STATE:] += dot_tn(ds, b)
    dbc[:, :STATE] += dot(ds, c)
    zb = zbc[...].astype(F32)
    sig = sigmoid(zb)
    dz = dbc[...] * (sig + zb * sig * (1.0 - sig))
    extbc[0:BLOCK, :] = dz
    bi = bc_in[...].astype(F32)
    gi = jnp.zeros((BLOCK, 256), F32)
    for j in range(4):
        moved = extbc[3 - j : 3 - j + BLOCK, :]
        gi = gi + conv_bc[j : j + 1, :] * moved
        acc_bc[j : j + 1, :] += jnp.sum(bi * moved, axis=0, keepdims=True)
    acc_bc[4:5, :] += jnp.sum(dz, axis=0, keepdims=True)
    cat_out[:, MORE:] = gi.astype(BF16)

    @pl.when(k == BLOCKS - 1)
    def _():
        rings[0].step3(wout_out)
        rings[1].step3(wgate_out)
        branch_out[...] = (tokens[...].astype(F32) + (ownb[...] + token.step3())).astype(BF16)
        for copy in net.copies:
            copy.left()


def run_backward(*args):
    rev = lambda k: BLOCKS - 1 - k
    cols = lambda n: pl.BlockSpec((BLOCK, n), lambda k: (rev(k), 0))
    small = lambda: pl.BlockSpec((GROUPS, BLOCK, 128), lambda k: (0, rev(k), 0))
    keep = lambda *s: pl.BlockSpec(s, lambda k: (0,) * len(s))
    bf = lambda *s: pltpu.VMEM(s, BF16)
    f32 = lambda *s: pltpu.VMEM(s, F32)
    return pl.pallas_call(
        backward_kernel,
        grid=(BLOCKS,),
        out_shape=[
            SHAPE((LEN, MORE + 256), BF16),
            SHAPE((GROUPS, 16, COLS), F32),
            SHAPE((8, 256), F32),
            SHAPE((256, D), BF16),
            SHAPE((96, COLS), F32),
            SHAPE((96, COLS), F32),
        ],
        in_specs=[cols(WIDE)] * 4
        + [
            pl.BlockSpec((1, GROUPS, STATE, COLS), lambda k: (rev(k), 0, 0, 0)),
            keep(GROUPS, 16, COLS),
            cols(256),
            small(),
            small(),
            keep(8, WIDE),
        ]
        + [ANY] * 5
        + [keep(256, D), cols(256), cols(256), keep(4, 256)],
        out_specs=[cols(MORE + 256), keep(GROUPS, 16, COLS), keep(8, 256), keep(256, D), keep(96, COLS), keep(96, COLS)],
        scratch_shapes=[
            f32(BLOCK + 8, WIDE),
            f32(BLOCK + 8, 256),
            f32(STATE, WIDE),
            f32(BLOCK, BLOCK),
            f32(BLOCK, 256),
            bf(2, 2, 4, 96, WIDE),
            bf(2, 2, 4, 96, WIDE),
            bf(2, 2, 4, 96, WIDE),
            bf(LEN, WIDE),
            bf(D, WIDE),
            bf(2, 2, 4, 96, LEN),
            bf(LEN, WIDE),
            bf(2, 2, 4, 96, LEN),
            f32(256, D),
        ]
        + token_scratch()
        + grid_scratch("y", COLS)
        + grid_scratch("x", COLS)
        + sems(26)
        + [pltpu.SemaphoreType.DMA((5,))],
        compiler_params=pltpu.CompilerParams(collective_id=2, has_side_effects=True, vmem_limit_bytes=ROOM),
        name="backward",
    )(*args)


def tail_kernel(
    gg, cat, wx, normed_t, normed, acc, acc_bc, wbc, gain,
    tokens_out, inner_out, bc_out, small_out,
    far_gg, far_cat, ggv, catv, wxv, ntv, nv, wv, ownb, held, got, away, dbw, heldb, gotb, small, sp0, sp1, sp2, sp3, bz, by,
    g0, g1, g2, g3, a1, a2, a3, b1, b2, b3, c1, c2, c3, send, recv, local,
):
    net = Net(send, recv)
    at = net.at
    yh, cx, cc, z, y = at["yh"], at["x"], at["c"], at["z"], at["y"]
    net.greet([(a, s) for a in ("z", "x", "y") for s in (1, -1, 2)] + [("c", 1)])
    far_rows = lambda ref: rows(ref, net.near("z", 2) * 256, 256)
    pairs = ((far_rows(cat), far_cat), (far_rows(gg), far_gg), (wx, wxv), (wbc, wv), (cat, catv), (gg, ggv), (normed_t, ntv), (normed, nv))
    loads = [pltpu.make_async_copy(src, dst, local.at[i]) for i, (src, dst) in enumerate(pairs)]
    for copy in loads:
        copy.start()
    token = TokenSum(net, (g0, g1, g2, g3))
    spans = ((0, COLS), (WIDE, 128))
    rings = (GridSum(net, "x", held, spans, (a1, a2, a3), (0, 48)), GridSum(net, "y", held, spans, (b1, b2, b3), (48, 48)))
    ring_bc = GridSum(net, "x", heldb, ((0, 128),), (c1, c2, c3))

    def product(gates, others):
        return dot_nt(gates, wxv[:, 0:WIDE]) + dot_nt(others[:, 0:MORE], wxv[:, WIDE:]) + dot_nt(others[:, MORE:], wv[...])

    def block(place):
        cut = pl.ds(pl.multiple_of(place * 256, 256), 256)
        return product(ggv[cut, :], catv[cut, :])

    def of_norm(place, grad):
        cut = pl.ds(pl.multiple_of(place * 256, 256), 256)
        return jnp.sum(grad * nv[cut, :].astype(F32), axis=0, keepdims=True)

    for copy in loads[:4]:
        copy.wait()
    far = product(far_gg[...], far_cat[...])
    g0[...] = far.astype(BF16)
    net.met()
    token.step1()
    for copy in loads[4:7]:
        copy.wait()
    grads = lambda core, cut, n: dot(ntv[core].reshape(8 * 96, LEN), catv[:, cut]).astype(BF16).reshape(2, 4, 96, n)
    for core in range(2):
        dbw[core] = grads(core, slice(MORE, MORE + 256), 256)
    crossb = net.start(dbw.at[net.other], gotb, "c")
    loads[7].wait()
    norm_part = of_norm(net.near("z", 2), far)
    for p, step in HALVES:
        out = block(net.near("z", step))
        g2[p] = out.astype(BF16)
        norm_part = norm_part + of_norm(net.near("z", step), out)
        if p == 0:
            crossb.arrived()
            heldb[...] = dbw[cc] + gotb[...]
            ring_bc.step1()
    ownb[...] = block(z)
    norm_part = (norm_part + of_norm(z, ownb[...])) / gain[...].reshape(1, D)
    small[0:16, :] = acc[0]
    small[16:32, :] = acc[1]
    small[32:48, :] = jnp.zeros((16, COLS), F32)
    for k in range(4):
        small[32 + k : 33 + k, :] = norm_part[:, k * COLS : (k + 1) * COLS]
    small[36:41, 0:256] = acc_bc[0:5, :]
    sp0[z] = small[32:48, :]
    q = net.around(sp0.at[z], sp0.at[z], "z")
    for p, _ in HALVES:
        token.folded(p)
    ring_bc.step2()
    away[...] = grads(net.other, slice(0, MORE), MORE)
    cross = net.start(away, got, "c")
    held[...] = grads(cc, slice(0, MORE), MORE)
    cross.arrived()
    held[...] += got[...]
    ring_bc.step3(by.at[yh])
    bz[z] = by[yh].astype(BF16)
    qb = net.around(bz.at[z], bz.at[z], "z")
    arrive(q)
    sp1[cx, 0:32, :] = small[0:32, :]
    sp1[cx, 32:48, :] = (sp0[0] + sp0[1]) + (sp0[2] + sp0[3])
    q = net.around(sp1.at[cx], sp1.at[cx], "x")
    for ring in rings:
        ring.step1()
    token.step2()
    arrive(q)
    sp2[y] = (sp1[0] + sp1[1]) + (sp1[2] + sp1[3])
    q = net.around(sp2.at[y], sp2.at[y], "y")
    for ring in rings:
        ring.step2()
    arrive(qb)
    by[yh] = (bz[0].astype(F32) + bz[1].astype(F32)) + (bz[2].astype(F32) + bz[3].astype(F32))
    qb = [net.start(by.at[yh], by.at[yh], "y", 2)]
    arrive(q)
    sp3[cc] = (sp2[0] + sp2[1]) + (sp2[2] + sp2[3])
    q = [net.start(sp3.at[cc], sp3.at[cc], "c")]
    for ring in rings:
        ring.step3(inner_out)
    arrive(q)
    small_out[...] = sp3[0] + sp3[1]
    tokens_out[...] = token.step3() + ownb[...]
    arrive(qb)
    bc_out[:, 0:128] = by[0]
    bc_out[:, 128:256] = by[1]
    net.finish()


def run_tail(*args):
    bf = lambda *s: pltpu.VMEM(s, BF16)
    f32 = lambda *s: pltpu.VMEM(s, F32)
    return pl.pallas_call(
        tail_kernel,
        out_shape=[
            SHAPE((256, D), F32),
            SHAPE((96, COLS + 128), F32),
            SHAPE((96, 256), F32),
            SHAPE((48, COLS), F32),
        ],
        in_specs=[ANY] * 5 + [VMEM, VMEM, ANY, VMEM],
        out_specs=[VMEM] * 4,
        scratch_shapes=[
            bf(256, WIDE),
            bf(256, MORE + 256),
            bf(LEN, WIDE),
            bf(LEN, MORE + 256),
            bf(D, PROJ),
            bf(2, 2, 4, 96, LEN),
            bf(LEN, D),
            bf(D, 256),
            f32(256, D),
            bf(2, 4, 96, MORE),
            bf(2, 4, 96, MORE),
            bf(2, 4, 96, MORE),
            bf(2, 2, 4, 96, 256),
            bf(2, 4, 96, 256),
            bf(2, 4, 96, 256),
            f32(48, COLS),
            f32(4, 16, COLS),
            f32(4, 48, COLS),
            f32(4, 48, COLS),
            f32(2, 48, COLS),
            bf(4, 96, 128),
            f32(2, 96, 128),
        ]
        + token_scratch()
        + grid_scratch("x", COLS + 128, 48)
        + grid_scratch("y", COLS + 128, 48)
        + grid_scratch("x", 128)
        + sems(64)
        + [pltpu.SemaphoreType.DMA((8,))],
        compiler_params=pltpu.CompilerParams(collective_id=3, has_side_effects=True, vmem_limit_bytes=ROOM),
        name="tail",
    )(*args)


def finish_kernel(grad, tokens, cot, branch, norm_gain, inner, bc, small, gate, wout, tokens_out, branch_out, inner_out, bc_out, gate_out, wout_out, step_out, norm, conv, bias, conv_bc, bias_bc, step_bias, decay, skip, gain):
    v = tokens[...].astype(F32)
    root = lax.rsqrt(jnp.mean(v * v, axis=1, keepdims=True) + EPS)
    scaled = grad[...] * norm_gain[...].reshape(1, D)
    tokens_out[...] = cot[...].astype(F32) + root * scaled - v * (root * root * root) * jnp.mean(scaled * v, axis=1, keepdims=True)
    branch_out[...] = branch[...]

    @pl.when(pl.program_id(0) == 0)
    def _():
        inner_out[...] = inner[:, :COLS]
        bc_out[...] = bc[...]
        gate_out[...] = gate[...]
        wout_out[...] = wout[...]
        step_out[...] = jnp.transpose(jnp.concatenate([inner[:, COLS:], jnp.zeros((32, 128), F32)], axis=0))[0:HEADS, 0:96]
        norm[...] = jnp.concatenate([small[32 + k : 33 + k, :] for k in range(4)], axis=1).reshape(D)
        conv_bc[...] = small[36:40, 0:256]
        bias_bc[...] = small[40:41, 0:256].reshape(256)
        mine = small[pl.ds(pl.multiple_of(lax.axis_index("yh") * 16, 8), 16), :]
        conv[...] = mine[0:4, :]
        bias[...] = mine[4:5, :].reshape(COLS)
        gain[...] = mine[5:6, :].reshape(COLS)
        step_bias[...] = mine[6:7, 0:HEADS].reshape(HEADS)
        decay[...] = mine[7:8, 0:HEADS].reshape(HEADS)
        skip[...] = mine[8:9, 0:HEADS].reshape(HEADS)


def run_finish(*args):
    f32 = lambda *s: SHAPE(s, F32)
    strip = lambda: pl.BlockSpec((128, D), lambda k: (k, 0))
    whole = lambda *s: pl.BlockSpec(s, lambda k: (0,) * len(s))
    shapes = (
        (96, COLS), (96, 256), (96, COLS), (96, COLS), (HEADS, 96), (D,), (4, COLS), (COLS,), (4, 256), (256,), (HEADS,), (HEADS,), (HEADS,), (COLS,),
    )
    return pl.pallas_call(
        finish_kernel,
        grid=(2,),
        out_shape=[f32(256, D), SHAPE((256, D), BF16)] + [f32(*s) for s in shapes],
        in_specs=[strip(), strip(), strip(), strip()]
        + [whole(*s) for s in ((D,), (96, COLS + 128), (96, 256), (48, COLS), (96, COLS), (96, COLS))],
        out_specs=[strip(), strip()] + [whole(*s) for s in shapes],
        compiler_params=pltpu.CompilerParams(vmem_limit_bytes=ROOM),
        name="finish",
    )(*args)


def shards(tokens, norm_gain, w_gate, w_inner, w_bc, w_step, conv_inner, bias_inner, conv_bc, bias_bc, step_bias, decay_log, skip_gain, gate_gain, w_out, cotangent):
    (
        inner, zin, y, hin, dt, r, bc, bc_in, zbc, normed_t, gains, mixed, gs, gg, cot_t, normed, wx, wout, wbc, prm,
    ) = run_front(
        tokens, norm_gain, w_gate, w_inner, w_out, w_bc, w_step.T, conv_inner, bias_inner, gate_gain, step_bias, decay_log,
        skip_gain, conv_bc, bias_bc, cotangent,
    )
    wx, wout, wbc = wx.reshape(D, PROJ), wout.reshape(D, WIDE), wbc.reshape(D, 256)
    cat, acc, acc_bc, output, wout_grad, gate_grad = run_backward(
        gs, inner, zin, y, hin, prm, bc, dt, r, gains, mixed, wout, cot_t, gg, normed_t, tokens, zbc, bc_in, conv_bc
    )
    grad, inner_grad, bc_grad, small = run_tail(gg, cat, wx, normed_t, normed, acc, acc_bc, wbc, norm_gain)
    (
        tokens_grad, output, inner_grad, bc_grad, gate_grad, wout_grad, step_grad,
        norm, conv, bias, conv_bc_grad, bias_bc_grad, step_bias_grad, decay, skip, gate_gain_grad,
    ) = run_finish(grad, tokens, cotangent, output, norm_gain, inner_grad, bc_grad, small, gate_grad, wout_grad)
    return (
        output, tokens_grad, norm, gate_grad, inner_grad, bc_grad, step_grad.T, conv, bias, conv_bc_grad,
        bias_bc_grad, step_bias_grad, decay, skip, gate_gain_grad, wout_grad,
    )


def solution(mesh):
    fine = Mesh(mesh.devices.reshape(2, 4, 2, 2, 4), AXES)
    dp, tensor = ("yl", "x", "c"), ("yh", "z")
    tokens, weight = P(dp + tensor, None), P(dp, tensor)
    heads, shared = P(tensor), P()
    return jax.shard_map(
        shards,
        mesh=fine,
        in_specs=(
            tokens, shared, weight, weight, P(dp, None), weight, P(None, tensor), heads,
            shared, shared, heads, heads, heads, heads, weight, tokens,
        ),
        out_specs=(
            tokens, tokens, shared, weight, weight, P(dp, None), weight, P(None, tensor), heads,
            shared, shared, heads, heads, heads, heads, weight,
        ),
        check_vma=False,
    )
```
